128 devices in a mesh: seq: 64 (over x, y, z), mlp: 2 (over core).
Axes of the slice: x: 4, y: 4, z: 4, core: 2. Of those that a mesh axis runs over, the one named last changes fastest.
Arguments:
- inputs: bfloat16 [8192, 2048], P(('seq', 'mlp')), may hold values from -6 to 6
- offsets: int32 [8192], P('seq'), may hold values from 0 to 4095, as said below
- norm1_gain: float32 [2048], replicated, may hold values from 0.5 to 1.5
- query_weight: bfloat16 [2048, 2048], P('seq', 'mlp'), may hold values from -0.125 to 0.125
- key_weight: bfloat16 [2048, 2048], P('seq', 'mlp'), may hold values from -0.125 to 0.125
- value_weight: bfloat16 [2048, 2048], P('seq', 'mlp'), may hold values from -0.125 to 0.125
- gate_weight: bfloat16 [2048, 2048], P('seq', 'mlp'), may hold values from -0.125 to 0.125
- out_weight: bfloat16 [2048, 2048], P('mlp', 'seq'), may hold values from -0.1875 to 0.1875
- low_down: bfloat16 [2048, 16], replicated, may hold values from -0.125 to 0.125
- low_up: bfloat16 [16, 256], replicated, may hold values from -1.5 to 1.5
- forget_bias: float32 [256], replicated, may hold values from 1.1 to 8.4
- head_gain: float32 [512], replicated, may hold values from 0.5 to 1.5
- norm2_gain: float32 [2048], replicated, may hold values from 0.5 to 1.5
- ffn_gate: bfloat16 [2048, 5632], P('seq', 'mlp'), may hold values from -0.125 to 0.125
- ffn_up: bfloat16 [2048, 5632], P('seq', 'mlp'), may hold values from -0.125 to 0.125
- ffn_down: bfloat16 [2048, 5632], P('seq', 'mlp'), may hold values from -0.078125 to 0.078125
- cotangent: bfloat16 [8192, 2048], P(('seq', 'mlp')), may hold values from -6 to 6
Outputs:
- output: bfloat16 [8192, 2048], P(('seq', 'mlp'))
- d_inputs: float32 [8192, 2048], P(('seq', 'mlp'))
- d_norm1_gain: float32 [2048], replicated
- d_query_weight: float32 [2048, 2048], P('seq', 'mlp')
- d_key_weight: float32 [2048, 2048], P('seq', 'mlp')
- d_value_weight: float32 [2048, 2048], P('seq', 'mlp')
- d_gate_weight: float32 [2048, 2048], P('seq', 'mlp')
- d_out_weight: float32 [2048, 2048], P('mlp', 'seq')
- d_low_down: float32 [2048, 16], replicated
- d_low_up: float32 [16, 256], replicated
- d_forget_bias: float32 [256], replicated
- d_head_gain: float32 [512], replicated
- d_norm2_gain: float32 [2048], replicated
- d_ffn_gate: float32 [2048, 5632], P('seq', 'mlp')
- d_ffn_up: float32 [2048, 5632], P('seq', 'mlp')
- d_ffn_down: float32 [2048, 5632], P('seq', 'mlp')
The draws below stay inside these ranges and needn't reach their ends.
Inputs may be any that keep to these rules, and one draw needn't show every extreme that they name: offsets rise by one from token to token within a sequence and restart at 0 where a new sequence begins; the first token has offset 0; a sequence has at most 4096 tokens, and one has exactly 4096.
All inputs are finite; a program needn't handle non-finite values.
Results may differ from the reference program's by a relative error of at most 0.023.
Values may be sent and summed in bfloat16 or wider, within the bound.
A program may use at most 384 MiB of HBM per device.

```python
import math
import jax
import jax.numpy as jnp
from jax import lax

D = 2048
HEADS = 4
DK = 512
SLOTS = 64
FF = 5632
RANK = 16
GROUP = 64
SEQ_LEN = 4096
TOK_DEV = 64
TOKENS = 8192


def draw_offsets(key, part):
    key = jax.random.fold_in(key, 11)
    place = jnp.arange(TOKENS, dtype=jnp.int32)
    shift_key, split_key = jax.random.split(key)
    if TOKENS > SEQ_LEN:
        longest = SEQ_LEN
        half = longest // 2
        offset = jax.random.randint(shift_key, (), 0, half, dtype=jnp.int32)
        shifted = place + offset
        window = shifted // longest
        inner = shifted % longest
        windows = (TOKENS + longest) // longest + 1
        flags = jax.random.randint(split_key, (windows,), 0, 2, dtype=jnp.int32)
        centre = (TOKENS // 2 + offset) // longest
        flags = jnp.where(jnp.arange(windows, dtype=jnp.int32) == centre, 0, flags)
        begin = flags[window] * (inner >= half).astype(jnp.int32) * half
        return jnp.minimum(inner - begin, place)
    longest = TOKENS - TOK_DEV
    start = jax.random.randint(shift_key, (), 0, TOK_DEV + 1, dtype=jnp.int32)
    inside = place - start
    after = place - start - longest
    return jnp.where(place < start, place, jnp.where(place < start + longest, inside, after))


def draw_forget_bias(key, part):
    key = jax.random.fold_in(key, 7)
    longest = min(SEQ_LEN, TOKENS)
    pick_key, time_key = jax.random.split(key)
    chooser = jax.random.uniform(pick_key, (HEADS * SLOTS,), jnp.float32)
    lower = math.log(30.0) + 0.0 * chooser
    upper = math.log(8.0 * longest)
    level = jax.random.uniform(time_key, (HEADS * SLOTS,), jnp.float32)
    keep_time = jnp.exp(lower + (upper - lower) * level)
    return -jnp.log(jnp.expm1(8.0 / keep_time))


def steps_of(rng, extent, shards, smallest, largest):
    def one(position, shards_of):
        draws = jax.random.uniform(jax.random.fold_in(jax.random.fold_in(rng, 6), position), (shards_of,), jnp.float32, smallest / len(shards), largest / len(shards))
        return jnp.repeat(jnp.exp(draws), extent[position] // shards_of).reshape((-1,) + (1,) * (len(extent) - position - 1))

    loudness = one(*shards[0])
    for cut in shards[1:]:
        loudness = loudness * one(*cut)
    return loudness


def scatter_about(stream_key, extent, deviation, bound, cuts=(), kind=jnp.bfloat16):
    level = steps_of(stream_key, extent, cuts, -0.22, 0.18) if cuts else 1.0
    entries = jax.random.normal(stream_key, extent, jnp.float32) * deviation * level
    return jnp.minimum(jnp.maximum(entries, -bound), bound).astype(kind)


def setup_inputs(seed: int = 0) -> dict:
    seeds = jax.random.split(jax.random.key(seed), 18)
    inputs = scatter_about(seeds[0], (TOKENS, D), 1.0, 6.0, ((0, 128),))
    offsets = draw_offsets(jax.random.fold_in(seeds[17], 71), 0)
    norm1_gain = jnp.clip(1.0 + 0.1 * jax.random.normal(seeds[2], (D,), jnp.float32), 0.5, 1.5)
    query_weight = scatter_about(seeds[3], (D, D), D ** -0.5, 0.125, ((0, 64), (1, 2)))
    key_weight = scatter_about(seeds[4], (D, D), D ** -0.5, 0.125, ((0, 64), (1, 2)))
    value_weight = scatter_about(seeds[5], (D, D), D ** -0.5, 0.125, ((0, 64), (1, 2)))
    gate_weight = scatter_about(seeds[6], (D, D), D ** -0.5, 0.125, ((0, 64), (1, 2)))
    out_weight = scatter_about(seeds[7], (D, D), (D // 2) ** -0.5, 0.1875, ((0, 2), (1, 64)))
    low_down = scatter_about(seeds[8], (D, RANK), D ** -0.5, 0.125)
    low_up = scatter_about(seeds[9], (RANK, HEADS * SLOTS), RANK ** -0.5, 1.5)
    forget_bias = draw_forget_bias(jax.random.fold_in(seeds[17], 71), 0)
    head_gain = jnp.clip(1.0 + 0.1 * jax.random.normal(seeds[11], (DK,), jnp.float32), 0.5, 1.5)
    norm2_gain = jnp.clip(1.0 + 0.1 * jax.random.normal(seeds[12], (D,), jnp.float32), 0.5, 1.5)
    ffn_gate = scatter_about(seeds[13], (D, FF), D ** -0.5, 0.125, ((0, 64), (1, 2)))
    ffn_up = scatter_about(seeds[14], (D, FF), D ** -0.5, 0.125, ((0, 64), (1, 2)))
    ffn_down = scatter_about(seeds[15], (D, FF), FF ** -0.5, 0.078125, ((0, 64), (1, 2)))
    cotangent = scatter_about(seeds[16], (TOKENS, D), 1.0, 6.0, ((0, 128),))
    return dict(inputs=inputs, offsets=offsets, norm1_gain=norm1_gain, query_weight=query_weight, key_weight=key_weight, value_weight=value_weight, gate_weight=gate_weight, out_weight=out_weight, low_down=low_down, low_up=low_up, forget_bias=forget_bias, head_gain=head_gain, norm2_gain=norm2_gain, ffn_gate=ffn_gate, ffn_up=ffn_up, ffn_down=ffn_down, cotangent=cotangent)


EPS = 1e-06
GATE_NORMALIZER = 8.0
LOGIT_SCALING = 0.125
HIGH_PRECISION_MODE = lax.Precision.HIGHEST

@jax.custom_vjp
def low(v):
    return lax.optimization_barrier(v.astype(jnp.bfloat16)).astype(jnp.float32)

@jax.custom_vjp
def low_back(v):
    return v

def low_keep(v):
    return (low(v), None)

def low_pass(kept, grad):
    return (grad,)

def back_keep(v):
    return (v, None)

def back_low(kept, grad):
    return (low(grad),)
low.defvjp(low_keep, low_pass)
low_back.defvjp(back_keep, back_low)

def rms_scale(value_vectors, gain):
    return value_vectors * lax.rsqrt(lax.optimization_barrier(jnp.mean(value_vectors * value_vectors, axis=-1, keepdims=True)) + EPS) * gain

def product(left, right):
    return jnp.dot(left, right, precision=HIGH_PRECISION_MODE, preferred_element_type=jnp.float32)

def advance(key_vectors, value_vectors, decay_log, offsets, key_slot_state, value_slot_state):
    length = offsets.shape[0]
    place = jnp.arange(length, dtype=jnp.int32)
    cumulative_decay = jnp.cumsum(decay_log, axis=0)
    write = -jnp.expm1(decay_log)
    final = offsets[length - 1]
    keep = (final > length - 1).astype(jnp.float32)
    tail = (final - offsets == length - 1 - place).astype(jnp.float32)
    ending_state = jnp.exp(cumulative_decay[length - 1][None] - cumulative_decay) * write * tail[:, None, None]
    decay_factor = keep * jnp.exp(cumulative_decay[length - 1])
    updated_key_state = decay_factor[:, :, None] * key_slot_state + jnp.einsum('aqo,aqf->qof', ending_state, key_vectors, precision=HIGH_PRECISION_MODE)
    updated_value_state = decay_factor[:, :, None] * value_slot_state + jnp.einsum('aqo,aqf->qof', ending_state, value_vectors, precision=HIGH_PRECISION_MODE)
    return (updated_key_state, updated_value_state, decay_factor)

def slot_group(query_vectors, key_vectors, value_vectors, logits, offsets, key_slot_state, value_slot_state):
    decay_log = jax.nn.log_sigmoid(logits) / GATE_NORMALIZER
    length = offsets.shape[0]
    place = jnp.arange(length, dtype=jnp.int32)
    cumulative_decay = jnp.cumsum(decay_log, axis=0)
    write = -jnp.expm1(decay_log)
    carried_over = (offsets > place).astype(jnp.float32)
    causal = (place[:, None] >= place[None, :]) & (offsets[:, None] - offsets[None, :] == place[:, None] - place[None, :])
    spread = cumulative_decay[:, None] - cumulative_decay[None, :]
    weights = jnp.exp(jnp.where(causal[:, :, None, None], spread, -1e+30)) * write[None]
    affinity = jnp.einsum('thd,ihd->thi', query_vectors, key_vectors, precision=HIGH_PRECISION_MODE) * LOGIT_SCALING
    scores = jnp.einsum('thi,tihm->thm', affinity, weights, precision=HIGH_PRECISION_MODE)
    earlier_tokens = jnp.einsum('vbn,bgn->vbg', query_vectors, key_slot_state, precision=HIGH_PRECISION_MODE) * LOGIT_SCALING
    scores = scores + carried_over[:, None, None] * jnp.exp(cumulative_decay) * earlier_tokens
    slot_probabilities = jax.nn.softmax(scores, axis=-1)
    mixing = jnp.einsum('thm,tihm->thi', slot_probabilities, weights, precision=HIGH_PRECISION_MODE)
    output = jnp.einsum('thi,ihd->thd', mixing, value_vectors, precision=HIGH_PRECISION_MODE)
    output = output + carried_over[:, None, None] * jnp.einsum('gnw,nwv->gnv', slot_probabilities * jnp.exp(cumulative_decay), value_slot_state, precision=HIGH_PRECISION_MODE)
    updated_key_state, updated_value_state, decay_factor = advance(key_vectors, value_vectors, decay_log, offsets, key_slot_state, value_slot_state)
    return (output, updated_key_state, updated_value_state)

def slot_attention(query_vectors, key_vectors, value_vectors, logits, offsets):
    count = TOKENS // GROUP
    blocks = (query_vectors.reshape(count, GROUP, HEADS, DK), key_vectors.reshape(count, GROUP, HEADS, DK), value_vectors.reshape(count, GROUP, HEADS, DK), logits.reshape(count, GROUP, HEADS, SLOTS), offsets.reshape(count, GROUP))

    def step(carry, block):
        output, updated_key_state, updated_value_state = slot_group(block[0], block[1], block[2], block[3], block[4], carry[0], carry[1])
        return ((updated_key_state, updated_value_state), output)
    start = (jnp.zeros((HEADS, SLOTS, DK), jnp.float32), jnp.zeros((HEADS, SLOTS, DK), jnp.float32))
    _, outputs = lax.scan(jax.checkpoint(step), start, blocks)
    return outputs.reshape(TOKENS, HEADS, DK)

def layer(resid, norm1_gain, query_weight, key_weight, value_weight, gate_weight, out_weight, low_down, low_up, forget_bias, head_gain, norm2_gain, ffn_gate, ffn_up, ffn_down, offsets):
    first = low(rms_scale(resid, norm1_gain))
    query_vectors = low(low_back(product(first, query_weight)))
    key_rows = low(low_back(product(first, key_weight)))
    value_rows = low(low_back(product(first, value_weight)))
    lowrank = product(first, low_down)
    logits = low(product(lowrank, low_up) + forget_bias)
    mixed = slot_attention(query_vectors.reshape(TOKENS, HEADS, DK), key_rows.reshape(TOKENS, HEADS, DK), value_rows.reshape(TOKENS, HEADS, DK), logits.reshape(TOKENS, HEADS, SLOTS), offsets)
    mixed = low_back(mixed)
    headnorm = rms_scale(mixed, head_gain).reshape(TOKENS, D)
    gate_lin = low_back(product(first, gate_weight))
    branch = low(headnorm * jax.nn.silu(gate_lin))
    resid1 = resid + low_back(product(branch, out_weight))
    second = low(rms_scale(resid1, norm2_gain))
    act_gate = low_back(product(second, ffn_gate))
    act_up = low_back(product(second, ffn_up))
    hidden = low(jax.nn.silu(act_gate) * act_up)
    return resid1 + product(hidden, ffn_down.T)

def reference(inputs, offsets, norm1_gain, query_weight, key_weight, value_weight, gate_weight, out_weight, low_down, low_up, forget_bias, head_gain, norm2_gain, ffn_gate, ffn_up, ffn_down, cotangent):
    floats = tuple((item.astype(jnp.float32) for item in (inputs, norm1_gain, query_weight, key_weight, value_weight, gate_weight, out_weight, low_down, low_up, forget_bias, head_gain, norm2_gain, ffn_gate, ffn_up, ffn_down)))

    def forward(*params):
        return layer(*params, offsets)
    result, pullback = jax.vjp(forward, *floats)
    grads = pullback(cotangent.astype(jnp.float32))
    return (result.astype(jnp.bfloat16), grads[0], grads[1], grads[2], grads[3], grads[4], grads[5], grads[6], grads[7], grads[8], grads[9], grads[10], grads[11], grads[12], grads[13], grads[14])
```

```python
import functools

import jax
import jax.numpy as jnp
from jax import lax
from jax.experimental import pallas as pl
from jax.experimental.pallas import tpu as pltpu
from jax.sharding import Mesh
from jax.sharding import PartitionSpec as P

DK = 512
SLOTS = 64
CHUNK = 64
HALF = 256
UNITS = 704
UNITS_PAD = 768
REACH = 8
EPS = 1e-06
SCALE = 0.125
BF = jnp.bfloat16
F32 = jnp.float32
HIGH = lax.Precision.HIGHEST
MESH = pl.DeviceIdType.MESH
ANY = pl.BlockSpec(memory_space=pl.ANY)
VMEM = pl.BlockSpec(memory_space=pltpu.VMEM)
DMA = pltpu.SemaphoreType.DMA
MIX = 5 * HALF
FFN = 3 * UNITS_PAD


def dot(left, right, dims=((1,), (0,)), precision=None):
    return lax.dot_general(
        left, right, (dims, ((), ())), precision=precision, preferred_element_type=F32
    )


def nt(left, right, precision=None):
    return dot(left, right, ((1,), (1,)), precision)


def tn(left, right, precision=None):
    return dot(left, right, ((0,), (0,)), precision)


def here():
    return tuple(lax.axis_index(a) for a in ("x", "y", "z", "c"))


def wrap(v, n=4):
    return lax.rem(v + n, n)


def greet(peers):
    barrier = pltpu.get_barrier_semaphore()
    for peer in peers:
        pl.semaphore_signal(barrier, inc=1, device_id=peer, device_id_type=MESH)
    pl.semaphore_wait(barrier, len(peers))


def push(src, dst, send, recv, peer):
    copy = pltpu.make_async_remote_copy(
        src_ref=src, dst_ref=dst, send_sem=send, recv_sem=recv, device_id=peer, device_id_type=MESH
    )
    copy.start()
    return copy


def remote_call(kernel, collective_id, operands, out_shape, in_specs, out_specs, scratch):
    return pl.pallas_call(
        kernel,
        out_shape=out_shape,
        in_specs=in_specs,
        out_specs=out_specs,
        scratch_shapes=scratch,
        compiler_params=pltpu.CompilerParams(
            collective_id=collective_id, has_side_effects=True, vmem_limit_bytes=56 * 2**20
        ),
    )(*operands)


def spread_axes(w_ref, sems, cols):
    x, y, z, c = here()
    near_s, near_r, far_s, far_r = sems
    first, second = pl.ds(0, cols // 2), pl.ds(cols // 2, cols // 2)
    sent = []
    for d in range(1, 4):
        block = w_ref.at[x, y, :, first]
        sent.append(
            push(block, block, near_s.at[0, d - 1], near_r.at[0, d - 1], (x, wrap(y + d), z, c))
        )
        block = w_ref.at[x, y, :, second]
        sent.append(
            push(block, block, near_s.at[1, d - 1], near_r.at[1, d - 1], (wrap(x + d), y, z, c))
        )
    for k in range(4):
        row, col = wrap(x - k), wrap(y - k)
        one = w_ref.at[x, col, :, first]
        two = w_ref.at[row, y, :, second]
        if k > 0:
            sent[2 * (k - 1)].wait_recv()
            sent[2 * (k - 1) + 1].wait_recv()
        for d in range(1, 4):
            sent.append(
                push(one, one, far_s.at[0, k, d - 1], far_r.at[0, k, d - 1], (wrap(x + d), y, z, c))
            )
            sent.append(
                push(two, two, far_s.at[1, k, d - 1], far_r.at[1, k, d - 1], (x, wrap(y + d), z, c))
            )
    return sent


def spread_sems():
    return [DMA((2, 3)), DMA((2, 3)), DMA((2, 4, 3)), DMA((2, 4, 3))]


def rows_start(src, out, sems):
    x, y, z, c = here()
    hop_s, hop_r, pair_s, pair_r, own = sems
    mine = pltpu.make_async_copy(src, out.at[c, z], own)
    mine.start()
    hops = [
        push(src, out.at[c, z], hop_s.at[d - 1], hop_r.at[d - 1], (x, y, wrap(z + d), c))
        for d in range(1, 4)
    ]
    pairs = [push(src, out.at[c, z], pair_s.at[0], pair_r.at[0], (x, y, z, 1 - c))]
    return mine, hops, pairs


def rows_finish(started, out, sems):
    x, y, z, c = here()
    hop_s, hop_r, pair_s, pair_r, own = sems
    mine, hops, pairs = started
    for d in range(1, 4):
        hops[d - 1].wait_recv()
        block = out.at[c, wrap(z - d)]
        pairs.append(push(block, block, pair_s.at[d], pair_r.at[d], (x, y, z, 1 - c)))
    mine.wait()
    for copy in hops:
        copy.wait_send()
    for copy in pairs:
        copy.wait()


def rows_sems():
    return [DMA((3,)), DMA((3,)), DMA((4,)), DMA((4,)), DMA(())]


def group_peers():
    x, y, z, c = here()
    return [(x, y, wrap(z + d), k) for d in range(1, 4) for k in range(2)] + [(x, y, z, 1 - c)]


def row_peers():
    x, y, z, c = here()
    return [(x, y, wrap(z + d), c) for d in range(1, 4)] + [(x, y, z, 1 - c)]


def plane_peers():
    x, y, z, c = here()
    return [(wrap(x + d), y, z, c) for d in range(1, 4)] + [
        (x, wrap(y + d), z, c) for d in range(1, 4)
    ]


def gather_kernel(wm, wf, rows_a, rows_b, wide_m, wide_f, all_a, all_b, *sems):
    x, y, z, c = here()
    a_sems, b_sems, m_sems, f_sems = sems[0:5], sems[5:10], sems[10:14], sems[14:18]
    m_send, m_recv, f_send, f_recv, f_own = sems[18:23]
    greet(group_peers() + plane_peers())
    m_sent = []
    for j in range(2):
        for k in range(2):
            to = 2 * c + j
            dst = wide_m.at[x, y, pl.ds(z * 32, 32), :]
            same = jnp.logical_and(to == z, c == k)
            copy = pltpu.make_async_remote_copy(
                src_ref=wm.at[j, k],
                dst_ref=dst,
                send_sem=m_send.at[j, k],
                recv_sem=m_recv.at[z],
                device_id=(x, y, to, k),
                device_id_type=MESH,
            )

            @pl.when(same)
            def _():
                pltpu.make_async_copy(wm.at[j, k], dst, m_recv.at[z]).start()

            @pl.when(jnp.logical_not(same))
            def _():
                copy.start()

            m_sent.append((same, copy))
    f_mine = pltpu.make_async_copy(wf.at[z], wide_f.at[x, y, pl.ds(z * 32, 32), :], f_own)
    f_mine.start()
    f_sent = [
        push(
            wf.at[wrap(z + d)],
            wide_f.at[x, y, pl.ds(z * 32, 32), :],
            f_send.at[d - 1],
            f_recv.at[d - 1],
            (x, y, wrap(z + d), c),
        )
        for d in range(1, 4)
    ]
    a_started = rows_start(rows_a, all_a, a_sems)
    for s in range(4):
        dst = wide_m.at[x, y, pl.ds(s * 32, 32), :]
        pltpu.make_async_copy(wm.at[0, 0], dst, m_recv.at[s]).wait()
    m_spread = spread_axes(wide_m, m_sems, MIX)
    f_mine.wait()
    for copy in f_sent:
        copy.wait_recv()
    b_started = rows_start(rows_b, all_b, b_sems)
    f_spread = spread_axes(wide_f, f_sems, FFN)
    rows_finish(a_started, all_a, a_sems)
    rows_finish(b_started, all_b, b_sems)
    for same, copy in m_sent:

        @pl.when(jnp.logical_not(same))
        def _():
            copy.wait_send()

    for copy in f_sent:
        copy.wait_send()
    for spread in (m_spread, f_spread):
        for copy in spread[:6]:
            copy.wait_send()
        for copy in spread[6:]:
            copy.wait()


def gather_all(wm, wf, rows_a, rows_b, collective_id):
    return remote_call(
        gather_kernel,
        collective_id,
        (wm, wf, rows_a, rows_b),
        [
            jax.ShapeDtypeStruct((4, 4, 128, MIX), BF),
            jax.ShapeDtypeStruct((4, 4, 128, FFN), BF),
            jax.ShapeDtypeStruct((2, 4, 64, 2048), BF),
            jax.ShapeDtypeStruct((2, 4, 64, 2048), BF),
        ],
        [ANY] * 4,
        [ANY] * 4,
        rows_sems()
        + rows_sems()
        + spread_sems()
        + spread_sems()
        + [DMA((2, 2)), DMA((4,)), DMA((3,)), DMA((3,)), DMA(())],
    )


def rows_kernel(src, out, *sems):
    greet(row_peers())
    rows_finish(rows_start(src, out, sems), out, sems)


def gather_rows(rows, collective_id):
    return remote_call(
        rows_kernel,
        collective_id,
        (rows,),
        jax.ShapeDtypeStruct((2, 4, 64, 2048), BF),
        [ANY],
        ANY,
        rows_sems(),
    ).reshape(512, 2048)


def sum_rows_kernel(count, *refs):
    parts, outs = refs[:count], refs[count : 2 * count]
    theirs, sending, landed, pair_s, pair_r, hop_s, hop_r = refs[2 * count :]
    x, y, z, c = here()
    greet(row_peers())
    pairs = []
    for n in range(count):
        for k in range(4):
            to = wrap(z + 1 + k)
            pairs.append(
                push(
                    parts[n].at[1 - c, to],
                    theirs.at[n, k],
                    pair_s.at[n, k],
                    pair_r.at[n, k],
                    (x, y, z, 1 - c),
                )
            )
    hops = []
    for n in range(count):
        for k in range(3):
            to = wrap(z + 1 + k)
            pairs[4 * n + k].wait_recv()
            both = parts[n][c, to].astype(F32) + theirs[n, k].astype(F32)
            sending[n, k] = both.astype(BF)
            hops.append(
                push(sending.at[n, k], landed.at[n, k], hop_s.at[n, k], hop_r.at[n, k], (x, y, to, c))
            )
    for n in range(count):
        pairs[4 * n + 3].wait_recv()
        outs[n][...] = parts[n][c, z].astype(F32) + theirs[n, 3].astype(F32)
    for n in range(count):
        for k in range(3):
            hops[3 * n + k].wait_recv()
            outs[n][...] += landed[n, k].astype(F32)
    for copy in pairs + hops:
        copy.wait_send()


def sum_rows(parts, collective_id):
    count = len(parts)
    return remote_call(
        functools.partial(sum_rows_kernel, count),
        collective_id,
        [part.astype(BF).reshape(2, 4, 64, 2048) for part in parts],
        [jax.ShapeDtypeStruct((64, 2048), F32)] * count,
        [VMEM] * count,
        [VMEM] * count,
        [
            pltpu.VMEM((count, 4, 64, 2048), BF),
            pltpu.VMEM((count, 3, 64, 2048), BF),
            pltpu.VMEM((count, 3, 64, 2048), BF),
            DMA((count, 4)),
            DMA((count, 4)),
            DMA((count, 3)),
            DMA((count, 3)),
        ],
    )


def swap_kernel(src, out, own, send, recv):
    x, y, z, c = here()
    greet([(x, y, z, 1 - c)])
    copy = push(src.at[1 - c], out.at[c], send, recv, (x, y, z, 1 - c))
    mine = pltpu.make_async_copy(src.at[c], out.at[c], own)
    mine.start()
    mine.wait()
    copy.wait()


def swap(value, collective_id):
    return remote_call(
        swap_kernel,
        collective_id,
        (value,),
        jax.ShapeDtypeStruct(value.shape, value.dtype),
        [ANY],
        ANY,
        [DMA(()), DMA(()), DMA(())],
    )


def scan_kernel(
    back, ends, out, every, total, sending, landed, entry, own, pair_s, pair_r, far_s, far_r, last_s, last_r
):
    x, y, z, c = here()
    group = x * 4 + y
    sign = -1 if back else 1

    def member(d):
        at = lax.rem(group + sign * d + 32, 16)
        return (at // 4, lax.rem(at, 4), z, c)

    partner = (x, y, z, 1 - c)
    barrier = pltpu.get_barrier_semaphore()
    pl.semaphore_signal(barrier, inc=1, device_id=partner, device_id_type=MESH)
    for d in range(1, REACH + 1):
        pl.semaphore_signal(barrier, inc=1, device_id=member(-d), device_id_type=MESH)
    pl.semaphore_wait(barrier, REACH + 1)
    pair = push(ends, every.at[c], pair_s, pair_r, partner)
    mine = pltpu.make_async_copy(ends, every.at[c], own)
    mine.start()
    mine.wait()
    pair.wait()
    half = pl.ds(pl.multiple_of(c * DK, DK), DK)
    order = [(n, k) for n in range(4) for k in range(2)]
    if back:
        order = order[::-1]

    def factor(k, n, width):
        return jnp.concatenate([every[k, n, :, 1024:1152]] * (width // 128), axis=1)

    n, k = (order[0][0], order[0][1])
    state = every[k, n, :, half]
    decay = every[k, n, :, 1024:1152]
    for n, k in order[1:]:
        state = factor(k, n, DK) * state + every[k, n, :, half]
        decay = every[k, n, :, 1024:1152] * decay
    sending[:, 0:512] = state.astype(BF)
    high = decay.astype(BF)
    sending[:, 512:640] = high
    sending[:, 640:768] = (decay - high.astype(F32)).astype(BF)
    far = [
        push(sending, landed.at[d - 1], far_s.at[d - 1], far_r.at[d - 1], member(d))
        for d in range(1, REACH + 1)
    ]
    total[...] = jnp.zeros_like(total)
    for d in range(REACH, 0, -1):
        far[d - 1].wait_recv()
        valid = (group + d < 16) if back else (group >= d)
        keep = landed[d - 1, :, 512:640].astype(F32) + landed[d - 1, :, 640:768].astype(F32)
        keep = jnp.concatenate([keep] * 4, axis=1)
        fresh = keep * total[...] + landed[d - 1, :, 0:512].astype(F32)
        total[...] = jnp.where(valid, fresh, 0.0)
    entry[c] = total[...]
    last = push(total, entry.at[c], last_s, last_r, partner)
    last.wait()
    for s in range(2):
        state = entry[s]
        cols = pl.ds(s * DK, DK)
        for n, k in order:

            @pl.when(c == k)
            def _():
                out[n, :, cols] = state

            state = factor(k, n, DK) * state + every[k, n, :, cols]
    for copy in far:
        copy.wait_send()


def scan_states(ends, back, collective_id):
    return remote_call(
        functools.partial(scan_kernel, back),
        collective_id,
        (ends,),
        jax.ShapeDtypeStruct((4, SLOTS, 1024), F32),
        [ANY],
        VMEM,
        [
            pltpu.VMEM((2, 4, SLOTS, 1152), F32),
            pltpu.VMEM((SLOTS, DK), F32),
            pltpu.VMEM((SLOTS, 768), BF),
            pltpu.VMEM((REACH, SLOTS, 768), BF),
            pltpu.VMEM((2, SLOTS, DK), F32),
            DMA(()),
            DMA(()),
            DMA(()),
            DMA((REACH,)),
            DMA((REACH,)),
            DMA(()),
            DMA(()),
        ],
    )


def tri(lower):
    row = lax.broadcasted_iota(jnp.int32, (CHUNK, CHUNK), 0)
    col = lax.broadcasted_iota(jnp.int32, (CHUNK, CHUNK), 1)
    return ((row >= col) if lower else (row <= col)).astype(F32)


def seen_mask(offs):
    row = lax.broadcasted_iota(jnp.int32, (CHUNK, CHUNK), 0)
    col = lax.broadcasted_iota(jnp.int32, (CHUNK, CHUNK), 1)
    return jnp.logical_and(row >= col, offs >= row - col)


def features(ref, which):
    cols = pl.ds(which * HALF, HALF)
    return jnp.concatenate([ref[0, 0, :, cols], ref[1, 0, :, cols]], axis=1)


def tiles(value):
    return [value[8 * b : 8 * b + 8] for b in range(CHUNK // 8)]


def one_row(blocks, i):
    return blocks[i // 8][i % 8 : i % 8 + 1]


def spans(cum, i):
    last = one_row(cum, i)
    return [(b, jnp.exp(jnp.minimum(cum[b] - last, 0.0))) for b in range(i // 8, CHUNK // 8)]


def weigh(cum, write, columns):
    cum, write, cols = tiles(cum), tiles(write), tiles(columns)
    total = [jnp.zeros((8, SLOTS), F32) for _ in range(CHUNK // 8)]
    for i in range(CHUNK):
        scale = one_row(write, i)
        for b, span in spans(cum, i):
            total[b] = total[b] + cols[b][:, i : i + 1] * (span * scale)
    return jnp.concatenate(total, axis=0)


def weigh_slots(cum, write, values):
    cum, write, vals = tiles(cum), tiles(write), tiles(values)
    lane = lax.broadcasted_iota(jnp.int32, (8, CHUNK), 1)
    total = [jnp.zeros((8, CHUNK), F32) for _ in range(CHUNK // 8)]
    for i in range(CHUNK):
        scale = one_row(write, i)
        for b, span in spans(cum, i):
            got = jnp.sum(vals[b] * (span * scale), axis=1, keepdims=True)
            total[b] = jnp.where(lane == i, got, total[b])
    return jnp.concatenate(total, axis=0)


def ends_kernel(qkv, lam, write, offs, ends, cum_ref, near_ref):
    query, key, value = (features(qkv, n) for n in range(3))
    decay = lam[0]
    cum = dot(tri(True), decay, precision=HIGH)
    cum_ref[0] = cum
    offsets = offs[0]
    final = offsets[CHUNK - 1 : CHUNK, :]
    row = lax.broadcasted_iota(jnp.int32, (CHUNK, 1), 0)
    tail = (row >= CHUNK - 1 - final).astype(F32)
    ending = jnp.exp(cum[CHUNK - 1 : CHUNK] - cum) * write[0] * tail
    ending = ending.astype(BF)
    ends[0, :, 0:512] = tn(ending, key)
    ends[0, :, 512:1024] = tn(ending, value)
    keep = (final > CHUNK - 1).astype(F32)
    ends[0, :, 1024:1152] = keep * jnp.exp(tn(decay, jnp.ones((CHUNK, 128), F32), HIGH))
    affinity = jnp.where(seen_mask(offsets), nt(query, key) * SCALE, 0.0)
    near_ref[0] = weigh(cum, write[0], affinity)


def out_kernel(qkv, cum_ref, write, offs, near, states, mixed, probs_ref, mixing_ref, far_ref):
    query, _, value = (features(qkv, n) for n in range(3))
    cum, offsets = cum_ref[0], offs[0]
    row = lax.broadcasted_iota(jnp.int32, (CHUNK, 1), 0)
    carry = jnp.exp(cum) * (offsets > row).astype(F32)
    far = nt(query, states[0, :, 0:512].astype(BF)) * SCALE
    far_ref[0] = far
    scores = near[0] + carry * far
    scores = jnp.exp(scores - jnp.max(scores, axis=1, keepdims=True))
    probs = scores / jnp.sum(scores, axis=1, keepdims=True)
    probs_ref[0] = probs
    mixing = jnp.where(seen_mask(offsets), weigh_slots(cum, write[0], probs), 0.0)
    mixing_ref[0] = mixing
    mixed[0] = dot(mixing.astype(BF), value) + dot(
        (probs * carry).astype(BF), states[0, :, 512:1024].astype(BF)
    )


def back_kernel(
    qkv, grad, cum_ref, write, offs, states, probs_ref, far_ref, decay_in, dmix_ref, dscore_ref, dprob_ref, dfar_ref, ends
):
    query, _, value = (features(qkv, n) for n in range(3))
    g, cum, offsets, probs = grad[0], cum_ref[0], offs[0], probs_ref[0]
    row = lax.broadcasted_iota(jnp.int32, (CHUNK, 1), 0)
    carry = jnp.exp(cum) * (offsets > row).astype(F32)
    dmix = jnp.where(seen_mask(offsets), nt(g, value), 0.0)
    dmix_ref[0] = dmix
    dcarry = nt(g, states[0, :, 512:1024].astype(BF))
    dnear = weigh(cum, write[0], dmix)
    dprob_ref[0] = dnear
    dfar_ref[0] = dcarry
    dprobs = dnear + carry * dcarry
    dscores = probs * (dprobs - jnp.sum(probs * dprobs, axis=1, keepdims=True))
    dscore_ref[0] = dscores
    ends[0, :, 0:512] = tn((SCALE * dscores * carry).astype(BF), query)
    ends[0, :, 512:1024] = tn((probs * carry).astype(BF), g)
    ends[0, :, 1024:1152] = decay_in[0, :, 1024:1152]


def last_kernel(
    qkv, grad, lam, cum_ref, write, slope, offs, states, near, probs_ref, mixing, far, dmix, dscore, dprob, dfar, nexts, dqkv, dlogit
):
    query, key, value = (features(qkv, n) for n in range(3))
    g, cum, offsets, probs, dscores = grad[0], cum_ref[0], offs[0], probs_ref[0], dscore[0]
    row = lax.broadcasted_iota(jnp.int32, (CHUNK, 1), 0)
    carry = jnp.exp(cum) * (offsets > row).astype(F32)
    seen = seen_mask(offsets)
    affinity = jnp.where(seen, nt(query, key) * SCALE, 0.0)
    cums, writes = tiles(cum), tiles(write[0])
    aff, dmx, dsc, prb = tiles(affinity), tiles(dmix[0]), tiles(dscores), tiles(probs)
    lane = lax.broadcasted_iota(jnp.int32, (8, CHUNK), 1)
    daff = [jnp.zeros((8, CHUNK), F32) for _ in range(CHUNK // 8)]
    fresh = []
    for i in range(CHUNK):
        scale = one_row(writes, i)
        gather = jnp.zeros((8, SLOTS), F32)
        for b, span in spans(cums, i):
            got = jnp.sum(dsc[b] * (span * scale), axis=1, keepdims=True)
            daff[b] = jnp.where(lane == i, got, daff[b])
            gather = gather + (dsc[b] * aff[b][:, i : i + 1] + prb[b] * dmx[b][:, i : i + 1]) * span
        fresh.append(jnp.sum(gather, axis=0, keepdims=True))
    fresh = jnp.concatenate(fresh, axis=0)
    daff = jnp.where(seen, jnp.concatenate(daff, axis=0) * SCALE, 0.0).astype(BF)
    final = offsets[CHUNK - 1 : CHUNK, :]
    tail = (row >= CHUNK - 1 - final).astype(F32)
    reach = jnp.exp(cum[CHUNK - 1 : CHUNK] - cum) * tail
    ending = (reach * write[0]).astype(BF)
    next_k, next_v = nexts[0, :, 0:512], nexts[0, :, 512:1024]
    state_k, state_v = states[0, :, 0:512], states[0, :, 512:1024]
    nk, nv = next_k.astype(BF), next_v.astype(BF)
    dq = dot(daff, key) + dot((SCALE * dscores * carry).astype(BF), state_k.astype(BF))
    dk = tn(daff, query) + dot(ending, nk)
    dv = tn(mixing[0].astype(BF), g) + dot(ending, nv)
    for n, part in enumerate((dq, dk, dv)):
        for s in range(2):
            dqkv[s, 0, :, pl.ds(n * HALF, HALF)] = part[:, s * HALF : (s + 1) * HALF].astype(BF)
    dend = (nt(key, nk) + nt(value, nv)) * reach
    ones = jnp.ones((8, DK), F32)
    dkeep = nt(ones, next_k * state_k + next_v * state_v, HIGH)[0:1]
    keep = (final > CHUNK - 1).astype(F32) * jnp.exp(cum[CHUNK - 1 : CHUNK])
    scaled = write[0] * dend
    dcum = (
        dscores * near[0]
        + probs * dprob[0]
        + carry * (dscores * far[0] + probs * dfar[0])
        - write[0] * fresh
        - scaled
    )
    at_end = jnp.sum(scaled, axis=0, keepdims=True) + dkeep * keep
    dcum = dcum + jnp.where(row == CHUNK - 1, at_end, 0.0)
    dlam = dot(tri(False), dcum, precision=HIGH) - jnp.exp(lam[0]) * (fresh + dend)
    dlogit[0] = dlam * slope[0]


def chunk_call(kernel, operands, outs, flops=0):
    def spec(shape, paired):
        if paired:
            return pl.BlockSpec((2, 1) + tuple(shape[2:]), lambda n: (0, n, 0, 0))
        return pl.BlockSpec((1,) + tuple(shape[1:]), lambda n: (n, 0, 0))

    return pl.pallas_call(
        kernel,
        grid=(4,),
        out_shape=[jax.ShapeDtypeStruct(shape, dtype) for shape, dtype in outs],
        in_specs=[spec(v.shape, v.ndim == 4) for v in operands],
        out_specs=[spec(shape, len(shape) == 4) for shape, _ in outs],
        compiler_params=pltpu.CompilerParams(vmem_limit_bytes=48 * 2**20),
    )(*operands)


def scatter_kernel(
    cols, grads, out_m, out_f, own, far, near, landed, ready, total, own_s, far_s, far_r, near_s, near_r, m_send, m_recv, f_send, f_recv, f_own
):
    x, y, z, c = here()
    half = cols // 2
    parts = (pl.ds(0, half), pl.ds(half, half))
    greet(group_peers() + plane_peers())
    order = (1, 2, 3, 0)

    def block(side, k, d):
        if side == 0:
            return grads.at[wrap(x + d), wrap(y + k), :, parts[0]]
        return grads.at[wrap(x + k), wrap(y + d), :, parts[1]]

    def peer(side, d):
        return (wrap(x + d), y, z, c) if side == 0 else (x, wrap(y + d), z, c)

    fars, owns = {}, {}
    for k in order:
        for side in range(2):
            owns[side, k] = pltpu.make_async_copy(
                block(side, k, 0), own.at[side, k], own_s.at[side, k]
            )
            owns[side, k].start()
            for d in range(1, 4):
                fars[side, k, d] = push(
                    block(side, k, d),
                    far.at[side, k, d - 1],
                    far_s.at[side, k, d - 1],
                    far_r.at[side, k, d - 1],
                    peer(side, d),
                )
    nears = {}
    for k in order:
        for side in range(2):
            owns[side, k].wait()
            for d in range(1, 4):
                fars[side, k, d].wait_recv()

            @pl.loop(0, 8)
            def _(r):
                rows = pl.ds(pl.multiple_of(r * 16, 16), 16)
                value = own[side, k, rows, :].astype(F32)
                for d in range(3):
                    value = value + far[side, k, d, rows, :].astype(F32)
                if k > 0:
                    near[side, k - 1, rows, :] = value.astype(BF)
                else:
                    total[side, rows, :] = value

            if k > 0:
                nears[side, k] = push(
                    near.at[side, k - 1],
                    landed.at[side, k - 1],
                    near_s.at[side, k - 1],
                    near_r.at[side, k - 1],
                    peer(1 - side, k),
                )
    for side in range(2):
        for k in range(1, 4):
            nears[side, k].wait_recv()

        @pl.loop(0, 8)
        def _(r):
            rows = pl.ds(pl.multiple_of(r * 16, 16), 16)
            value = total[side, rows, :]
            for k in range(3):
                value = value + landed[side, k, rows, :].astype(F32)
            ready[rows, parts[side]] = value.astype(BF)

    m_sent = []
    for to in range(4):
        src = ready.at[pl.ds(to * 32, 32), pl.ds(0, MIX)]
        dst = out_m.at[lax.rem(z, 2), c]
        same = jnp.logical_and(to == z, c == z // 2)
        copy = pltpu.make_async_remote_copy(
            src_ref=src,
            dst_ref=dst,
            send_sem=m_send.at[to],
            recv_sem=m_recv.at[lax.rem(z, 2), c],
            device_id=(x, y, to, z // 2),
            device_id_type=MESH,
        )

        @pl.when(same)
        def _():
            pltpu.make_async_copy(src, dst, m_recv.at[lax.rem(z, 2), c]).start()

        @pl.when(jnp.logical_not(same))
        def _():
            copy.start()

        m_sent.append((same, copy))

    def ffn_rows(to):
        return ready.at[pl.ds(pl.multiple_of(to * 32, 32), 32), pl.ds(MIX, FFN)]

    f_mine = pltpu.make_async_copy(ffn_rows(z), out_f.at[z], f_own)
    f_mine.start()
    f_sent = [
        push(
            ffn_rows(wrap(z + d)),
            out_f.at[z],
            f_send.at[d - 1],
            f_recv.at[d - 1],
            (x, y, wrap(z + d), c),
        )
        for d in range(1, 4)
    ]
    for j in range(2):
        for k in range(2):
            pltpu.make_async_copy(
                ready.at[pl.ds(0, 32), pl.ds(0, MIX)], out_m.at[j, k], m_recv.at[j, k]
            ).wait()
    f_mine.wait()
    for copy in f_sent:
        copy.wait()
    for same, copy in m_sent:

        @pl.when(jnp.logical_not(same))
        def _():
            copy.wait_send()

    for copy in list(fars.values()) + list(nears.values()):
        copy.wait_send()


def scatter_all(grads, collective_id):
    cols = grads.shape[1]
    half = cols // 2
    return remote_call(
        functools.partial(scatter_kernel, cols),
        collective_id,
        (grads.reshape(4, 4, 128, cols),),
        [jax.ShapeDtypeStruct((2, 2, 32, MIX), BF), jax.ShapeDtypeStruct((4, 32, FFN), BF)],
        [ANY],
        [ANY, ANY],
        [
            pltpu.VMEM((2, 4, 128, half), BF),
            pltpu.VMEM((2, 4, 3, 128, half), BF),
            pltpu.VMEM((2, 3, 128, half), BF),
            pltpu.VMEM((2, 3, 128, half), BF),
            pltpu.VMEM((128, cols), BF),
            pltpu.VMEM((2, 128, half), F32),
            DMA((2, 4)),
            DMA((2, 4, 3)),
            DMA((2, 4, 3)),
            DMA((2, 3)),
            DMA((2, 3)),
            DMA((4,)),
            DMA((2, 2)),
            DMA((3,)),
            DMA((3,)),
            DMA(()),
        ],
    )


def small_kernel(src, out, held, here_s, own_s, send, recv, pair_s, pair_r):
    x, y, z, c = here()
    rows = src.shape[0] // 2
    partner = (x, y, z, 1 - c)
    greet(plane_peers() + row_peers())

    def half(k):
        return pl.ds(pl.multiple_of(k * rows, 8), rows)

    copy = push(src.at[half(1 - c)], held.at[0, c], pair_s.at[0], pair_r.at[0], partner)
    mine = pltpu.make_async_copy(src.at[half(c)], held.at[0, c], own_s)
    mine.start()
    mine.wait()
    copy.wait()
    here_s[...] = held[0, 0] + held[0, 1]
    for stage, at in enumerate((x, y, z)):
        held[stage + 1, at] = here_s[...]
        sent = []
        for d in range(1, 4):
            peer = [x, y, z, c]
            peer[stage] = wrap(at + d)
            sent.append(
                push(
                    held.at[stage + 1, at],
                    held.at[stage + 1, at],
                    send.at[stage, d - 1],
                    recv.at[stage, d - 1],
                    tuple(peer),
                )
            )
        for copy in sent:
            copy.wait()
        value = held[stage + 1, 0]
        for k in range(1, 4):
            value = value + held[stage + 1, k]
        here_s[...] = value
    copy = push(here_s, out.at[half(c)], pair_s.at[1], pair_r.at[1], partner)
    out[half(c)] = here_s[...]
    copy.wait()


def small_sum(values, collective_id):
    flat = jnp.concatenate([v.reshape(-1) for v in values])
    size = flat.shape[0]
    rows = -(-size // 2048) * 16
    flat = jnp.pad(flat, (0, rows * 128 - size)).reshape(rows, 128)
    flat = remote_call(
        small_kernel,
        collective_id,
        (flat,),
        jax.ShapeDtypeStruct((rows, 128), F32),
        [VMEM],
        VMEM,
        [
            pltpu.VMEM((4, 4, rows // 2, 128), F32),
            pltpu.VMEM((rows // 2, 128), F32),
            DMA(()),
            DMA((3, 3)),
            DMA((3, 3)),
            DMA((2,)),
            DMA((2,)),
        ],
    ).reshape(-1)
    outs, at = [], 0
    for v in values:
        outs.append(flat[at : at + v.size].reshape(v.shape))
        at += v.size
    return outs


def rms(v, gain):
    return v * lax.rsqrt(jnp.mean(v * v, axis=-1, keepdims=True) + EPS) * gain


def rms_back(v, gain, e):
    r = lax.rsqrt(jnp.mean(v * v, axis=-1, keepdims=True) + EPS)
    grad = r * gain * e - v * (r**3) * jnp.mean(v * gain * e, axis=-1, keepdims=True)
    return grad, jnp.sum(e * v * r, axis=0)


def body(
    inputs,
    offsets,
    norm1_gain,
    query_weight,
    key_weight,
    value_weight,
    gate_weight,
    out_weight,
    low_down,
    low_up,
    forget_bias,
    head_gain,
    norm2_gain,
    ffn_gate,
    ffn_up,
    ffn_down,
    cotangent,
):
    head, core = lax.axis_index("z"), lax.axis_index("c")
    mixer = (query_weight, key_weight, value_weight, gate_weight, out_weight.T)
    wm = jnp.stack([w.reshape(32, 2, 2, HALF) for w in mixer], axis=3)
    wm = wm.transpose(1, 2, 0, 3, 4).reshape(2, 2, 32, MIX)
    wf = jnp.stack([w.reshape(32, 4, UNITS) for w in (ffn_gate, ffn_up, ffn_down)], axis=2)
    wf = jnp.pad(wf, ((0, 0), (0, 0), (0, 0), (0, UNITS_PAD - UNITS)))
    wf = wf.transpose(1, 0, 2, 3).reshape(4, 32, FFN)
    resid = inputs.astype(F32)
    first_own = rms(resid, norm1_gain).astype(BF)
    wide_m, wide_f, first, cot = gather_all(wm, wf, first_own, cotangent, 1)
    wide_m, wide_f = wide_m.reshape(2048, MIX), wide_f.reshape(2048, FFN)
    tokens = first
    first, cot = first.reshape(512, 2048), cot.reshape(512, 2048)
    w_qkvg, w_out = wide_m[:, : 4 * HALF], wide_m[:, 4 * HALF :]
    w_gate, w_up, w_down = (wide_f[:, n * UNITS_PAD : (n + 1) * UNITS_PAD] for n in range(3))

    qkv = dot(first, wide_m[:, : 3 * HALF]).astype(BF)
    gate_lin = dot(first, wide_m[:, 3 * HALF : 4 * HALF])
    qkv = swap(qkv.reshape(2, 4, 64, 3 * HALF), 2)
    mine = lax.dynamic_index_in_dim(tokens, core, 0, keepdims=False).reshape(256, 2048)
    up_cols = lax.dynamic_slice_in_dim(low_up.astype(F32), head * SLOTS, SLOTS, 1)
    bias = lax.dynamic_slice_in_dim(forget_bias, head * SLOTS, SLOTS, 0)
    lowrank = dot(mine, low_down)
    logits = (dot(lowrank, up_cols, precision=HIGH) + bias).astype(BF).astype(F32)
    lam = (jax.nn.log_sigmoid(logits) / 8.0).reshape(4, 64, SLOTS)
    write = -jnp.expm1(lam)
    slope = (jax.nn.sigmoid(-logits) / 8.0).reshape(4, 64, SLOTS)
    pair = lax.all_gather(offsets.reshape(2, 64), "z")
    offs = lax.dynamic_index_in_dim(pair, core, 1, keepdims=False).reshape(4, 64, 1)

    square = ((4, 64, 64), F32)
    ends, cum, near = chunk_call(
        ends_kernel, (qkv, lam, write, offs), [((4, SLOTS, 1152), F32), square, square]
    )
    states = scan_states(ends, False, 3)
    mixed, probs, mixing, far = chunk_call(
        out_kernel,
        (qkv, cum, write, offs, near, states),
        [((4, 64, DK), F32), square, square, square],
    )
    mixed = mixed.reshape(256, DK)
    headnorm = rms(mixed, head_gain).reshape(4, 64, 2, HALF).transpose(2, 0, 1, 3)
    headnorm = swap(headnorm, 4).reshape(512, HALF)
    branch = (headnorm * jax.nn.silu(gate_lin)).astype(BF)
    (mixer_out,) = sum_rows([nt(branch, w_out)], 5)
    resid1 = resid + mixer_out
    second_own = rms(resid1, norm2_gain).astype(BF)
    second = gather_rows(second_own, 6)

    act_gate, act_up = dot(second, w_gate), dot(second, w_up)
    sig = jax.nn.sigmoid(act_gate)
    silu = act_gate * sig
    hidden = (silu * act_up).astype(BF)
    grad_hidden = dot(cot, w_down)
    grad_gate = (grad_hidden * act_up * sig * (1 + act_gate * (1 - sig))).astype(BF)
    grad_up = (grad_hidden * silu).astype(BF)
    ffn_part = nt(hidden, w_down)
    second_part = nt(grad_gate, w_gate) + nt(grad_up, w_up)
    ffn_out, grad_second = sum_rows([ffn_part, second_part], 7)
    output = (resid1 + ffn_out).astype(BF)
    grad_norm, d_norm2 = rms_back(resid1, norm2_gain, grad_second)
    grad_resid1 = cotangent.astype(F32) + grad_norm
    grad_attn = gather_rows(grad_resid1.astype(BF), 8)

    grad_branch = dot(grad_attn, w_out)
    sig = jax.nn.sigmoid(gate_lin)
    grad_lin = (grad_branch * headnorm * sig * (1 + gate_lin * (1 - sig))).astype(BF)
    grad_headnorm = (grad_branch * gate_lin * sig).reshape(2, 4, 64, HALF)
    grad_headnorm = swap(grad_headnorm, 9).transpose(1, 2, 0, 3).reshape(256, DK)
    grad_mixed, d_head = rms_back(mixed, head_gain, grad_headnorm)
    grad_mixed = grad_mixed.astype(BF).reshape(4, 64, DK)

    dmix, dscore, dprob, dfar, back_ends = chunk_call(
        back_kernel,
        (qkv, grad_mixed, cum, write, offs, states, probs, far, ends),
        [square, square, square, square, ((4, SLOTS, 1152), F32)],
    )
    nexts = scan_states(back_ends, True, 10)
    dqkv, dlogit = chunk_call(
        last_kernel,
        (qkv, grad_mixed, lam, cum, write, slope, offs, states, near, probs, mixing, far, dmix, dscore, dprob, dfar, nexts),
        [((2, 4, 64, 3 * HALF), BF), square],
    )
    dqkv = swap(dqkv, 11).reshape(512, 3 * HALF)
    dlogit = dlogit.reshape(256, SLOTS)
    grad_low = dot(dlogit, up_cols.T, precision=HIGH)
    dproj = jnp.concatenate([dqkv, grad_lin], axis=1)
    first_part = nt(dproj, w_qkvg).reshape(2, 256, 2048)
    low_part = nt(grad_low, low_down.astype(F32), precision=HIGH)
    own = (jnp.arange(2) == core).astype(F32)[:, None, None]
    first_part = (first_part + own * low_part[None]).reshape(512, 2048)
    (grad_first,) = sum_rows([first_part], 12)
    grad_in, d_norm1 = rms_back(resid, norm1_gain, grad_first)
    d_inputs = grad_resid1 + grad_in

    grads = jnp.concatenate(
        [
            tn(first, dproj).astype(BF),
            tn(grad_attn, branch).astype(BF),
            tn(second, grad_gate).astype(BF),
            tn(second, grad_up).astype(BF),
            tn(cot, hidden).astype(BF),
        ],
        axis=1,
    )
    sums_m, sums_f = scatter_all(grads, 13)
    sums_m = sums_m.reshape(2, 2, 32, 5, HALF).transpose(3, 2, 0, 1, 4).reshape(5, 32, 1024)
    sums_m = sums_m.astype(F32)
    sums_f = sums_f.reshape(4, 32, 3, UNITS_PAD)[..., :UNITS].transpose(2, 1, 0, 3)
    sums_f = sums_f.reshape(3, 32, 4 * UNITS).astype(F32)

    d_up = jnp.zeros(low_up.shape, F32)
    d_up = lax.dynamic_update_slice_in_dim(d_up, tn(lowrank, dlogit, HIGH), head * SLOTS, 1)
    d_bias = jnp.zeros(forget_bias.shape, F32)
    d_bias = lax.dynamic_update_slice_in_dim(d_bias, jnp.sum(dlogit, axis=0), head * SLOTS, 0)
    d_down = tn(grad_low, mine.astype(F32), HIGH)
    small = small_sum([d_norm1, d_norm2, d_head, d_down, d_up, d_bias], 14)
    return (
        output,
        d_inputs,
        small[0],
        sums_m[0],
        sums_m[1],
        sums_m[2],
        sums_m[3],
        sums_m[4].T,
        small[3].T,
        small[4],
        small[5],
        small[2],
        small[1],
        sums_f[0],
        sums_f[1],
        sums_f[2],
    )


def solution(mesh):
    fine = Mesh(mesh.devices.reshape(4, 4, 4, 2), ("x", "y", "z", "c"))
    seq = ("x", "y", "z")
    rows = P(("x", "y", "z", "c"), None)
    wide = P(seq, "c")
    placed = (
        (rows, P(seq), P())
        + (wide,) * 4
        + (P("c", seq), P(), P(), P(), P(), P(), wide, wide, wide, rows)
    )
    return jax.shard_map(
        body,
        mesh=fine,
        in_specs=placed,
        out_specs=(rows, rows, P())
        + (wide,) * 4
        + (P("c", seq), P(), P(), P(), P(), P(), wide, wide, wide),
        check_vma=False,
    )
```

```python
import functools

import jax
import jax.numpy as jnp
from jax import lax
from jax.experimental import pallas as pl
from jax.experimental.pallas import tpu as pltpu
from jax.sharding import Mesh
from jax.sharding import PartitionSpec as P

DK = 512
SLOTS = 64
CHUNK = 64
HALF = 256
UNITS = 704
UNITS_PAD = 768
REACH = 8
EPS = 1e-06
SCALE = 0.125
BF = jnp.bfloat16
F32 = jnp.float32
HIGH = lax.Precision.HIGHEST
MESH = pl.DeviceIdType.MESH
ANY = pl.BlockSpec(memory_space=pl.ANY)
VMEM = pl.BlockSpec(memory_space=pltpu.VMEM)
DMA = pltpu.SemaphoreType.DMA
MIX = 5 * HALF
FFN = 3 * UNITS_PAD


def dot(left, right, dims=((1,), (0,)), precision=None):
    return lax.dot_general(
        left, right, (dims, ((), ())), precision=precision, preferred_element_type=F32
    )


def nt(left, right, precision=None):
    return dot(left, right, ((1,), (1,)), precision)


def tn(left, right, precision=None):
    return dot(left, right, ((0,), (0,)), precision)


def here():
    return tuple(lax.axis_index(a) for a in ("x", "y", "z", "c"))


def wrap(v, n=4):
    return lax.rem(v + n, n)


def greet(peers):
    barrier = pltpu.get_barrier_semaphore()
    for peer in peers:
        pl.semaphore_signal(barrier, inc=1, device_id=peer, device_id_type=MESH)
    pl.semaphore_wait(barrier, len(peers))


def push(src, dst, send, recv, peer):
    copy = pltpu.make_async_remote_copy(
        src_ref=src, dst_ref=dst, send_sem=send, recv_sem=recv, device_id=peer, device_id_type=MESH
    )
    copy.start()
    return copy


class Refs:
    pass


def remote_call(kernel, collective_id, operands, outs, scratch):
    names = list(operands) + list(outs) + list(scratch)

    def run(*refs):
        r = Refs()
        for name, ref in zip(names, refs):
            setattr(r, name, ref)
        kernel(r)

    results = pl.pallas_call(
        run,
        out_shape=[jax.ShapeDtypeStruct(shape, dtype) for shape, dtype, _ in outs.values()],
        in_specs=[spec for _, spec in operands.values()],
        out_specs=[spec for _, _, spec in outs.values()],
        scratch_shapes=list(scratch.values()),
        compiler_params=pltpu.CompilerParams(
            collective_id=collective_id, has_side_effects=True, vmem_limit_bytes=63 * 2**20
        ),
    )(*[array for array, _ in operands.values()])
    return dict(zip(outs, results))


def spread_block(w_ref, side, k, cols):
    x, y, z, c = here()
    part = pl.ds(side * (cols // 2), cols // 2)
    if side == 0:
        return w_ref.at[x, wrap(y - k), :, part]
    return w_ref.at[wrap(x - k), y, :, part]


def spread_near(w_ref, sems, cols):
    x, y, z, c = here()
    sent = {}
    for d in range(1, 4):
        for side in range(2):
            block = spread_block(w_ref, side, 0, cols)
            peer = (x, wrap(y + d), z, c) if side == 0 else (wrap(x + d), y, z, c)
            sent[side, d] = push(
                block, block, sems[0].at[side, d - 1], sems[1].at[side, d - 1], peer
            )
    return sent


def spread_far(w_ref, sems, cols, near, k):
    x, y, z, c = here()
    sent = []
    for side in range(2):
        if k > 0:
            near[side, k].wait_recv()
        block = spread_block(w_ref, side, k, cols)
        for d in range(1, 4):
            peer = (wrap(x + d), y, z, c) if side == 0 else (x, wrap(y + d), z, c)
            sent.append(
                push(
                    block, block, sems[2].at[side, k, d - 1], sems[3].at[side, k, d - 1], peer
                )
            )
    return sent


def rows_start(src, out, sems):
    x, y, z, c = here()
    hop_s, hop_r, pair_s, pair_r, own = sems
    mine = pltpu.make_async_copy(src, out.at[c, z], own)
    mine.start()
    hops = [
        push(src, out.at[c, z], hop_s.at[d - 1], hop_r.at[d - 1], (x, y, wrap(z + d), c))
        for d in range(1, 4)
    ]
    pairs = [push(src, out.at[c, z], pair_s.at[0], pair_r.at[0], (x, y, z, 1 - c))]
    return mine, hops, pairs


def rows_finish(started, out, sems):
    x, y, z, c = here()
    hop_s, hop_r, pair_s, pair_r, own = sems
    mine, hops, pairs = started
    for d in range(1, 4):
        hops[d - 1].wait_recv()
        block = out.at[c, wrap(z - d)]
        pairs.append(push(block, block, pair_s.at[d], pair_r.at[d], (x, y, z, 1 - c)))
    mine.wait()
    for copy in hops:
        copy.wait_send()
    for copy in pairs:
        copy.wait()


def group_peers():
    x, y, z, c = here()
    return [(x, y, wrap(z + d), k) for d in range(1, 4) for k in range(2)] + [(x, y, z, 1 - c)]


def row_peers():
    x, y, z, c = here()
    return [(x, y, wrap(z + d), c) for d in range(1, 4)] + [(x, y, z, 1 - c)]


def plane_peers():
    x, y, z, c = here()
    return [(wrap(x + d), y, z, c) for d in range(1, 4)] + [
        (x, wrap(y + d), z, c) for d in range(1, 4)
    ]


def all_peers():
    return group_peers() + plane_peers()


def spread_sems(name):
    kinds = ((2, 3), (2, 3), (2, 4, 3), (2, 4, 3))
    return {f"{name}{n}": DMA(shape) for n, shape in enumerate(kinds)}


def rows_sems(name):
    kinds = ((3,), (3,), (4,), (4,), ())
    return {f"{name}{n}": DMA(shape) for n, shape in enumerate(kinds)}


def sems_of(r, name, count):
    return [getattr(r, f"{name}{n}") for n in range(count)]


def deal_start(src, wide, send, recv):
    x, y, z, c = here()
    dst = wide.at[x, y, pl.ds(pl.multiple_of(z * 32, 32), 32), :]
    sent = []
    for j in range(2):
        for k in range(2):
            same = jnp.logical_and(2 * c + j == z, c == k)
            copy = pltpu.make_async_remote_copy(
                src_ref=src.at[j, k],
                dst_ref=dst,
                send_sem=send.at[j, k],
                recv_sem=recv.at[z],
                device_id=(x, y, 2 * c + j, k),
                device_id_type=MESH,
            )

            @pl.when(same)
            def _():
                pltpu.make_async_copy(src.at[j, k], dst, recv.at[z]).start()

            @pl.when(jnp.logical_not(same))
            def _():
                copy.start()

            sent.append((same, copy))
    return sent


def deal_wait(src, wide, recv):
    x, y, z, c = here()
    for s in range(4):
        dst = wide.at[x, y, pl.ds(s * 32, 32), :]
        pltpu.make_async_copy(src.at[0, 0], dst, recv.at[s]).wait()


def deal_done(sent):
    for same, copy in sent:

        @pl.when(jnp.logical_not(same))
        def _():
            copy.wait_send()


def shuffle_start(block, dst, send, recv, own):
    x, y, z, c = here()
    mine = pltpu.make_async_copy(block(z), dst, own)
    mine.start()
    sent = [
        push(block(wrap(z + d)), dst, send.at[d - 1], recv.at[d - 1], (x, y, wrap(z + d), c))
        for d in range(1, 4)
    ]
    return mine, sent


def shuffle_wait(started):
    started[0].wait()
    for copy in started[1]:
        copy.wait_recv()


def shuffle_done(started):
    for copy in started[1]:
        copy.wait_send()


def shuffle_sems(name):
    return {f"{name}0": DMA((3,)), f"{name}1": DMA((3,)), f"{name}2": DMA(())}


class RowSum:
    def __init__(self, r, name, parts, own):
        self.parts, self.own = parts, own
        self.theirs, self.landed = sems_of(r, name + "b", 2)
        self.sems = sems_of(r, name + "s", 4)

    def pairs(self):
        x, y, z, c = here()
        self.pair = [
            push(
                self.parts.at[1 - c, wrap(z + 1 + k)],
                self.theirs.at[k],
                self.sems[0].at[k],
                self.sems[1].at[k],
                (x, y, z, 1 - c),
            )
            for k in range(4)
        ]

    def hops(self):
        x, y, z, c = here()
        self.hop = []
        for k in range(3):
            to = wrap(z + 1 + k)
            self.pair[k].wait_recv()
            both = self.own(to).astype(F32) + self.theirs[k].astype(F32)
            self.theirs[k] = both.astype(BF)
            self.hop.append(
                push(
                    self.theirs.at[k],
                    self.landed.at[k],
                    self.sems[2].at[k],
                    self.sems[3].at[k],
                    (x, y, to, c),
                )
            )

    def result(self):
        x, y, z, c = here()
        self.pair[3].wait_recv()
        value = self.own(z).astype(F32) + self.theirs[3].astype(F32)
        for k in range(3):
            self.hop[k].wait_recv()
            value = value + self.landed[k].astype(F32)
        return value

    def done(self):
        for copy in self.pair + self.hop:
            copy.wait_send()


def sum_scratch(name):
    out = {f"{name}b{n}": pltpu.VMEM((k, 64, 2048), BF) for n, k in enumerate((4, 3))}
    out.update({f"{name}s{n}": DMA((k,)) for n, k in enumerate((4, 4, 3, 3))})
    return out


class Scan:
    def __init__(self, r, back):
        self.back, self.every = back, r.every
        self.total, self.sending, self.landed, self.entry = r.total, r.scan_out, r.scan_in, r.entry
        self.sems = sems_of(r, "scan", 6)
        self.order = [(n, k) for n in range(4) for k in range(2)]
        if back:
            self.order = self.order[::-1]

    def member(self, d):
        x, y, z, c = here()
        at = lax.rem(x * 4 + y + (-d if self.back else d) + 32, 16)
        return (at // 4, lax.rem(at, 4), z, c)

    def senders(self):
        return [self.member(-d) for d in range(1, REACH + 1)]

    def factor(self, k, n, width):
        return jnp.concatenate([self.every[k, n, :, 1024:1152]] * (width // 128), axis=1)

    def pair(self):
        x, y, z, c = here()
        self.swap = push(
            self.every.at[c], self.every.at[c], self.sems[0], self.sems[1], (x, y, z, 1 - c)
        )

    def send(self):
        x, y, z, c = here()
        self.swap.wait_recv()
        half = pl.ds(pl.multiple_of(c * DK, DK), DK)
        n, k = self.order[0]
        state = self.every[k, n, :, half]
        decay = self.every[k, n, :, 1024:1152]
        for n, k in self.order[1:]:
            state = self.factor(k, n, DK) * state + self.every[k, n, :, half]
            decay = self.every[k, n, :, 1024:1152] * decay
        self.sending[:, 0:512] = state.astype(BF)
        high = decay.astype(BF)
        self.sending[:, 512:640] = high
        self.sending[:, 640:768] = (decay - high.astype(F32)).astype(BF)
        self.far = [
            push(
                self.sending,
                self.landed.at[d - 1],
                self.sems[2].at[d - 1],
                self.sems[3].at[d - 1],
                self.member(d),
            )
            for d in range(1, REACH + 1)
        ]

    def fold(self, out):
        x, y, z, c = here()
        group = x * 4 + y
        state = jnp.zeros((SLOTS, DK), F32)
        for d in range(REACH, 0, -1):
            self.far[d - 1].wait_recv()
            valid = (group + d < 16) if self.back else (group >= d)
            block = self.landed.at[d - 1]
            keep = block[:, 512:640].astype(F32) + block[:, 640:768].astype(F32)
            fresh = jnp.concatenate([keep] * 4, axis=1) * state + block[:, 0:512].astype(F32)
            state = jnp.where(valid, fresh, 0.0)
        self.total[...] = state
        self.entry[c] = state
        self.last = push(
            self.total, self.entry.at[c], self.sems[4], self.sems[5], (x, y, z, 1 - c)
        )
        self.last.wait_recv()
        for s in range(2):
            state = self.entry[s]
            cols = pl.ds(s * DK, DK)
            for n, k in self.order:

                @pl.when(c == k)
                def _():
                    out[n, :, cols] = state

                state = self.factor(k, n, DK) * state + self.every[k, n, :, cols]

    def done(self):
        for copy in self.far + [self.swap, self.last]:
            copy.wait_send()


def scan_scratch():
    out = dict(
        every=pltpu.VMEM((2, 4, SLOTS, 1152), F32),
        total=pltpu.VMEM((SLOTS, DK), F32),
        scan_out=pltpu.VMEM((SLOTS, 768), BF),
        scan_in=pltpu.VMEM((REACH, SLOTS, 768), BF),
        entry=pltpu.VMEM((2, SLOTS, DK), F32),
    )
    kinds = ((), (), (REACH,), (REACH,), (), ())
    out.update({f"scan{n}": DMA(shape) for n, shape in enumerate(kinds)})
    return out


def places():
    row = lax.broadcasted_iota(jnp.int32, (CHUNK, CHUNK), 0)
    col = lax.broadcasted_iota(jnp.int32, (CHUNK, CHUNK), 1)
    return row, col


def tri(lower):
    row, col = places()
    return ((row >= col) if lower else (row <= col)).astype(F32)


def seen_mask(offs):
    row, col = places()
    return jnp.logical_and(row >= col, offs >= (row - col).astype(F32))


def carried(cum, offs):
    return jnp.exp(cum) * (offs > places()[0].astype(F32)).astype(F32)


def reaching(cum, offs):
    final = offs[CHUNK - 1 : CHUNK]
    tail = (places()[0].astype(F32) >= CHUNK - 1 - final).astype(F32)
    return jnp.exp(cum[CHUNK - 1 : CHUNK] - cum) * tail


def features(ref, n, which):
    cols = pl.ds(which * HALF, HALF)
    return jnp.concatenate([ref[0, n, :, cols], ref[1, n, :, cols]], axis=1)


def tiles(value):
    return [value[8 * b : 8 * b + 8] for b in range(CHUNK // 8)]


def one_row(blocks, i):
    return blocks[i // 8][i % 8 : i % 8 + 1]


def spans(cum, i):
    last = one_row(cum, i)
    return [(b, jnp.exp(jnp.minimum(cum[b] - last, 0.0))) for b in range(i // 8, CHUNK // 8)]


def weigh(cum, write, columns):
    cum, write, cols = tiles(cum), tiles(write), tiles(columns)
    total = [jnp.zeros((8, SLOTS), F32) for _ in range(CHUNK // 8)]
    for i in range(CHUNK):
        scale = one_row(write, i)
        for b, span in spans(cum, i):
            total[b] = total[b] + cols[b][:, i : i + 1] * (span * scale)
    return jnp.concatenate(total, axis=0)


def weigh_slots(cum, write, values):
    cum, write, vals = tiles(cum), tiles(write), tiles(values)
    lane = lax.broadcasted_iota(jnp.int32, (8, CHUNK), 1)
    total = [jnp.zeros((8, CHUNK), F32) for _ in range(CHUNK // 8)]
    for i in range(CHUNK):
        scale = one_row(write, i)
        for b, span in spans(cum, i):
            got = jnp.sum(vals[b] * (span * scale), axis=1, keepdims=True)
            total[b] = jnp.where(lane == i, got, total[b])
    return jnp.concatenate(total, axis=0)


def chunk_ends(key, value, lam, write, offs):
    cum = dot(tri(True), lam, precision=HIGH)
    ending = (reaching(cum, offs) * write).astype(BF)
    keep = (offs[CHUNK - 1 : CHUNK, 0:1] > CHUNK - 1).astype(F32)
    keep = keep * jnp.exp(tn(lam, jnp.ones((CHUNK, 128), F32), HIGH))
    return cum, jnp.concatenate([tn(ending, key), tn(ending, value), keep], axis=1)


def chunk_near(query, key, cum, write, offs):
    return weigh(cum, write, jnp.where(seen_mask(offs), nt(query, key) * SCALE, 0.0))


def chunk_out(query, value, cum, write, offs, near, state):
    carry = carried(cum, offs)
    far = nt(query, state[:, 0:512].astype(BF)) * SCALE
    scores = near + carry * far
    scores = jnp.exp(scores - jnp.max(scores, axis=1, keepdims=True))
    probs = scores / jnp.sum(scores, axis=1, keepdims=True)
    mixing = jnp.where(seen_mask(offs), weigh_slots(cum, write, probs), 0.0)
    mixed = dot(mixing.astype(BF), value) + dot(
        (probs * carry).astype(BF), state[:, 512:1024].astype(BF)
    )
    return far, probs, mixing, mixed


def chunk_back(query, value, g, cum, write, offs, probs, state):
    carry = carried(cum, offs)
    dmix = jnp.where(seen_mask(offs), nt(g, value), 0.0)
    dfar = nt(g, state[:, 512:1024].astype(BF))
    dnear = weigh(cum, write, dmix)
    dprobs = dnear + carry * dfar
    dscore = probs * (dprobs - jnp.sum(probs * dprobs, axis=1, keepdims=True))
    ends_k = tn((SCALE * dscore * carry).astype(BF), query)
    ends_v = tn((probs * carry).astype(BF), g)
    return dmix, dfar, dnear, dscore, ends_k, ends_v


def chunk_pairs(cum, write, affinity, dmix, dscore, probs):
    cums, writes = tiles(cum), tiles(write)
    aff, dmx, dsc, prb = tiles(affinity), tiles(dmix), tiles(dscore), tiles(probs)
    lane = lax.broadcasted_iota(jnp.int32, (8, CHUNK), 1)
    daff = [jnp.zeros((8, CHUNK), F32) for _ in range(CHUNK // 8)]
    fresh = []
    for i in range(CHUNK):
        scale = one_row(writes, i)
        both = jnp.zeros((8, SLOTS), F32)
        for b, span in spans(cums, i):
            got = jnp.sum(dsc[b] * (span * scale), axis=1, keepdims=True)
            daff[b] = jnp.where(lane == i, got, daff[b])
            both = both + (dsc[b] * aff[b][:, i : i + 1] + prb[b] * dmx[b][:, i : i + 1]) * span
        fresh.append(jnp.sum(both, axis=0, keepdims=True))
    return jnp.concatenate(daff, axis=0), jnp.concatenate(fresh, axis=0)


def chunk_last(
    query, key, value, g, lam, write, slope, offs, cum, near, far, probs, mixing, state, dmix, dfar, dnear, dscore, after
):
    carry, seen, reach = carried(cum, offs), seen_mask(offs), reaching(cum, offs)
    affinity = jnp.where(seen, nt(query, key) * SCALE, 0.0)
    daff, fresh = chunk_pairs(cum, write, affinity, dmix, dscore, probs)
    daff = jnp.where(seen, daff * SCALE, 0.0).astype(BF)
    ending = (reach * write).astype(BF)
    nk, nv = after[:, 0:512].astype(BF), after[:, 512:1024].astype(BF)
    dq = dot(daff, key) + dot((SCALE * dscore * carry).astype(BF), state[:, 0:512].astype(BF))
    dk = tn(daff, query) + dot(ending, nk)
    dv = tn(mixing.astype(BF), g) + dot(ending, nv)
    dend = (nt(key, nk) + nt(value, nv)) * reach
    dkeep = nt(jnp.ones((8, 1024), F32), after * state, HIGH)[0:1]
    keep = (offs[CHUNK - 1 : CHUNK] > CHUNK - 1).astype(F32) * jnp.exp(cum[CHUNK - 1 : CHUNK])
    scaled = write * dend
    dcum = dscore * near + probs * dnear + carry * (dscore * far + probs * dfar)
    dcum = dcum - write * fresh - scaled
    at_end = jnp.sum(scaled, axis=0, keepdims=True) + dkeep * keep
    dcum = dcum + jnp.where(places()[0] == CHUNK - 1, at_end, 0.0)
    dlam = dot(tri(False), dcum, precision=HIGH) - jnp.exp(lam) * (fresh + dend)
    return dq, dk, dv, dlam * slope


def forward_kernel(r):
    x, y, z, c = here()
    partner = (x, y, z, 1 - c)
    scan = Scan(r, False)
    greet(all_peers() + scan.senders())
    q_deal = deal_start(r.wq, r.wide_q, r.q_send, r.q_recv)
    a_sems, b_sems, s_sems = (sems_of(r, n, 5) for n in ("rows_a_", "rows_b_", "rows_s_"))
    a_rows = rows_start(r.rows_a, r.first, a_sems)
    gates = shuffle_start(lambda k: r.packed.at[k], r.gates.at[z], *sems_of(r, "gate", 3))
    g_deal = deal_start(r.wg, r.wide_g, r.g_send, r.g_recv)
    f_deal = shuffle_start(
        lambda k: r.wf.at[k],
        r.wide_f.at[x, y, pl.ds(pl.multiple_of(z * 32, 32), 32), :],
        *sems_of(r, "deal", 3),
    )
    b_rows = rows_start(r.rows_b, r.cot, b_sems)
    q_sems, g_sems, f_sems = (sems_of(r, n, 4) for n in ("q_spread", "g_spread", "f_spread"))
    deal_wait(r.wq, r.wide_q, r.q_recv)
    q_near = spread_near(r.wide_q, q_sems, 3 * HALF)
    q_far = spread_far(r.wide_q, q_sems, 3 * HALF, q_near, 0)
    for k in range(1, 4):
        q_far += spread_far(r.wide_q, q_sems, 3 * HALF, q_near, k)
    deal_wait(r.wg, r.wide_g, r.g_recv)
    g_near = spread_near(r.wide_g, g_sems, 2 * HALF)
    rows_finish(a_rows, r.first, a_sems)
    shuffle_wait(gates)
    for copy in q_far:
        copy.wait_recv()
    g_far = []
    for k in range(4):
        g_far += spread_far(r.wide_g, g_sems, 2 * HALF, g_near, k)
    shuffle_wait(f_deal)
    f_near = spread_near(r.wide_f, f_sems, FFN)

    @pl.loop(0, 3)
    def _(n):
        cols = pl.ds(pl.multiple_of(n * HALF, HALF), HALF)
        rows = r.first[...].reshape(512, 2048)
        got = dot(rows, r.wide_q[:, :, :, cols].reshape(2048, HALF))
        r.proj[:, :, :, cols] = got.astype(BF).reshape(2, 4, 64, HALF)

    swap = push(r.proj.at[1 - c], r.qkv.at[c], r.swap_s.at[0], r.swap_r.at[0], partner)
    r.qkv[c] = r.proj[c]
    swap.wait()

    @pl.loop(0, 4)
    def _(n):
        lam, write, offs = r.gates[n, 0], r.gates[n, 1], r.gates[n, 3]
        cum, ends = chunk_ends(features(r.qkv, n, 1), features(r.qkv, n, 2), lam, write, offs)
        r.cum[n] = cum
        r.every[c, n] = ends
        r.decays[n] = ends[:, 1024:1152]

    scan.pair()
    scan.send()

    @pl.loop(0, 4)
    def _(n):
        query, key = features(r.qkv, n, 0), features(r.qkv, n, 1)
        r.near[n] = chunk_near(query, key, r.cum[n], r.gates[n, 1], r.gates[n, 3])

    for copy in g_far:
        copy.wait_recv()
    r.gate_lin[...] = dot(
        r.first[...].reshape(512, 2048), r.wide_g[:, :, :, 0:HALF].reshape(2048, HALF)
    ).reshape(2, 4, 64, HALF)
    scan.fold(r.states)
    f_far = []
    for k in range(4):
        f_far += spread_far(r.wide_f, f_sems, FFN, f_near, k)

    @pl.loop(0, 4)
    def _(n):
        query, value = features(r.qkv, n, 0), features(r.qkv, n, 2)
        far, probs, mixing, mixed = chunk_out(
            query, value, r.cum[n], r.gates[n, 1], r.gates[n, 3], r.near[n], r.states[n]
        )
        r.far[n], r.probs[n], r.mixing[n], r.mixed[n] = far, probs, mixing, mixed
        normed = rms(mixed, r.head_gain[...])
        for s in range(2):
            r.normed[s, n] = normed[:, s * HALF : (s + 1) * HALF]

    swap2 = push(r.normed.at[1 - c], r.headnorm.at[c], r.swap_s.at[1], r.swap_r.at[1], partner)
    r.headnorm[c] = r.normed[c]
    rows_finish(b_rows, r.cot, b_sems)
    swap2.wait()
    sums = RowSum(r, "mix", r.parts, lambda k: r.parts[c, k])
    for core in (1 - c, c):
        lin = r.gate_lin[core].reshape(256, HALF)
        branch = (r.headnorm[core].reshape(256, HALF) * (lin * jax.nn.sigmoid(lin))).astype(BF)
        r.branch[core] = branch.reshape(4, 64, HALF)

        @pl.loop(0, 4)
        def _(n):
            got = nt(branch, r.wide_g[n, :, :, HALF : 2 * HALF].reshape(512, HALF))
            cols = pl.ds(pl.multiple_of(n * 512, 512), 512)
            r.parts[core, :, :, cols] = got.astype(BF).reshape(4, 64, 512)

        if core is not c:
            sums.pairs()
    sums.hops()
    resid1 = r.resid[...] + sums.result()
    r.resid1[...] = resid1
    r.second_own[...] = rms(resid1, r.norm2_gain[...]).astype(BF)
    s_rows = rows_start(r.second_own, r.second, s_sems)
    rows_finish(s_rows, r.second, s_sems)
    for copy in f_far:
        copy.wait()
    for sent in (q_deal, g_deal):
        deal_done(sent)
    for sent in (gates, f_deal):
        shuffle_done(sent)
    for near in (q_near, g_near, f_near):
        for copy in near.values():
            copy.wait_send()
    for copy in q_far + g_far:
        copy.wait_send()
    scan.done()
    sums.done()


def forward(wq, wg, wf, rows_a, rows_b, packed, resid, head_gain, norm2_gain):
    square = ((4, 64, 64), F32, VMEM)
    rows = (2, 4, 64, 2048)
    scratch = dict(
        proj=pltpu.VMEM((2, 4, 64, 3 * HALF), BF),
        normed=pltpu.VMEM((2, 4, 64, HALF), F32),
        parts=pltpu.VMEM(rows, BF),
        second_own=pltpu.VMEM((64, 2048), BF),
        q_send=DMA((2, 2)),
        q_recv=DMA((4,)),
        g_send=DMA((2, 2)),
        g_recv=DMA((4,)),
        swap_s=DMA((2,)),
        swap_r=DMA((2,)),
    )
    for name in ("rows_a_", "rows_b_", "rows_s_"):
        scratch.update(rows_sems(name))
    for name in ("q_spread", "g_spread", "f_spread"):
        scratch.update(spread_sems(name))
    for name in ("gate", "deal"):
        scratch.update(shuffle_sems(name))
    scratch.update(scan_scratch())
    scratch.update(sum_scratch("mix"))
    return remote_call(
        forward_kernel,
        1,
        dict(
            wq=(wq, ANY),
            wg=(wg, ANY),
            wf=(wf, ANY),
            rows_a=(rows_a, ANY),
            rows_b=(rows_b, ANY),
            packed=(packed, ANY),
            resid=(resid, VMEM),
            head_gain=(head_gain, VMEM),
            norm2_gain=(norm2_gain, VMEM),
        ),
        dict(
            wide_q=((4, 4, 128, 3 * HALF), BF, VMEM),
            wide_g=((4, 4, 128, 2 * HALF), BF, VMEM),
            wide_f=((4, 4, 128, FFN), BF, ANY),
            first=(rows, BF, VMEM),
            cot=(rows, BF, ANY),
            second=(rows, BF, VMEM),
            gates=((4, 4, 64, 64), F32, VMEM),
            qkv=((2, 4, 64, 3 * HALF), BF, VMEM),
            cum=square,
            near=square,
            far=square,
            probs=square,
            mixing=square,
            decays=((4, SLOTS, 128), F32, VMEM),
            states=((4, SLOTS, 1024), F32, VMEM),
            mixed=((4, 64, DK), F32, VMEM),
            gate_lin=((2, 4, 64, HALF), F32, VMEM),
            headnorm=((2, 4, 64, HALF), F32, VMEM),
            branch=((2, 4, 64, HALF), BF, VMEM),
            resid1=((64, 2048), F32, VMEM),
        ),
        scratch,
    )


class WeightSum:
    def __init__(self, r, name, grads, cols, loaded):
        self.grads, self.cols, self.half, self.loaded = grads, cols, cols // 2, loaded
        self.far, self.landed, self.ready = sems_of(r, name + "b", 3)
        self.own = getattr(r, name + "own") if loaded else None
        self.sems = sems_of(r, name + "s", 4)
        self.own_sem = getattr(r, name + "own_s") if loaded else None
        self.fars, self.nears, self.owns = {}, {}, {}

    def part(self, side):
        return pl.ds(side * self.half, self.half)

    def block(self, side, k, d):
        x, y, z, c = here()
        if side == 0:
            return self.grads.at[wrap(x + d), wrap(y + k), :, self.part(0)]
        return self.grads.at[wrap(x + k), wrap(y + d), :, self.part(1)]

    def peer(self, side, d):
        x, y, z, c = here()
        return (wrap(x + d), y, z, c) if side == 0 else (x, wrap(y + d), z, c)

    def mine(self, side, k):
        return self.own.at[side, k] if self.loaded else self.block(side, k, 0)

    def load(self):
        if self.loaded:
            for k in (1, 2, 3, 0):
                for side in range(2):
                    self.owns[side, k] = pltpu.make_async_copy(
                        self.block(side, k, 0), self.own.at[side, k], self.own_sem.at[side, k]
                    )
                    self.owns[side, k].start()

    def send(self, k):
        for d in range(1, 4):
            for side in range(2):
                self.fars[side, k, d] = push(
                    self.block(side, k, d),
                    self.far.at[side, k, d - 1],
                    self.sems[0].at[side, k, d - 1],
                    self.sems[1].at[side, k, d - 1],
                    self.peer(side, d),
                )

    def arrive(self, side, k):
        if self.loaded:
            self.owns[side, k].wait()
        for d in range(1, 4):
            self.fars[side, k, d].wait_recv()

    def total(self, side, k, rows):
        value = self.mine(side, k)[rows, :].astype(F32)
        for d in range(3):
            value = value + self.far[side, k, d, rows, :].astype(F32)
        return value

    def turn(self, k):
        for side in range(2):
            self.arrive(side, k)

            @pl.loop(0, 8)
            def _(t):
                rows = pl.ds(pl.multiple_of(t * 16, 16), 16)
                self.mine(side, k)[rows, :] = self.total(side, k, rows).astype(BF)

            self.nears[side, k] = push(
                self.mine(side, k),
                self.landed.at[side, k - 1],
                self.sems[2].at[side, k - 1],
                self.sems[3].at[side, k - 1],
                self.peer(1 - side, k),
            )

    def finish(self):
        for side in range(2):
            self.arrive(side, 0)
            for k in range(1, 4):
                self.nears[side, k].wait_recv()

            @pl.loop(0, 8)
            def _(t):
                rows = pl.ds(pl.multiple_of(t * 16, 16), 16)
                value = self.total(side, 0, rows)
                for k in range(3):
                    value = value + self.landed[side, k, rows, :].astype(F32)
                self.ready[rows, self.part(side)] = value.astype(BF)

    def done(self):
        for copy in list(self.fars.values()) + list(self.nears.values()):
            copy.wait_send()


def weight_scratch(name, cols, loaded):
    half = cols // 2
    out = {
        f"{name}b0": pltpu.VMEM((2, 4, 3, 128, half), BF),
        f"{name}b1": pltpu.VMEM((2, 3, 128, half), BF),
        f"{name}b2": pltpu.VMEM((128, cols), BF),
        f"{name}s0": DMA((2, 4, 3)),
        f"{name}s1": DMA((2, 4, 3)),
        f"{name}s2": DMA((2, 3)),
        f"{name}s3": DMA((2, 3)),
    }
    if loaded:
        out[f"{name}own"] = pltpu.VMEM((2, 4, 128, half), BF)
        out[f"{name}own_s"] = DMA((2, 4))
    return out


def return_start(ready, out, send, recv):
    x, y, z, c = here()
    dst, arrived = out.at[lax.rem(z, 2), c], recv.at[lax.rem(z, 2), c]
    sent = []
    for k in range(4):
        src = ready.at[pl.ds(k * 32, 32), :]
        same = jnp.logical_and(k == z, c == z // 2)
        copy = pltpu.make_async_remote_copy(
            src_ref=src,
            dst_ref=dst,
            send_sem=send.at[k],
            recv_sem=arrived,
            device_id=(x, y, k, z // 2),
            device_id_type=MESH,
        )

        @pl.when(same)
        def _():
            pltpu.make_async_copy(src, dst, arrived).start()

        @pl.when(jnp.logical_not(same))
        def _():
            copy.start()

        sent.append((same, copy))
    return sent


def return_wait(ready, out, recv):
    for j in range(2):
        for k in range(2):
            pltpu.make_async_copy(ready.at[pl.ds(0, 32), :], out.at[j, k], recv.at[j, k]).wait()


class SmallSum:
    def __init__(self, r, name, src, out):
        self.src, self.out = src, out
        self.held, self.now = sems_of(r, name + "b", 2)
        self.sems = sems_of(r, name + "s", 4)
        self.sends = []

    def half(self, k):
        width = self.src.shape[1] // 2
        return pl.ds(pl.multiple_of(k * width, 128), width)

    def pair(self):
        x, y, z, c = here()
        self.copy = push(
            self.src.at[:, self.half(1 - c)],
            self.held.at[0, c],
            self.sems[0].at[0],
            self.sems[1].at[0],
            (x, y, z, 1 - c),
        )
        self.held[0, c] = self.src[:, self.half(c)]

    def send(self, stage):
        x, y, z, c = here()
        if stage == 0:
            self.copy.wait()
            self.now[...] = self.held[0, 0] + self.held[0, 1]
        else:
            self.collect(stage)
        at = (z, y, x)[stage]
        self.held[stage + 1, at] = self.now[...]
        self.sent = []
        for d in range(1, 4):
            peer = [x, y, z, c]
            peer[2 - stage] = wrap(at + d)
            self.sent.append(
                push(
                    self.held.at[stage + 1, at],
                    self.held.at[stage + 1, at],
                    self.sems[2].at[stage, d - 1],
                    self.sems[3].at[stage, d - 1],
                    tuple(peer),
                )
            )

    def collect(self, stage):
        for copy in self.sent:
            copy.wait()
        value = self.held[stage, 0]
        for k in range(1, 4):
            value = value + self.held[stage, k]
        self.now[...] = value

    def close(self):
        x, y, z, c = here()
        self.collect(3)
        self.out[:, self.half(c)] = self.now[...]
        self.copy = push(
            self.now,
            self.out.at[:, self.half(c)],
            self.sems[0].at[1],
            self.sems[1].at[1],
            (x, y, z, 1 - c),
        )

    def done(self):
        self.copy.wait()


def small_scratch(name, rows, cols):
    return {
        f"{name}b0": pltpu.VMEM((4, 4, rows, cols // 2), F32),
        f"{name}b1": pltpu.VMEM((rows, cols // 2), F32),
        f"{name}s0": DMA((2,)),
        f"{name}s1": DMA((2,)),
        f"{name}s2": DMA((3, 3)),
        f"{name}s3": DMA((3, 3)),
    }


def backward_kernel(r):
    x, y, z, c = here()
    partner = (x, y, z, 1 - c)
    scan = Scan(r, True)
    greet(all_peers() + scan.senders())
    second = RowSum(r, "sec", r.second_part, lambda k: r.second_mine[k])
    ffn = RowSum(r, "ffn", r.ffn_part, lambda k: r.ffn_mine[k])
    one = WeightSum(r, "one", r.grads_one, 6 * HALF, True)
    two = WeightSum(r, "two", r.grads_two, 3 * HALF, True)
    tail = WeightSum(r, "tail", r.grads_tail, 2 * HALF, False)
    last = WeightSum(r, "last", r.grads_last, 3 * HALF, False)
    second.pairs()
    mine = [
        pltpu.make_async_copy(part.at[c], dst, r.mine_s.at[n])
        for n, (part, dst) in enumerate(
            ((r.second_part, r.second_mine), (r.ffn_part, r.ffn_mine))
        )
    ]
    for copy in mine:
        copy.start()
    one.load()
    for k in (1, 2, 3, 0):
        one.send(k)
    for copy in mine:
        copy.wait()
    second.hops()
    two.load()
    for k in (1, 2, 3, 0):
        two.send(k)
    ffn.pairs()
    e = second.result()
    v = r.resid1[...]
    grad, d_norm2 = rms_back(v, r.norm2_gain[...], e)
    r.small[...] = jnp.zeros_like(r.small)
    r.small[17:18, 0:2048] = d_norm2
    grad_resid1 = r.cot_own[...].astype(F32) + grad
    r.attn_own[...] = grad_resid1.astype(BF)
    r.grad_resid1[...] = grad_resid1
    a_sems = sems_of(r, "rows_a_", 5)
    a_rows = rows_start(r.attn_own, r.attn, a_sems)
    ffn.hops()
    rows_finish(a_rows, r.attn, a_sems)

    attn = r.attn[...].reshape(512, 2048)
    grad_branch = dot(attn, r.wide_g[:, :, :, HALF : 2 * HALF].reshape(2048, HALF))
    lin = r.gate_lin[...].reshape(512, HALF)
    sig = jax.nn.sigmoid(lin)
    normed = r.headnorm[...].reshape(512, HALF)
    r.grad_lin[...] = (
        (grad_branch * normed * sig * (1 + lin * (1 - sig))).astype(BF).reshape(2, 4, 64, HALF)
    )
    r.grad_out[...] = (grad_branch * lin * sig).reshape(2, 4, 64, HALF)
    swap = push(r.grad_out.at[1 - c], r.grad_norm.at[c], r.swap_s.at[0], r.swap_r.at[0], partner)
    r.grad_norm[c] = r.grad_out[c]
    swap.wait()

    def all_rows(ref):
        return ref[...].reshape(512, ref.shape[-1])

    def weight_rows(ref, n):
        return ref[:, :, :, pl.ds(pl.multiple_of(n * 512, 512), 512)].reshape(512, 512)

    r.d_head[...] = jnp.zeros_like(r.d_head)

    @pl.loop(0, 4)
    def _(n):
        mixed = r.mixed[n]
        e = jnp.concatenate([r.grad_norm[0, n], r.grad_norm[1, n]], axis=1)
        grad, d_head = rms_back(mixed, r.head_gain[...], e)
        r.d_head[0:1] += d_head
        g = grad.astype(BF)
        r.grad_mixed[n] = g
        dmix, dfar, dnear, dscore, ends_k, ends_v = chunk_back(
            features(r.qkv, n, 0),
            features(r.qkv, n, 2),
            g,
            r.cum[n],
            r.gates[n, 1],
            r.gates[n, 3],
            r.probs[n],
            r.states[n],
        )
        r.dmix[n], r.dfar[n], r.dnear[n], r.dscore[n] = dmix, dfar, dnear, dscore
        r.every[c, n] = jnp.concatenate([ends_k, ends_v, r.decays[n]], axis=1)

    scan.pair()
    r.small[18:19, 0:512] = r.d_head[0:1]
    scan.send()

    @pl.loop(0, 4)
    def _(n):
        r.grads_tail[n, :, :, 0:HALF] = (
            tn(weight_rows(r.first, n), all_rows(r.grad_lin)).astype(BF).reshape(4, 128, HALF)
        )
        r.grads_tail[n, :, :, HALF : 2 * HALF] = (
            tn(weight_rows(r.attn, n), all_rows(r.branch)).astype(BF).reshape(4, 128, HALF)
        )

    scan.fold(r.nexts)
    for k in (1, 2, 3, 0):
        tail.send(k)

    @pl.loop(0, 4)
    def _(n):
        dq, dk, dv, dlogit = chunk_last(
            features(r.qkv, n, 0),
            features(r.qkv, n, 1),
            features(r.qkv, n, 2),
            r.grad_mixed[n],
            r.gates[n, 0],
            r.gates[n, 1],
            r.gates[n, 2],
            r.gates[n, 3],
            r.cum[n],
            r.near[n],
            r.far[n],
            r.probs[n],
            r.mixing[n],
            r.states[n],
            r.dmix[n],
            r.dfar[n],
            r.dnear[n],
            r.dscore[n],
            r.nexts[n],
        )
        for m, part in enumerate((dq, dk, dv)):
            for s in range(2):
                r.dproj[s, n, :, pl.ds(m * HALF, HALF)] = part[
                    :, s * HALF : (s + 1) * HALF
                ].astype(BF)
        r.dlogit[n] = dlogit

    swap2 = push(r.dproj.at[1 - c], r.dqkv.at[c], r.swap_s.at[1], r.swap_r.at[1], partner)
    r.dqkv[c] = r.dproj[c]
    logits = shuffle_start(lambda k: r.dlogit.at[k], r.dl.at[z], *sems_of(r, "gate", 3))
    swap2.wait()

    first_part = r.attn
    first = RowSum(r, "fst", first_part, lambda k: first_part[c, k])
    for core in (1 - c, c):

        @pl.loop(0, 4)
        def _(n):
            got = nt(
                r.dqkv[core].reshape(256, 3 * HALF), r.wide_q[n].reshape(512, 3 * HALF)
            ) + nt(
                r.grad_lin[core].reshape(256, HALF),
                r.wide_g[n, :, :, 0:HALF].reshape(512, HALF),
            )
            cols = pl.ds(pl.multiple_of(n * 512, 512), 512)
            first_part[core, :, :, cols] = got.astype(BF).reshape(4, 64, 512)

        if core is not c:
            first.pairs()

    first.hops()

    @pl.loop(0, 4)
    def _(n):
        r.grads_last[n] = (
            tn(weight_rows(r.first, n), all_rows(r.dqkv)).astype(BF).reshape(4, 128, 3 * HALF)
        )

    for k in (1, 2, 3, 0):
        last.send(k)
    for k in range(1, 4):
        one.turn(k)
    for k in range(1, 4):
        two.turn(k)
    for k in range(1, 4):
        tail.turn(k)

    shuffle_wait(logits)
    low = jnp.zeros((64, 16), F32)
    bias = []
    for h in range(4):
        dl = r.dl[h]
        low = low + nt(dl, r.up[h], HIGH)
        r.small[0:16, 2048 + h * 64 : 2112 + h * 64] = tn(r.lowrank[...], dl, HIGH)
        bias.append(jnp.sum(dl, axis=0, keepdims=True))
    r.small[18:19, 512:768] = jnp.concatenate(bias, axis=1)
    r.small[0:16, 0:2048] = tn(low, r.first_own[...].astype(F32), HIGH)
    small = SmallSum(r, "sml", r.small, r.small_out)
    small.pair()
    small.send(0)
    grad_first = first.result() + dot(low, r.down[...], precision=HIGH)
    grad, d_norm1 = rms_back(r.resid[...], r.norm1_gain[...], grad_first)
    r.d_inputs[...] = r.grad_resid1[...] + grad
    r.tiny[...] = jnp.zeros_like(r.tiny)
    r.tiny[0:1, :] = d_norm1
    tiny = SmallSum(r, "tny", r.tiny, r.tiny_out)
    tiny.pair()
    tiny.send(0)
    one.finish()
    one_back = shuffle_start(
        lambda k: one.ready.at[pl.ds(pl.multiple_of(k * 32, 32), 32), :],
        r.out_one.at[z],
        *sems_of(r, "back_one", 3),
    )
    two.finish()
    two_back = shuffle_start(
        lambda k: two.ready.at[pl.ds(pl.multiple_of(k * 32, 32), 32), :],
        r.out_two.at[z],
        *sems_of(r, "back_two", 3),
    )
    small.send(1)
    tiny.send(1)
    tail.finish()
    tail_back = return_start(tail.ready, r.out_tail, r.tail_send, r.tail_recv)
    r.output[...] = (r.resid1[...] + ffn.result()).astype(BF)
    for k in range(1, 4):
        last.turn(k)
    small.send(2)
    tiny.send(2)
    last.finish()
    last_back = return_start(last.ready, r.out_last, r.last_send, r.last_recv)
    small.close()
    tiny.close()
    for sent in (one_back, two_back):
        shuffle_wait(sent)
        shuffle_done(sent)
    shuffle_done(logits)
    return_wait(tail.ready, r.out_tail, r.tail_recv)
    return_wait(last.ready, r.out_last, r.last_recv)
    deal_done(tail_back)
    deal_done(last_back)
    small.done()
    tiny.done()
    for part in (second, ffn, first, one, two, tail, last, scan):
        part.done()


def backward(operands):
    rows = (2, 4, 64, 2048)
    small = pltpu.VMEM((4, 64, 64), F32)
    scratch = dict(
        small=pltpu.VMEM((24, 2304), F32),
        tiny=pltpu.VMEM((8, 2048), F32),
        attn_own=pltpu.VMEM((64, 2048), BF),
        grad_resid1=pltpu.VMEM((64, 2048), F32),
        attn=pltpu.VMEM(rows, BF),
        grad_lin=pltpu.VMEM((2, 4, 64, HALF), BF),
        grad_out=pltpu.VMEM((2, 4, 64, HALF), F32),
        grad_norm=pltpu.VMEM((2, 4, 64, HALF), F32),
        grad_mixed=pltpu.VMEM((4, 64, DK), BF),
        d_head=pltpu.VMEM((8, DK), F32),
        dmix=small,
        dfar=small,
        dnear=small,
        dscore=small,
        dlogit=small,
        dl=small,
        nexts=pltpu.VMEM((4, SLOTS, 1024), F32),
        dproj=pltpu.VMEM((2, 4, 64, 3 * HALF), BF),
        dqkv=pltpu.VMEM((2, 4, 64, 3 * HALF), BF),
        second_mine=pltpu.VMEM((4, 64, 2048), BF),
        ffn_mine=pltpu.VMEM((4, 64, 2048), BF),
        mine_s=DMA((2,)),
        grads_tail=pltpu.VMEM((4, 4, 128, 2 * HALF), BF),
        grads_last=pltpu.VMEM((4, 4, 128, 3 * HALF), BF),
        swap_s=DMA((2,)),
        swap_r=DMA((2,)),
        tail_send=DMA((4,)),
        tail_recv=DMA((2, 2)),
        last_send=DMA((4,)),
        last_recv=DMA((2, 2)),
    )
    for name, cols, loaded in (
        ("one", 6 * HALF, True),
        ("two", 3 * HALF, True),
        ("tail", 2 * HALF, False),
        ("last", 3 * HALF, False),
    ):
        scratch.update(weight_scratch(name, cols, loaded))
    for name in ("sec", "ffn", "fst"):
        scratch.update(sum_scratch(name))
    for name in ("gate", "back_one", "back_two"):
        scratch.update(shuffle_sems(name))
    scratch.update(rows_sems("rows_a_"))
    scratch.update(scan_scratch())
    scratch.update(small_scratch("sml", 24, 2304))
    scratch.update(small_scratch("tny", 8, 2048))
    in_hbm = ("grads_one", "grads_two", "second_part", "ffn_part")
    return remote_call(
        backward_kernel,
        2,
        {name: (value, ANY if name in in_hbm else VMEM) for name, value in operands.items()},
        dict(
            output=((64, 2048), BF, VMEM),
            d_inputs=((64, 2048), F32, VMEM),
            out_last=((2, 2, 32, 3 * HALF), BF, VMEM),
            out_tail=((2, 2, 32, 2 * HALF), BF, VMEM),
            out_one=((4, 32, 6 * HALF), BF, VMEM),
            out_two=((4, 32, 3 * HALF), BF, VMEM),
            small_out=((24, 2304), F32, VMEM),
            tiny_out=((8, 2048), F32, VMEM),
        ),
        scratch,
    )


def rms(v, gain):
    return v * lax.rsqrt(jnp.mean(v * v, axis=-1, keepdims=True) + EPS) * gain


def rms_back(v, gain, e):
    r = lax.rsqrt(jnp.mean(v * v, axis=-1, keepdims=True) + EPS)
    grad = r * gain * e - v * (r * r * r) * jnp.mean(v * gain * e, axis=-1, keepdims=True)
    return grad, jnp.sum(e * v * r, axis=0, keepdims=True)


def body(
    inputs,
    offsets,
    norm1_gain,
    query_weight,
    key_weight,
    value_weight,
    gate_weight,
    out_weight,
    low_down,
    low_up,
    forget_bias,
    head_gain,
    norm2_gain,
    ffn_gate,
    ffn_up,
    ffn_down,
    cotangent,
):
    core = lax.axis_index("c")

    def dealt(weights):
        out = jnp.stack([w.reshape(32, 2, 2, HALF) for w in weights], axis=3)
        return out.transpose(1, 2, 0, 3, 4).reshape(2, 2, 32, len(weights) * HALF)

    wq = dealt((query_weight, key_weight, value_weight))
    wg = dealt((gate_weight, out_weight.T))
    wf = jnp.stack([w.reshape(32, 4, UNITS) for w in (ffn_gate, ffn_up, ffn_down)], axis=2)
    wf = jnp.pad(wf, ((0, 0), (0, 0), (0, 0), (0, UNITS_PAD - UNITS)))
    wf = wf.transpose(1, 0, 2, 3).reshape(4, 32, FFN)
    resid = inputs.astype(F32)
    gain1, gain2, gain_head = norm1_gain[None], norm2_gain[None], head_gain[None]
    first_own = rms(resid, gain1).astype(BF)

    lowrank = dot(first_own, low_down)
    up = low_up.astype(F32)
    logits = (dot(lowrank, up, precision=HIGH) + forget_bias).astype(BF).astype(F32)
    lam = jax.nn.log_sigmoid(logits) / 8.0
    offs = lax.dynamic_slice_in_dim(offsets, core * 64, 64, 0).astype(F32)
    offs = jnp.broadcast_to(offs[:, None], (64, 256))
    packed = jnp.stack([lam, -jnp.expm1(lam), jax.nn.sigmoid(-logits) / 8.0, offs])
    packed = packed.reshape(4, 64, 4, SLOTS).transpose(2, 0, 1, 3)

    f = forward(wq, wg, wf, first_own, cotangent, packed, resid, gain_head, gain2)

    second, cot = f["second"].reshape(512, 2048), f["cot"].reshape(512, 2048)
    wide_f = f["wide_f"].reshape(2048, FFN)
    w_gate, w_up, w_down = (wide_f[:, n * UNITS_PAD : (n + 1) * UNITS_PAD] for n in range(3))
    act_gate, act_up = dot(second, w_gate), dot(second, w_up)
    sig = jax.nn.sigmoid(act_gate)
    silu = act_gate * sig
    hidden = (silu * act_up).astype(BF)
    grad_hidden = dot(cot, w_down)
    grad_gate = (grad_hidden * act_up * sig * (1 + act_gate * (1 - sig))).astype(BF)
    grad_up = (grad_hidden * silu).astype(BF)
    ffn_part = nt(hidden, w_down).astype(BF).reshape(2, 4, 64, 2048)
    grad_acts = jnp.concatenate([grad_gate, grad_up], axis=1)
    second_part = nt(grad_acts, wide_f[:, : 2 * UNITS_PAD]).astype(BF).reshape(2, 4, 64, 2048)
    grads_one = tn(second, grad_acts).astype(BF).reshape(4, 4, 128, 2 * UNITS_PAD)
    grads_two = tn(cot, hidden).astype(BF).reshape(4, 4, 128, UNITS_PAD)

    done = ("wide_f", "cot", "second")
    operands = {name: value for name, value in f.items() if name not in done}
    operands.update(
        grads_one=grads_one,
        grads_two=grads_two,
        second_part=second_part,
        ffn_part=ffn_part,
        cot_own=cotangent,
        resid=resid,
        first_own=first_own,
        lowrank=lowrank,
        up=up.reshape(16, 4, SLOTS).transpose(1, 0, 2),
        down=low_down.astype(F32).T,
        norm1_gain=gain1,
        norm2_gain=gain2,
        head_gain=gain_head,
    )
    b = backward(operands)

    def owned(value, count):
        value = value.reshape(2, 2, 32, count, HALF).transpose(3, 2, 0, 1, 4)
        return value.reshape(count, 32, 1024).astype(F32)

    def units(value, count):
        value = value.reshape(4, 32, count, UNITS_PAD)[..., :UNITS].transpose(2, 1, 0, 3)
        return value.reshape(count, 32, 4 * UNITS).astype(F32)

    last, tail = owned(b["out_last"], 3), owned(b["out_tail"], 2)
    one, two = units(b["out_one"], 2), units(b["out_two"], 1)
    small, tiny = b["small_out"], b["tiny_out"]
    return (
        b["output"],
        b["d_inputs"],
        tiny[0],
        last[0],
        last[1],
        last[2],
        tail[0],
        tail[1].T,
        small[0:16, 0:2048].T,
        small[0:16, 2048:2304],
        small[18, 512:768],
        small[18, 0:512],
        small[17, 0:2048],
        one[0],
        one[1],
        two[0],
    )


def solution(mesh):
    fine = Mesh(mesh.devices.reshape(4, 4, 4, 2), ("x", "y", "z", "c"))
    seq = ("x", "y", "z")
    rows = P(("x", "y", "z", "c"), None)
    wide = P(seq, "c")
    placed = (
        (rows, P(seq), P())
        + (wide,) * 4
        + (P("c", seq), P(), P(), P(), P(), P(), wide, wide, wide, rows)
    )
    return jax.shard_map(
        body,
        mesh=fine,
        in_specs=placed,
        out_specs=(rows, rows, P())
        + (wide,) * 4
        + (P("c", seq), P(), P(), P(), P(), P(), wide, wide, wide),
        check_vma=False,
    )
```

```python
import functools

import jax
import jax.numpy as jnp
from jax import lax
from jax.experimental import pallas as pl
from jax.experimental.pallas import tpu as pltpu
from jax.sharding import Mesh
from jax.sharding import PartitionSpec as P

DK = 512
SLOTS = 64
CHUNK = 64
HALF = 256
UNITS = 704
UNITS_PAD = 768
EPS = 1e-06
SCALE = 0.125
BF = jnp.bfloat16
F32 = jnp.float32
HIGH = lax.Precision.HIGHEST
MESH = pl.DeviceIdType.MESH
ANY = pl.BlockSpec(memory_space=pl.ANY)
VMEM = pl.BlockSpec(memory_space=pltpu.VMEM)
DMA = pltpu.SemaphoreType.DMA
MIX = 5 * HALF
FFN = 3 * UNITS_PAD


def dot(left, right, dims=((1,), (0,)), precision=None):
    return lax.dot_general(
        left, right, (dims, ((), ())), precision=precision, preferred_element_type=F32
    )


def nt(left, right, precision=None):
    return dot(left, right, ((1,), (1,)), precision)


def tn(left, right, precision=None):
    return dot(left, right, ((0,), (0,)), precision)


def here():
    return tuple(lax.axis_index(a) for a in ("x", "y", "z", "c"))


def wrap(v, n=4):
    return lax.rem(v + n, n)


def greet(peers):
    barrier = pltpu.get_barrier_semaphore()
    for peer in peers:
        pl.semaphore_signal(barrier, inc=1, device_id=peer, device_id_type=MESH)


def greeted(peers):
    pl.semaphore_wait(pltpu.get_barrier_semaphore(), len(peers))


def push(src, dst, send, recv, peer):
    copy = pltpu.make_async_remote_copy(
        src_ref=src, dst_ref=dst, send_sem=send, recv_sem=recv, device_id=peer, device_id_type=MESH
    )
    copy.start()
    return copy


class Refs:
    pass


def remote_call(kernel, collective_id, operands, outs, scratch):
    names = list(operands) + list(outs) + list(scratch)

    def run(*refs):
        r = Refs()
        for name, ref in zip(names, refs):
            setattr(r, name, ref)
        kernel(r)

    results = pl.pallas_call(
        run,
        out_shape=[jax.ShapeDtypeStruct(shape, dtype) for shape, dtype, _ in outs.values()],
        in_specs=[spec for _, spec in operands.values()],
        out_specs=[spec for _, _, spec in outs.values()],
        scratch_shapes=list(scratch.values()),
        compiler_params=pltpu.CompilerParams(
            collective_id=collective_id, has_side_effects=True, vmem_limit_bytes=63 * 2**20
        ),
    )(*[array for array, _ in operands.values()])
    return dict(zip(outs, results))


def spread_block(w_ref, side, k, cols):
    x, y, z, c = here()
    part = pl.ds(side * (cols // 2), cols // 2)
    if side == 0:
        return w_ref.at[x, wrap(y - k), :, part]
    return w_ref.at[wrap(x - k), y, :, part]


def spread_near(w_ref, sems, cols):
    x, y, z, c = here()
    sent = {}
    for d in range(1, 4):
        for side in range(2):
            block = spread_block(w_ref, side, 0, cols)
            peer = (x, wrap(y + d), z, c) if side == 0 else (wrap(x + d), y, z, c)
            sent[side, d] = push(
                block, block, sems[0].at[side, d - 1], sems[1].at[side, d - 1], peer
            )
    return sent


def spread_far(w_ref, sems, cols, near, k):
    x, y, z, c = here()
    sent = []
    for side in range(2):
        if k > 0:
            near[side, k].wait_recv()
        block = spread_block(w_ref, side, k, cols)
        for d in range(1, 4):
            peer = (wrap(x + d), y, z, c) if side == 0 else (x, wrap(y + d), z, c)
            sent.append(
                push(
                    block, block, sems[2].at[side, k, d - 1], sems[3].at[side, k, d - 1], peer
                )
            )
    return sent


def rows_start(src, out, sems):
    x, y, z, c = here()
    hop_s, hop_r, pair_s, pair_r, own = sems
    mine = pltpu.make_async_copy(src, out.at[c, z], own)
    mine.start()
    hops = [
        push(src, out.at[c, z], hop_s.at[d - 1], hop_r.at[d - 1], (x, y, wrap(z + d), c))
        for d in range(1, 4)
    ]
    pairs = [push(src, out.at[c, z], pair_s.at[0], pair_r.at[0], (x, y, z, 1 - c))]
    return mine, hops, pairs


def rows_finish(started, out, sems):
    x, y, z, c = here()
    hop_s, hop_r, pair_s, pair_r, own = sems
    mine, hops, pairs = started
    for d in range(1, 4):
        hops[d - 1].wait_recv()
        block = out.at[c, wrap(z - d)]
        pairs.append(push(block, block, pair_s.at[d], pair_r.at[d], (x, y, z, 1 - c)))
    mine.wait()
    for copy in hops:
        copy.wait_send()
    for copy in pairs:
        copy.wait()


def group_peers():
    x, y, z, c = here()
    return [(x, y, wrap(z + d), k) for d in range(1, 4) for k in range(2)] + [(x, y, z, 1 - c)]


def row_peers():
    x, y, z, c = here()
    return [(x, y, wrap(z + d), c) for d in range(1, 4)] + [(x, y, z, 1 - c)]


def plane_peers():
    x, y, z, c = here()
    return [(wrap(x + d), y, z, c) for d in range(1, 4)] + [
        (x, wrap(y + d), z, c) for d in range(1, 4)
    ]


def all_peers():
    return group_peers() + plane_peers()


def spread_sems(name):
    kinds = ((2, 3), (2, 3), (2, 4, 3), (2, 4, 3))
    return {f"{name}{n}": DMA(shape) for n, shape in enumerate(kinds)}


def rows_sems(name):
    kinds = ((3,), (3,), (4,), (4,), ())
    return {f"{name}{n}": DMA(shape) for n, shape in enumerate(kinds)}


def sems_of(r, name, count):
    return [getattr(r, f"{name}{n}") for n in range(count)]


def deal_start(src, wide, send, recv):
    x, y, z, c = here()
    dst = wide.at[x, y, pl.ds(pl.multiple_of(z * 32, 32), 32), :]
    sent = []
    for j in range(2):
        for k in range(2):
            same = jnp.logical_and(2 * c + j == z, c == k)
            copy = pltpu.make_async_remote_copy(
                src_ref=src.at[j, k],
                dst_ref=dst,
                send_sem=send.at[j, k],
                recv_sem=recv.at[z],
                device_id=(x, y, 2 * c + j, k),
                device_id_type=MESH,
            )

            @pl.when(same)
            def _():
                pltpu.make_async_copy(src.at[j, k], dst, recv.at[z]).start()

            @pl.when(jnp.logical_not(same))
            def _():
                copy.start()

            sent.append((same, copy))
    return sent


def deal_wait(src, wide, recv):
    x, y, z, c = here()
    for s in range(4):
        dst = wide.at[x, y, pl.ds(s * 32, 32), :]
        pltpu.make_async_copy(src.at[0, 0], dst, recv.at[s]).wait()


def deal_done(sent):
    for same, copy in sent:

        @pl.when(jnp.logical_not(same))
        def _():
            copy.wait_send()


def shuffle_start(block, dst, send, recv, own):
    x, y, z, c = here()
    mine = pltpu.make_async_copy(block(z), dst, own)
    mine.start()
    sent = [
        push(block(wrap(z + d)), dst, send.at[d - 1], recv.at[d - 1], (x, y, wrap(z + d), c))
        for d in range(1, 4)
    ]
    return mine, sent


def shuffle_wait(started):
    started[0].wait()
    for copy in started[1]:
        copy.wait_recv()


def shuffle_done(started):
    for copy in started[1]:
        copy.wait_send()


def shuffle_sems(name):
    return {f"{name}0": DMA((3,)), f"{name}1": DMA((3,)), f"{name}2": DMA(())}


class RowSum:
    def __init__(self, r, name, parts, own):
        self.parts, self.own = parts, own
        self.theirs, self.landed = sems_of(r, name + "b", 2)
        self.sems = sems_of(r, name + "s", 4)

    def pairs(self):
        x, y, z, c = here()
        self.pair = [
            push(
                self.parts.at[1 - c, wrap(z + 1 + k)],
                self.theirs.at[k],
                self.sems[0].at[k],
                self.sems[1].at[k],
                (x, y, z, 1 - c),
            )
            for k in range(4)
        ]

    def hops(self):
        x, y, z, c = here()
        self.hop = []
        for k in range(3):
            to = wrap(z + 1 + k)
            self.pair[k].wait_recv()
            both = self.own(to).astype(F32) + self.theirs[k].astype(F32)
            self.theirs[k] = both.astype(BF)
            self.hop.append(
                push(
                    self.theirs.at[k],
                    self.landed.at[k],
                    self.sems[2].at[k],
                    self.sems[3].at[k],
                    (x, y, to, c),
                )
            )

    def result(self):
        x, y, z, c = here()
        self.pair[3].wait_recv()
        value = self.own(z).astype(F32) + self.theirs[3].astype(F32)
        for k in range(3):
            self.hop[k].wait_recv()
            value = value + self.landed[k].astype(F32)
        return value

    def done(self):
        for copy in self.pair + self.hop:
            copy.wait_send()


def sum_scratch(name):
    out = {f"{name}b{n}": pltpu.VMEM((k, 64, 2048), BF) for n, k in enumerate((4, 3))}
    out.update({f"{name}s{n}": DMA((k,)) for n, k in enumerate((4, 4, 3, 3))})
    return out


class Scan:
    def __init__(self, r, back):
        self.back, self.every = back, r.every
        self.total, self.rows, self.cols, self.entry = r.total, r.scan_y, r.scan_x, r.entry
        self.lead_b, self.lead_a = r.lead_b, r.lead_a
        self.sems = sems_of(r, "scan", 8)
        self.order = [(n, k) for n in range(4) for k in range(2)]
        self.line = list(range(4))
        if back:
            self.order, self.line = self.order[::-1], self.line[::-1]

    def before(self, other, mine):
        return (other > mine) if self.back else (other < mine)

    def pack(self, block, state, decay):
        block[:, 0:512] = state.astype(BF)
        high = decay.astype(BF)
        block[:, 512:640] = high
        block[:, 640:768] = (decay - high.astype(F32)).astype(BF)

    def unpack(self, block):
        keep = block[:, 512:640].astype(F32) + block[:, 640:768].astype(F32)
        return block[:, 0:512].astype(F32), keep

    def factor(self, k, n, width):
        return jnp.concatenate([self.every[k, n, :, 1024:1152]] * (width // 128), axis=1)

    def pair(self):
        x, y, z, c = here()
        self.swap = push(
            self.every.at[c], self.every.at[c], self.sems[0], self.sems[1], (x, y, z, 1 - c)
        )

    def send(self):
        x, y, z, c = here()
        self.swap.wait_recv()
        half = pl.ds(pl.multiple_of(c * DK, DK), DK)
        n, k = self.order[0]
        state = self.every[k, n, :, half]
        decay = self.every[k, n, :, 1024:1152]
        for n, k in self.order[1:]:
            state = self.factor(k, n, DK) * state + self.every[k, n, :, half]
            decay = self.every[k, n, :, 1024:1152] * decay
        self.pack(self.rows.at[y], state, decay)
        self.far = [
            push(
                self.rows.at[y],
                self.rows.at[y],
                self.sems[2].at[d - 1],
                self.sems[3].at[d - 1],
                (x, wrap(y + d), z, c),
            )
            for d in range(1, 4)
        ]

    def middle(self):
        x, y, z, c = here()
        for copy in self.far:
            copy.wait_recv()
        state, decay = jnp.zeros((SLOTS, DK), F32), jnp.ones((SLOTS, 128), F32)
        lead_b, lead_a = state, decay
        for k in self.line:
            term, keep = self.unpack(self.rows.at[k])
            wide = jnp.concatenate([keep] * 4, axis=1)
            valid = self.before(k, y)
            lead_b = jnp.where(valid, wide * lead_b + term, lead_b)
            lead_a = jnp.where(valid, keep * lead_a, lead_a)
            state, decay = wide * state + term, keep * decay
        self.lead_b[...], self.lead_a[...] = lead_b, lead_a
        self.pack(self.cols.at[x], state, decay)
        self.far += [
            push(
                self.cols.at[x],
                self.cols.at[x],
                self.sems[6].at[d - 1],
                self.sems[7].at[d - 1],
                (wrap(x + d), y, z, c),
            )
            for d in range(1, 4)
        ]

    def fold(self, out):
        x, y, z, c = here()
        for copy in self.far[3:]:
            copy.wait_recv()
        state = jnp.zeros((SLOTS, DK), F32)
        for k in self.line:
            term, keep = self.unpack(self.cols.at[k])
            fresh = jnp.concatenate([keep] * 4, axis=1) * state + term
            state = jnp.where(self.before(k, x), fresh, state)
        state = jnp.concatenate([self.lead_a[...]] * 4, axis=1) * state + self.lead_b[...]
        self.total[...] = state
        self.entry[c] = state
        self.last = push(
            self.total, self.entry.at[c], self.sems[4], self.sems[5], (x, y, z, 1 - c)
        )
        self.last.wait_recv()
        for s in range(2):
            state = self.entry[s]
            cols = pl.ds(s * DK, DK)
            for n, k in self.order:

                @pl.when(c == k)
                def _():
                    out[n, :, cols] = state

                state = self.factor(k, n, DK) * state + self.every[k, n, :, cols]

    def done(self):
        for copy in self.far + [self.swap, self.last]:
            copy.wait_send()


def scan_scratch():
    out = dict(
        every=pltpu.VMEM((2, 4, SLOTS, 1152), F32),
        total=pltpu.VMEM((SLOTS, DK), F32),
        scan_y=pltpu.VMEM((4, SLOTS, 768), BF),
        scan_x=pltpu.VMEM((4, SLOTS, 768), BF),
        lead_b=pltpu.VMEM((SLOTS, DK), F32),
        lead_a=pltpu.VMEM((SLOTS, 128), F32),
        entry=pltpu.VMEM((2, SLOTS, DK), F32),
    )
    kinds = ((), (), (3,), (3,), (), (), (3,), (3,))
    out.update({f"scan{n}": DMA(shape) for n, shape in enumerate(kinds)})
    return out


def places():
    row = lax.broadcasted_iota(jnp.int32, (CHUNK, CHUNK), 0)
    col = lax.broadcasted_iota(jnp.int32, (CHUNK, CHUNK), 1)
    return row, col


def tri(lower):
    row, col = places()
    return ((row >= col) if lower else (row <= col)).astype(F32)


def seen_mask(offs):
    row, col = places()
    return jnp.logical_and(row >= col, offs >= (row - col).astype(F32))


def carried(cum, offs):
    return jnp.exp(cum) * (offs > places()[0].astype(F32)).astype(F32)


def reaching(cum, offs):
    final = offs[CHUNK - 1 : CHUNK]
    tail = (places()[0].astype(F32) >= CHUNK - 1 - final).astype(F32)
    return jnp.exp(cum[CHUNK - 1 : CHUNK] - cum) * tail


def features(ref, n, which):
    cols = pl.ds(which * HALF, HALF)
    return jnp.concatenate([ref[0, n, :, cols], ref[1, n, :, cols]], axis=1)


def tiles(value):
    return [value[8 * b : 8 * b + 8] for b in range(CHUNK // 8)]


def one_row(blocks, i):
    return blocks[i // 8][i % 8 : i % 8 + 1]


def spans(cum, i):
    last = one_row(cum, i)
    return [(b, jnp.exp(jnp.minimum(cum[b] - last, 0.0))) for b in range(i // 8, CHUNK // 8)]


def weigh(cum, write, columns):
    cum, write, cols = tiles(cum), tiles(write), tiles(columns)
    total = [jnp.zeros((8, SLOTS), F32) for _ in range(CHUNK // 8)]
    for i in range(CHUNK):
        scale = one_row(write, i)
        for b, span in spans(cum, i):
            total[b] = total[b] + cols[b][:, i : i + 1] * (span * scale)
    return jnp.concatenate(total, axis=0)


def weigh_slots(cum, write, values):
    cum, write, vals = tiles(cum), tiles(write), tiles(values)
    lane = lax.broadcasted_iota(jnp.int32, (8, CHUNK), 1)
    total = [jnp.zeros((8, CHUNK), F32) for _ in range(CHUNK // 8)]
    for i in range(CHUNK):
        scale = one_row(write, i)
        for b, span in spans(cum, i):
            got = jnp.sum(vals[b] * (span * scale), axis=1, keepdims=True)
            total[b] = jnp.where(lane == i, got, total[b])
    return jnp.concatenate(total, axis=0)


def chunk_ends(key, value, lam, write, offs):
    cum = dot(tri(True), lam, precision=HIGH)
    ending = (reaching(cum, offs) * write).astype(BF)
    keep = (offs[CHUNK - 1 : CHUNK, 0:1] > CHUNK - 1).astype(F32)
    keep = keep * jnp.exp(tn(lam, jnp.ones((CHUNK, 128), F32), HIGH))
    return cum, jnp.concatenate([tn(ending, key), tn(ending, value), keep], axis=1)


def chunk_near(query, key, cum, write, offs):
    return weigh(cum, write, jnp.where(seen_mask(offs), nt(query, key) * SCALE, 0.0))


def chunk_out(query, value, cum, write, offs, near, state):
    carry = carried(cum, offs)
    far = nt(query, state[:, 0:512].astype(BF)) * SCALE
    scores = near + carry * far
    scores = jnp.exp(scores - jnp.max(scores, axis=1, keepdims=True))
    probs = scores / jnp.sum(scores, axis=1, keepdims=True)
    mixing = jnp.where(seen_mask(offs), weigh_slots(cum, write, probs), 0.0)
    mixed = dot(mixing.astype(BF), value) + dot(
        (probs * carry).astype(BF), state[:, 512:1024].astype(BF)
    )
    return far, probs, mixing, mixed


def chunk_back(query, value, g, cum, write, offs, probs, state):
    carry = carried(cum, offs)
    dmix = jnp.where(seen_mask(offs), nt(g, value), 0.0)
    dfar = nt(g, state[:, 512:1024].astype(BF))
    dnear = weigh(cum, write, dmix)
    dprobs = dnear + carry * dfar
    dscore = probs * (dprobs - jnp.sum(probs * dprobs, axis=1, keepdims=True))
    ends_k = tn((SCALE * dscore * carry).astype(BF), query)
    ends_v = tn((probs * carry).astype(BF), g)
    return dmix, dfar, dnear, dscore, ends_k, ends_v


def chunk_pairs(cum, write, affinity, dmix, dscore, probs):
    cums, writes = tiles(cum), tiles(write)
    aff, dmx, dsc, prb = tiles(affinity), tiles(dmix), tiles(dscore), tiles(probs)
    lane = lax.broadcasted_iota(jnp.int32, (8, CHUNK), 1)
    daff = [jnp.zeros((8, CHUNK), F32) for _ in range(CHUNK // 8)]
    fresh = []
    for i in range(CHUNK):
        scale = one_row(writes, i)
        both = jnp.zeros((8, SLOTS), F32)
        for b, span in spans(cums, i):
            got = jnp.sum(dsc[b] * (span * scale), axis=1, keepdims=True)
            daff[b] = jnp.where(lane == i, got, daff[b])
            both = both + (dsc[b] * aff[b][:, i : i + 1] + prb[b] * dmx[b][:, i : i + 1]) * span
        fresh.append(jnp.sum(both, axis=0, keepdims=True))
    return jnp.concatenate(daff, axis=0), jnp.concatenate(fresh, axis=0)


def chunk_last(
    query, key, value, g, lam, write, slope, offs, cum, near, far, probs, mixing, state, dmix, dfar, dnear, dscore, after
):
    carry, seen, reach = carried(cum, offs), seen_mask(offs), reaching(cum, offs)
    affinity = jnp.where(seen, nt(query, key) * SCALE, 0.0)
    daff, fresh = chunk_pairs(cum, write, affinity, dmix, dscore, probs)
    daff = jnp.where(seen, daff * SCALE, 0.0).astype(BF)
    ending = (reach * write).astype(BF)
    nk, nv = after[:, 0:512].astype(BF), after[:, 512:1024].astype(BF)
    dq = dot(daff, key) + dot((SCALE * dscore * carry).astype(BF), state[:, 0:512].astype(BF))
    dk = tn(daff, query) + dot(ending, nk)
    dv = tn(mixing.astype(BF), g) + dot(ending, nv)
    dend = (nt(key, nk) + nt(value, nv)) * reach
    dkeep = nt(jnp.ones((8, 1024), F32), after * state, HIGH)[0:1]
    keep = (offs[CHUNK - 1 : CHUNK] > CHUNK - 1).astype(F32) * jnp.exp(cum[CHUNK - 1 : CHUNK])
    scaled = write * dend
    dcum = dscore * near + probs * dnear + carry * (dscore * far + probs * dfar)
    dcum = dcum - write * fresh - scaled
    at_end = jnp.sum(scaled, axis=0, keepdims=True) + dkeep * keep
    dcum = dcum + jnp.where(places()[0] == CHUNK - 1, at_end, 0.0)
    dlam = dot(tri(False), dcum, precision=HIGH) - jnp.exp(lam) * (fresh + dend)
    return dq, dk, dv, dlam * slope


def log1p_small(u):
    series = u * (1 - u * (1 / 2 - u * (1 / 3 - u / 4)))
    return jnp.where(u < 0.01, series, jnp.log(1 + u))


def one_less_exp(v):
    series = -v * (1 + v * (1 / 2 + v * (1 / 6 + v / 24)))
    return jnp.where(v > -0.03, series, 1 - jnp.exp(v))


def forget_gate(logits):
    small = jnp.exp(-jnp.abs(logits))
    lam = (jnp.minimum(logits, 0.0) - log1p_small(small)) / 8
    slope = jnp.where(logits >= 0, small, 1.0) / (1 + small) / 8
    return lam, one_less_exp(lam), slope


def prepare(r):
    x, y, z, c = here()
    first = rms(r.inputs[...].astype(F32), r.norm1_gain[...]).astype(BF)
    r.first_own[...] = first
    eye = (
        lax.broadcasted_iota(jnp.int32, (32, 32), 0) == lax.broadcasted_iota(jnp.int32, (32, 32), 1)
    ).astype(BF)
    out_t = nt(eye, r.out_weight[...]).astype(BF)
    for j in range(2):
        for k in range(2):
            cols = slice((2 * j + k) * HALF, (2 * j + k + 1) * HALF)
            for n, w in enumerate((r.query_weight, r.key_weight, r.value_weight)):
                r.wq[j, k, :, n * HALF : (n + 1) * HALF] = w[:, cols]
            r.wg[j, k, :, 0:HALF] = r.gate_weight[:, cols]
            r.wg[j, k, :, HALF : 2 * HALF] = out_t[:, cols]
    lowrank = dot(first, r.low_down[...])
    r.lowrank[...] = lowrank
    logits = dot(lowrank, r.low_up[...].astype(F32), precision=HIGH) + r.forget_bias[...]
    lam, write, slope = forget_gate(logits.astype(BF).astype(F32))
    row = lax.broadcasted_iota(jnp.int32, (64, 128), 0)
    col = lax.broadcasted_iota(jnp.int32, (64, 128), 1)
    offs = jnp.where(col == row + 64 * c, r.offsets[...].astype(F32), 0.0)
    offs = jnp.broadcast_to(jnp.sum(offs, axis=1, keepdims=True), (64, SLOTS))
    for h in range(4):
        cols = slice(h * SLOTS, (h + 1) * SLOTS)
        for n, value in enumerate((lam, write, slope)):
            r.packed[h, n] = value[:, cols]
        r.packed[h, 3] = offs
    for k in range(4):
        for n, w in enumerate((r.ffn_gate, r.ffn_up, r.ffn_down)):
            piece = w[:, k * UNITS : (k + 1) * UNITS]
            pad = jnp.zeros((32, UNITS_PAD - UNITS), BF)
            r.wf[k, :, n * UNITS_PAD : (n + 1) * UNITS_PAD] = jnp.concatenate([piece, pad], axis=1)


def forward_kernel(r):
    x, y, z, c = here()
    partner = (x, y, z, 1 - c)
    scan = Scan(r, False)
    greet(all_peers())
    prepare(r)
    greeted(all_peers())
    q_deal = deal_start(r.wq, r.wide_q, r.q_send, r.q_recv)
    a_sems, b_sems, s_sems = (sems_of(r, n, 5) for n in ("rows_a_", "rows_b_", "rows_s_"))
    a_rows = rows_start(r.first_own, r.first, a_sems)
    gates = shuffle_start(lambda k: r.packed.at[k], r.gates.at[z], *sems_of(r, "gate", 3))
    g_deal = deal_start(r.wg, r.wide_g, r.g_send, r.g_recv)
    f_deal = shuffle_start(
        lambda k: r.wf.at[k],
        r.wide_f.at[x, y, pl.ds(pl.multiple_of(z * 32, 32), 32), :],
        *sems_of(r, "deal", 3),
    )
    q_sems, g_sems, f_sems = (sems_of(r, n, 4) for n in ("q_spread", "g_spread", "f_spread"))
    deal_wait(r.wq, r.wide_q, r.q_recv)
    q_near = spread_near(r.wide_q, q_sems, 3 * HALF)
    q_far = spread_far(r.wide_q, q_sems, 3 * HALF, q_near, 0)
    for k in range(1, 4):
        q_far += spread_far(r.wide_q, q_sems, 3 * HALF, q_near, k)
    deal_wait(r.wg, r.wide_g, r.g_recv)
    g_near = spread_near(r.wide_g, g_sems, 2 * HALF)
    rows_finish(a_rows, r.first, a_sems)
    shuffle_wait(gates)
    for copy in q_far:
        copy.wait_recv()
    g_far = []
    for k in range(4):
        g_far += spread_far(r.wide_g, g_sems, 2 * HALF, g_near, k)
    shuffle_wait(f_deal)
    f_near = spread_near(r.wide_f, f_sems, FFN)

    @pl.loop(0, 3)
    def _(n):
        cols = pl.ds(pl.multiple_of(n * HALF, HALF), HALF)
        rows = r.first[...].reshape(512, 2048)
        got = dot(rows, r.wide_q[:, :, :, cols].reshape(2048, HALF))
        r.proj[:, :, :, cols] = got.astype(BF).reshape(2, 4, 64, HALF)

    swap = push(r.proj.at[1 - c], r.qkv.at[c], r.swap_s.at[0], r.swap_r.at[0], partner)
    r.qkv[c] = r.proj[c]
    swap.wait()

    @pl.loop(0, 4)
    def _(n):
        lam, write, offs = r.gates[n, 0], r.gates[n, 1], r.gates[n, 3]
        cum, ends = chunk_ends(features(r.qkv, n, 1), features(r.qkv, n, 2), lam, write, offs)
        r.cum[n] = cum
        r.every[c, n] = ends
        r.decays[n] = ends[:, 1024:1152]

    scan.pair()
    scan.send()
    b_rows = rows_start(r.rows_b, r.cot, b_sems)

    @pl.loop(0, 4)
    def _(n):
        query, key = features(r.qkv, n, 0), features(r.qkv, n, 1)
        r.near[n] = chunk_near(query, key, r.cum[n], r.gates[n, 1], r.gates[n, 3])

    scan.middle()
    f_far = spread_far(r.wide_f, f_sems, FFN, f_near, 0)
    for copy in g_far:
        copy.wait_recv()
    r.gate_lin[...] = dot(
        r.first[...].reshape(512, 2048), r.wide_g[:, :, :, 0:HALF].reshape(2048, HALF)
    ).reshape(2, 4, 64, HALF)
    scan.fold(r.states)
    for k in range(1, 4):
        f_far += spread_far(r.wide_f, f_sems, FFN, f_near, k)

    @pl.loop(0, 4)
    def _(n):
        query, value = features(r.qkv, n, 0), features(r.qkv, n, 2)
        far, probs, mixing, mixed = chunk_out(
            query, value, r.cum[n], r.gates[n, 1], r.gates[n, 3], r.near[n], r.states[n]
        )
        r.far[n], r.probs[n], r.mixing[n], r.mixed[n] = far, probs, mixing, mixed
        normed = rms(mixed, r.head_gain[...])
        for s in range(2):
            r.normed[s, n] = normed[:, s * HALF : (s + 1) * HALF]

    swap2 = push(r.normed.at[1 - c], r.headnorm.at[c], r.swap_s.at[1], r.swap_r.at[1], partner)
    r.headnorm[c] = r.normed[c]
    rows_finish(b_rows, r.cot, b_sems)
    swap2.wait()
    sums = RowSum(r, "mix", r.parts, lambda k: r.parts[c, k])
    for core in (1 - c, c):
        lin = r.gate_lin[core].reshape(256, HALF)
        branch = (r.headnorm[core].reshape(256, HALF) * (lin * jax.nn.sigmoid(lin))).astype(BF)
        r.branch[core] = branch.reshape(4, 64, HALF)

        @pl.loop(0, 4)
        def _(n):
            got = nt(branch, r.wide_g[n, :, :, HALF : 2 * HALF].reshape(512, HALF))
            cols = pl.ds(pl.multiple_of(n * 512, 512), 512)
            r.parts[core, :, :, cols] = got.astype(BF).reshape(4, 64, 512)

        if core is not c:
            sums.pairs()
    sums.hops()
    resid1 = r.inputs[...].astype(F32) + sums.result()
    r.resid1[...] = resid1
    r.second_own[...] = rms(resid1, r.norm2_gain[...]).astype(BF)
    s_rows = rows_start(r.second_own, r.second, s_sems)
    rows_finish(s_rows, r.second, s_sems)
    for copy in f_far:
        copy.wait()
    for sent in (q_deal, g_deal):
        deal_done(sent)
    for sent in (gates, f_deal):
        shuffle_done(sent)
    for near in (q_near, g_near, f_near):
        for copy in near.values():
            copy.wait_send()
    for copy in q_far + g_far:
        copy.wait_send()
    scan.done()
    sums.done()


def forward(operands):
    square = ((4, 64, 64), F32, VMEM)
    rows = (2, 4, 64, 2048)
    scratch = dict(
        proj=pltpu.VMEM((2, 4, 64, 3 * HALF), BF),
        normed=pltpu.VMEM((2, 4, 64, HALF), F32),
        parts=pltpu.VMEM(rows, BF),
        second_own=pltpu.VMEM((64, 2048), BF),
        wq=pltpu.VMEM((2, 2, 32, 3 * HALF), BF),
        wg=pltpu.VMEM((2, 2, 32, 2 * HALF), BF),
        wf=pltpu.VMEM((4, 32, FFN), BF),
        packed=pltpu.VMEM((4, 4, 64, SLOTS), F32),
        q_send=DMA((2, 2)),
        q_recv=DMA((4,)),
        g_send=DMA((2, 2)),
        g_recv=DMA((4,)),
        swap_s=DMA((2,)),
        swap_r=DMA((2,)),
    )
    for name in ("rows_a_", "rows_b_", "rows_s_"):
        scratch.update(rows_sems(name))
    for name in ("q_spread", "g_spread", "f_spread"):
        scratch.update(spread_sems(name))
    for name in ("gate", "deal"):
        scratch.update(shuffle_sems(name))
    scratch.update(scan_scratch())
    scratch.update(sum_scratch("mix"))
    return remote_call(
        forward_kernel,
        1,
        {name: (value, ANY if name == "rows_b" else VMEM) for name, value in operands.items()},
        dict(
            wide_q=((4, 4, 128, 3 * HALF), BF, VMEM),
            wide_g=((4, 4, 128, 2 * HALF), BF, VMEM),
            wide_f=((4, 4, 128, FFN), BF, ANY),
            first_own=((64, 2048), BF, VMEM),
            lowrank=((64, 16), F32, VMEM),
            first=(rows, BF, VMEM),
            cot=(rows, BF, ANY),
            second=(rows, BF, VMEM),
            gates=((4, 4, 64, 64), F32, VMEM),
            qkv=((2, 4, 64, 3 * HALF), BF, VMEM),
            cum=square,
            near=square,
            far=square,
            probs=square,
            mixing=square,
            decays=((4, SLOTS, 128), F32, VMEM),
            states=((4, SLOTS, 1024), F32, VMEM),
            mixed=((4, 64, DK), F32, VMEM),
            gate_lin=((2, 4, 64, HALF), F32, VMEM),
            headnorm=((2, 4, 64, HALF), F32, VMEM),
            branch=((2, 4, 64, HALF), BF, VMEM),
            resid1=((64, 2048), F32, VMEM),
        ),
        scratch,
    )


class WeightSum:
    def __init__(self, r, name, grads, cols, loaded):
        self.grads, self.cols, self.half, self.loaded = grads, cols, cols // 2, loaded
        self.far, self.landed, self.ready = sems_of(r, name + "b", 3)
        self.own = getattr(r, name + "own") if loaded else None
        self.sems = sems_of(r, name + "s", 4)
        self.own_sem = getattr(r, name + "own_s") if loaded else None
        self.fars, self.nears, self.owns = {}, {}, {}

    def part(self, side):
        return pl.ds(side * self.half, self.half)

    def block(self, side, k, d):
        x, y, z, c = here()
        if side == 0:
            return self.grads.at[wrap(x + d), wrap(y + k), :, self.part(0)]
        return self.grads.at[wrap(x + k), wrap(y + d), :, self.part(1)]

    def peer(self, side, d):
        x, y, z, c = here()
        return (wrap(x + d), y, z, c) if side == 0 else (x, wrap(y + d), z, c)

    def mine(self, side, k):
        return self.own.at[side, k] if self.loaded else self.block(side, k, 0)

    def load(self):
        if self.loaded:
            for k in (1, 2, 3, 0):
                for side in range(2):
                    self.owns[side, k] = pltpu.make_async_copy(
                        self.block(side, k, 0), self.own.at[side, k], self.own_sem.at[side, k]
                    )
                    self.owns[side, k].start()

    def send(self, k):
        for d in range(1, 4):
            for side in range(2):
                self.fars[side, k, d] = push(
                    self.block(side, k, d),
                    self.far.at[side, k, d - 1],
                    self.sems[0].at[side, k, d - 1],
                    self.sems[1].at[side, k, d - 1],
                    self.peer(side, d),
                )

    def arrive(self, side, k):
        if self.loaded:
            self.owns[side, k].wait()
        for d in range(1, 4):
            self.fars[side, k, d].wait_recv()

    def total(self, side, k, rows):
        value = self.mine(side, k)[rows, :].astype(F32)
        for d in range(3):
            value = value + self.far[side, k, d, rows, :].astype(F32)
        return value

    def turn(self, k):
        for side in range(2):
            self.arrive(side, k)

            @pl.loop(0, 8)
            def _(t):
                rows = pl.ds(pl.multiple_of(t * 16, 16), 16)
                self.mine(side, k)[rows, :] = self.total(side, k, rows).astype(BF)

            self.nears[side, k] = push(
                self.mine(side, k),
                self.landed.at[side, k - 1],
                self.sems[2].at[side, k - 1],
                self.sems[3].at[side, k - 1],
                self.peer(1 - side, k),
            )

    def finish(self):
        for side in range(2):
            self.arrive(side, 0)
            for k in range(1, 4):
                self.nears[side, k].wait_recv()

            @pl.loop(0, 8)
            def _(t):
                rows = pl.ds(pl.multiple_of(t * 16, 16), 16)
                value = self.total(side, 0, rows)
                for k in range(3):
                    value = value + self.landed[side, k, rows, :].astype(F32)
                self.ready[rows, self.part(side)] = value.astype(BF)

    def done(self):
        for copy in list(self.fars.values()) + list(self.nears.values()):
            copy.wait_send()


def weight_scratch(name, cols, loaded):
    half = cols // 2
    out = {
        f"{name}b0": pltpu.VMEM((2, 4, 3, 128, half), BF),
        f"{name}b1": pltpu.VMEM((2, 3, 128, half), BF),
        f"{name}b2": pltpu.VMEM((128, cols), BF),
        f"{name}s0": DMA((2, 4, 3)),
        f"{name}s1": DMA((2, 4, 3)),
        f"{name}s2": DMA((2, 3)),
        f"{name}s3": DMA((2, 3)),
    }
    if loaded:
        out[f"{name}own"] = pltpu.VMEM((2, 4, 128, half), BF)
        out[f"{name}own_s"] = DMA((2, 4))
    return out


def return_start(ready, out, send, recv):
    x, y, z, c = here()
    dst, arrived = out.at[lax.rem(z, 2), c], recv.at[lax.rem(z, 2), c]
    sent = []
    for k in range(4):
        src = ready.at[pl.ds(k * 32, 32), :]
        same = jnp.logical_and(k == z, c == z // 2)
        copy = pltpu.make_async_remote_copy(
            src_ref=src,
            dst_ref=dst,
            send_sem=send.at[k],
            recv_sem=arrived,
            device_id=(x, y, k, z // 2),
            device_id_type=MESH,
        )

        @pl.when(same)
        def _():
            pltpu.make_async_copy(src, dst, arrived).start()

        @pl.when(jnp.logical_not(same))
        def _():
            copy.start()

        sent.append((same, copy))
    return sent


def return_wait(ready, out, recv):
    for j in range(2):
        for k in range(2):
            pltpu.make_async_copy(ready.at[pl.ds(0, 32), :], out.at[j, k], recv.at[j, k]).wait()


class SmallSum:
    def __init__(self, r, name, src, out):
        self.src, self.out = src, out
        self.held, self.now = sems_of(r, name + "b", 2)
        self.sems = sems_of(r, name + "s", 4)
        self.sends = []

    def half(self, k):
        width = self.src.shape[1] // 2
        return pl.ds(pl.multiple_of(k * width, 128), width)

    def pair(self):
        x, y, z, c = here()
        self.copy = push(
            self.src.at[:, self.half(1 - c)],
            self.held.at[0, c],
            self.sems[0].at[0],
            self.sems[1].at[0],
            (x, y, z, 1 - c),
        )
        self.held[0, c] = self.src[:, self.half(c)]

    def send(self, stage):
        x, y, z, c = here()
        if stage == 0:
            self.copy.wait()
            self.now[...] = self.held[0, 0] + self.held[0, 1]
        else:
            self.collect(stage)
        at = (z, y, x)[stage]
        self.held[stage + 1, at] = self.now[...]
        self.sent = []
        for d in range(1, 4):
            peer = [x, y, z, c]
            peer[2 - stage] = wrap(at + d)
            self.sent.append(
                push(
                    self.held.at[stage + 1, at],
                    self.held.at[stage + 1, at],
                    self.sems[2].at[stage, d - 1],
                    self.sems[3].at[stage, d - 1],
                    tuple(peer),
                )
            )

    def collect(self, stage):
        for copy in self.sent:
            copy.wait()
        value = self.held[stage, 0]
        for k in range(1, 4):
            value = value + self.held[stage, k]
        self.now[...] = value

    def close(self):
        x, y, z, c = here()
        self.collect(3)
        self.out[:, self.half(c)] = self.now[...]
        self.copy = push(
            self.now,
            self.out.at[:, self.half(c)],
            self.sems[0].at[1],
            self.sems[1].at[1],
            (x, y, z, 1 - c),
        )

    def done(self):
        self.copy.wait()


def small_scratch(name, rows, cols):
    return {
        f"{name}b0": pltpu.VMEM((4, 4, rows, cols // 2), F32),
        f"{name}b1": pltpu.VMEM((rows, cols // 2), F32),
        f"{name}s0": DMA((2,)),
        f"{name}s1": DMA((2,)),
        f"{name}s2": DMA((3, 3)),
        f"{name}s3": DMA((3, 3)),
    }


def backward_kernel(r):
    x, y, z, c = here()
    partner = (x, y, z, 1 - c)
    scan = Scan(r, True)
    greet(all_peers())
    greeted(all_peers())
    second = RowSum(r, "sec", r.second_part, lambda k: r.second_mine[k])
    ffn = RowSum(r, "ffn", r.ffn_part, lambda k: r.ffn_mine[k])
    one = WeightSum(r, "one", r.grads_one, 6 * HALF, True)
    two = WeightSum(r, "two", r.grads_two, 3 * HALF, True)
    tail = WeightSum(r, "tail", r.grads_tail, 2 * HALF, False)
    last = WeightSum(r, "last", r.grads_last, 3 * HALF, False)
    second.pairs()
    mine = [
        pltpu.make_async_copy(part.at[c], dst, r.mine_s.at[n])
        for n, (part, dst) in enumerate(
            ((r.second_part, r.second_mine), (r.ffn_part, r.ffn_mine))
        )
    ]
    for copy in mine:
        copy.start()
    one.load()
    for k in (1, 2, 3, 0):
        one.send(k)
    for copy in mine:
        copy.wait()
    second.hops()
    two.load()
    for k in (1, 2, 3, 0):
        two.send(k)
    e = second.result()
    v = r.resid1[...]
    grad, d_norm2 = rms_back(v, r.norm2_gain[...], e)
    r.small[...] = jnp.zeros_like(r.small)
    r.small[17:18, 0:2048] = d_norm2
    grad_resid1 = r.cot_own[...].astype(F32) + grad
    r.attn_own[...] = grad_resid1.astype(BF)
    r.grad_resid1[...] = grad_resid1
    a_sems = sems_of(r, "rows_a_", 5)
    a_rows = rows_start(r.attn_own, r.attn, a_sems)
    rows_finish(a_rows, r.attn, a_sems)
    ffn.pairs()

    attn = r.attn[...].reshape(512, 2048)
    grad_branch = dot(attn, r.wide_g[:, :, :, HALF : 2 * HALF].reshape(2048, HALF))
    lin = r.gate_lin[...].reshape(512, HALF)
    sig = jax.nn.sigmoid(lin)
    normed = r.headnorm[...].reshape(512, HALF)
    r.grad_lin[...] = (
        (grad_branch * normed * sig * (1 + lin * (1 - sig))).astype(BF).reshape(2, 4, 64, HALF)
    )
    r.grad_out[...] = (grad_branch * lin * sig).reshape(2, 4, 64, HALF)
    swap = push(r.grad_out.at[1 - c], r.grad_norm.at[c], r.swap_s.at[0], r.swap_r.at[0], partner)
    r.grad_norm[c] = r.grad_out[c]
    swap.wait()
    ffn.hops()

    def all_rows(ref):
        return ref[...].reshape(512, ref.shape[-1])

    def weight_rows(ref, n):
        return ref[:, :, :, pl.ds(pl.multiple_of(n * 512, 512), 512)].reshape(512, 512)

    r.d_head[...] = jnp.zeros_like(r.d_head)

    @pl.loop(0, 4)
    def _(n):
        mixed = r.mixed[n]
        e = jnp.concatenate([r.grad_norm[0, n], r.grad_norm[1, n]], axis=1)
        grad, d_head = rms_back(mixed, r.head_gain[...], e)
        r.d_head[0:1] += d_head
        g = grad.astype(BF)
        r.grad_mixed[n] = g
        dmix, dfar, dnear, dscore, ends_k, ends_v = chunk_back(
            features(r.qkv, n, 0),
            features(r.qkv, n, 2),
            g,
            r.cum[n],
            r.gates[n, 1],
            r.gates[n, 3],
            r.probs[n],
            r.states[n],
        )
        r.dmix[n], r.dfar[n], r.dnear[n], r.dscore[n] = dmix, dfar, dnear, dscore
        r.every[c, n] = jnp.concatenate([ends_k, ends_v, r.decays[n]], axis=1)

    scan.pair()
    r.small[18:19, 0:512] = r.d_head[0:1]
    scan.send()

    @pl.loop(0, 4)
    def _(n):
        r.grads_tail[n, :, :, 0:HALF] = (
            tn(weight_rows(r.first, n), all_rows(r.grad_lin)).astype(BF).reshape(4, 128, HALF)
        )
        r.grads_tail[n, :, :, HALF : 2 * HALF] = (
            tn(weight_rows(r.attn, n), all_rows(r.branch)).astype(BF).reshape(4, 128, HALF)
        )

    scan.middle()
    for k in range(1, 4):
        one.turn(k)
    scan.fold(r.nexts)
    for k in (1, 2, 3, 0):
        tail.send(k)

    @pl.loop(0, 4)
    def _(n):
        dq, dk, dv, dlogit = chunk_last(
            features(r.qkv, n, 0),
            features(r.qkv, n, 1),
            features(r.qkv, n, 2),
            r.grad_mixed[n],
            r.gates[n, 0],
            r.gates[n, 1],
            r.gates[n, 2],
            r.gates[n, 3],
            r.cum[n],
            r.near[n],
            r.far[n],
            r.probs[n],
            r.mixing[n],
            r.states[n],
            r.dmix[n],
            r.dfar[n],
            r.dnear[n],
            r.dscore[n],
            r.nexts[n],
        )
        for m, part in enumerate((dq, dk, dv)):
            for s in range(2):
                r.dproj[s, n, :, pl.ds(m * HALF, HALF)] = part[
                    :, s * HALF : (s + 1) * HALF
                ].astype(BF)
        r.dlogit[n] = dlogit

    swap2 = push(r.dproj.at[1 - c], r.dqkv.at[c], r.swap_s.at[1], r.swap_r.at[1], partner)
    r.dqkv[c] = r.dproj[c]
    logits = shuffle_start(lambda k: r.dlogit.at[k], r.dl.at[z], *sems_of(r, "gate", 3))
    for k in range(1, 4):
        two.turn(k)
    swap2.wait()

    @pl.loop(0, 4)
    def _(n):
        r.grads_last[n] = (
            tn(weight_rows(r.first, n), all_rows(r.dqkv)).astype(BF).reshape(4, 128, 3 * HALF)
        )

    for k in (1, 2, 3, 0):
        last.send(k)
    first_part = r.attn
    first = RowSum(r, "fst", first_part, lambda k: first_part[c, k])
    for core in (1 - c, c):

        @pl.loop(0, 4)
        def _(n):
            got = nt(
                r.dqkv[core].reshape(256, 3 * HALF), r.wide_q[n].reshape(512, 3 * HALF)
            ) + nt(
                r.grad_lin[core].reshape(256, HALF),
                r.wide_g[n, :, :, 0:HALF].reshape(512, HALF),
            )
            cols = pl.ds(pl.multiple_of(n * 512, 512), 512)
            first_part[core, :, :, cols] = got.astype(BF).reshape(4, 64, 512)

        if core is not c:
            first.pairs()

    first.hops()

    for k in range(1, 4):
        tail.turn(k)

    shuffle_wait(logits)
    low = jnp.zeros((64, 16), F32)
    bias = []
    for h in range(4):
        dl = r.dl[h]
        low = low + nt(dl, r.up[h], HIGH)
        r.small[0:16, 2048 + h * 64 : 2112 + h * 64] = tn(r.lowrank[...], dl, HIGH)
        bias.append(jnp.sum(dl, axis=0, keepdims=True))
    r.small[18:19, 512:768] = jnp.concatenate(bias, axis=1)
    r.small[0:16, 0:2048] = tn(low, r.first_own[...].astype(F32), HIGH)
    small = SmallSum(r, "sml", r.small, r.small_out)
    small.pair()
    small.send(0)
    grad_first = first.result() + dot(low, r.down[...], precision=HIGH)
    grad, d_norm1 = rms_back(r.inputs[...].astype(F32), r.norm1_gain[...], grad_first)
    r.d_inputs[...] = r.grad_resid1[...] + grad
    r.tiny[...] = jnp.zeros_like(r.tiny)
    r.tiny[0:1, :] = d_norm1
    tiny = SmallSum(r, "tny", r.tiny, r.tiny_out)
    tiny.pair()
    tiny.send(0)
    one.finish()
    one_back = shuffle_start(
        lambda k: one.ready.at[pl.ds(pl.multiple_of(k * 32, 32), 32), :],
        r.out_one.at[z],
        *sems_of(r, "back_one", 3),
    )
    two.finish()
    two_back = shuffle_start(
        lambda k: two.ready.at[pl.ds(pl.multiple_of(k * 32, 32), 32), :],
        r.out_two.at[z],
        *sems_of(r, "back_two", 3),
    )
    small.send(1)
    tiny.send(1)
    tail.finish()
    tail_back = return_start(tail.ready, r.out_tail, r.tail_send, r.tail_recv)
    r.output[...] = (r.resid1[...] + ffn.result()).astype(BF)
    for k in range(1, 4):
        last.turn(k)
    small.send(2)
    tiny.send(2)
    last.finish()
    last_back = return_start(last.ready, r.out_last, r.last_send, r.last_recv)
    small.close()
    tiny.close()
    for sent in (one_back, two_back):
        shuffle_wait(sent)
        shuffle_done(sent)
    shuffle_done(logits)
    return_wait(tail.ready, r.out_tail, r.tail_recv)
    return_wait(last.ready, r.out_last, r.last_recv)
    deal_done(tail_back)
    deal_done(last_back)
    small.done()
    tiny.done()
    for part in (second, ffn, first, one, two, tail, last, scan):
        part.done()


def backward(operands):
    rows = (2, 4, 64, 2048)
    small = pltpu.VMEM((4, 64, 64), F32)
    scratch = dict(
        small=pltpu.VMEM((24, 2304), F32),
        tiny=pltpu.VMEM((8, 2048), F32),
        attn_own=pltpu.VMEM((64, 2048), BF),
        grad_resid1=pltpu.VMEM((64, 2048), F32),
        attn=pltpu.VMEM(rows, BF),
        grad_lin=pltpu.VMEM((2, 4, 64, HALF), BF),
        grad_out=pltpu.VMEM((2, 4, 64, HALF), F32),
        grad_norm=pltpu.VMEM((2, 4, 64, HALF), F32),
        grad_mixed=pltpu.VMEM((4, 64, DK), BF),
        d_head=pltpu.VMEM((8, DK), F32),
        dmix=small,
        dfar=small,
        dnear=small,
        dscore=small,
        dlogit=small,
        dl=small,
        nexts=pltpu.VMEM((4, SLOTS, 1024), F32),
        dproj=pltpu.VMEM((2, 4, 64, 3 * HALF), BF),
        dqkv=pltpu.VMEM((2, 4, 64, 3 * HALF), BF),
        second_mine=pltpu.VMEM((4, 64, 2048), BF),
        ffn_mine=pltpu.VMEM((4, 64, 2048), BF),
        mine_s=DMA((2,)),
        grads_tail=pltpu.VMEM((4, 4, 128, 2 * HALF), BF),
        grads_last=pltpu.VMEM((4, 4, 128, 3 * HALF), BF),
        swap_s=DMA((2,)),
        swap_r=DMA((2,)),
        tail_send=DMA((4,)),
        tail_recv=DMA((2, 2)),
        last_send=DMA((4,)),
        last_recv=DMA((2, 2)),
    )
    for name, cols, loaded in (
        ("one", 6 * HALF, True),
        ("two", 3 * HALF, True),
        ("tail", 2 * HALF, False),
        ("last", 3 * HALF, False),
    ):
        scratch.update(weight_scratch(name, cols, loaded))
    for name in ("sec", "ffn", "fst"):
        scratch.update(sum_scratch(name))
    for name in ("gate", "back_one", "back_two"):
        scratch.update(shuffle_sems(name))
    scratch.update(rows_sems("rows_a_"))
    scratch.update(scan_scratch())
    scratch.update(small_scratch("sml", 24, 2304))
    scratch.update(small_scratch("tny", 8, 2048))
    in_hbm = ("grads_one", "grads_two", "second_part", "ffn_part")
    return remote_call(
        backward_kernel,
        2,
        {name: (value, ANY if name in in_hbm else VMEM) for name, value in operands.items()},
        dict(
            output=((64, 2048), BF, VMEM),
            d_inputs=((64, 2048), F32, VMEM),
            out_last=((2, 2, 32, 3 * HALF), BF, VMEM),
            out_tail=((2, 2, 32, 2 * HALF), BF, VMEM),
            out_one=((4, 32, 6 * HALF), BF, VMEM),
            out_two=((4, 32, 3 * HALF), BF, VMEM),
            small_out=((24, 2304), F32, VMEM),
            tiny_out=((8, 2048), F32, VMEM),
        ),
        scratch,
    )


def results_kernel(
    out, d_in, last, tail, one, two, small, tiny, output, d_inputs, norm1, q, k, v, g, o, down, up, bias, head, norm2, fg, fu, fd
):
    output[...] = out[...]
    d_inputs[...] = d_in[...]
    for j in range(2):
        for n in range(2):
            at = slice((2 * j + n) * HALF, (2 * j + n + 1) * HALF)
            for m, ref in enumerate((q, k, v)):
                ref[:, at] = last[j, n, :, m * HALF : (m + 1) * HALF].astype(F32)
            g[:, at] = tail[j, n, :, 0:HALF].astype(F32)
            row = lax.broadcasted_iota(jnp.int32, (HALF, HALF), 0)
            col = lax.broadcasted_iota(jnp.int32, (HALF, HALF), 1)
            o[at, :] = nt((row == col).astype(BF), tail[j, n, :, HALF : 2 * HALF])
    for n in range(4):
        at = slice(n * UNITS, (n + 1) * UNITS)
        fg[:, at] = one[n, :, 0:UNITS].astype(F32)
        fu[:, at] = one[n, :, UNITS_PAD : UNITS_PAD + UNITS].astype(F32)
        fd[:, at] = two[n, :, 0:UNITS].astype(F32)
    norm1[...] = tiny[0:1, :]
    norm2[...] = small[17:18, 0:2048]
    head[...] = small[18:19, 0:512]
    bias[...] = small[18:19, 512:768]
    up[...] = small[0:16, 2048:2304]
    down[...] = small[0:16, 0:2048]


def results(b):
    shapes = [((64, 2048), BF), ((64, 2048), F32), ((1, 2048), F32)]
    shapes += [((32, 1024), F32)] * 4 + [((1024, 32), F32), ((16, 2048), F32), ((16, 256), F32)]
    shapes += [((1, 256), F32), ((1, 512), F32), ((1, 2048), F32)] + [((32, 4 * UNITS), F32)] * 3
    names = ("output", "d_inputs", "out_last", "out_tail", "out_one", "out_two")
    names += ("small_out", "tiny_out")
    call = pl.pallas_call(
        results_kernel,
        out_shape=[jax.ShapeDtypeStruct(shape, dtype) for shape, dtype in shapes],
        compiler_params=pltpu.CompilerParams(vmem_limit_bytes=32 * 2**20),
    )
    out = list(call(*[b[name] for name in names]))
    out[8] = out[8].T
    for n in (2, 10, 11, 12):
        out[n] = out[n][0]
    return tuple(out)


def rms(v, gain):
    return v * lax.rsqrt(jnp.mean(v * v, axis=-1, keepdims=True) + EPS) * gain


def rms_back(v, gain, e):
    r = lax.rsqrt(jnp.mean(v * v, axis=-1, keepdims=True) + EPS)
    grad = r * gain * e - v * (r * r * r) * jnp.mean(v * gain * e, axis=-1, keepdims=True)
    return grad, jnp.sum(e * v * r, axis=0, keepdims=True)


def body(
    inputs,
    offsets,
    norm1_gain,
    query_weight,
    key_weight,
    value_weight,
    gate_weight,
    out_weight,
    low_down,
    low_up,
    forget_bias,
    head_gain,
    norm2_gain,
    ffn_gate,
    ffn_up,
    ffn_down,
    cotangent,
):
    gain1, gain2, gain_head = norm1_gain[None], norm2_gain[None], head_gain[None]
    f = forward(
        dict(
            query_weight=query_weight,
            key_weight=key_weight,
            value_weight=value_weight,
            gate_weight=gate_weight,
            out_weight=out_weight,
            ffn_gate=ffn_gate,
            ffn_up=ffn_up,
            ffn_down=ffn_down,
            inputs=inputs,
            rows_b=cotangent,
            offsets=offsets[None],
            low_down=low_down,
            low_up=low_up,
            forget_bias=forget_bias[None],
            norm1_gain=gain1,
            norm2_gain=gain2,
            head_gain=gain_head,
        )
    )

    second, cot = f["second"].reshape(512, 2048), f["cot"].reshape(512, 2048)
    wide_f = f["wide_f"].reshape(2048, FFN)
    w_gate, w_up, w_down = (wide_f[:, n * UNITS_PAD : (n + 1) * UNITS_PAD] for n in range(3))
    act_gate, act_up = dot(second, w_gate), dot(second, w_up)
    sig = jax.nn.sigmoid(act_gate)
    silu = act_gate * sig
    hidden = (silu * act_up).astype(BF)
    grad_hidden = dot(cot, w_down)
    grad_gate = (grad_hidden * act_up * sig * (1 + act_gate * (1 - sig))).astype(BF)
    grad_up = (grad_hidden * silu).astype(BF)
    ffn_part = nt(hidden, w_down).astype(BF).reshape(2, 4, 64, 2048)
    grad_acts = jnp.concatenate([grad_gate, grad_up], axis=1)
    second_part = nt(grad_acts, wide_f[:, : 2 * UNITS_PAD]).astype(BF).reshape(2, 4, 64, 2048)
    grads_one = tn(second, grad_acts).astype(BF).reshape(4, 4, 128, 2 * UNITS_PAD)
    grads_two = tn(cot, hidden).astype(BF).reshape(4, 4, 128, UNITS_PAD)

    done = ("wide_f", "cot", "second")
    operands = {name: value for name, value in f.items() if name not in done}
    operands.update(
        grads_one=grads_one,
        grads_two=grads_two,
        second_part=second_part,
        ffn_part=ffn_part,
        cot_own=cotangent,
        inputs=inputs,
        up=low_up.astype(F32).reshape(16, 4, SLOTS).transpose(1, 0, 2),
        down=low_down.astype(F32).T,
        norm1_gain=gain1,
        norm2_gain=gain2,
        head_gain=gain_head,
    )
    b = backward(operands)

    return results(b)


def solution(mesh):
    fine = Mesh(mesh.devices.reshape(4, 4, 4, 2), ("x", "y", "z", "c"))
    seq = ("x", "y", "z")
    rows = P(("x", "y", "z", "c"), None)
    wide = P(seq, "c")
    placed = (
        (rows, P(seq), P())
        + (wide,) * 4
        + (P("c", seq), P(), P(), P(), P(), P(), wide, wide, wide, rows)
    )
    return jax.shard_map(
        body,
        mesh=fine,
        in_specs=placed,
        out_specs=(rows, rows, P())
        + (wide,) * 4
        + (P("c", seq), P(), P(), P(), P(), P(), wide, wide, wide),
        check_vma=False,
    )
```

```python
import functools

import jax
import jax.numpy as jnp
from jax import lax
from jax.experimental import pallas as pl
from jax.experimental.pallas import tpu as pltpu
from jax.sharding import Mesh
from jax.sharding import PartitionSpec as P

DK = 512
SLOTS = 64
CHUNK = 64
HALF = 256
UNITS = 704
UNITS_PAD = 768
EPS = 1e-06
SCALE = 0.125
BF = jnp.bfloat16
F32 = jnp.float32
HIGH = lax.Precision.HIGHEST
MESH = pl.DeviceIdType.MESH
ANY = pl.BlockSpec(memory_space=pl.ANY)
VMEM = pl.BlockSpec(memory_space=pltpu.VMEM)
DMA = pltpu.SemaphoreType.DMA
FFN = 3 * UNITS_PAD


def dot(left, right, dims=((1,), (0,)), precision=None):
    return lax.dot_general(
        left, right, (dims, ((), ())), precision=precision, preferred_element_type=F32
    )


def nt(left, right, precision=None):
    return dot(left, right, ((1,), (1,)), precision)


def tn(left, right, precision=None):
    return dot(left, right, ((0,), (0,)), precision)


def here():
    return tuple(lax.axis_index(a) for a in ("x", "y", "z", "c"))


def wrap(v, n=4):
    return lax.rem(v + n, n)


def greet(peers):
    barrier = pltpu.get_barrier_semaphore()
    for peer in peers:
        pl.semaphore_signal(barrier, inc=1, device_id=peer, device_id_type=MESH)


def greeted(peers):
    pl.semaphore_wait(pltpu.get_barrier_semaphore(), len(peers))


def push(src, dst, send, recv, peer):
    copy = pltpu.make_async_remote_copy(
        src_ref=src, dst_ref=dst, send_sem=send, recv_sem=recv, device_id=peer, device_id_type=MESH
    )
    copy.start()
    return copy


class Refs:
    def start(self):
        self.loads = {}
        for n, name in enumerate(self.loaded):
            copy = pltpu.make_async_copy(
                getattr(self, "in_" + name), getattr(self, name), self.load_sem.at[n]
            )
            copy.start()
            self.loads[name] = copy
        self.saves = []

    def need(self, *names):
        for name in names:
            copy = self.loads.pop(name, None)
            if copy is not None:
                copy.wait()

    def save(self, *names):
        for name in names:
            copy = pltpu.make_async_copy(
                getattr(self, name),
                getattr(self, "out_" + name),
                self.save_sem.at[len(self.saves)],
            )
            copy.start()
            self.saves.append(copy)

    def finish(self):
        for copy in self.saves:
            copy.wait()


def remote_call(kernel, collective_id, operands, outs, scratch, loaded=(), saved=()):
    loaded, saved = dict(loaded), dict(saved)
    operands = dict(operands)
    operands.update({"in_" + name: (value, ANY) for name, value in loaded.items()})
    outs = dict(outs)
    outs.update({"out_" + name: (shape, dtype, ANY) for name, (shape, dtype) in saved.items()})
    scratch = dict(scratch)
    scratch.update({name: pltpu.VMEM(v.shape, v.dtype) for name, v in loaded.items()})
    scratch.update({name: pltpu.VMEM(shape, dtype) for name, (shape, dtype) in saved.items()})
    scratch["load_sem"] = DMA((max(len(loaded), 1),))
    scratch["save_sem"] = DMA((max(len(saved), 1),))
    names = list(operands) + list(outs) + list(scratch)

    def run(*refs):
        r = Refs()
        for name, ref in zip(names, refs):
            setattr(r, name, ref)
        r.loaded = list(loaded)
        kernel(r)

    results = pl.pallas_call(
        run,
        out_shape=[jax.ShapeDtypeStruct(shape, dtype) for shape, dtype, _ in outs.values()],
        in_specs=[spec for _, spec in operands.values()],
        out_specs=[spec for _, _, spec in outs.values()],
        scratch_shapes=list(scratch.values()),
        compiler_params=pltpu.CompilerParams(
            collective_id=collective_id, has_side_effects=True, vmem_limit_bytes=63 * 2**20
        ),
    )(*[array for array, _ in operands.values()])
    return {name.removeprefix("out_"): value for name, value in zip(outs, results)}


class Spread:
    def __init__(self, r, name, ref, start, width):
        self.ref, self.start, self.half = ref, start, width // 2
        self.sems = sems_of(r, name, 4)
        self.nears, self.fars = {}, []

    def block(self, side, k):
        x, y, z, c = here()
        part = pl.ds(self.start + side * self.half, self.half)
        if side == 0:
            return self.ref.at[x, wrap(y - k), :, part]
        return self.ref.at[wrap(x - k), y, :, part]

    def near(self):
        x, y, z, c = here()
        for d in range(1, 4):
            for side in range(2):
                block = self.block(side, 0)
                peer = (x, wrap(y + d), z, c) if side == 0 else (wrap(x + d), y, z, c)
                self.nears[side, d] = push(
                    block, block, self.sems[0].at[side, d - 1], self.sems[1].at[side, d - 1], peer
                )

    def far(self, *steps):
        x, y, z, c = here()
        for k in steps:
            for side in range(2):
                if k > 0:
                    self.nears[side, k].wait_recv()
                block = self.block(side, k)
                for d in range(1, 4):
                    peer = (wrap(x + d), y, z, c) if side == 0 else (x, wrap(y + d), z, c)
                    self.fars.append(
                        push(
                            block,
                            block,
                            self.sems[2].at[side, k, d - 1],
                            self.sems[3].at[side, k, d - 1],
                            peer,
                        )
                    )

    def arrive(self):
        for copy in self.fars:
            copy.wait_recv()

    def done(self):
        for copy in list(self.nears.values()) + self.fars:
            copy.wait_send()


def spread_sems(name):
    kinds = ((2, 3), (2, 3), (2, 4, 3), (2, 4, 3))
    return {f"{name}{n}": DMA(shape) for n, shape in enumerate(kinds)}


def rows_start(src, out, sems):
    x, y, z, c = here()
    hop_s, hop_r, pair_s, pair_r, own = sems
    mine = pltpu.make_async_copy(src, out.at[c, z], own)
    mine.start()
    hops = [
        push(src, out.at[c, z], hop_s.at[d - 1], hop_r.at[d - 1], (x, y, wrap(z + d), c))
        for d in range(1, 4)
    ]
    pairs = [push(src, out.at[c, z], pair_s.at[0], pair_r.at[0], (x, y, z, 1 - c))]
    return mine, hops, pairs


def rows_finish(started, out, sems):
    x, y, z, c = here()
    hop_s, hop_r, pair_s, pair_r, own = sems
    mine, hops, pairs = started
    for d in range(1, 4):
        hops[d - 1].wait_recv()
        block = out.at[c, wrap(z - d)]
        pairs.append(push(block, block, pair_s.at[d], pair_r.at[d], (x, y, z, 1 - c)))
    mine.wait()
    for copy in hops:
        copy.wait_send()
    for copy in pairs:
        copy.wait()


def group_peers():
    x, y, z, c = here()
    return [(x, y, wrap(z + d), k) for d in range(1, 4) for k in range(2)] + [(x, y, z, 1 - c)]


def row_peers():
    x, y, z, c = here()
    return [(x, y, wrap(z + d), c) for d in range(1, 4)] + [(x, y, z, 1 - c)]


def plane_peers():
    x, y, z, c = here()
    return [(wrap(x + d), y, z, c) for d in range(1, 4)] + [
        (x, wrap(y + d), z, c) for d in range(1, 4)
    ]


def all_peers():
    return group_peers() + plane_peers()


def rows_sems(name):
    kinds = ((3,), (3,), (4,), (4,), ())
    return {f"{name}{n}": DMA(shape) for n, shape in enumerate(kinds)}


def sems_of(r, name, count):
    return [getattr(r, f"{name}{n}") for n in range(count)]


def deal_start(src, wide, send, recv):
    x, y, z, c = here()
    dst = wide.at[x, y, pl.ds(pl.multiple_of(z * 32, 32), 32), :]
    sent = []
    for j in range(2):
        for k in range(2):
            same = jnp.logical_and(2 * c + j == z, c == k)
            copy = pltpu.make_async_remote_copy(
                src_ref=src.at[j, k],
                dst_ref=dst,
                send_sem=send.at[j, k],
                recv_sem=recv.at[z],
                device_id=(x, y, 2 * c + j, k),
                device_id_type=MESH,
            )

            @pl.when(same)
            def _():
                pltpu.make_async_copy(src.at[j, k], dst, recv.at[z]).start()

            @pl.when(jnp.logical_not(same))
            def _():
                copy.start()

            sent.append((same, copy))
    return sent


def deal_wait(src, wide, recv):
    x, y, z, c = here()
    for s in range(4):
        dst = wide.at[x, y, pl.ds(s * 32, 32), :]
        pltpu.make_async_copy(src.at[0, 0], dst, recv.at[s]).wait()


def deal_done(sent):
    for same, copy in sent:

        @pl.when(jnp.logical_not(same))
        def _():
            copy.wait_send()


def shuffle_start(block, dst, send, recv, own):
    x, y, z, c = here()
    mine = pltpu.make_async_copy(block(z), dst, own)
    mine.start()
    sent = [
        push(block(wrap(z + d)), dst, send.at[d - 1], recv.at[d - 1], (x, y, wrap(z + d), c))
        for d in range(1, 4)
    ]
    return mine, sent


def shuffle_wait(started):
    started[0].wait()
    for copy in started[1]:
        copy.wait_recv()


def shuffle_done(started):
    for copy in started[1]:
        copy.wait_send()


def shuffle_sems(name):
    return {f"{name}0": DMA((3,)), f"{name}1": DMA((3,)), f"{name}2": DMA(())}


class RowSum:
    def __init__(self, r, name, parts, own):
        self.parts, self.own = parts, own
        self.theirs, self.landed = r.theirs, r.landed
        self.sems = sems_of(r, name + "s", 4)

    def pairs(self):
        x, y, z, c = here()
        self.pair = [
            push(
                self.parts.at[1 - c, wrap(z + 1 + k)],
                self.theirs.at[k],
                self.sems[0].at[k],
                self.sems[1].at[k],
                (x, y, z, 1 - c),
            )
            for k in range(4)
        ]

    def hops(self):
        x, y, z, c = here()
        self.hop = []
        for k in range(3):
            to = wrap(z + 1 + k)
            self.pair[k].wait_recv()
            both = self.own(to).astype(F32) + self.theirs[k].astype(F32)
            self.theirs[k] = both.astype(BF)
            self.hop.append(
                push(
                    self.theirs.at[k],
                    self.landed.at[k],
                    self.sems[2].at[k],
                    self.sems[3].at[k],
                    (x, y, to, c),
                )
            )

    def result(self):
        x, y, z, c = here()
        self.pair[3].wait_recv()
        value = self.own(z).astype(F32) + self.theirs[3].astype(F32)
        for k in range(3):
            self.hop[k].wait_recv()
            value = value + self.landed[k].astype(F32)
        return value

    def done(self):
        for copy in self.pair + self.hop:
            copy.wait_send()


def sum_scratch(*names):
    out = dict(theirs=pltpu.VMEM((4, 64, 2048), BF), landed=pltpu.VMEM((3, 64, 2048), BF))
    for name in names:
        out.update({f"{name}s{n}": DMA((k,)) for n, k in enumerate((4, 4, 3, 3))})
    return out


class Scan:
    def __init__(self, r, back):
        self.back, self.every = back, r.every
        self.total, self.rows, self.cols, self.entry = r.total, r.scan_y, r.scan_x, r.entry
        self.lead_b, self.lead_a = r.lead_b, r.lead_a
        self.sems = sems_of(r, "scan", 8)
        self.order = [(n, k) for n in range(4) for k in range(2)]
        self.line = list(range(4))
        if back:
            self.order, self.line = self.order[::-1], self.line[::-1]

    def before(self, other, mine):
        return (other > mine) if self.back else (other < mine)

    def pack(self, block, state, decay):
        block[:, 0:512] = state.astype(BF)
        high = decay.astype(BF)
        block[:, 512:640] = high
        block[:, 640:768] = (decay - high.astype(F32)).astype(BF)

    def unpack(self, block):
        keep = block[:, 512:640].astype(F32) + block[:, 640:768].astype(F32)
        return block[:, 0:512].astype(F32), keep

    def factor(self, k, n, width):
        return jnp.concatenate([self.every[k, n, :, 1024:1152]] * (width // 128), axis=1)

    def pair(self):
        x, y, z, c = here()
        self.swap = push(
            self.every.at[c], self.every.at[c], self.sems[0], self.sems[1], (x, y, z, 1 - c)
        )

    def send(self):
        x, y, z, c = here()
        self.swap.wait_recv()
        half = pl.ds(pl.multiple_of(c * DK, DK), DK)
        n, k = self.order[0]
        state = self.every[k, n, :, half]
        decay = self.every[k, n, :, 1024:1152]
        for n, k in self.order[1:]:
            state = self.factor(k, n, DK) * state + self.every[k, n, :, half]
            decay = self.every[k, n, :, 1024:1152] * decay
        self.pack(self.rows.at[y], state, decay)
        self.far = [
            push(
                self.rows.at[y],
                self.rows.at[y],
                self.sems[2].at[d - 1],
                self.sems[3].at[d - 1],
                (x, wrap(y + d), z, c),
            )
            for d in range(1, 4)
        ]

    def middle(self):
        x, y, z, c = here()
        for copy in self.far:
            copy.wait_recv()
        state, decay = jnp.zeros((SLOTS, DK), F32), jnp.ones((SLOTS, 128), F32)
        lead_b, lead_a = state, decay
        for k in self.line:
            term, keep = self.unpack(self.rows.at[k])
            wide = jnp.concatenate([keep] * 4, axis=1)
            valid = self.before(k, y)
            lead_b = jnp.where(valid, wide * lead_b + term, lead_b)
            lead_a = jnp.where(valid, keep * lead_a, lead_a)
            state, decay = wide * state + term, keep * decay
        self.lead_b[...], self.lead_a[...] = lead_b, lead_a
        self.pack(self.cols.at[x], state, decay)
        self.far += [
            push(
                self.cols.at[x],
                self.cols.at[x],
                self.sems[6].at[d - 1],
                self.sems[7].at[d - 1],
                (wrap(x + d), y, z, c),
            )
            for d in range(1, 4)
        ]

    def fold(self, out):
        x, y, z, c = here()
        for copy in self.far[3:]:
            copy.wait_recv()
        state = jnp.zeros((SLOTS, DK), F32)
        for k in self.line:
            term, keep = self.unpack(self.cols.at[k])
            fresh = jnp.concatenate([keep] * 4, axis=1) * state + term
            state = jnp.where(self.before(k, x), fresh, state)
        state = jnp.concatenate([self.lead_a[...]] * 4, axis=1) * state + self.lead_b[...]
        self.total[...] = state
        self.entry[c] = state
        self.last = push(
            self.total, self.entry.at[c], self.sems[4], self.sems[5], (x, y, z, 1 - c)
        )
        self.last.wait_recv()
        for s in range(2):
            state = self.entry[s]
            cols = pl.ds(s * DK, DK)
            for n, k in self.order:

                @pl.when(c == k)
                def _():
                    out[n, :, cols] = state

                state = self.factor(k, n, DK) * state + self.every[k, n, :, cols]

    def done(self):
        for copy in self.far + [self.swap, self.last]:
            copy.wait_send()


def scan_scratch():
    out = dict(
        every=pltpu.VMEM((2, 4, SLOTS, 1152), F32),
        total=pltpu.VMEM((SLOTS, DK), F32),
        scan_y=pltpu.VMEM((4, SLOTS, 768), BF),
        scan_x=pltpu.VMEM((4, SLOTS, 768), BF),
        lead_b=pltpu.VMEM((SLOTS, DK), F32),
        lead_a=pltpu.VMEM((SLOTS, 128), F32),
        entry=pltpu.VMEM((2, SLOTS, DK), F32),
    )
    kinds = ((), (), (3,), (3,), (), (), (3,), (3,))
    out.update({f"scan{n}": DMA(shape) for n, shape in enumerate(kinds)})
    return out


def places():
    row = lax.broadcasted_iota(jnp.int32, (CHUNK, CHUNK), 0)
    col = lax.broadcasted_iota(jnp.int32, (CHUNK, CHUNK), 1)
    return row, col


def tri(lower):
    row, col = places()
    return ((row >= col) if lower else (row <= col)).astype(F32)


def seen_mask(offs):
    row, col = places()
    return jnp.logical_and(row >= col, offs >= (row - col).astype(F32))


def carried(cum, offs):
    return jnp.exp(cum) * (offs > places()[0].astype(F32)).astype(F32)


def reaching(cum, offs):
    final = offs[CHUNK - 1 : CHUNK]
    tail = (places()[0].astype(F32) >= CHUNK - 1 - final).astype(F32)
    return jnp.exp(cum[CHUNK - 1 : CHUNK] - cum) * tail


def features(ref, n, which):
    cols = pl.ds(which * HALF, HALF)
    return jnp.concatenate([ref[0, n, :, cols], ref[1, n, :, cols]], axis=1)


def tiles(value):
    return [value[8 * b : 8 * b + 8] for b in range(CHUNK // 8)]


def one_row(blocks, i):
    return blocks[i // 8][i % 8 : i % 8 + 1]


def spans(cum, i):
    last = one_row(cum, i)
    return [(b, jnp.exp(jnp.minimum(cum[b] - last, 0.0))) for b in range(i // 8, CHUNK // 8)]


def weigh(cum, write, columns):
    cum, write, cols = tiles(cum), tiles(write), tiles(columns)
    total = [jnp.zeros((8, SLOTS), F32) for _ in range(CHUNK // 8)]
    for i in range(CHUNK):
        scale = one_row(write, i)
        for b, span in spans(cum, i):
            total[b] = total[b] + cols[b][:, i : i + 1] * (span * scale)
    return jnp.concatenate(total, axis=0)


def weigh_slots(cum, write, values):
    cum, write, vals = tiles(cum), tiles(write), tiles(values)
    lane = lax.broadcasted_iota(jnp.int32, (8, CHUNK), 1)
    total = [jnp.zeros((8, CHUNK), F32) for _ in range(CHUNK // 8)]
    for i in range(CHUNK):
        scale = one_row(write, i)
        for b, span in spans(cum, i):
            got = jnp.sum(vals[b] * (span * scale), axis=1, keepdims=True)
            total[b] = jnp.where(lane == i, got, total[b])
    return jnp.concatenate(total, axis=0)


def chunk_ends(key, value, lam, write, offs):
    cum = dot(tri(True), lam, precision=HIGH)
    ending = (reaching(cum, offs) * write).astype(BF)
    keep = (offs[CHUNK - 1 : CHUNK, 0:1] > CHUNK - 1).astype(F32)
    keep = keep * jnp.exp(tn(lam, jnp.ones((CHUNK, 128), F32), HIGH))
    return cum, jnp.concatenate([tn(ending, key), tn(ending, value), keep], axis=1)


def chunk_near(query, key, cum, write, offs):
    return weigh(cum, write, jnp.where(seen_mask(offs), nt(query, key) * SCALE, 0.0))


def chunk_out(query, value, cum, write, offs, near, state):
    carry = carried(cum, offs)
    far = nt(query, state[:, 0:512].astype(BF)) * SCALE
    scores = near + carry * far
    scores = jnp.exp(scores - jnp.max(scores, axis=1, keepdims=True))
    probs = scores / jnp.sum(scores, axis=1, keepdims=True)
    mixing = jnp.where(seen_mask(offs), weigh_slots(cum, write, probs), 0.0)
    mixed = dot(mixing.astype(BF), value) + dot(
        (probs * carry).astype(BF), state[:, 512:1024].astype(BF)
    )
    return far, probs, mixing, mixed


def chunk_back(query, value, g, cum, write, offs, probs, state):
    carry = carried(cum, offs)
    dmix = jnp.where(seen_mask(offs), nt(g, value), 0.0)
    dfar = nt(g, state[:, 512:1024].astype(BF))
    dnear = weigh(cum, write, dmix)
    dprobs = dnear + carry * dfar
    dscore = probs * (dprobs - jnp.sum(probs * dprobs, axis=1, keepdims=True))
    ends_k = tn((SCALE * dscore * carry).astype(BF), query)
    ends_v = tn((probs * carry).astype(BF), g)
    return dmix, dfar, dnear, dscore, ends_k, ends_v


def chunk_pairs(query, key, cum, write, offs, dmix, dscore, probs):
    affinity = jnp.where(seen_mask(offs), nt(query, key) * SCALE, 0.0)
    cums, writes = tiles(cum), tiles(write)
    aff, dmx, dsc, prb = tiles(affinity), tiles(dmix), tiles(dscore), tiles(probs)
    lane = lax.broadcasted_iota(jnp.int32, (8, CHUNK), 1)
    daff = [jnp.zeros((8, CHUNK), F32) for _ in range(CHUNK // 8)]
    fresh = []
    for i in range(CHUNK):
        scale = one_row(writes, i)
        both = jnp.zeros((8, SLOTS), F32)
        for b, span in spans(cums, i):
            got = jnp.sum(dsc[b] * (span * scale), axis=1, keepdims=True)
            daff[b] = jnp.where(lane == i, got, daff[b])
            both = both + (dsc[b] * aff[b][:, i : i + 1] + prb[b] * dmx[b][:, i : i + 1]) * span
        fresh.append(jnp.sum(both, axis=0, keepdims=True))
    return jnp.concatenate(daff, axis=0), jnp.concatenate(fresh, axis=0)


def chunk_last(
    query, key, value, g, lam, write, slope, offs, cum, near, far, probs, mixing, state, dfar, dnear, dscore, daff, fresh, after
):
    carry, seen, reach = carried(cum, offs), seen_mask(offs), reaching(cum, offs)
    daff = jnp.where(seen, daff * SCALE, 0.0).astype(BF)
    ending = (reach * write).astype(BF)
    nk, nv = after[:, 0:512].astype(BF), after[:, 512:1024].astype(BF)
    dq = dot(daff, key) + dot((SCALE * dscore * carry).astype(BF), state[:, 0:512].astype(BF))
    dk = tn(daff, query) + dot(ending, nk)
    dv = tn(mixing.astype(BF), g) + dot(ending, nv)
    dend = (nt(key, nk) + nt(value, nv)) * reach
    dkeep = nt(jnp.ones((8, 1024), F32), after * state, HIGH)[0:1]
    keep = (offs[CHUNK - 1 : CHUNK] > CHUNK - 1).astype(F32) * jnp.exp(cum[CHUNK - 1 : CHUNK])
    scaled = write * dend
    dcum = dscore * near + probs * dnear + carry * (dscore * far + probs * dfar)
    dcum = dcum - write * fresh - scaled
    at_end = jnp.sum(scaled, axis=0, keepdims=True) + dkeep * keep
    dcum = dcum + jnp.where(places()[0] == CHUNK - 1, at_end, 0.0)
    dlam = dot(tri(False), dcum, precision=HIGH) - jnp.exp(lam) * (fresh + dend)
    return dq, dk, dv, dlam * slope


def log1p_small(u):
    series = u * (1 - u * (1 / 2 - u * (1 / 3 - u / 4)))
    return jnp.where(u < 0.01, series, jnp.log(1 + u))


def one_less_exp(v):
    series = -v * (1 + v * (1 / 2 + v * (1 / 6 + v / 24)))
    return jnp.where(v > -0.03, series, 1 - jnp.exp(v))


def forget_gate(logits):
    small = jnp.exp(-jnp.abs(logits))
    lam = (jnp.minimum(logits, 0.0) - log1p_small(small)) / 8
    slope = jnp.where(logits >= 0, small, 1.0) / (1 + small) / 8
    return lam, one_less_exp(lam), slope


def prepare(r):
    x, y, z, c = here()
    first = rms(r.inputs[...].astype(F32), r.norm1_gain[...]).astype(BF)
    r.first_own[...] = first
    for j in range(2):
        for k in range(2):
            cols = slice((2 * j + k) * HALF, (2 * j + k + 1) * HALF)
            for n, w in enumerate((r.key_weight, r.value_weight)):
                r.wk[j, k, :, n * HALF : (n + 1) * HALF] = w[:, cols]
            for n, w in enumerate((r.query_weight, r.gate_weight, r.out_weight)):
                r.wm[j, k, :, n * HALF : (n + 1) * HALF] = w[:, cols]
    lowrank = nt(first, r.low_down[...])
    r.lowrank[...] = lowrank
    logits = dot(lowrank, r.low_up[...].astype(F32), precision=HIGH) + r.forget_bias[...]
    lam, write, slope = forget_gate(logits.astype(BF).astype(F32))
    row = lax.broadcasted_iota(jnp.int32, (64, 128), 0)
    col = lax.broadcasted_iota(jnp.int32, (64, 128), 1)
    offs = jnp.where(col == row + 64 * c, r.offsets[...].astype(F32), 0.0)
    offs = jnp.broadcast_to(jnp.sum(offs, axis=1, keepdims=True), (64, SLOTS))
    for h in range(4):
        cols = slice(h * SLOTS, (h + 1) * SLOTS)
        r.packed[h, 0] = jnp.concatenate([lam[:, cols], write[:, cols]], axis=1)
        r.packed[h, 1] = jnp.concatenate([slope[:, cols], offs], axis=1)
    for k in range(4):
        for n, w in enumerate((r.ffn_gate, r.ffn_up, r.ffn_down)):
            piece = w[:, k * UNITS : (k + 1) * UNITS]
            pad = jnp.zeros((32, UNITS_PAD - UNITS), BF)
            r.wf[k, :, n * UNITS_PAD : (n + 1) * UNITS_PAD] = jnp.concatenate([piece, pad], axis=1)


def gate_of(r, n, kind):
    return r.gate[n, kind]


def tile(n, width=HALF, start=0):
    return pl.ds(pl.multiple_of(start + n * width, width), width)


def all_rows(ref, *at):
    value = ref[at] if at else ref[...]
    return value.reshape(512, value.shape[-1])


def columns(ref, cols):
    return ref[:, :, :, cols].reshape(2048, -1)


def forward_kernel(r):
    x, y, z, c = here()
    partner = (x, y, z, 1 - c)
    scan = Scan(r, False)
    r.start()
    greet(all_peers())
    prepare(r)
    greeted(all_peers())
    kv = Spread(r, "kv_spread", r.wide_k, 0, 2 * HALF)
    mix = Spread(r, "m_spread", r.wide_m, 0, 3 * HALF)
    down = Spread(r, "d_spread", r.wide_f, 2 * UNITS_PAD, UNITS_PAD)
    acts = Spread(r, "f_spread", r.wide_f, 0, 2 * UNITS_PAD)
    a_sems, b_sems, s_sems = (sems_of(r, n, 5) for n in ("rows_a_", "rows_b_", "rows_s_"))
    k_deal = deal_start(r.wk, r.wide_k, r.k_send, r.k_recv)
    deal_wait(r.wk, r.wide_k, r.k_recv)
    kv.near()
    kv.far(0)
    a_rows = rows_start(r.first_own, r.first, a_sems)
    gates = shuffle_start(lambda k: r.packed.at[k], r.gates.at[z], *sems_of(r, "gate", 3))
    m_deal = deal_start(r.wm, r.wide_m, r.m_send, r.m_recv)
    f_deal = shuffle_start(
        lambda k: r.wf.at[k],
        r.wide_f.at[x, y, pl.ds(pl.multiple_of(z * 32, 32), 32), :],
        *sems_of(r, "deal", 3),
    )
    kv.far(1, 2, 3)
    deal_wait(r.wm, r.wide_m, r.m_recv)
    mix.near()
    rows_finish(a_rows, r.first, a_sems)
    shuffle_wait(gates)
    for n in range(4):
        for kind in range(4):
            r.gate[n, kind] = r.gates[n, kind // 2, :, (kind % 2) * SLOTS : (kind % 2 + 1) * SLOTS]
    kv.arrive()
    mix.far(0, 1, 2, 3)
    r.save("wide_k", "first", "gate")

    @pl.loop(0, 2)
    def _(n):
        got = dot(all_rows(r.first), columns(r.wide_k, tile(n)))
        r.proj[:, :, :, tile(n, start=HALF)] = got.astype(BF).reshape(2, 4, 64, HALF)

    key_value = pl.ds(HALF, 2 * HALF)
    swap = push(
        r.proj.at[1 - c, :, :, key_value],
        r.qkv.at[c, :, :, key_value],
        r.swap_s.at[0],
        r.swap_r.at[0],
        partner,
    )
    r.qkv[c, :, :, key_value] = r.proj[c, :, :, key_value]
    shuffle_wait(f_deal)
    swap.wait()

    @pl.loop(0, 4)
    def _(n):
        cum, ends = chunk_ends(
            features(r.qkv, n, 1), features(r.qkv, n, 2), gate_of(r, n, 0), gate_of(r, n, 1), gate_of(r, n, 3)
        )
        r.cum[n] = cum
        r.every[c, n] = ends
        r.decays[n] = ends[:, 1024:1152]

    scan.pair()
    scan.send()
    down.near()
    acts.near()
    b_rows = rows_start(r.rows_b, r.cot, b_sems)
    mix.arrive()
    r.save("wide_m")
    got = dot(all_rows(r.first), columns(r.wide_m, pl.ds(0, HALF)))
    query = pl.ds(0, HALF)
    r.proj[:, :, :, query] = got.astype(BF).reshape(2, 4, 64, HALF)
    swap_q = push(
        r.proj.at[1 - c, :, :, query],
        r.qkv.at[c, :, :, query],
        r.swap_s.at[1],
        r.swap_r.at[1],
        partner,
    )
    r.qkv[c, :, :, query] = r.proj[c, :, :, query]
    scan.middle()
    down.far(0)
    got = dot(all_rows(r.first), columns(r.wide_m, pl.ds(HALF, HALF)))
    r.gate_lin[...] = got.reshape(2, 4, 64, HALF)
    swap_q.wait()
    r.save("qkv")

    @pl.loop(0, 4)
    def _(n):
        r.near[n] = chunk_near(
            features(r.qkv, n, 0), features(r.qkv, n, 1), r.cum[n], gate_of(r, n, 1), gate_of(r, n, 3)
        )

    scan.fold(r.states)
    down.far(1, 2, 3)
    acts.far(0, 1, 2, 3)

    @pl.loop(0, 4)
    def _(n):
        far, probs, mixing, mixed = chunk_out(
            features(r.qkv, n, 0),
            features(r.qkv, n, 2),
            r.cum[n],
            gate_of(r, n, 1),
            gate_of(r, n, 3),
            r.near[n],
            r.states[n],
        )
        r.far[n], r.probs[n], r.mixing[n], r.mixed[n] = far, probs, mixing, mixed
        normed = rms(mixed, r.head_gain[...])
        for s in range(2):
            r.normed[s, n] = normed[:, s * HALF : (s + 1) * HALF]

    swap2 = push(r.normed.at[1 - c], r.headnorm.at[c], r.swap_s.at[2], r.swap_r.at[2], partner)
    r.headnorm[c] = r.normed[c]
    r.save("cum", "decays", "states", "near", "far", "probs", "mixing", "mixed", "gate_lin")
    rows_finish(b_rows, r.cot, b_sems)
    r.save("cot")
    swap2.wait()
    sums = RowSum(r, "mix", r.parts, lambda k: r.parts[c, k])
    for core in (1 - c, c):
        lin = r.gate_lin[core].reshape(256, HALF)
        branch = (r.headnorm[core].reshape(256, HALF) * (lin * jax.nn.sigmoid(lin))).astype(BF)
        r.branch[core] = branch.reshape(4, 64, HALF)

        @pl.loop(0, 4)
        def _(n):
            got = nt(branch, r.wide_m[n, :, :, 2 * HALF : 3 * HALF].reshape(512, HALF))
            r.parts[core, :, :, tile(n, 512)] = got.astype(BF).reshape(4, 64, 512)

        if core is not c:
            sums.pairs()
    r.save("headnorm", "branch")
    sums.hops()
    resid1 = r.inputs[...].astype(F32) + sums.result()
    r.resid1[...] = resid1
    r.second_own[...] = rms(resid1, r.norm2_gain[...]).astype(BF)
    s_rows = rows_start(r.second_own, r.second, s_sems)
    down.arrive()

    @pl.loop(0, 3)
    def _(n):
        r.grad_hidden[:, tile(n)] = dot(
            all_rows(r.cot), columns(r.wide_f, tile(n, start=2 * UNITS_PAD))
        )

    rows_finish(s_rows, r.second, s_sems)
    r.save("second")
    acts.arrive()

    @pl.loop(0, 3)
    def _(n):
        second = all_rows(r.second)
        gate = dot(second, columns(r.wide_f, tile(n)))
        up = dot(second, columns(r.wide_f, tile(n, start=UNITS_PAD)))
        grad = r.grad_hidden[:, tile(n)]
        sig = jax.nn.sigmoid(gate)
        silu = gate * sig
        parts = (grad * up * sig * (1 + gate * (1 - sig)), grad * silu, silu * up)
        for m, part in enumerate(parts):
            r.acts[m, :, :, :, tile(n)] = part.astype(BF).reshape(2, 4, 64, HALF)

    r.save("acts")

    @pl.loop(0, 4)
    def _(n):
        got = nt(all_rows(r.acts, 0), r.wide_f[n, :, :, 0:UNITS_PAD].reshape(512, UNITS_PAD))
        got = got + nt(
            all_rows(r.acts, 1), r.wide_f[n, :, :, UNITS_PAD : 2 * UNITS_PAD].reshape(512, UNITS_PAD)
        )
        r.second_part[:, :, :, tile(n, 512)] = got.astype(BF).reshape(2, 4, 64, 512)

    r.save("second_part")

    @pl.loop(0, 4)
    def _(n):
        got = nt(all_rows(r.acts, 2), r.wide_f[n, :, :, 2 * UNITS_PAD :].reshape(512, UNITS_PAD))
        r.ffn_part[:, :, :, tile(n, 512)] = got.astype(BF).reshape(2, 4, 64, 512)

    r.save("ffn_part")
    for sent in (k_deal, m_deal):
        deal_done(sent)
    for sent in (gates, f_deal):
        shuffle_done(sent)
    for part in (kv, mix, down, acts, scan, sums):
        part.done()
    r.finish()


def forward(operands):
    square = ((4, 64, 64), F32)
    rows = (2, 4, 64, 2048)
    scratch = dict(
        proj=pltpu.VMEM((2, 4, 64, 3 * HALF), BF),
        normed=pltpu.VMEM((2, 4, 64, HALF), F32),
        parts=pltpu.VMEM(rows, BF),
        second_own=pltpu.VMEM((64, 2048), BF),
        grad_hidden=pltpu.VMEM((512, UNITS_PAD), F32),
        wide_f=pltpu.VMEM((4, 4, 128, FFN), BF),
        wk=pltpu.VMEM((2, 2, 32, 2 * HALF), BF),
        wm=pltpu.VMEM((2, 2, 32, 3 * HALF), BF),
        wf=pltpu.VMEM((4, 32, FFN), BF),
        packed=pltpu.VMEM((4, 2, 64, 2 * SLOTS), F32),
        gates=pltpu.VMEM((4, 2, 64, 2 * SLOTS), F32),
        k_send=DMA((2, 2)),
        k_recv=DMA((4,)),
        m_send=DMA((2, 2)),
        m_recv=DMA((4,)),
        swap_s=DMA((3,)),
        swap_r=DMA((3,)),
    )
    for name in ("rows_a_", "rows_b_", "rows_s_"):
        scratch.update(rows_sems(name))
    for name in ("kv_spread", "m_spread", "d_spread", "f_spread"):
        scratch.update(spread_sems(name))
    for name in ("gate", "deal"):
        scratch.update(shuffle_sems(name))
    scratch.update(scan_scratch())
    scratch.update(sum_scratch("mix"))
    return remote_call(
        forward_kernel,
        1,
        {name: (value, ANY if name == "rows_b" else VMEM) for name, value in operands.items()},
        dict(
            first_own=((64, 2048), BF, VMEM),
            lowrank=((64, 16), F32, VMEM),
            resid1=((64, 2048), F32, VMEM),
        ),
        scratch,
        saved=dict(
            wide_k=((4, 4, 128, 2 * HALF), BF),
            wide_m=((4, 4, 128, 3 * HALF), BF),
            first=(rows, BF),
            cot=(rows, BF),
            second=(rows, BF),
            gate=((4, 4, 64, SLOTS), F32),
            qkv=((2, 4, 64, 3 * HALF), BF),
            cum=square,
            near=square,
            far=square,
            probs=square,
            mixing=square,
            decays=((4, SLOTS, 128), F32),
            states=((4, SLOTS, 1024), F32),
            mixed=((4, 64, DK), F32),
            gate_lin=((2, 4, 64, HALF), F32),
            headnorm=((2, 4, 64, HALF), F32),
            branch=((2, 4, 64, HALF), BF),
            acts=((3, 2, 4, 64, UNITS_PAD), BF),
            second_part=(rows, BF),
            ffn_part=(rows, BF),
        ),
    )


class WeightSum:
    def __init__(self, r, name, grads, cols, loaded):
        self.grads, self.cols, self.half, self.loaded = grads, cols, cols // 2, loaded
        self.far, self.landed, self.ready = sems_of(r, name + "b", 3)
        self.own = getattr(r, name + "own") if loaded else None
        self.sems = sems_of(r, name + "s", 4)
        self.own_sem = getattr(r, name + "own_s") if loaded else None
        self.fars, self.nears, self.owns = {}, {}, {}

    def part(self, side):
        return pl.ds(side * self.half, self.half)

    def block(self, side, k, d):
        x, y, z, c = here()
        if side == 0:
            return self.grads.at[wrap(x + d), wrap(y + k), :, self.part(0)]
        return self.grads.at[wrap(x + k), wrap(y + d), :, self.part(1)]

    def peer(self, side, d):
        x, y, z, c = here()
        return (wrap(x + d), y, z, c) if side == 0 else (x, wrap(y + d), z, c)

    def mine(self, side, k):
        return self.own.at[side, k] if self.loaded else self.block(side, k, 0)

    def load(self, side, k):
        if self.loaded:
            self.owns[side, k] = pltpu.make_async_copy(
                self.block(side, k, 0), self.own.at[side, k], self.own_sem.at[side, k]
            )
            self.owns[side, k].start()

    def push_one(self, side, k, d):
        self.fars[side, k, d] = push(
            self.block(side, k, d),
            self.far.at[side, k, d - 1],
            self.sems[0].at[side, k, d - 1],
            self.sems[1].at[side, k, d - 1],
            self.peer(side, d),
        )

    def send(self, e):
        for k in (1, 2, 3, 0):
            if e > 0:
                self.push_one(0, k, e)
            else:
                self.load(0, k)
            if k > 0:
                self.push_one(1, e, k)
        self.load(1, e)

    def arrive(self, side, k):
        if self.loaded:
            self.owns[side, k].wait()
        for d in range(1, 4):
            self.fars[side, k, d].wait_recv()

    def total(self, side, k, rows):
        value = self.mine(side, k)[rows, :].astype(F32)
        for d in range(3):
            value = value + self.far[side, k, d, rows, :].astype(F32)
        return value

    def turn(self, k):
        for side in range(2):
            self.arrive(side, k)

            @pl.loop(0, 8)
            def _(t):
                rows = pl.ds(pl.multiple_of(t * 16, 16), 16)
                self.mine(side, k)[rows, :] = self.total(side, k, rows).astype(BF)

            self.nears[side, k] = push(
                self.mine(side, k),
                self.landed.at[side, k - 1],
                self.sems[2].at[side, k - 1],
                self.sems[3].at[side, k - 1],
                self.peer(1 - side, k),
            )

    def finish(self):
        for side in range(2):
            self.arrive(side, 0)
            for k in range(1, 4):
                self.nears[side, k].wait_recv()

            @pl.loop(0, 8)
            def _(t):
                rows = pl.ds(pl.multiple_of(t * 16, 16), 16)
                value = self.total(side, 0, rows)
                for k in range(3):
                    value = value + self.landed[side, k, rows, :].astype(F32)
                self.ready[rows, self.part(side)] = value.astype(BF)

    def done(self):
        for copy in list(self.fars.values()) + list(self.nears.values()):
            copy.wait_send()


def weight_scratch(name, cols, loaded):
    half = cols // 2
    out = {
        f"{name}b0": pltpu.VMEM((2, 4, 3, 128, half), BF),
        f"{name}b1": pltpu.VMEM((2, 3, 128, half), BF),
        f"{name}b2": pltpu.VMEM((128, cols), BF),
        f"{name}s0": DMA((2, 4, 3)),
        f"{name}s1": DMA((2, 4, 3)),
        f"{name}s2": DMA((2, 3)),
        f"{name}s3": DMA((2, 3)),
    }
    if loaded:
        out[f"{name}own"] = pltpu.VMEM((2, 4, 128, half), BF)
        out[f"{name}own_s"] = DMA((2, 4))
    return out


def return_start(ready, out, send, recv):
    x, y, z, c = here()
    dst, arrived = out.at[lax.rem(z, 2), c], recv.at[lax.rem(z, 2), c]
    sent = []
    for k in range(4):
        src = ready.at[pl.ds(k * 32, 32), :]
        same = jnp.logical_and(k == z, c == z // 2)
        copy = pltpu.make_async_remote_copy(
            src_ref=src,
            dst_ref=dst,
            send_sem=send.at[k],
            recv_sem=arrived,
            device_id=(x, y, k, z // 2),
            device_id_type=MESH,
        )

        @pl.when(same)
        def _():
            pltpu.make_async_copy(src, dst, arrived).start()

        @pl.when(jnp.logical_not(same))
        def _():
            copy.start()

        sent.append((same, copy))
    return sent


def return_wait(ready, out, recv):
    for j in range(2):
        for k in range(2):
            pltpu.make_async_copy(ready.at[pl.ds(0, 32), :], out.at[j, k], recv.at[j, k]).wait()


class SmallSum:
    def __init__(self, r, name, src, out):
        self.src, self.out = src, out
        self.held, self.now = sems_of(r, name + "b", 2)
        self.sems = sems_of(r, name + "s", 4)
        self.sends = []

    def half(self, k):
        width = self.src.shape[1] // 2
        return pl.ds(pl.multiple_of(k * width, 128), width)

    def pair(self):
        x, y, z, c = here()
        self.copy = push(
            self.src.at[:, self.half(1 - c)],
            self.held.at[0, c],
            self.sems[0].at[0],
            self.sems[1].at[0],
            (x, y, z, 1 - c),
        )
        self.held[0, c] = self.src[:, self.half(c)]

    def send(self, stage):
        x, y, z, c = here()
        if stage == 0:
            self.copy.wait()
            self.now[...] = self.held[0, 0] + self.held[0, 1]
        else:
            self.collect(stage)
        at = (z, y, x)[stage]
        self.held[stage + 1, at] = self.now[...]
        self.sent = []
        for d in range(1, 4):
            peer = [x, y, z, c]
            peer[2 - stage] = wrap(at + d)
            self.sent.append(
                push(
                    self.held.at[stage + 1, at],
                    self.held.at[stage + 1, at],
                    self.sems[2].at[stage, d - 1],
                    self.sems[3].at[stage, d - 1],
                    tuple(peer),
                )
            )

    def collect(self, stage):
        for copy in self.sent:
            copy.wait()
        value = self.held[stage, 0]
        for k in range(1, 4):
            value = value + self.held[stage, k]
        self.now[...] = value

    def close(self):
        x, y, z, c = here()
        self.collect(3)
        self.out[:, self.half(c)] = self.now[...]
        self.copy = push(
            self.now,
            self.out.at[:, self.half(c)],
            self.sems[0].at[1],
            self.sems[1].at[1],
            (x, y, z, 1 - c),
        )

    def done(self):
        self.copy.wait()


def small_scratch(name, rows, cols):
    return {
        f"{name}b0": pltpu.VMEM((4, 4, rows, cols // 2), F32),
        f"{name}b1": pltpu.VMEM((rows, cols // 2), F32),
        f"{name}s0": DMA((2,)),
        f"{name}s1": DMA((2,)),
        f"{name}s2": DMA((3, 3)),
        f"{name}s3": DMA((3, 3)),
    }


def backward_kernel(r):
    x, y, z, c = here()
    partner = (x, y, z, 1 - c)
    scan = Scan(r, True)
    greet(all_peers())
    mine = pltpu.make_async_copy(r.second_part.at[c], r.mine, r.mine_s.at[0])
    mine.start()
    r.start()
    greeted(all_peers())
    second = RowSum(r, "sec", r.second_part, lambda k: r.mine[k])
    ffn = RowSum(r, "ffn", r.ffn_part, lambda k: r.mine[k])
    units = WeightSum(r, "units", r.out_grads, FFN, True)
    tail = WeightSum(r, "tail", r.grads_tail, 2 * HALF, False)
    last = WeightSum(r, "last", r.grads_last, 3 * HALF, False)
    second.pairs()
    mine.wait()
    second.hops()

    r.need("acts", "second", "cot")
    for e in (1, 2, 3, 0):
        at = wrap(x + e)
        steps = [
            pltpu.make_async_copy(
                r.grads_last.at[n], r.out_grads.at[at, :, :, pl.ds(n * UNITS_PAD, UNITS_PAD)], r.stage_s.at[n]
            )
            for n in range(3)
        ]
        for n, left in enumerate((r.second, r.second, r.cot)):
            got = tn(left[:, :, :, tile(at, 512)].reshape(512, 512), all_rows(r.acts, n))
            r.grads_last[n] = got.astype(BF).reshape(4, 128, UNITS_PAD)
            steps[n].start()
        for copy in steps:
            copy.wait()
        units.send(e)
    r.need("resid1", "cot_own")
    e = second.result()
    second.done()
    mine = pltpu.make_async_copy(r.ffn_part.at[c], r.mine, r.mine_s.at[1])
    mine.start()
    grad, d_norm2 = rms_back(r.resid1[...], r.norm2_gain[...], e)
    r.small[...] = jnp.zeros_like(r.small)
    r.small[17:18, 0:2048] = d_norm2
    grad_resid1 = r.cot_own[...].astype(F32) + grad
    r.attn_own[...] = grad_resid1.astype(BF)
    r.grad_resid1[...] = grad_resid1
    a_sems = sems_of(r, "rows_a_", 5)
    a_rows = rows_start(r.attn_own, r.attn, a_sems)
    rows_finish(a_rows, r.attn, a_sems)
    ffn.pairs()

    r.need("wide_m", "gate_lin", "headnorm")
    grad_branch = dot(all_rows(r.attn), columns(r.wide_m, pl.ds(2 * HALF, HALF)))
    lin, normed = all_rows(r.gate_lin), all_rows(r.headnorm)
    sig = jax.nn.sigmoid(lin)
    grad_lin = (grad_branch * normed * sig * (1 + lin * (1 - sig))).astype(BF)
    r.grad_lin[...] = grad_lin.reshape(2, 4, 64, HALF)
    r.grad_out[...] = (grad_branch * lin * sig).reshape(2, 4, 64, HALF)
    swap = push(r.grad_out.at[1 - c], r.grad_norm.at[c], r.swap_s.at[0], r.swap_r.at[0], partner)
    r.grad_norm[c] = r.grad_out[c]
    r.need("mixed", "qkv", "cum", "gate", "probs", "states", "decays")
    swap.wait()
    mine.wait()
    ffn.hops()

    r.d_head[...] = jnp.zeros_like(r.d_head)

    @pl.loop(0, 4)
    def _(n):
        e = jnp.concatenate([r.grad_norm[0, n], r.grad_norm[1, n]], axis=1)
        grad, d_head = rms_back(r.mixed[n], r.head_gain[...], e)
        r.d_head[0:1] += d_head
        g = grad.astype(BF)
        r.grad_mixed[n] = g
        dmix, dfar, dnear, dscore, ends_k, ends_v = chunk_back(
            features(r.qkv, n, 0),
            features(r.qkv, n, 2),
            g,
            r.cum[n],
            gate_of(r, n, 1),
            gate_of(r, n, 3),
            r.probs[n],
            r.states[n],
        )
        r.dmix[n], r.dfar[n], r.dnear[n], r.dscore[n] = dmix, dfar, dnear, dscore
        r.every[c, n] = jnp.concatenate([ends_k, ends_v, r.decays[n]], axis=1)

    scan.pair()
    r.small[18:19, 0:512] = r.d_head[0:1]
    scan.send()

    @pl.loop(0, 4)
    def _(n):
        r.daff[n], r.fresh[n] = chunk_pairs(
            features(r.qkv, n, 0),
            features(r.qkv, n, 1),
            r.cum[n],
            gate_of(r, n, 1),
            gate_of(r, n, 3),
            r.dmix[n],
            r.dscore[n],
            r.probs[n],
        )

    scan.middle()
    for k in range(1, 4):
        units.turn(k)
    r.need("first", "branch")

    @pl.loop(0, 4)
    def _(n):
        got = tn(r.first[:, :, :, tile(n, 512)].reshape(512, 512), all_rows(r.grad_lin))
        r.grads_tail[n, :, :, 0:HALF] = got.astype(BF).reshape(4, 128, HALF)
        got = tn(r.attn[:, :, :, tile(n, 512)].reshape(512, 512), all_rows(r.branch))
        r.grads_tail[n, :, :, HALF : 2 * HALF] = got.astype(BF).reshape(4, 128, HALF)

    r.need("near", "far", "mixing")
    scan.fold(r.nexts)
    for e in (1, 2, 3, 0):
        tail.send(e)
    r.output[...] = (r.resid1[...] + ffn.result()).astype(BF)
    ffn.done()

    @pl.loop(0, 4)
    def _(n):
        dq, dk, dv, dlogit = chunk_last(
            features(r.qkv, n, 0),
            features(r.qkv, n, 1),
            features(r.qkv, n, 2),
            r.grad_mixed[n],
            gate_of(r, n, 0),
            gate_of(r, n, 1),
            gate_of(r, n, 2),
            gate_of(r, n, 3),
            r.cum[n],
            r.near[n],
            r.far[n],
            r.probs[n],
            r.mixing[n],
            r.states[n],
            r.dfar[n],
            r.dnear[n],
            r.dscore[n],
            r.daff[n],
            r.fresh[n],
            r.nexts[n],
        )
        for m, part in enumerate((dq, dk, dv)):
            for s in range(2):
                r.dproj[s, n, :, pl.ds(m * HALF, HALF)] = part[
                    :, s * HALF : (s + 1) * HALF
                ].astype(BF)
        r.dlogit[n] = dlogit

    swap2 = push(r.dproj.at[1 - c], r.dqkv.at[c], r.swap_s.at[1], r.swap_r.at[1], partner)
    r.dqkv[c] = r.dproj[c]
    logits = shuffle_start(lambda k: r.dlogit.at[k], r.dl.at[z], *sems_of(r, "gate", 3))
    swap2.wait()

    for e in (1, 2, 3, 0):
        at = wrap(x + e)
        got = tn(r.first[:, :, :, tile(at, 512)].reshape(512, 512), all_rows(r.dqkv))
        r.grads_last[at] = got.astype(BF).reshape(4, 128, 3 * HALF)
        last.send(e)
    r.need("wide_k")
    first_part = r.attn
    first = RowSum(r, "fst", first_part, lambda k: first_part[c, k])
    for core in (1 - c, c):

        @pl.loop(0, 4)
        def _(n):
            dqkv = r.dqkv[core].reshape(256, 3 * HALF)
            got = nt(dqkv[:, HALF:], r.wide_k[n].reshape(512, 2 * HALF))
            left = jnp.concatenate([dqkv[:, 0:HALF], r.grad_lin[core].reshape(256, HALF)], axis=1)
            got = got + nt(left, r.wide_m[n, :, :, 0 : 2 * HALF].reshape(512, 2 * HALF))
            first_part[core, :, :, tile(n, 512)] = got.astype(BF).reshape(4, 64, 512)

        if core is not c:
            first.pairs()

    shuffle_wait(logits)
    first.hops()
    for k in range(1, 4):
        tail.turn(k)

    r.need("lowrank", "up", "down", "first_own", "inputs")
    low = jnp.zeros((64, 16), F32)
    bias = []
    for h in range(4):
        dl = r.dl[h]
        low = low + nt(dl, r.up[:, h * SLOTS : (h + 1) * SLOTS].astype(F32), HIGH)
        r.small[0:16, 2048 + h * 64 : 2112 + h * 64] = tn(r.lowrank[...], dl, HIGH)
        bias.append(jnp.sum(dl, axis=0, keepdims=True))
    r.small[18:19, 512:768] = jnp.concatenate(bias, axis=1)
    r.small[0:16, 0:2048] = tn(low, r.first_own[...].astype(F32), HIGH)
    small = SmallSum(r, "sml", r.small, r.small_out)
    small.pair()
    small.send(0)
    units.finish()
    units_back = shuffle_start(
        lambda k: units.ready.at[pl.ds(pl.multiple_of(k * 32, 32), 32), :],
        r.units_out.at[z],
        *sems_of(r, "back", 3),
    )
    grad_first = first.result() + dot(low, r.down[...].astype(F32), precision=HIGH)
    grad, d_norm1 = rms_back(r.inputs[...].astype(F32), r.norm1_gain[...], grad_first)
    r.d_inputs[...] = r.grad_resid1[...] + grad
    r.tiny[...] = jnp.zeros_like(r.tiny)
    r.tiny[0:1, :] = d_norm1
    tiny = SmallSum(r, "tny", r.tiny, r.tiny_out)
    tiny.pair()
    tiny.send(0)
    small.send(1)
    for k in range(1, 4):
        last.turn(k)
    tiny.send(1)
    tail.finish()
    tail_back = return_start(tail.ready, r.tail_out, r.tail_send, r.tail_recv)
    small.send(2)
    last.finish()
    last_back = return_start(last.ready, r.last_out, r.last_send, r.last_recv)
    tiny.send(2)
    small.close()
    tiny.close()
    shuffle_wait(units_back)
    shuffle_done(units_back)
    shuffle_done(logits)
    return_wait(tail.ready, r.tail_out, r.tail_recv)
    return_wait(last.ready, r.last_out, r.last_recv)
    deal_done(tail_back)
    deal_done(last_back)
    small.done()
    tiny.done()
    for part in (first, units, tail, last, scan):
        part.done()


def backward(operands):
    rows = (2, 4, 64, 2048)
    small = pltpu.VMEM((4, 64, 64), F32)
    scratch = dict(
        small=pltpu.VMEM((24, 2304), F32),
        tiny=pltpu.VMEM((8, 2048), F32),
        attn_own=pltpu.VMEM((64, 2048), BF),
        grad_resid1=pltpu.VMEM((64, 2048), F32),
        attn=pltpu.VMEM(rows, BF),
        grad_lin=pltpu.VMEM((2, 4, 64, HALF), BF),
        grad_out=pltpu.VMEM((2, 4, 64, HALF), F32),
        grad_norm=pltpu.VMEM((2, 4, 64, HALF), F32),
        grad_mixed=pltpu.VMEM((4, 64, DK), BF),
        d_head=pltpu.VMEM((8, DK), F32),
        dmix=small,
        dfar=small,
        dnear=small,
        dscore=small,
        daff=small,
        fresh=small,
        dlogit=small,
        dl=small,
        nexts=pltpu.VMEM((4, SLOTS, 1024), F32),
        dproj=pltpu.VMEM((2, 4, 64, 3 * HALF), BF),
        dqkv=pltpu.VMEM((2, 4, 64, 3 * HALF), BF),
        mine=pltpu.VMEM((4, 64, 2048), BF),
        mine_s=DMA((2,)),
        stage_s=DMA((3,)),
        grads_tail=pltpu.VMEM((4, 4, 128, 2 * HALF), BF),
        grads_last=pltpu.VMEM((4, 4, 128, 3 * HALF), BF),
        swap_s=DMA((2,)),
        swap_r=DMA((2,)),
        tail_send=DMA((4,)),
        tail_recv=DMA((2, 2)),
        last_send=DMA((4,)),
        last_recv=DMA((2, 2)),
    )
    for name, cols, loaded in (
        ("units", FFN, True),
        ("tail", 2 * HALF, False),
        ("last", 3 * HALF, False),
    ):
        scratch.update(weight_scratch(name, cols, loaded))
    scratch.update(sum_scratch("sec", "ffn", "fst"))
    for name in ("gate", "back"):
        scratch.update(shuffle_sems(name))
    scratch.update(rows_sems("rows_a_"))
    scratch.update(scan_scratch())
    scratch.update(small_scratch("sml", 24, 2304))
    scratch.update(small_scratch("tny", 8, 2048))
    in_hbm = ("second_part", "ffn_part")
    in_vmem = ("norm1_gain", "norm2_gain", "head_gain")
    order = ("acts", "second", "cot", "resid1", "cot_own", "wide_m", "gate_lin", "headnorm")
    order += tuple(name for name in operands if name not in order + in_hbm + in_vmem)
    direct = {name: (operands[name], ANY) for name in in_hbm}
    direct.update({name: (operands[name], VMEM) for name in in_vmem})
    return remote_call(
        backward_kernel,
        2,
        direct,
        dict(
            output=((64, 2048), BF, VMEM),
            d_inputs=((64, 2048), F32, VMEM),
            last_out=((2, 2, 32, 3 * HALF), BF, VMEM),
            tail_out=((2, 2, 32, 2 * HALF), BF, VMEM),
            units_out=((4, 32, FFN), BF, VMEM),
            small_out=((24, 2304), F32, VMEM),
            tiny_out=((8, 2048), F32, VMEM),
            out_grads=((4, 4, 128, FFN), BF, ANY),
        ),
        scratch,
        loaded={name: operands[name] for name in order},
    )


def results_kernel(*refs):
    sources, outs, held, sems = refs[:7], refs[7:23], refs[23:30], refs[30]
    copies = [
        pltpu.make_async_copy(src, dst, sems.at[n]) for n, (src, dst) in enumerate(zip(sources, held))
    ]
    for copy in copies:
        copy.start()
    for copy in copies:
        copy.wait()
    out, d_in, last, tail, units, small, tiny = held
    output, d_inputs, norm1, q, k, v, g, o, down, up, bias, head, norm2, fg, fu, fd = outs
    output[...] = out[...]
    d_inputs[...] = d_in[...]
    for j in range(2):
        for n in range(2):
            at = slice((2 * j + n) * HALF, (2 * j + n + 1) * HALF)
            for m, ref in enumerate((q, k, v)):
                ref[:, at] = last[j, n, :, m * HALF : (m + 1) * HALF].astype(F32)
            g[:, at] = tail[j, n, :, 0:HALF].astype(F32)
            o[:, at] = tail[j, n, :, HALF : 2 * HALF].astype(F32)
    for n in range(4):
        at = slice(n * UNITS, (n + 1) * UNITS)
        for m, ref in enumerate((fg, fu, fd)):
            ref[:, at] = units[n, :, m * UNITS_PAD : m * UNITS_PAD + UNITS].astype(F32)
    norm1[...] = tiny[0:1, :]
    norm2[...] = small[17:18, 0:2048]
    head[...] = small[18:19, 0:512]
    bias[...] = small[18:19, 512:768]
    up[...] = small[0:16, 2048:2304]
    down[...] = small[0:16, 0:2048]


def results(b):
    shapes = [((64, 2048), BF), ((64, 2048), F32), ((1, 2048), F32)]
    shapes += [((32, 1024), F32)] * 5 + [((16, 2048), F32), ((16, 256), F32)]
    shapes += [((1, 256), F32), ((1, 512), F32), ((1, 2048), F32)] + [((32, 4 * UNITS), F32)] * 3
    names = ("output", "d_inputs", "last_out", "tail_out", "units_out", "small_out", "tiny_out")
    sources = [b[name] for name in names]
    call = pl.pallas_call(
        results_kernel,
        out_shape=[jax.ShapeDtypeStruct(shape, dtype) for shape, dtype in shapes],
        in_specs=[ANY] * 7,
        scratch_shapes=[pltpu.VMEM(v.shape, v.dtype) for v in sources] + [DMA((7,))],
        compiler_params=pltpu.CompilerParams(vmem_limit_bytes=63 * 2**20),
    )
    out = list(call(*sources))
    out[7], out[8] = out[7].T, out[8].T
    for n in (2, 10, 11, 12):
        out[n] = out[n][0]
    return tuple(out)


def rms(v, gain):
    return v * lax.rsqrt(jnp.mean(v * v, axis=-1, keepdims=True) + EPS) * gain


def rms_back(v, gain, e):
    r = lax.rsqrt(jnp.mean(v * v, axis=-1, keepdims=True) + EPS)
    grad = r * gain * e - v * (r * r * r) * jnp.mean(v * gain * e, axis=-1, keepdims=True)
    return grad, jnp.sum(e * v * r, axis=0, keepdims=True)


def body(
    inputs,
    offsets,
    norm1_gain,
    query_weight,
    key_weight,
    value_weight,
    gate_weight,
    out_weight,
    low_down,
    low_up,
    forget_bias,
    head_gain,
    norm2_gain,
    ffn_gate,
    ffn_up,
    ffn_down,
    cotangent,
):
    gain1, gain2, gain_head = norm1_gain[None], norm2_gain[None], head_gain[None]
    f = forward(
        dict(
            query_weight=query_weight,
            key_weight=key_weight,
            value_weight=value_weight,
            gate_weight=gate_weight,
            out_weight=out_weight.T,
            ffn_gate=ffn_gate,
            ffn_up=ffn_up,
            ffn_down=ffn_down,
            inputs=inputs,
            rows_b=cotangent,
            offsets=offsets[None],
            low_down=low_down.T,
            low_up=low_up,
            forget_bias=forget_bias[None],
            norm1_gain=gain1,
            norm2_gain=gain2,
            head_gain=gain_head,
        )
    )

    operands = dict(
        f,
        cot_own=cotangent,
        inputs=inputs,
        up=low_up,
        down=low_down.T,
        norm1_gain=gain1,
        norm2_gain=gain2,
        head_gain=gain_head,
    )
    b = backward(operands)
    return results(b)


def solution(mesh):
    fine = Mesh(mesh.devices.reshape(4, 4, 4, 2), ("x", "y", "z", "c"))
    seq = ("x", "y", "z")
    rows = P(("x", "y", "z", "c"), None)
    wide = P(seq, "c")
    placed = (
        (rows, P(seq), P())
        + (wide,) * 4
        + (P("c", seq), P(), P(), P(), P(), P(), wide, wide, wide, rows)
    )
    return jax.shard_map(
        body,
        mesh=fine,
        in_specs=placed,
        out_specs=(rows, rows, P())
        + (wide,) * 4
        + (P("c", seq), P(), P(), P(), P(), P(), wide, wide, wide),
        check_vma=False,
    )
```

```python
import functools

import jax
import jax.numpy as jnp
from jax import lax
from jax.experimental import pallas as pl
from jax.experimental.pallas import tpu as pltpu
from jax.sharding import Mesh
from jax.sharding import PartitionSpec as P

DK = 512
SLOTS = 64
CHUNK = 64
HALF = 256
UNITS = 704
UNITS_PAD = 768
EPS = 1e-06
SCALE = 0.125
BF = jnp.bfloat16
F32 = jnp.float32
HIGH = lax.Precision.HIGHEST
MESH = pl.DeviceIdType.MESH
ANY = pl.BlockSpec(memory_space=pl.ANY)
VMEM = pl.BlockSpec(memory_space=pltpu.VMEM)
DMA = pltpu.SemaphoreType.DMA
FFN = 3 * UNITS_PAD


def dot(left, right, dims=((1,), (0,)), precision=None):
    return lax.dot_general(
        left, right, (dims, ((), ())), precision=precision, preferred_element_type=F32
    )


def nt(left, right, precision=None):
    return dot(left, right, ((1,), (1,)), precision)


def tn(left, right, precision=None):
    return dot(left, right, ((0,), (0,)), precision)


def here():
    return tuple(lax.axis_index(a) for a in ("x", "y", "z", "c"))


def wrap(v, n=4):
    return lax.rem(v + n, n)


def greet(peers):
    barrier = pltpu.get_barrier_semaphore()
    for peer in peers:
        pl.semaphore_signal(barrier, inc=1, device_id=peer, device_id_type=MESH)


def greeted(peers):
    pl.semaphore_wait(pltpu.get_barrier_semaphore(), len(peers))


def push(src, dst, send, recv, peer):
    copy = pltpu.make_async_remote_copy(
        src_ref=src, dst_ref=dst, send_sem=send, recv_sem=recv, device_id=peer, device_id_type=MESH
    )
    copy.start()
    return copy


class Refs:
    def start(self):
        self.loads = {}
        for n, name in enumerate(self.loaded):
            copy = pltpu.make_async_copy(
                getattr(self, "in_" + name), getattr(self, name), self.load_sem.at[n]
            )
            copy.start()
            self.loads[name] = copy
        self.saves = []

    def need(self, *names):
        for name in names:
            copy = self.loads.pop(name, None)
            if copy is not None:
                copy.wait()

    def save(self, *names):
        for name in names:
            copy = pltpu.make_async_copy(
                getattr(self, name),
                getattr(self, "out_" + name),
                self.save_sem.at[len(self.saves)],
            )
            copy.start()
            self.saves.append(copy)

    def finish(self):
        for copy in self.saves:
            copy.wait()


def remote_call(kernel, collective_id, operands, outs, scratch, loaded=(), saved=()):
    loaded, saved = dict(loaded), dict(saved)
    operands = dict(operands)
    operands.update({"in_" + name: (value, ANY) for name, value in loaded.items()})
    outs = dict(outs)
    outs.update({"out_" + name: (shape, dtype, ANY) for name, (shape, dtype) in saved.items()})
    scratch = dict(scratch)
    scratch.update({name: pltpu.VMEM(v.shape, v.dtype) for name, v in loaded.items()})
    scratch.update({name: pltpu.VMEM(shape, dtype) for name, (shape, dtype) in saved.items()})
    scratch["load_sem"] = DMA((max(len(loaded), 1),))
    scratch["save_sem"] = DMA((max(len(saved), 1),))
    names = list(operands) + list(outs) + list(scratch)

    def run(*refs):
        r = Refs()
        for name, ref in zip(names, refs):
            setattr(r, name, ref)
        r.loaded = list(loaded)
        kernel(r)

    results = pl.pallas_call(
        run,
        out_shape=[jax.ShapeDtypeStruct(shape, dtype) for shape, dtype, _ in outs.values()],
        in_specs=[spec for _, spec in operands.values()],
        out_specs=[spec for _, _, spec in outs.values()],
        scratch_shapes=list(scratch.values()),
        compiler_params=pltpu.CompilerParams(
            collective_id=collective_id, has_side_effects=True, vmem_limit_bytes=63 * 2**20
        ),
    )(*[array for array, _ in operands.values()])
    return {name.removeprefix("out_"): value for name, value in zip(outs, results)}


class Spread:
    def __init__(self, r, name, ref, start, width, ring=True):
        self.ref, self.start, self.half, self.ring = ref, start, width // 2, ring
        self.sems = sems_of(r, name, 4)
        self.nears, self.fars, self.arrived = {}, {}, set()

    def block(self, side, k, d=0, rows=slice(None)):
        x, y, z, c = here()
        part = pl.ds(self.start + side * self.half, self.half)
        if side == 0:
            return self.ref.at[wrap(x + d), wrap(y - k), rows, part]
        return self.ref.at[wrap(x - k), wrap(y + d), rows, part]

    def peer(self, side, d):
        x, y, z, c = here()
        return (wrap(x + d), y, z, c) if side == 0 else (x, wrap(y + d), z, c)

    def near(self):
        for d in range(1, 4):
            for side in range(2):
                block = self.block(side, 0)
                self.nears[side, d] = push(
                    block,
                    block,
                    self.sems[0].at[side, d - 1],
                    self.sems[1].at[side, d - 1],
                    self.peer(1 - side, d),
                )

    def pass_on(self, key, block, d):
        side, k, n = key
        self.fars[key] = push(
            block, block, self.sems[2].at[side, k, n], self.sems[3].at[side, k, n], self.peer(side, d)
        )

    def far(self, *steps):
        for k in steps:
            for side in range(2):
                if k > 0:
                    self.nears[side, k].wait_recv()
                for d in (1, 3) if self.ring else (1, 3, 2):
                    self.pass_on((side, k, d - 1), self.block(side, k), d)

    def wait(self, key):
        if key not in self.arrived:
            self.arrived.add(key)
            self.fars[key].wait_recv()

    def relay(self, *steps):
        for k in steps:
            for side in range(2):
                self.wait((side, k, 0))
                self.pass_on((side, k, 1), self.block(side, k, -1, pl.ds(0, 64)), 1)
                self.wait((side, k, 2))
                self.pass_on((side, k, 3), self.block(side, k, 1, pl.ds(64, 64)), 3)

    def arrive(self):
        for key in self.fars:
            self.wait(key)

    def done(self):
        for copy in list(self.nears.values()) + list(self.fars.values()):
            copy.wait_send()


def spread_sems(name):
    kinds = ((2, 3), (2, 3), (2, 4, 4), (2, 4, 4))
    return {f"{name}{n}": DMA(shape) for n, shape in enumerate(kinds)}


def rows_start(src, out, sems):
    x, y, z, c = here()
    hop_s, hop_r, pair_s, pair_r, own = sems
    half = src.shape[0] // 2
    mine = pltpu.make_async_copy(src, out.at[c, z], own)
    mine.start()
    hops = {}
    for h in range(2):
        rows = pl.ds(h * half, half)
        for d in range(1, 4):
            hops[h, d] = push(
                src.at[rows],
                out.at[c, z, rows],
                hop_s.at[h, d - 1],
                hop_r.at[h, d - 1],
                (x, y, wrap(z + d), c),
            )
    pairs = [push(src, out.at[c, z], pair_s.at[0, 3], pair_r.at[0, 3], (x, y, z, 1 - c))]
    return mine, hops, pairs


def rows_finish(started, out, sems):
    x, y, z, c = here()
    hop_s, hop_r, pair_s, pair_r, own = sems
    mine, hops, pairs = started
    half = out.shape[2] // 2
    for h, d in hops:
        hops[h, d].wait_recv()
        block = out.at[c, wrap(z - d), pl.ds(h * half, half)]
        pairs.append(
            push(block, block, pair_s.at[h, d - 1], pair_r.at[h, d - 1], (x, y, z, 1 - c))
        )
    mine.wait()
    for copy in hops.values():
        copy.wait_send()
    for copy in pairs:
        copy.wait()


def rows_sems(name):
    kinds = ((2, 3), (2, 3), (2, 4), (2, 4), ())
    return {f"{name}{n}": DMA(shape) for n, shape in enumerate(kinds)}


def group_peers():
    x, y, z, c = here()
    return [(x, y, wrap(z + d), k) for d in range(1, 4) for k in range(2)] + [(x, y, z, 1 - c)]


def row_peers():
    x, y, z, c = here()
    return [(x, y, wrap(z + d), c) for d in range(1, 4)] + [(x, y, z, 1 - c)]


def plane_peers():
    x, y, z, c = here()
    return [(wrap(x + d), y, z, c) for d in range(1, 4)] + [
        (x, wrap(y + d), z, c) for d in range(1, 4)
    ]


def all_peers():
    return group_peers() + plane_peers()


def sems_of(r, name, count):
    return [getattr(r, f"{name}{n}") for n in range(count)]


def deal_start(src, wide, send, recv):
    x, y, z, c = here()
    dst = wide.at[x, y, pl.ds(pl.multiple_of(z * 32, 32), 32), :]
    sent = []
    for j in range(2):
        for k in range(2):
            same = jnp.logical_and(2 * c + j == z, c == k)
            copy = pltpu.make_async_remote_copy(
                src_ref=src.at[j, k],
                dst_ref=dst,
                send_sem=send.at[j, k],
                recv_sem=recv.at[z],
                device_id=(x, y, 2 * c + j, k),
                device_id_type=MESH,
            )

            @pl.when(same)
            def _():
                pltpu.make_async_copy(src.at[j, k], dst, recv.at[z]).start()

            @pl.when(jnp.logical_not(same))
            def _():
                copy.start()

            sent.append((same, copy))
    return sent


def deal_wait(src, wide, recv):
    x, y, z, c = here()
    for s in range(4):
        dst = wide.at[x, y, pl.ds(s * 32, 32), :]
        pltpu.make_async_copy(src.at[0, 0], dst, recv.at[s]).wait()


def deal_done(sent):
    for same, copy in sent:

        @pl.when(jnp.logical_not(same))
        def _():
            copy.wait_send()


def shuffle_start(block, dst, send, recv, own):
    x, y, z, c = here()
    mine = pltpu.make_async_copy(block(z), dst, own)
    mine.start()
    sent = [
        push(block(wrap(z + d)), dst, send.at[d - 1], recv.at[d - 1], (x, y, wrap(z + d), c))
        for d in range(1, 4)
    ]
    return mine, sent


def shuffle_wait(started):
    started[0].wait()
    for copy in started[1]:
        copy.wait_recv()


def shuffle_done(started):
    for copy in started[1]:
        copy.wait_send()


def shuffle_sems(name):
    return {f"{name}0": DMA((3,)), f"{name}1": DMA((3,)), f"{name}2": DMA(())}


class RowSum:
    def __init__(self, r, name, parts, own):
        self.parts, self.own = parts, own
        self.theirs, self.landed = r.theirs, r.landed
        self.sems = sems_of(r, name + "s", 4)

    def pairs(self):
        x, y, z, c = here()
        self.pair = [
            push(
                self.parts.at[1 - c, wrap(z + 1 + k)],
                self.theirs.at[k],
                self.sems[0].at[k],
                self.sems[1].at[k],
                (x, y, z, 1 - c),
            )
            for k in range(4)
        ]

    def hops(self):
        x, y, z, c = here()
        self.hop = []
        for k in range(3):
            to = wrap(z + 1 + k)
            self.pair[k].wait_recv()
            both = self.own(to).astype(F32) + self.theirs[k].astype(F32)
            self.theirs[k] = both.astype(BF)
            self.hop.append(
                push(
                    self.theirs.at[k],
                    self.landed.at[k],
                    self.sems[2].at[k],
                    self.sems[3].at[k],
                    (x, y, to, c),
                )
            )

    def result(self):
        x, y, z, c = here()
        self.pair[3].wait_recv()
        value = self.own(z).astype(F32) + self.theirs[3].astype(F32)
        for k in range(3):
            self.hop[k].wait_recv()
            value = value + self.landed[k].astype(F32)
        return value

    def done(self):
        for copy in self.pair + self.hop:
            copy.wait_send()


def sum_scratch(*names):
    out = dict(theirs=pltpu.VMEM((4, 64, 2048), BF), landed=pltpu.VMEM((3, 64, 2048), BF))
    for name in names:
        out.update({f"{name}s{n}": DMA((k,)) for n, k in enumerate((4, 4, 3, 3))})
    return out


class Scan:
    def __init__(self, r, back):
        self.back, self.every = back, r.every
        self.total, self.rows, self.cols, self.entry = r.total, r.scan_y, r.scan_x, r.entry
        self.lead_b, self.lead_a = r.lead_b, r.lead_a
        self.sems = sems_of(r, "scan", 8)
        self.order = [(n, k) for n in range(4) for k in range(2)]
        self.line = list(range(4))
        if back:
            self.order, self.line = self.order[::-1], self.line[::-1]

    def before(self, other, mine):
        return (other > mine) if self.back else (other < mine)

    def pack(self, block, state, decay):
        block[:, 0:512] = state.astype(BF)
        high = decay.astype(BF)
        block[:, 512:640] = high
        block[:, 640:768] = (decay - high.astype(F32)).astype(BF)

    def unpack(self, block):
        keep = block[:, 512:640].astype(F32) + block[:, 640:768].astype(F32)
        return block[:, 0:512].astype(F32), keep

    def factor(self, k, n, width):
        return jnp.concatenate([self.every[k, n, :, 1024:1152]] * (width // 128), axis=1)

    def pair(self):
        x, y, z, c = here()
        self.swap = push(
            self.every.at[c], self.every.at[c], self.sems[0], self.sems[1], (x, y, z, 1 - c)
        )

    def send(self):
        x, y, z, c = here()
        self.swap.wait_recv()
        half = pl.ds(pl.multiple_of(c * DK, DK), DK)
        n, k = self.order[0]
        state = self.every[k, n, :, half]
        decay = self.every[k, n, :, 1024:1152]
        for n, k in self.order[1:]:
            state = self.factor(k, n, DK) * state + self.every[k, n, :, half]
            decay = self.every[k, n, :, 1024:1152] * decay
        self.pack(self.rows.at[y], state, decay)
        self.far = [
            push(
                self.rows.at[y],
                self.rows.at[y],
                self.sems[2].at[d - 1],
                self.sems[3].at[d - 1],
                (x, wrap(y + d), z, c),
            )
            for d in range(1, 4)
        ]

    def middle(self):
        x, y, z, c = here()
        for copy in self.far:
            copy.wait_recv()
        state, decay = jnp.zeros((SLOTS, DK), F32), jnp.ones((SLOTS, 128), F32)
        lead_b, lead_a = state, decay
        for k in self.line:
            term, keep = self.unpack(self.rows.at[k])
            wide = jnp.concatenate([keep] * 4, axis=1)
            valid = self.before(k, y)
            lead_b = jnp.where(valid, wide * lead_b + term, lead_b)
            lead_a = jnp.where(valid, keep * lead_a, lead_a)
            state, decay = wide * state + term, keep * decay
        self.lead_b[...], self.lead_a[...] = lead_b, lead_a
        self.pack(self.cols.at[x], state, decay)
        self.far += [
            push(
                self.cols.at[x],
                self.cols.at[x],
                self.sems[6].at[d - 1],
                self.sems[7].at[d - 1],
                (wrap(x + d), y, z, c),
            )
            for d in range(1, 4)
        ]

    def fold(self, out):
        x, y, z, c = here()
        for copy in self.far[3:]:
            copy.wait_recv()
        state = jnp.zeros((SLOTS, DK), F32)
        for k in self.line:
            term, keep = self.unpack(self.cols.at[k])
            fresh = jnp.concatenate([keep] * 4, axis=1) * state + term
            state = jnp.where(self.before(k, x), fresh, state)
        state = jnp.concatenate([self.lead_a[...]] * 4, axis=1) * state + self.lead_b[...]
        self.total[...] = state
        self.entry[c] = state
        self.last = push(
            self.total, self.entry.at[c], self.sems[4], self.sems[5], (x, y, z, 1 - c)
        )
        self.last.wait_recv()
        for s in range(2):
            state = self.entry[s]
            cols = pl.ds(s * DK, DK)
            for n, k in self.order:

                @pl.when(c == k)
                def _():
                    out[n, :, cols] = state

                state = self.factor(k, n, DK) * state + self.every[k, n, :, cols]

    def done(self):
        for copy in self.far + [self.swap, self.last]:
            copy.wait_send()


def scan_scratch():
    out = dict(
        every=pltpu.VMEM((2, 4, SLOTS, 1152), F32),
        total=pltpu.VMEM((SLOTS, DK), F32),
        scan_y=pltpu.VMEM((4, SLOTS, 768), BF),
        scan_x=pltpu.VMEM((4, SLOTS, 768), BF),
        lead_b=pltpu.VMEM((SLOTS, DK), F32),
        lead_a=pltpu.VMEM((SLOTS, 128), F32),
        entry=pltpu.VMEM((2, SLOTS, DK), F32),
    )
    kinds = ((), (), (3,), (3,), (), (), (3,), (3,))
    out.update({f"scan{n}": DMA(shape) for n, shape in enumerate(kinds)})
    return out


def places():
    row = lax.broadcasted_iota(jnp.int32, (CHUNK, CHUNK), 0)
    col = lax.broadcasted_iota(jnp.int32, (CHUNK, CHUNK), 1)
    return row, col


def tri(lower):
    row, col = places()
    return ((row >= col) if lower else (row <= col)).astype(F32)


def seen_mask(offs):
    row, col = places()
    return jnp.logical_and(row >= col, offs >= (row - col).astype(F32))


def carried(cum, offs):
    return jnp.exp(cum) * (offs > places()[0].astype(F32)).astype(F32)


def reaching(cum, offs):
    final = offs[CHUNK - 1 : CHUNK]
    tail = (places()[0].astype(F32) >= CHUNK - 1 - final).astype(F32)
    return jnp.exp(cum[CHUNK - 1 : CHUNK] - cum) * tail


def features(ref, n, which):
    cols = pl.ds(which * HALF, HALF)
    return jnp.concatenate([ref[0, n, :, cols], ref[1, n, :, cols]], axis=1)


def tiles(value):
    return [value[8 * b : 8 * b + 8] for b in range(CHUNK // 8)]


def one_row(blocks, i):
    return blocks[i // 8][i % 8 : i % 8 + 1]


def spans(cum, i):
    last = one_row(cum, i)
    return [(b, jnp.exp(jnp.minimum(cum[b] - last, 0.0))) for b in range(i // 8, CHUNK // 8)]


def weigh(cum, write, columns):
    cum, write, cols = tiles(cum), tiles(write), tiles(columns)
    total = [jnp.zeros((8, SLOTS), F32) for _ in range(CHUNK // 8)]
    for i in range(CHUNK):
        scale = one_row(write, i)
        for b, span in spans(cum, i):
            total[b] = total[b] + cols[b][:, i : i + 1] * (span * scale)
    return jnp.concatenate(total, axis=0)


def weigh_slots(cum, write, values):
    cum, write, vals = tiles(cum), tiles(write), tiles(values)
    lane = lax.broadcasted_iota(jnp.int32, (8, CHUNK), 1)
    total = [jnp.zeros((8, CHUNK), F32) for _ in range(CHUNK // 8)]
    for i in range(CHUNK):
        scale = one_row(write, i)
        for b, span in spans(cum, i):
            got = jnp.sum(vals[b] * (span * scale), axis=1, keepdims=True)
            total[b] = jnp.where(lane == i, got, total[b])
    return jnp.concatenate(total, axis=0)


def chunk_ends(key, value, lam, write, offs):
    cum = dot(tri(True), lam, precision=HIGH)
    ending = (reaching(cum, offs) * write).astype(BF)
    keep = (offs[CHUNK - 1 : CHUNK, 0:1] > CHUNK - 1).astype(F32)
    keep = keep * jnp.exp(tn(lam, jnp.ones((CHUNK, 128), F32), HIGH))
    return cum, jnp.concatenate([tn(ending, key), tn(ending, value), keep], axis=1)


def chunk_near(query, key, cum, write, offs):
    return weigh(cum, write, jnp.where(seen_mask(offs), nt(query, key) * SCALE, 0.0))


def chunk_out(query, value, cum, write, offs, near, state):
    carry = carried(cum, offs)
    far = nt(query, state[:, 0:512].astype(BF)) * SCALE
    scores = near + carry * far
    scores = jnp.exp(scores - jnp.max(scores, axis=1, keepdims=True))
    probs = scores / jnp.sum(scores, axis=1, keepdims=True)
    mixing = jnp.where(seen_mask(offs), weigh_slots(cum, write, probs), 0.0)
    mixed = dot(mixing.astype(BF), value) + dot(
        (probs * carry).astype(BF), state[:, 512:1024].astype(BF)
    )
    return far, probs, mixing, mixed


def chunk_back(query, value, g, cum, write, offs, probs, state):
    carry = carried(cum, offs)
    dmix = jnp.where(seen_mask(offs), nt(g, value), 0.0)
    dfar = nt(g, state[:, 512:1024].astype(BF))
    dnear = weigh(cum, write, dmix)
    dprobs = dnear + carry * dfar
    dscore = probs * (dprobs - jnp.sum(probs * dprobs, axis=1, keepdims=True))
    ends_k = tn((SCALE * dscore * carry).astype(BF), query)
    ends_v = tn((probs * carry).astype(BF), g)
    return dmix, dfar, dnear, dscore, ends_k, ends_v


def chunk_pairs(query, key, cum, write, offs, dmix, dscore, probs):
    affinity = jnp.where(seen_mask(offs), nt(query, key) * SCALE, 0.0)
    cums, writes = tiles(cum), tiles(write)
    aff, dmx, dsc, prb = tiles(affinity), tiles(dmix), tiles(dscore), tiles(probs)
    lane = lax.broadcasted_iota(jnp.int32, (8, CHUNK), 1)
    daff = [jnp.zeros((8, CHUNK), F32) for _ in range(CHUNK // 8)]
    fresh = []
    for i in range(CHUNK):
        scale = one_row(writes, i)
        both = jnp.zeros((8, SLOTS), F32)
        for b, span in spans(cums, i):
            got = jnp.sum(dsc[b] * (span * scale), axis=1, keepdims=True)
            daff[b] = jnp.where(lane == i, got, daff[b])
            both = both + (dsc[b] * aff[b][:, i : i + 1] + prb[b] * dmx[b][:, i : i + 1]) * span
        fresh.append(jnp.sum(both, axis=0, keepdims=True))
    return jnp.concatenate(daff, axis=0), jnp.concatenate(fresh, axis=0)


def chunk_last(
    query, key, value, g, lam, write, slope, offs, cum, near, far, probs, mixing, state, dfar, dnear, dscore, daff, fresh, after
):
    carry, seen, reach = carried(cum, offs), seen_mask(offs), reaching(cum, offs)
    daff = jnp.where(seen, daff * SCALE, 0.0).astype(BF)
    ending = (reach * write).astype(BF)
    nk, nv = after[:, 0:512].astype(BF), after[:, 512:1024].astype(BF)
    dq = dot(daff, key) + dot((SCALE * dscore * carry).astype(BF), state[:, 0:512].astype(BF))
    dk = tn(daff, query) + dot(ending, nk)
    dv = tn(mixing.astype(BF), g) + dot(ending, nv)
    dend = (nt(key, nk) + nt(value, nv)) * reach
    dkeep = nt(jnp.ones((8, 1024), F32), after * state, HIGH)[0:1]
    keep = (offs[CHUNK - 1 : CHUNK] > CHUNK - 1).astype(F32) * jnp.exp(cum[CHUNK - 1 : CHUNK])
    scaled = write * dend
    dcum = dscore * near + probs * dnear + carry * (dscore * far + probs * dfar)
    dcum = dcum - write * fresh - scaled
    at_end = jnp.sum(scaled, axis=0, keepdims=True) + dkeep * keep
    dcum = dcum + jnp.where(places()[0] == CHUNK - 1, at_end, 0.0)
    dlam = dot(tri(False), dcum, precision=HIGH) - jnp.exp(lam) * (fresh + dend)
    return dq, dk, dv, dlam * slope


def log1p_small(u):
    series = u * (1 - u * (1 / 2 - u * (1 / 3 - u / 4)))
    return jnp.where(u < 0.01, series, jnp.log(1 + u))


def one_less_exp(v):
    series = -v * (1 + v * (1 / 2 + v * (1 / 6 + v / 24)))
    return jnp.where(v > -0.03, series, 1 - jnp.exp(v))


def forget_gate(logits):
    small = jnp.exp(-jnp.abs(logits))
    lam = (jnp.minimum(logits, 0.0) - log1p_small(small)) / 8
    slope = jnp.where(logits >= 0, small, 1.0) / (1 + small) / 8
    return lam, one_less_exp(lam), slope


def prepare(r):
    x, y, z, c = here()
    first = rms(r.inputs[...].astype(F32), r.norm1_gain[...]).astype(BF)
    r.first_own[...] = first
    for j in range(2):
        for k in range(2):
            cols = slice((2 * j + k) * HALF, (2 * j + k + 1) * HALF)
            for n, w in enumerate((r.key_weight, r.value_weight)):
                r.wk[j, k, :, n * HALF : (n + 1) * HALF] = w[:, cols]
            for n, w in enumerate((r.query_weight, r.gate_weight, r.out_weight)):
                r.wm[j, k, :, n * HALF : (n + 1) * HALF] = w[:, cols]
    lowrank = nt(first, r.low_down[...])
    r.lowrank[...] = lowrank
    logits = dot(lowrank, r.low_up[...].astype(F32), precision=HIGH) + r.forget_bias[...]
    lam, write, slope = forget_gate(logits.astype(BF).astype(F32))
    row = lax.broadcasted_iota(jnp.int32, (64, 128), 0)
    col = lax.broadcasted_iota(jnp.int32, (64, 128), 1)
    offs = jnp.where(col == row + 64 * c, r.offsets[...].astype(F32), 0.0)
    offs = jnp.broadcast_to(jnp.sum(offs, axis=1, keepdims=True), (64, SLOTS))
    for h in range(4):
        cols = slice(h * SLOTS, (h + 1) * SLOTS)
        r.packed[h, 0] = jnp.concatenate([lam[:, cols], write[:, cols]], axis=1)
        r.packed[h, 1] = jnp.concatenate([slope[:, cols], offs], axis=1)
    for k in range(4):
        for n, w in enumerate((r.ffn_gate, r.ffn_up, r.ffn_down)):
            piece = w[:, k * UNITS : (k + 1) * UNITS]
            pad = jnp.zeros((32, UNITS_PAD - UNITS), BF)
            r.wf[k, :, n * UNITS_PAD : (n + 1) * UNITS_PAD] = jnp.concatenate([piece, pad], axis=1)


def gate_of(r, n, kind):
    return r.gate[n, kind]


def tile(n, width=HALF, start=0):
    return pl.ds(pl.multiple_of(start + n * width, width), width)


def all_rows(ref, *at):
    value = ref[at] if at else ref[...]
    return value.reshape(512, value.shape[-1])


def columns(ref, cols):
    return ref[:, :, :, cols].reshape(2048, -1)


def forward_kernel(r):
    x, y, z, c = here()
    partner = (x, y, z, 1 - c)
    scan = Scan(r, False)
    r.start()
    greet(all_peers())
    prepare(r)
    greeted(all_peers())
    kv = Spread(r, "kv_spread", r.wide_k, 0, 2 * HALF, ring=False)
    mix = Spread(r, "m_spread", r.wide_m, 0, 3 * HALF)
    down = Spread(r, "d_spread", r.wide_f, 2 * UNITS_PAD, UNITS_PAD)
    acts = Spread(r, "f_spread", r.wide_f, 0, 2 * UNITS_PAD)
    a_sems, b_sems, s_sems = (sems_of(r, n, 5) for n in ("rows_a_", "rows_b_", "rows_s_"))
    k_deal = deal_start(r.wk, r.wide_k, r.k_send, r.k_recv)
    deal_wait(r.wk, r.wide_k, r.k_recv)
    kv.near()
    kv.far(0)
    a_rows = rows_start(r.first_own, r.first, a_sems)
    gates = shuffle_start(lambda k: r.packed.at[k], r.gates.at[z], *sems_of(r, "gate", 3))
    m_deal = deal_start(r.wm, r.wide_m, r.m_send, r.m_recv)
    kv.far(1, 2, 3)
    deal_wait(r.wm, r.wide_m, r.m_recv)
    mix.near()
    rows_finish(a_rows, r.first, a_sems)
    f_deal = shuffle_start(
        lambda k: r.wf.at[k],
        r.wide_f.at[x, y, pl.ds(pl.multiple_of(z * 32, 32), 32), :],
        *sems_of(r, "deal", 3),
    )
    shuffle_wait(gates)
    for n in range(4):
        for kind in range(4):
            r.gate[n, kind] = r.gates[n, kind // 2, :, (kind % 2) * SLOTS : (kind % 2 + 1) * SLOTS]
    kv.arrive()
    mix.far(0, 1, 2, 3)
    r.save("wide_k", "first", "gate")

    @pl.loop(0, 2)
    def _(n):
        got = dot(all_rows(r.first), columns(r.wide_k, tile(n)))
        r.proj[:, :, :, tile(n, start=HALF)] = got.astype(BF).reshape(2, 4, 64, HALF)

    key_value = pl.ds(HALF, 2 * HALF)
    swap = push(
        r.proj.at[1 - c, :, :, key_value],
        r.qkv.at[c, :, :, key_value],
        r.swap_s.at[0],
        r.swap_r.at[0],
        partner,
    )
    r.qkv[c, :, :, key_value] = r.proj[c, :, :, key_value]
    shuffle_wait(f_deal)
    down.near()
    swap.wait()

    @pl.loop(0, 4)
    def _(n):
        cum, ends = chunk_ends(
            features(r.qkv, n, 1), features(r.qkv, n, 2), gate_of(r, n, 0), gate_of(r, n, 1), gate_of(r, n, 3)
        )
        r.cum[n] = cum
        r.every[c, n] = ends
        r.decays[n] = ends[:, 1024:1152]

    scan.pair()
    mix.relay(0, 1, 2, 3)
    scan.send()
    acts.near()
    acts.far(0)
    b_rows = rows_start(r.rows_b, r.cot, b_sems)
    mix.arrive()
    r.save("wide_m")
    got = dot(all_rows(r.first), columns(r.wide_m, pl.ds(0, HALF)))
    query = pl.ds(0, HALF)
    r.proj[:, :, :, query] = got.astype(BF).reshape(2, 4, 64, HALF)
    swap_q = push(
        r.proj.at[1 - c, :, :, query],
        r.qkv.at[c, :, :, query],
        r.swap_s.at[1],
        r.swap_r.at[1],
        partner,
    )
    r.qkv[c, :, :, query] = r.proj[c, :, :, query]
    scan.middle()
    down.far(0)
    got = dot(all_rows(r.first), columns(r.wide_m, pl.ds(HALF, HALF)))
    r.gate_lin[...] = got.reshape(2, 4, 64, HALF)
    swap_q.wait()
    r.save("qkv")

    @pl.loop(0, 4)
    def _(n):
        r.near[n] = chunk_near(
            features(r.qkv, n, 0), features(r.qkv, n, 1), r.cum[n], gate_of(r, n, 1), gate_of(r, n, 3)
        )

    scan.fold(r.states)
    acts.far(1, 2, 3)
    down.far(1, 2, 3)

    @pl.loop(0, 4)
    def _(n):
        far, probs, mixing, mixed = chunk_out(
            features(r.qkv, n, 0),
            features(r.qkv, n, 2),
            r.cum[n],
            gate_of(r, n, 1),
            gate_of(r, n, 3),
            r.near[n],
            r.states[n],
        )
        r.far[n], r.probs[n], r.mixing[n], r.mixed[n] = far, probs, mixing, mixed
        normed = rms(mixed, r.head_gain[...])
        for s in range(2):
            r.normed[s, n] = normed[:, s * HALF : (s + 1) * HALF]

    swap2 = push(r.normed.at[1 - c], r.headnorm.at[c], r.swap_s.at[2], r.swap_r.at[2], partner)
    r.headnorm[c] = r.normed[c]
    r.save("cum", "decays", "states", "near", "far", "probs", "mixing", "mixed", "gate_lin")
    rows_finish(b_rows, r.cot, b_sems)
    r.save("cot")
    acts.relay(0)
    down.relay(0)
    swap2.wait()
    sums = RowSum(r, "mix", r.parts, lambda k: r.parts[c, k])
    for core in (1 - c, c):
        lin = r.gate_lin[core].reshape(256, HALF)
        branch = (r.headnorm[core].reshape(256, HALF) * (lin * jax.nn.sigmoid(lin))).astype(BF)
        r.branch[core] = branch.reshape(4, 64, HALF)

        @pl.loop(0, 4)
        def _(n):
            got = nt(branch, r.wide_m[n, :, :, 2 * HALF : 3 * HALF].reshape(512, HALF))
            r.parts[core, :, :, tile(n, 512)] = got.astype(BF).reshape(4, 64, 512)

        if core is not c:
            sums.pairs()
    r.save("headnorm", "branch")
    sums.hops()
    resid1 = r.inputs[...].astype(F32) + sums.result()
    r.resid1[...] = resid1
    r.second_own[...] = rms(resid1, r.norm2_gain[...]).astype(BF)
    s_rows = rows_start(r.second_own, r.second, s_sems)
    down.relay(1, 2, 3)
    acts.relay(1, 2, 3)
    down.arrive()

    @pl.loop(0, 3)
    def _(n):
        r.grad_hidden[:, tile(n)] = dot(
            all_rows(r.cot), columns(r.wide_f, tile(n, start=2 * UNITS_PAD))
        )

    rows_finish(s_rows, r.second, s_sems)
    r.save("second")
    acts.arrive()

    @pl.loop(0, 3)
    def _(n):
        second = all_rows(r.second)
        gate = dot(second, columns(r.wide_f, tile(n)))
        up = dot(second, columns(r.wide_f, tile(n, start=UNITS_PAD)))
        grad = r.grad_hidden[:, tile(n)]
        sig = jax.nn.sigmoid(gate)
        silu = gate * sig
        parts = (grad * up * sig * (1 + gate * (1 - sig)), grad * silu, silu * up)
        for m, part in enumerate(parts):
            r.acts[m, :, :, :, tile(n)] = part.astype(BF).reshape(2, 4, 64, HALF)

    r.save("acts")

    @pl.loop(0, 4)
    def _(n):
        got = nt(all_rows(r.acts, 0), r.wide_f[n, :, :, 0:UNITS_PAD].reshape(512, UNITS_PAD))
        got = got + nt(
            all_rows(r.acts, 1), r.wide_f[n, :, :, UNITS_PAD : 2 * UNITS_PAD].reshape(512, UNITS_PAD)
        )
        r.second_part[:, :, :, tile(n, 512)] = got.astype(BF).reshape(2, 4, 64, 512)

    r.save("second_part")

    @pl.loop(0, 4)
    def _(n):
        got = nt(all_rows(r.acts, 2), r.wide_f[n, :, :, 2 * UNITS_PAD :].reshape(512, UNITS_PAD))
        r.ffn_part[:, :, :, tile(n, 512)] = got.astype(BF).reshape(2, 4, 64, 512)

    r.save("ffn_part")
    for sent in (k_deal, m_deal):
        deal_done(sent)
    for sent in (gates, f_deal):
        shuffle_done(sent)
    for part in (kv, mix, down, acts, scan, sums):
        part.done()
    r.finish()


def forward(operands):
    square = ((4, 64, 64), F32)
    rows = (2, 4, 64, 2048)
    scratch = dict(
        proj=pltpu.VMEM((2, 4, 64, 3 * HALF), BF),
        normed=pltpu.VMEM((2, 4, 64, HALF), F32),
        parts=pltpu.VMEM(rows, BF),
        second_own=pltpu.VMEM((64, 2048), BF),
        grad_hidden=pltpu.VMEM((512, UNITS_PAD), F32),
        wide_f=pltpu.VMEM((4, 4, 128, FFN), BF),
        wk=pltpu.VMEM((2, 2, 32, 2 * HALF), BF),
        wm=pltpu.VMEM((2, 2, 32, 3 * HALF), BF),
        wf=pltpu.VMEM((4, 32, FFN), BF),
        packed=pltpu.VMEM((4, 2, 64, 2 * SLOTS), F32),
        gates=pltpu.VMEM((4, 2, 64, 2 * SLOTS), F32),
        k_send=DMA((2, 2)),
        k_recv=DMA((4,)),
        m_send=DMA((2, 2)),
        m_recv=DMA((4,)),
        swap_s=DMA((3,)),
        swap_r=DMA((3,)),
    )
    for name in ("rows_a_", "rows_b_", "rows_s_"):
        scratch.update(rows_sems(name))
    for name in ("kv_spread", "m_spread", "d_spread", "f_spread"):
        scratch.update(spread_sems(name))
    for name in ("gate", "deal"):
        scratch.update(shuffle_sems(name))
    scratch.update(scan_scratch())
    scratch.update(sum_scratch("mix"))
    return remote_call(
        forward_kernel,
        1,
        {name: (value, ANY if name == "rows_b" else VMEM) for name, value in operands.items()},
        dict(
            first_own=((64, 2048), BF, VMEM),
            lowrank=((64, 16), F32, VMEM),
            resid1=((64, 2048), F32, VMEM),
        ),
        scratch,
        saved=dict(
            wide_k=((4, 4, 128, 2 * HALF), BF),
            wide_m=((4, 4, 128, 3 * HALF), BF),
            first=(rows, BF),
            cot=(rows, BF),
            second=(rows, BF),
            gate=((4, 4, 64, SLOTS), F32),
            qkv=((2, 4, 64, 3 * HALF), BF),
            cum=square,
            near=square,
            far=square,
            probs=square,
            mixing=square,
            decays=((4, SLOTS, 128), F32),
            states=((4, SLOTS, 1024), F32),
            mixed=((4, 64, DK), F32),
            gate_lin=((2, 4, 64, HALF), F32),
            headnorm=((2, 4, 64, HALF), F32),
            branch=((2, 4, 64, HALF), BF),
            acts=((3, 2, 4, 64, UNITS_PAD), BF),
            second_part=(rows, BF),
            ffn_part=(rows, BF),
        ),
    )


class WeightSum:
    def __init__(self, r, name, grads, cols, loaded):
        self.grads, self.cols, self.half, self.loaded = grads, cols, cols // 2, loaded
        self.far, self.landed, self.ready, self.past = sems_of(r, name + "b", 4)
        self.sems = sems_of(r, name + "s", 6)
        if loaded:
            self.own, self.own_sem = getattr(r, name + "own"), getattr(r, name + "own_s")
            self.held, self.held_sem = getattr(r, name + "held"), getattr(r, name + "held_s")
        self.fars, self.nears, self.owns, self.pasts = {}, {}, {}, {}

    def part(self, side):
        return pl.ds(side * self.half, self.half)

    def block(self, side, k, d, rows=slice(None)):
        x, y, z, c = here()
        if side == 0:
            return self.grads.at[wrap(x + d), wrap(y + k), rows, self.part(0)]
        return self.grads.at[wrap(x + k), wrap(y + d), rows, self.part(1)]

    def peer(self, side, d):
        x, y, z, c = here()
        return (wrap(x + d), y, z, c) if side == 0 else (x, wrap(y + d), z, c)

    def mine(self, side, k):
        return self.own.at[side, k] if self.loaded else self.block(side, k, 0)

    def load(self, side, k):
        if self.loaded:
            self.owns[side, k] = pltpu.make_async_copy(
                self.block(side, k, 0), self.own.at[side, k], self.own_sem.at[side, k]
            )
            self.owns[side, k].start()

    def push_far(self, src, side, k, d, n, rows):
        self.fars[side, k, n] = push(
            src,
            self.far.at[side, k, d // 2, rows],
            self.sems[0].at[side, k, n],
            self.sems[1].at[side, k, n],
            self.peer(side, d),
        )

    def push_one(self, side, k, d):
        if d == 2:
            for n, to in enumerate((1, 3)):
                self.pasts[side, k, n] = push(
                    self.block(side, k, 2, pl.ds(n * 64, 64)),
                    self.past.at[side, k, n],
                    self.sems[4].at[side, k, n],
                    self.sems[5].at[side, k, n],
                    self.peer(side, to),
                )
        else:
            rows = pl.ds(64 if d == 1 else 0, 64)
            self.push_far(self.block(side, k, d, rows), side, k, d, d // 2, rows)

    def send(self, e):
        for k in (1, 2, 3, 0):
            if e > 0:
                self.push_one(0, k, e)
            else:
                self.load(0, k)
            if k > 0:
                self.push_one(1, e, k)
        self.load(1, e)

    def relay(self, order):
        keys = [(side, k, n) for k in order for side in range(2) for n in range(2)]
        loads = {}

        def block(at):
            side, k, n = keys[at]
            return self.block(side, k, 2 * n + 1, pl.ds(n * 64, 64))

        def fetch(at):
            loads[at] = pltpu.make_async_copy(
                block(at), self.held.at[at % 4], self.held_sem.at[at % 4]
            )
            loads[at].start()

        if self.loaded:
            for at in range(4):
                fetch(at)
        for at, (side, k, n) in enumerate(keys):
            if self.loaded:
                loads[at].wait()
            self.pasts[side, k, n].wait_recv()
            mine = self.held.at[at % 4] if self.loaded else block(at)

            @pl.loop(0, 4)
            def _(t):
                rows = pl.ds(pl.multiple_of(t * 16, 16), 16)
                both = self.past[side, k, n, rows, :].astype(F32) + mine[rows, :].astype(F32)
                self.past[side, k, n, rows, :] = both.astype(BF)

            rows = pl.ds(n * 64, 64)
            self.push_far(self.past.at[side, k, n], side, k, 2 * n + 1, 2 + n, rows)
            if self.loaded and at + 4 < len(keys):
                fetch(at + 4)

    def arrive(self, side, k):
        if self.loaded:
            self.owns[side, k].wait()
        for n in range(4):
            self.fars[side, k, n].wait_recv()

    def total(self, side, k, rows):
        value = self.mine(side, k)[rows, :].astype(F32)
        for d in range(2):
            value = value + self.far[side, k, d, rows, :].astype(F32)
        return value

    def turn(self, k):
        for side in range(2):
            self.arrive(side, k)

            @pl.loop(0, 8)
            def _(t):
                rows = pl.ds(pl.multiple_of(t * 16, 16), 16)
                self.mine(side, k)[rows, :] = self.total(side, k, rows).astype(BF)

            self.nears[side, k] = push(
                self.mine(side, k),
                self.landed.at[side, k - 1],
                self.sems[2].at[side, k - 1],
                self.sems[3].at[side, k - 1],
                self.peer(1 - side, k),
            )

    def finish(self):
        for side in range(2):
            self.arrive(side, 0)
            for k in range(1, 4):
                self.nears[side, k].wait_recv()

            @pl.loop(0, 8)
            def _(t):
                rows = pl.ds(pl.multiple_of(t * 16, 16), 16)
                value = self.total(side, 0, rows)
                for k in range(3):
                    value = value + self.landed[side, k, rows, :].astype(F32)
                self.ready[rows, self.part(side)] = value.astype(BF)

    def done(self):
        for copies in (self.fars, self.nears, self.pasts):
            for copy in copies.values():
                copy.wait_send()


def weight_scratch(name, cols, loaded):
    half = cols // 2
    out = {
        f"{name}b0": pltpu.VMEM((2, 4, 2, 128, half), BF),
        f"{name}b1": pltpu.VMEM((2, 3, 128, half), BF),
        f"{name}b2": pltpu.VMEM((128, cols), BF),
        f"{name}b3": pltpu.VMEM((2, 4, 2, 64, half), BF),
    }
    kinds = ((2, 4, 4), (2, 4, 4), (2, 3), (2, 3), (2, 4, 2), (2, 4, 2))
    out.update({f"{name}s{n}": DMA(shape) for n, shape in enumerate(kinds)})
    if loaded:
        out[f"{name}own"] = pltpu.VMEM((2, 4, 128, half), BF)
        out[f"{name}own_s"] = DMA((2, 4))
        out[f"{name}held"] = pltpu.VMEM((4, 64, half), BF)
        out[f"{name}held_s"] = DMA((4,))
    return out


def return_start(ready, out, send, recv):
    x, y, z, c = here()
    dst, arrived = out.at[lax.rem(z, 2), c], recv.at[lax.rem(z, 2), c]
    sent = []
    for k in range(4):
        src = ready.at[pl.ds(k * 32, 32), :]
        same = jnp.logical_and(k == z, c == z // 2)
        copy = pltpu.make_async_remote_copy(
            src_ref=src,
            dst_ref=dst,
            send_sem=send.at[k],
            recv_sem=arrived,
            device_id=(x, y, k, z // 2),
            device_id_type=MESH,
        )

        @pl.when(same)
        def _():
            pltpu.make_async_copy(src, dst, arrived).start()

        @pl.when(jnp.logical_not(same))
        def _():
            copy.start()

        sent.append((same, copy))
    return sent


def return_wait(ready, out, recv):
    for j in range(2):
        for k in range(2):
            pltpu.make_async_copy(ready.at[pl.ds(0, 32), :], out.at[j, k], recv.at[j, k]).wait()


class SmallSum:
    def __init__(self, r, name, axes):
        self.now, self.held, self.send, self.recv = sems_of(r, name, 4)
        self.axes, self.sent = axes, []

    def start(self, n):
        place = dict(zip("xyzc", here()))
        axis, at = self.axes[n], place[self.axes[n]]
        size = 2 if axis == "c" else 4
        self.held[n, at] = self.now[...]
        self.sent = []
        for d in range(1, size):
            peer = dict(place)
            peer[axis] = wrap(at + d, size)
            self.sent.append(
                push(
                    self.held.at[n, at],
                    self.held.at[n, at],
                    self.send.at[n, d - 1],
                    self.recv.at[n, d - 1],
                    tuple(peer.values()),
                )
            )

    def collect(self, n):
        for copy in self.sent:
            copy.wait()
        value = self.held[n, 0]
        for k in range(1, 2 if self.axes[n] == "c" else 4):
            value = value + self.held[n, k]
        self.now[...] = value


def small_scratch(name, rows, count):
    return {
        f"{name}0": pltpu.VMEM((rows, HALF), F32),
        f"{name}1": pltpu.VMEM((count, 4, rows, HALF), F32),
        f"{name}2": DMA((count, 3)),
        f"{name}3": DMA((count, 3)),
    }


def backward_kernel(r):
    x, y, z, c = here()
    partner = (x, y, z, 1 - c)
    scan = Scan(r, True)
    greet(all_peers())
    mine = pltpu.make_async_copy(r.second_part.at[c], r.mine, r.mine_s.at[0])
    mine.start()
    r.start()
    greeted(all_peers())
    second = RowSum(r, "sec", r.second_part, lambda k: r.mine[k])
    ffn = RowSum(r, "ffn", r.ffn_part, lambda k: r.mine[k])
    units = WeightSum(r, "units", r.out_grads, FFN, True)
    tail = WeightSum(r, "tail", r.grads_tail, 2 * HALF, False)
    last = WeightSum(r, "last", r.grads_last, 3 * HALF, False)
    second.pairs()
    mine.wait()
    second.hops()

    r.need("acts", "second", "cot")
    for e in (1, 2, 3, 0):
        at = wrap(x + e)
        steps = [
            pltpu.make_async_copy(
                r.grads_last.at[n], r.out_grads.at[at, :, :, pl.ds(n * UNITS_PAD, UNITS_PAD)], r.stage_s.at[n]
            )
            for n in range(3)
        ]
        for n, left in enumerate((r.second, r.second, r.cot)):
            got = tn(left[:, :, :, tile(at, 512)].reshape(512, 512), all_rows(r.acts, n))
            r.grads_last[n] = got.astype(BF).reshape(4, 128, UNITS_PAD)
            steps[n].start()
        for copy in steps:
            copy.wait()
        units.send(e)
    r.need("resid1", "cot_own")
    e = second.result()
    second.done()
    mine = pltpu.make_async_copy(r.ffn_part.at[c], r.mine, r.mine_s.at[1])
    mine.start()
    grad, d_norm2 = rms_back(r.resid1[...], r.norm2_gain[...], e)
    group = SmallSum(r, "group", ("c", "z"))
    plane = SmallSum(r, "plane", ("y", "x"))
    tiny = SmallSum(r, "tiny", ("c", "z", "y", "x"))
    group.now[...] = jnp.zeros_like(group.now)

    def split_rows(dst, start, value):
        for n in range(value.shape[1] // HALF):
            dst[start + n : start + n + 1, :] = value[:, n * HALF : (n + 1) * HALF]

    split_rows(group.now, 16, d_norm2)
    grad_resid1 = r.cot_own[...].astype(F32) + grad
    r.attn_own[...] = grad_resid1.astype(BF)
    r.grad_resid1[...] = grad_resid1
    a_sems = sems_of(r, "rows_a_", 5)
    a_rows = rows_start(r.attn_own, r.attn, a_sems)
    rows_finish(a_rows, r.attn, a_sems)
    ffn.pairs()
    units.relay((1, 2, 3, 0))

    r.need("wide_m", "gate_lin", "headnorm")
    grad_branch = dot(all_rows(r.attn), columns(r.wide_m, pl.ds(2 * HALF, HALF)))
    lin, normed = all_rows(r.gate_lin), all_rows(r.headnorm)
    sig = jax.nn.sigmoid(lin)
    grad_lin = (grad_branch * normed * sig * (1 + lin * (1 - sig))).astype(BF)
    r.grad_lin[...] = grad_lin.reshape(2, 4, 64, HALF)
    r.grad_out[...] = (grad_branch * lin * sig).reshape(2, 4, 64, HALF)
    swap = push(r.grad_out.at[1 - c], r.grad_norm.at[c], r.swap_s.at[0], r.swap_r.at[0], partner)
    r.grad_norm[c] = r.grad_out[c]
    r.need("first", "branch")

    @pl.loop(0, 4)
    def _(n):
        got = tn(r.first[:, :, :, tile(n, 512)].reshape(512, 512), all_rows(r.grad_lin))
        r.grads_tail[n, :, :, 0:HALF] = got.astype(BF).reshape(4, 128, HALF)
        got = tn(r.attn[:, :, :, tile(n, 512)].reshape(512, 512), all_rows(r.branch))
        r.grads_tail[n, :, :, HALF : 2 * HALF] = got.astype(BF).reshape(4, 128, HALF)

    for e in (1, 2, 3, 0):
        tail.send(e)
    r.need("mixed", "qkv", "cum", "gate", "probs", "states", "decays")
    swap.wait()
    mine.wait()
    ffn.hops()

    r.d_head[...] = jnp.zeros_like(r.d_head)

    @pl.loop(0, 4)
    def _(n):
        e = jnp.concatenate([r.grad_norm[0, n], r.grad_norm[1, n]], axis=1)
        grad, d_head = rms_back(r.mixed[n], r.head_gain[...], e)
        r.d_head[0:1] += d_head
        g = grad.astype(BF)
        r.grad_mixed[n] = g
        dmix, dfar, dnear, dscore, ends_k, ends_v = chunk_back(
            features(r.qkv, n, 0),
            features(r.qkv, n, 2),
            g,
            r.cum[n],
            gate_of(r, n, 1),
            gate_of(r, n, 3),
            r.probs[n],
            r.states[n],
        )
        r.dmix[n], r.dfar[n], r.dnear[n], r.dscore[n] = dmix, dfar, dnear, dscore
        r.every[c, n] = jnp.concatenate([ends_k, ends_v, r.decays[n]], axis=1)

    scan.pair()
    split_rows(group.now, 24, r.d_head[0:1])
    scan.send()

    def pairs_of(n):
        r.daff[n], r.fresh[n] = chunk_pairs(
            features(r.qkv, n, 0),
            features(r.qkv, n, 1),
            r.cum[n],
            gate_of(r, n, 1),
            gate_of(r, n, 3),
            r.dmix[n],
            r.dscore[n],
            r.probs[n],
        )

    pl.loop(0, 2)(pairs_of)
    scan.middle()
    tail.relay((1, 2, 3, 0))
    pl.loop(2, 4)(pairs_of)
    for k in range(1, 4):
        units.turn(k)
    r.need("near", "far", "mixing")
    scan.fold(r.nexts)
    r.output[...] = (r.resid1[...] + ffn.result()).astype(BF)
    ffn.done()

    @pl.loop(0, 4)
    def _(n):
        dq, dk, dv, dlogit = chunk_last(
            features(r.qkv, n, 0),
            features(r.qkv, n, 1),
            features(r.qkv, n, 2),
            r.grad_mixed[n],
            gate_of(r, n, 0),
            gate_of(r, n, 1),
            gate_of(r, n, 2),
            gate_of(r, n, 3),
            r.cum[n],
            r.near[n],
            r.far[n],
            r.probs[n],
            r.mixing[n],
            r.states[n],
            r.dfar[n],
            r.dnear[n],
            r.dscore[n],
            r.daff[n],
            r.fresh[n],
            r.nexts[n],
        )
        for m, part in enumerate((dq, dk, dv)):
            for s in range(2):
                r.dproj[s, n, :, pl.ds(m * HALF, HALF)] = part[
                    :, s * HALF : (s + 1) * HALF
                ].astype(BF)
        r.dlogit[n] = dlogit

    swap2 = push(r.dproj.at[1 - c], r.dqkv.at[c], r.swap_s.at[1], r.swap_r.at[1], partner)
    r.dqkv[c] = r.dproj[c]
    logits = shuffle_start(lambda k: r.dlogit.at[k], r.dl.at[z], *sems_of(r, "gate", 3))
    swap2.wait()

    for e in (1, 2, 3, 0):
        at = wrap(x + e)
        got = tn(r.first[:, :, :, tile(at, 512)].reshape(512, 512), all_rows(r.dqkv))
        r.grads_last[at] = got.astype(BF).reshape(4, 128, 3 * HALF)
        last.send(e)

    shuffle_wait(logits)
    r.need("lowrank", "up", "down", "inputs", "wide_k")
    low = jnp.zeros((64, 16), F32)
    bias = []
    for h in range(4):
        dl = r.dl[h]
        low = low + nt(dl, r.up[:, h * SLOTS : (h + 1) * SLOTS].astype(F32), HIGH)
        group.now[0:16, h * SLOTS : (h + 1) * SLOTS] = tn(r.lowrank[...], dl, HIGH)
        bias.append(jnp.sum(dl, axis=0, keepdims=True))
    split_rows(group.now, 26, jnp.concatenate(bias, axis=1))
    r.low_own[...] = low
    l_sems, d_sems = sems_of(r, "rows_l_", 5), sems_of(r, "rows_d_", 5)
    l_rows = rows_start(r.low_own, r.lows, l_sems)
    group.start(0)
    first_part = r.attn
    first = RowSum(r, "fst", first_part, lambda k: first_part[c, k])
    for core in (1 - c, c):

        @pl.loop(0, 4)
        def _(n):
            dqkv = r.dqkv[core].reshape(256, 3 * HALF)
            got = nt(dqkv[:, HALF:], r.wide_k[n].reshape(512, 2 * HALF))
            left = jnp.concatenate([dqkv[:, 0:HALF], r.grad_lin[core].reshape(256, HALF)], axis=1)
            got = got + nt(left, r.wide_m[n, :, :, 0 : 2 * HALF].reshape(512, 2 * HALF))
            first_part[core, :, :, tile(n, 512)] = got.astype(BF).reshape(4, 64, 512)

        if core is not c:
            first.pairs()
            group.collect(0)
            group.start(1)

    first.hops()
    for k in range(1, 4):
        tail.turn(k)
    last.relay((1, 2, 3, 0))
    rows_finish(l_rows, r.lows, l_sems)
    group.collect(1)
    at = 2 * z + c
    plane.now[0:32] = group.now[...]
    plane.now[32:48] = tn(
        r.lows[...].reshape(512, 16), all_rows(r.first, slice(None), slice(None), slice(None), tile(at)).astype(F32), HIGH
    )
    plane.start(0)
    units.finish()
    units_back = shuffle_start(
        lambda k: units.ready.at[pl.ds(pl.multiple_of(k * 32, 32), 32), :],
        r.units_out.at[z],
        *sems_of(r, "back", 3),
    )
    tail.finish()
    tail_back = return_start(tail.ready, r.tail_out, r.tail_send, r.tail_recv)
    grad_first = first.result() + dot(low, r.down[...].astype(F32), precision=HIGH)
    grad, d_norm1 = rms_back(r.inputs[...].astype(F32), r.norm1_gain[...], grad_first)
    split_rows(tiny.now, 0, d_norm1)
    tiny.start(0)
    r.d_inputs[...] = r.grad_resid1[...] + grad
    tiny.collect(0)
    tiny.start(1)
    last.turn(1)
    last.turn(2)
    last.turn(3)
    plane.collect(0)
    plane.start(1)
    tiny.collect(1)
    tiny.start(2)
    last.finish()
    last_back = return_start(last.ready, r.last_out, r.last_send, r.last_recv)
    plane.collect(1)
    r.down_own[...] = plane.now[32:48]
    d_rows = rows_start(r.down_own, r.down_out, d_sems)
    tiny.collect(2)
    tiny.start(3)
    rows_finish(d_rows, r.down_out, d_sems)
    tiny.collect(3)
    r.small_out[0:32] = plane.now[0:32]
    r.small_out[32:40] = tiny.now[...]
    shuffle_wait(units_back)
    shuffle_done(units_back)
    shuffle_done(logits)
    return_wait(tail.ready, r.tail_out, r.tail_recv)
    return_wait(last.ready, r.last_out, r.last_recv)
    deal_done(tail_back)
    deal_done(last_back)
    for part in (first, units, tail, last, scan):
        part.done()


def backward(operands):
    rows = (2, 4, 64, 2048)
    small = pltpu.VMEM((4, 64, 64), F32)
    scratch = dict(
        low_own=pltpu.VMEM((64, 16), F32),
        lows=pltpu.VMEM((2, 4, 64, 16), F32),
        down_own=pltpu.VMEM((16, HALF), F32),
        attn_own=pltpu.VMEM((64, 2048), BF),
        grad_resid1=pltpu.VMEM((64, 2048), F32),
        attn=pltpu.VMEM(rows, BF),
        grad_lin=pltpu.VMEM((2, 4, 64, HALF), BF),
        grad_out=pltpu.VMEM((2, 4, 64, HALF), F32),
        grad_norm=pltpu.VMEM((2, 4, 64, HALF), F32),
        grad_mixed=pltpu.VMEM((4, 64, DK), BF),
        d_head=pltpu.VMEM((8, DK), F32),
        dmix=small,
        dfar=small,
        dnear=small,
        dscore=small,
        daff=small,
        fresh=small,
        dlogit=small,
        dl=small,
        nexts=pltpu.VMEM((4, SLOTS, 1024), F32),
        dproj=pltpu.VMEM((2, 4, 64, 3 * HALF), BF),
        dqkv=pltpu.VMEM((2, 4, 64, 3 * HALF), BF),
        mine=pltpu.VMEM((4, 64, 2048), BF),
        mine_s=DMA((2,)),
        stage_s=DMA((3,)),
        grads_tail=pltpu.VMEM((4, 4, 128, 2 * HALF), BF),
        grads_last=pltpu.VMEM((4, 4, 128, 3 * HALF), BF),
        swap_s=DMA((2,)),
        swap_r=DMA((2,)),
        tail_send=DMA((4,)),
        tail_recv=DMA((2, 2)),
        last_send=DMA((4,)),
        last_recv=DMA((2, 2)),
    )
    for name, cols, loaded in (
        ("units", FFN, True),
        ("tail", 2 * HALF, False),
        ("last", 3 * HALF, False),
    ):
        scratch.update(weight_scratch(name, cols, loaded))
    scratch.update(sum_scratch("sec", "ffn", "fst"))
    for name in ("gate", "back"):
        scratch.update(shuffle_sems(name))
    scratch.update(rows_sems("rows_a_"))
    scratch.update(scan_scratch())
    for name in ("rows_l_", "rows_d_"):
        scratch.update(rows_sems(name))
    for name, height, count in (("group", 32, 2), ("plane", 48, 2), ("tiny", 8, 4)):
        scratch.update(small_scratch(name, height, count))
    in_hbm = ("second_part", "ffn_part")
    in_vmem = ("norm1_gain", "norm2_gain", "head_gain")
    order = ("acts", "second", "cot", "resid1", "cot_own", "wide_m", "gate_lin", "headnorm")
    order += tuple(name for name in operands if name not in order + in_hbm + in_vmem)
    direct = {name: (operands[name], ANY) for name in in_hbm}
    direct.update({name: (operands[name], VMEM) for name in in_vmem})
    return remote_call(
        backward_kernel,
        2,
        direct,
        dict(
            output=((64, 2048), BF, VMEM),
            d_inputs=((64, 2048), F32, VMEM),
            last_out=((2, 2, 32, 3 * HALF), BF, VMEM),
            tail_out=((2, 2, 32, 2 * HALF), BF, VMEM),
            units_out=((4, 32, FFN), BF, VMEM),
            small_out=((40, HALF), F32, VMEM),
            down_out=((2, 4, 16, HALF), F32, VMEM),
            out_grads=((4, 4, 128, FFN), BF, ANY),
        ),
        scratch,
        loaded={name: operands[name] for name in order},
    )


def results_kernel(*refs):
    sources, outs, held, sems = refs[:7], refs[7:23], refs[23:30], refs[30]
    copies = [
        pltpu.make_async_copy(src, dst, sems.at[n]) for n, (src, dst) in enumerate(zip(sources, held))
    ]
    for copy in copies:
        copy.start()
    for copy in copies:
        copy.wait()
    out, d_in, last, tail, units, small, factor = held
    output, d_inputs, norm1, q, k, v, g, o, down, up, bias, head, norm2, fg, fu, fd = outs
    output[...] = out[...]
    d_inputs[...] = d_in[...]
    for j in range(2):
        for n in range(2):
            at = slice((2 * j + n) * HALF, (2 * j + n + 1) * HALF)
            for m, ref in enumerate((q, k, v)):
                ref[:, at] = last[j, n, :, m * HALF : (m + 1) * HALF].astype(F32)
            g[:, at] = tail[j, n, :, 0:HALF].astype(F32)
            o[:, at] = tail[j, n, :, HALF : 2 * HALF].astype(F32)
    for n in range(4):
        at = slice(n * UNITS, (n + 1) * UNITS)
        for m, ref in enumerate((fg, fu, fd)):
            ref[:, at] = units[n, :, m * UNITS_PAD : m * UNITS_PAD + UNITS].astype(F32)
    up[...] = small[0:16]
    for n in range(8):
        cols = slice(n * HALF, (n + 1) * HALF)
        norm2[:, cols] = small[16 + n : 17 + n]
        norm1[:, cols] = small[32 + n : 33 + n]
        down[:, cols] = factor[n % 2, n // 2]
    for n in range(2):
        head[:, n * HALF : (n + 1) * HALF] = small[24 + n : 25 + n]
    bias[...] = small[26:27]


def results(b):
    shapes = [((64, 2048), BF), ((64, 2048), F32), ((1, 2048), F32)]
    shapes += [((32, 1024), F32)] * 5 + [((16, 2048), F32), ((16, 256), F32)]
    shapes += [((1, 256), F32), ((1, 512), F32), ((1, 2048), F32)] + [((32, 4 * UNITS), F32)] * 3
    names = ("output", "d_inputs", "last_out", "tail_out", "units_out", "small_out", "down_out")
    sources = [b[name] for name in names]
    call = pl.pallas_call(
        results_kernel,
        out_shape=[jax.ShapeDtypeStruct(shape, dtype) for shape, dtype in shapes],
        in_specs=[ANY] * 7,
        scratch_shapes=[pltpu.VMEM(v.shape, v.dtype) for v in sources] + [DMA((7,))],
        compiler_params=pltpu.CompilerParams(vmem_limit_bytes=63 * 2**20),
    )
    out = list(call(*sources))
    out[7], out[8] = out[7].T, out[8].T
    for n in (2, 10, 11, 12):
        out[n] = out[n][0]
    return tuple(out)


def rms(v, gain):
    return v * lax.rsqrt(jnp.mean(v * v, axis=-1, keepdims=True) + EPS) * gain


def rms_back(v, gain, e):
    r = lax.rsqrt(jnp.mean(v * v, axis=-1, keepdims=True) + EPS)
    grad = r * gain * e - v * (r * r * r) * jnp.mean(v * gain * e, axis=-1, keepdims=True)
    return grad, jnp.sum(e * v * r, axis=0, keepdims=True)


def body(
    inputs,
    offsets,
    norm1_gain,
    query_weight,
    key_weight,
    value_weight,
    gate_weight,
    out_weight,
    low_down,
    low_up,
    forget_bias,
    head_gain,
    norm2_gain,
    ffn_gate,
    ffn_up,
    ffn_down,
    cotangent,
):
    gain1, gain2, gain_head = norm1_gain[None], norm2_gain[None], head_gain[None]
    f = forward(
        dict(
            query_weight=query_weight,
            key_weight=key_weight,
            value_weight=value_weight,
            gate_weight=gate_weight,
            out_weight=out_weight.T,
            ffn_gate=ffn_gate,
            ffn_up=ffn_up,
            ffn_down=ffn_down,
            inputs=inputs,
            rows_b=cotangent,
            offsets=offsets[None],
            low_down=low_down.T,
            low_up=low_up,
            forget_bias=forget_bias[None],
            norm1_gain=gain1,
            norm2_gain=gain2,
            head_gain=gain_head,
        )
    )

    operands = dict(
        {name: value for name, value in f.items() if name != "first_own"},
        cot_own=cotangent,
        inputs=inputs,
        up=low_up,
        down=low_down.T,
        norm1_gain=gain1,
        norm2_gain=gain2,
        head_gain=gain_head,
    )
    b = backward(operands)
    return results(b)


def solution(mesh):
    fine = Mesh(mesh.devices.reshape(4, 4, 4, 2), ("x", "y", "z", "c"))
    seq = ("x", "y", "z")
    rows = P(("x", "y", "z", "c"), None)
    wide = P(seq, "c")
    placed = (
        (rows, P(seq), P())
        + (wide,) * 4
        + (P("c", seq), P(), P(), P(), P(), P(), wide, wide, wide, rows)
    )
    return jax.shard_map(
        body,
        mesh=fine,
        in_specs=placed,
        out_specs=(rows, rows, P())
        + (wide,) * 4
        + (P("c", seq), P(), P(), P(), P(), P(), wide, wide, wide),
        check_vma=False,
    )
```

```python
import functools

import jax
import jax.numpy as jnp
from jax import lax
from jax.experimental import pallas as pl
from jax.experimental.pallas import tpu as pltpu
from jax.sharding import Mesh
from jax.sharding import PartitionSpec as P

DK = 512
SLOTS = 64
CHUNK = 64
HALF = 256
UNITS = 704
UNITS_PAD = 768
EPS = 1e-06
SCALE = 0.125
BF = jnp.bfloat16
F32 = jnp.float32
HIGH = lax.Precision.HIGHEST
MESH = pl.DeviceIdType.MESH
ANY = pl.BlockSpec(memory_space=pl.ANY)
VMEM = pl.BlockSpec(memory_space=pltpu.VMEM)
DMA = pltpu.SemaphoreType.DMA
FFN = 3 * UNITS_PAD


def dot(left, right, dims=((1,), (0,)), precision=None):
    return lax.dot_general(
        left, right, (dims, ((), ())), precision=precision, preferred_element_type=F32
    )


def nt(left, right, precision=None):
    return dot(left, right, ((1,), (1,)), precision)


def tn(left, right, precision=None):
    return dot(left, right, ((0,), (0,)), precision)


def here():
    return tuple(lax.axis_index(a) for a in ("x", "y", "z", "c"))


def wrap(v, n=4):
    return lax.rem(v + n, n)


def greet(peers):
    barrier = pltpu.get_barrier_semaphore()
    for peer in peers:
        pl.semaphore_signal(barrier, inc=1, device_id=peer, device_id_type=MESH)


def greeted(peers):
    pl.semaphore_wait(pltpu.get_barrier_semaphore(), len(peers))


def push(src, dst, send, recv, peer):
    copy = pltpu.make_async_remote_copy(
        src_ref=src, dst_ref=dst, send_sem=send, recv_sem=recv, device_id=peer, device_id_type=MESH
    )
    copy.start()
    return copy


class Pieces:
    def __init__(self, src, dst, send, recv, peer):
        self.args = (src, dst, send, recv, peer)

    def copy(self, n):
        src, dst, send, recv, peer = self.args
        return pltpu.make_async_remote_copy(
            src_ref=src(n),
            dst_ref=dst(n),
            send_sem=send.at[n],
            recv_sem=recv.at[n],
            device_id=peer,
            device_id_type=MESH,
        )

    def start(self, n):
        self.copy(n).start()

    def wait_recv(self, count):
        for n in range(count):
            self.copy(n).wait_recv()

    def wait_send(self, count):
        for n in range(count):
            self.copy(n).wait_send()


class Refs:
    def start(self):
        self.loads = {}
        for n, name in enumerate(self.loaded):
            copy = pltpu.make_async_copy(
                getattr(self, "in_" + name), getattr(self, name), self.load_sem.at[n]
            )
            copy.start()
            self.loads[name] = copy
        self.saves = []

    def need(self, *names):
        for name in names:
            copy = self.loads.pop(name, None)
            if copy is not None:
                copy.wait()

    def save(self, *names):
        for name in names:
            copy = pltpu.make_async_copy(
                getattr(self, name),
                getattr(self, "out_" + name),
                self.save_sem.at[len(self.saves)],
            )
            copy.start()
            self.saves.append(copy)

    def finish(self):
        for copy in self.saves:
            copy.wait()


def remote_call(kernel, collective_id, operands, outs, scratch, loaded=(), saved=()):
    loaded, saved = dict(loaded), dict(saved)
    operands = dict(operands)
    operands.update({"in_" + name: (value, ANY) for name, value in loaded.items()})
    outs = dict(outs)
    outs.update({"out_" + name: (shape, dtype, ANY) for name, (shape, dtype) in saved.items()})
    scratch = dict(scratch)
    scratch.update({name: pltpu.VMEM(v.shape, v.dtype) for name, v in loaded.items()})
    scratch.update({name: pltpu.VMEM(shape, dtype) for name, (shape, dtype) in saved.items()})
    scratch["load_sem"] = DMA((max(len(loaded), 1),))
    scratch["save_sem"] = DMA((max(len(saved), 1),))
    names = list(operands) + list(outs) + list(scratch)

    def run(*refs):
        r = Refs()
        for name, ref in zip(names, refs):
            setattr(r, name, ref)
        r.loaded = list(loaded)
        kernel(r)

    results = pl.pallas_call(
        run,
        out_shape=[jax.ShapeDtypeStruct(shape, dtype) for shape, dtype, _ in outs.values()],
        in_specs=[spec for _, spec in operands.values()],
        out_specs=[spec for _, _, spec in outs.values()],
        scratch_shapes=list(scratch.values()),
        compiler_params=pltpu.CompilerParams(
            collective_id=collective_id, has_side_effects=True, vmem_limit_bytes=63 * 2**20
        ),
    )(*[array for array, _ in operands.values()])
    return {name.removeprefix("out_"): value for name, value in zip(outs, results)}


class Spread:
    def __init__(self, r, name, ref, start, width, ring=True):
        self.ref, self.start, self.half, self.ring = ref, start, width // 2, ring
        self.sems = sems_of(r, name, 4)
        self.nears, self.fars, self.arrived = {}, {}, set()

    def block(self, side, k, d=0, rows=slice(None)):
        x, y, z, c = here()
        part = pl.ds(self.start + side * self.half, self.half)
        if side == 0:
            return self.ref.at[wrap(x + d), wrap(y - k), rows, part]
        return self.ref.at[wrap(x - k), wrap(y + d), rows, part]

    def peer(self, side, d):
        x, y, z, c = here()
        return (wrap(x + d), y, z, c) if side == 0 else (x, wrap(y + d), z, c)

    def near(self):
        for d in range(1, 4):
            for side in range(2):
                block = self.block(side, 0)
                self.nears[side, d] = push(
                    block,
                    block,
                    self.sems[0].at[side, d - 1],
                    self.sems[1].at[side, d - 1],
                    self.peer(1 - side, d),
                )

    def pass_on(self, key, block, d):
        side, k, n = key
        self.fars[key] = push(
            block, block, self.sems[2].at[side, k, n], self.sems[3].at[side, k, n], self.peer(side, d)
        )

    def far(self, *steps):
        for k in steps:
            for side in range(2):
                if k > 0:
                    self.nears[side, k].wait_recv()
                for d in (1, 3) if self.ring else (1, 3, 2):
                    self.pass_on((side, k, d - 1), self.block(side, k), d)

    def wait(self, key):
        if key not in self.arrived:
            self.arrived.add(key)
            self.fars[key].wait_recv()

    def relay(self, *steps):
        for k in steps:
            for side in range(2):
                self.wait((side, k, 0))
                self.pass_on((side, k, 1), self.block(side, k, -1, pl.ds(0, 64)), 1)
                self.wait((side, k, 2))
                self.pass_on((side, k, 3), self.block(side, k, 1, pl.ds(64, 64)), 3)

    def arrive(self):
        for key in self.fars:
            self.wait(key)

    def done(self):
        for copy in list(self.nears.values()) + list(self.fars.values()):
            copy.wait_send()


def spread_sems(name):
    kinds = ((2, 3), (2, 3), (2, 4, 4), (2, 4, 4))
    return {f"{name}{n}": DMA(shape) for n, shape in enumerate(kinds)}


def rows_start(src, out, sems):
    x, y, z, c = here()
    hop_s, hop_r, pair_s, pair_r, own = sems
    half = src.shape[0] // 2
    mine = pltpu.make_async_copy(src, out.at[c, z], own)
    mine.start()
    hops = {}
    for h in range(2):
        rows = pl.ds(h * half, half)
        for d in range(1, 4):
            hops[h, d] = push(
                src.at[rows],
                out.at[c, z, rows],
                hop_s.at[h, d - 1],
                hop_r.at[h, d - 1],
                (x, y, wrap(z + d), c),
            )
    pairs = [push(src, out.at[c, z], pair_s.at[0, 3], pair_r.at[0, 3], (x, y, z, 1 - c))]
    return mine, hops, pairs


def rows_finish(started, out, sems):
    x, y, z, c = here()
    hop_s, hop_r, pair_s, pair_r, own = sems
    mine, hops, pairs = started
    half = out.shape[2] // 2
    for h, d in hops:
        hops[h, d].wait_recv()
        block = out.at[c, wrap(z - d), pl.ds(h * half, half)]
        pairs.append(
            push(block, block, pair_s.at[h, d - 1], pair_r.at[h, d - 1], (x, y, z, 1 - c))
        )
    mine.wait()
    for copy in hops.values():
        copy.wait_send()
    for copy in pairs:
        copy.wait()


def rows_sems(name):
    kinds = ((2, 3), (2, 3), (2, 4), (2, 4), ())
    return {f"{name}{n}": DMA(shape) for n, shape in enumerate(kinds)}


def group_peers():
    x, y, z, c = here()
    return [(x, y, wrap(z + d), k) for d in range(1, 4) for k in range(2)] + [(x, y, z, 1 - c)]


def row_peers():
    x, y, z, c = here()
    return [(x, y, wrap(z + d), c) for d in range(1, 4)] + [(x, y, z, 1 - c)]


def plane_peers():
    x, y, z, c = here()
    return [(wrap(x + d), y, z, c) for d in range(1, 4)] + [
        (x, wrap(y + d), z, c) for d in range(1, 4)
    ]


def all_peers():
    return group_peers() + plane_peers()


def sems_of(r, name, count):
    return [getattr(r, f"{name}{n}") for n in range(count)]


def deal_start(src, wide, send, recv):
    x, y, z, c = here()
    dst = wide.at[x, y, pl.ds(pl.multiple_of(z * 32, 32), 32), :]
    sent = []
    for j in range(2):
        for k in range(2):
            same = jnp.logical_and(2 * c + j == z, c == k)
            copy = pltpu.make_async_remote_copy(
                src_ref=src.at[j, k],
                dst_ref=dst,
                send_sem=send.at[j, k],
                recv_sem=recv.at[z],
                device_id=(x, y, 2 * c + j, k),
                device_id_type=MESH,
            )

            @pl.when(same)
            def _():
                pltpu.make_async_copy(src.at[j, k], dst, recv.at[z]).start()

            @pl.when(jnp.logical_not(same))
            def _():
                copy.start()

            sent.append((same, copy))
    return sent


def deal_wait(src, wide, recv):
    x, y, z, c = here()
    for s in range(4):
        dst = wide.at[x, y, pl.ds(s * 32, 32), :]
        pltpu.make_async_copy(src.at[0, 0], dst, recv.at[s]).wait()


def deal_done(sent):
    for same, copy in sent:

        @pl.when(jnp.logical_not(same))
        def _():
            copy.wait_send()


def shuffle_start(block, dst, send, recv, own):
    x, y, z, c = here()
    mine = pltpu.make_async_copy(block(z), dst, own)
    mine.start()
    sent = [
        push(block(wrap(z + d)), dst, send.at[d - 1], recv.at[d - 1], (x, y, wrap(z + d), c))
        for d in range(1, 4)
    ]
    return mine, sent


def shuffle_wait(started):
    started[0].wait()
    for copy in started[1]:
        copy.wait_recv()


def shuffle_done(started):
    for copy in started[1]:
        copy.wait_send()


def shuffle_sems(name):
    return {f"{name}0": DMA((3,)), f"{name}1": DMA((3,)), f"{name}2": DMA(())}


class RowSum:
    def __init__(self, r, name, parts, own):
        self.parts, self.own = parts, own
        self.theirs, self.landed = r.theirs, r.landed
        self.sems = sems_of(r, name + "s", 4)

    def pairs(self):
        x, y, z, c = here()
        self.pair = [
            push(
                self.parts.at[1 - c, wrap(z + 1 + k)],
                self.theirs.at[k],
                self.sems[0].at[k],
                self.sems[1].at[k],
                (x, y, z, 1 - c),
            )
            for k in range(4)
        ]

    def hops(self):
        x, y, z, c = here()
        self.hop = []
        for k in range(3):
            to = wrap(z + 1 + k)
            self.pair[k].wait_recv()
            both = self.own(to).astype(F32) + self.theirs[k].astype(F32)
            self.theirs[k] = both.astype(BF)
            self.hop.append(
                push(
                    self.theirs.at[k],
                    self.landed.at[k],
                    self.sems[2].at[k],
                    self.sems[3].at[k],
                    (x, y, to, c),
                )
            )

    def result(self):
        x, y, z, c = here()
        self.pair[3].wait_recv()
        value = self.own(z).astype(F32) + self.theirs[3].astype(F32)
        for k in range(3):
            self.hop[k].wait_recv()
            value = value + self.landed[k].astype(F32)
        return value

    def done(self):
        for copy in self.pair + self.hop:
            copy.wait_send()


def sum_scratch(*names):
    out = dict(theirs=pltpu.VMEM((4, 64, 2048), BF), landed=pltpu.VMEM((3, 64, 2048), BF))
    for name in names:
        out.update({f"{name}s{n}": DMA((k,)) for n, k in enumerate((4, 4, 3, 3))})
    return out


class Scan:
    def __init__(self, r, back):
        self.back, self.every = back, r.every
        self.total, self.rows, self.cols, self.entry = r.total, r.scan_y, r.scan_x, r.entry
        self.lead_b, self.lead_a = r.lead_b, r.lead_a
        x, y, z, c = here()
        self.sems = sems_of(r, "scan", 8)
        self.swap = Pieces(
            lambda n: self.every.at[c, n],
            lambda n: self.every.at[c, n],
            self.sems[0],
            self.sems[1],
            (x, y, z, 1 - c),
        )
        self.order = [(n, k) for n in range(4) for k in range(2)]
        self.line = list(range(4))
        if back:
            self.order, self.line = self.order[::-1], self.line[::-1]

    def before(self, other, mine):
        return (other > mine) if self.back else (other < mine)

    def pack(self, block, state, decay):
        block[:, 0:512] = state.astype(BF)
        high = decay[:, 0:64].astype(BF).astype(F32)
        both = jnp.concatenate([high, decay[:, 0:64] - high], axis=1)
        block[:, 512:640] = both.astype(BF)

    def unpack(self, block):
        both = block[:, 512:640].astype(F32)
        keep = both[:, 0:64] + both[:, 64:128]
        return block[:, 0:512].astype(F32), jnp.concatenate([keep, keep], axis=1)

    def factor(self, k, n, width):
        return jnp.concatenate([self.every[k, n, :, 1024:1152]] * (width // 128), axis=1)

    def pair(self, n):
        self.swap.start(n)

    def send(self):
        x, y, z, c = here()
        self.swap.wait_recv(4)
        half = pl.ds(pl.multiple_of(c * DK, DK), DK)
        n, k = self.order[0]
        state = self.every[k, n, :, half]
        decay = self.every[k, n, :, 1024:1152]
        for n, k in self.order[1:]:
            state = self.factor(k, n, DK) * state + self.every[k, n, :, half]
            decay = self.every[k, n, :, 1024:1152] * decay
        self.pack(self.rows.at[y], state, decay)
        self.far = [
            push(
                self.rows.at[y],
                self.rows.at[y],
                self.sems[2].at[d - 1],
                self.sems[3].at[d - 1],
                (x, wrap(y + d), z, c),
            )
            for d in range(1, 4)
        ]

    def middle(self):
        x, y, z, c = here()
        for copy in self.far:
            copy.wait_recv()
        state, decay = jnp.zeros((SLOTS, DK), F32), jnp.ones((SLOTS, 128), F32)
        lead_b, lead_a = state, decay
        for k in self.line:
            term, keep = self.unpack(self.rows.at[k])
            wide = jnp.concatenate([keep] * 4, axis=1)
            valid = self.before(k, y)
            lead_b = jnp.where(valid, wide * lead_b + term, lead_b)
            lead_a = jnp.where(valid, keep * lead_a, lead_a)
            state, decay = wide * state + term, keep * decay
        self.lead_b[...], self.lead_a[...] = lead_b, lead_a
        self.pack(self.cols.at[x], state, decay)
        self.far += [
            push(
                self.cols.at[x],
                self.cols.at[x],
                self.sems[6].at[d - 1],
                self.sems[7].at[d - 1],
                (wrap(x + d), y, z, c),
            )
            for d in range(1, 4)
        ]

    def fold(self, out):
        x, y, z, c = here()
        for copy in self.far[3:]:
            copy.wait_recv()
        state = jnp.zeros((SLOTS, DK), F32)
        for k in self.line:
            term, keep = self.unpack(self.cols.at[k])
            fresh = jnp.concatenate([keep] * 4, axis=1) * state + term
            state = jnp.where(self.before(k, x), fresh, state)
        state = jnp.concatenate([self.lead_a[...]] * 4, axis=1) * state + self.lead_b[...]
        self.total[...] = state
        self.entry[c] = state
        self.last = push(
            self.total, self.entry.at[c], self.sems[4], self.sems[5], (x, y, z, 1 - c)
        )
        self.last.wait_recv()
        for s in range(2):
            state = self.entry[s]
            cols = pl.ds(s * DK, DK)
            for n, k in self.order:

                @pl.when(c == k)
                def _():
                    out[n, :, cols] = state

                state = self.factor(k, n, DK) * state + self.every[k, n, :, cols]

    def done(self):
        self.swap.wait_send(4)
        for copy in self.far + [self.last]:
            copy.wait_send()


def scan_scratch():
    out = dict(
        every=pltpu.VMEM((2, 4, SLOTS, 1152), F32),
        total=pltpu.VMEM((SLOTS, DK), F32),
        scan_y=pltpu.VMEM((4, SLOTS, 640), BF),
        scan_x=pltpu.VMEM((4, SLOTS, 640), BF),
        lead_b=pltpu.VMEM((SLOTS, DK), F32),
        lead_a=pltpu.VMEM((SLOTS, 128), F32),
        entry=pltpu.VMEM((2, SLOTS, DK), F32),
    )
    kinds = ((4,), (4,), (3,), (3,), (), (), (3,), (3,))
    out.update({f"scan{n}": DMA(shape) for n, shape in enumerate(kinds)})
    return out


def places():
    row = lax.broadcasted_iota(jnp.int32, (CHUNK, CHUNK), 0)
    col = lax.broadcasted_iota(jnp.int32, (CHUNK, CHUNK), 1)
    return row, col


def tri(lower):
    row, col = places()
    return ((row >= col) if lower else (row <= col)).astype(F32)


def seen_mask(offs):
    row, col = places()
    return jnp.logical_and(row >= col, offs >= (row - col).astype(F32))


def carried(cum, offs):
    return jnp.exp(cum) * (offs > places()[0].astype(F32)).astype(F32)


def reaching(cum, offs):
    final = offs[CHUNK - 1 : CHUNK]
    tail = (places()[0].astype(F32) >= CHUNK - 1 - final).astype(F32)
    return jnp.exp(cum[CHUNK - 1 : CHUNK] - cum) * tail


def features(ref, n, which):
    cols = pl.ds(which * HALF, HALF)
    return jnp.concatenate([ref[0, n, :, cols], ref[1, n, :, cols]], axis=1)


def tiles(value):
    return [value[8 * b : 8 * b + 8] for b in range(CHUNK // 8)]


def one_row(blocks, i):
    return blocks[i // 8][i % 8 : i % 8 + 1]


def spans(cum, i):
    last = one_row(cum, i)
    return [(b, jnp.exp(jnp.minimum(cum[b] - last, 0.0))) for b in range(i // 8, CHUNK // 8)]


def weigh(cum, write, columns):
    cum, write, cols = tiles(cum), tiles(write), tiles(columns)
    total = [jnp.zeros((8, SLOTS), F32) for _ in range(CHUNK // 8)]
    for i in range(CHUNK):
        scale = one_row(write, i)
        for b, span in spans(cum, i):
            total[b] = total[b] + cols[b][:, i : i + 1] * (span * scale)
    return jnp.concatenate(total, axis=0)


def weigh_slots(cum, write, values):
    cum, write, vals = tiles(cum), tiles(write), tiles(values)
    lane = lax.broadcasted_iota(jnp.int32, (8, CHUNK), 1)
    total = [jnp.zeros((8, CHUNK), F32) for _ in range(CHUNK // 8)]
    for i in range(CHUNK):
        scale = one_row(write, i)
        for b, span in spans(cum, i):
            got = jnp.sum(vals[b] * (span * scale), axis=1, keepdims=True)
            total[b] = jnp.where(lane == i, got, total[b])
    return jnp.concatenate(total, axis=0)


def chunk_ends(key, value, lam, write, offs):
    cum = dot(tri(True), lam, precision=HIGH)
    ending = (reaching(cum, offs) * write).astype(BF)
    keep = (offs[CHUNK - 1 : CHUNK, 0:1] > CHUNK - 1).astype(F32)
    keep = keep * jnp.exp(tn(lam, jnp.ones((CHUNK, 128), F32), HIGH))
    return cum, jnp.concatenate([tn(ending, key), tn(ending, value), keep], axis=1)


def chunk_near(query, key, cum, write, offs):
    return weigh(cum, write, jnp.where(seen_mask(offs), nt(query, key) * SCALE, 0.0))


def chunk_out(query, value, cum, write, offs, near, state):
    carry = carried(cum, offs)
    far = nt(query, state[:, 0:512].astype(BF)) * SCALE
    scores = near + carry * far
    scores = jnp.exp(scores - jnp.max(scores, axis=1, keepdims=True))
    probs = scores / jnp.sum(scores, axis=1, keepdims=True)
    mixing = jnp.where(seen_mask(offs), weigh_slots(cum, write, probs), 0.0)
    mixed = dot(mixing.astype(BF), value) + dot(
        (probs * carry).astype(BF), state[:, 512:1024].astype(BF)
    )
    return far, probs, mixing, mixed


def chunk_back(query, value, g, cum, write, offs, probs, state):
    carry = carried(cum, offs)
    dmix = jnp.where(seen_mask(offs), nt(g, value), 0.0)
    dfar = nt(g, state[:, 512:1024].astype(BF))
    dnear = weigh(cum, write, dmix)
    dprobs = dnear + carry * dfar
    dscore = probs * (dprobs - jnp.sum(probs * dprobs, axis=1, keepdims=True))
    ends_k = tn((SCALE * dscore * carry).astype(BF), query)
    ends_v = tn((probs * carry).astype(BF), g)
    return dmix, dfar, dnear, dscore, ends_k, ends_v


def chunk_pairs(query, key, cum, write, offs, dmix, dscore, probs):
    affinity = jnp.where(seen_mask(offs), nt(query, key) * SCALE, 0.0)
    cums, writes = tiles(cum), tiles(write)
    aff, dmx, dsc, prb = tiles(affinity), tiles(dmix), tiles(dscore), tiles(probs)
    lane = lax.broadcasted_iota(jnp.int32, (8, CHUNK), 1)
    daff = [jnp.zeros((8, CHUNK), F32) for _ in range(CHUNK // 8)]
    fresh = []
    for i in range(CHUNK):
        scale = one_row(writes, i)
        both = jnp.zeros((8, SLOTS), F32)
        for b, span in spans(cums, i):
            got = jnp.sum(dsc[b] * (span * scale), axis=1, keepdims=True)
            daff[b] = jnp.where(lane == i, got, daff[b])
            both = both + (dsc[b] * aff[b][:, i : i + 1] + prb[b] * dmx[b][:, i : i + 1]) * span
        fresh.append(jnp.sum(both, axis=0, keepdims=True))
    return jnp.concatenate(daff, axis=0), jnp.concatenate(fresh, axis=0)


def chunk_last(
    query, key, value, g, lam, write, slope, offs, cum, near, far, probs, mixing, state, dfar, dnear, dscore, daff, fresh, after
):
    carry, seen, reach = carried(cum, offs), seen_mask(offs), reaching(cum, offs)
    daff = jnp.where(seen, daff * SCALE, 0.0).astype(BF)
    ending = (reach * write).astype(BF)
    nk, nv = after[:, 0:512].astype(BF), after[:, 512:1024].astype(BF)
    dq = dot(daff, key) + dot((SCALE * dscore * carry).astype(BF), state[:, 0:512].astype(BF))
    dk = tn(daff, query) + dot(ending, nk)
    dv = tn(mixing.astype(BF), g) + dot(ending, nv)
    dend = (nt(key, nk) + nt(value, nv)) * reach
    dkeep = nt(jnp.ones((8, 1024), F32), after * state, HIGH)[0:1]
    keep = (offs[CHUNK - 1 : CHUNK] > CHUNK - 1).astype(F32) * jnp.exp(cum[CHUNK - 1 : CHUNK])
    scaled = write * dend
    dcum = dscore * near + probs * dnear + carry * (dscore * far + probs * dfar)
    dcum = dcum - write * fresh - scaled
    at_end = jnp.sum(scaled, axis=0, keepdims=True) + dkeep * keep
    dcum = dcum + jnp.where(places()[0] == CHUNK - 1, at_end, 0.0)
    dlam = dot(tri(False), dcum, precision=HIGH) - jnp.exp(lam) * (fresh + dend)
    return dq, dk, dv, dlam * slope


def log1p_small(u):
    series = u * (1 - u * (1 / 2 - u * (1 / 3 - u / 4)))
    return jnp.where(u < 0.01, series, jnp.log(1 + u))


def one_less_exp(v):
    series = -v * (1 + v * (1 / 2 + v * (1 / 6 + v / 24)))
    return jnp.where(v > -0.03, series, 1 - jnp.exp(v))


def forget_gate(logits):
    small = jnp.exp(-jnp.abs(logits))
    lam = (jnp.minimum(logits, 0.0) - log1p_small(small)) / 8
    slope = jnp.where(logits >= 0, small, 1.0) / (1 + small) / 8
    return lam, one_less_exp(lam), slope


def prepare(r):
    x, y, z, c = here()
    first = rms(r.inputs[...].astype(F32), r.norm1_gain[...]).astype(BF)
    r.first_own[...] = first
    for j in range(2):
        for k in range(2):
            cols = slice((2 * j + k) * HALF, (2 * j + k + 1) * HALF)
            for n, w in enumerate((r.key_weight, r.value_weight)):
                r.wk[j, k, :, n * HALF : (n + 1) * HALF] = w[:, cols]
            for n, w in enumerate((r.query_weight, r.gate_weight, r.out_weight)):
                r.wm[j, k, :, n * HALF : (n + 1) * HALF] = w[:, cols]
    lowrank = nt(first, r.low_down[...])
    r.lowrank[...] = lowrank
    logits = dot(lowrank, r.low_up[...].astype(F32), precision=HIGH) + r.forget_bias[...]
    lam, write, slope = forget_gate(logits.astype(BF).astype(F32))
    row = lax.broadcasted_iota(jnp.int32, (64, 128), 0)
    col = lax.broadcasted_iota(jnp.int32, (64, 128), 1)
    offs = jnp.where(col == row + 64 * c, r.offsets[...].astype(F32), 0.0)
    offs = jnp.broadcast_to(jnp.sum(offs, axis=1, keepdims=True), (64, SLOTS))
    for h in range(4):
        cols = slice(h * SLOTS, (h + 1) * SLOTS)
        r.packed[h, 0] = jnp.concatenate([lam[:, cols], write[:, cols]], axis=1)
        r.packed[h, 1] = jnp.concatenate([slope[:, cols], offs], axis=1)
    for k in range(4):
        for n, w in enumerate((r.ffn_gate, r.ffn_up, r.ffn_down)):
            piece = w[:, k * UNITS : (k + 1) * UNITS]
            pad = jnp.zeros((32, UNITS_PAD - UNITS), BF)
            r.wf[k, :, n * UNITS_PAD : (n + 1) * UNITS_PAD] = jnp.concatenate([piece, pad], axis=1)


def gate_of(r, n, kind):
    return r.gate[n, kind]


def tile(n, width=HALF, start=0):
    return pl.ds(pl.multiple_of(start + n * width, width), width)


def all_rows(ref, *at):
    value = ref[at] if at else ref[...]
    return value.reshape(512, value.shape[-1])


def columns(ref, cols):
    return ref[:, :, :, cols].reshape(2048, -1)


def forward_kernel(r):
    x, y, z, c = here()
    partner = (x, y, z, 1 - c)
    scan = Scan(r, False)
    r.start()
    greet(all_peers())
    prepare(r)
    greeted(all_peers())
    kv = Spread(r, "kv_spread", r.wide_k, 0, 2 * HALF, ring=False)
    mix = Spread(r, "m_spread", r.wide_m, 0, 3 * HALF)
    down = Spread(r, "d_spread", r.wide_f, 2 * UNITS_PAD, UNITS_PAD)
    acts = Spread(r, "f_spread", r.wide_f, 0, 2 * UNITS_PAD)
    a_sems, b_sems, s_sems = (sems_of(r, n, 5) for n in ("rows_a_", "rows_b_", "rows_s_"))
    k_deal = deal_start(r.wk, r.wide_k, r.k_send, r.k_recv)
    deal_wait(r.wk, r.wide_k, r.k_recv)
    kv.near()
    kv.far(0)
    a_rows = rows_start(r.first_own, r.first, a_sems)
    gates = shuffle_start(lambda k: r.packed.at[k], r.gates.at[z], *sems_of(r, "gate", 3))
    m_deal = deal_start(r.wm, r.wide_m, r.m_send, r.m_recv)
    kv.far(1, 2, 3)
    deal_wait(r.wm, r.wide_m, r.m_recv)
    mix.near()
    rows_finish(a_rows, r.first, a_sems)
    f_deal = shuffle_start(
        lambda k: r.wf.at[k],
        r.wide_f.at[x, y, pl.ds(pl.multiple_of(z * 32, 32), 32), :],
        *sems_of(r, "deal", 3),
    )
    shuffle_wait(gates)
    for n in range(4):
        for kind in range(4):
            r.gate[n, kind] = r.gates[n, kind // 2, :, (kind % 2) * SLOTS : (kind % 2 + 1) * SLOTS]
    kv.arrive()
    mix.far(0, 1, 2, 3)
    r.save("wide_k", "first", "gate")

    swap = Pieces(
        lambda n: r.proj.at[1 - c, :, :, tile(n, start=HALF)],
        lambda n: r.qkv.at[c, :, :, tile(n, start=HALF)],
        r.swap_s,
        r.swap_r,
        partner,
    )

    @pl.loop(0, 2)
    def _(n):
        got = dot(all_rows(r.first), columns(r.wide_k, tile(n)))
        r.proj[:, :, :, tile(n, start=HALF)] = got.astype(BF).reshape(2, 4, 64, HALF)
        swap.start(n)
        r.qkv[c, :, :, tile(n, start=HALF)] = r.proj[c, :, :, tile(n, start=HALF)]

    shuffle_wait(f_deal)
    down.near()
    swap.wait_recv(2)

    @pl.loop(0, 4)
    def _(n):
        cum, ends = chunk_ends(
            features(r.qkv, n, 1), features(r.qkv, n, 2), gate_of(r, n, 0), gate_of(r, n, 1), gate_of(r, n, 3)
        )
        r.cum[n] = cum
        r.every[c, n] = ends
        r.decays[n] = ends[:, 1024:1152]
        scan.pair(n)

    mix.relay(0, 1, 2, 3)
    scan.send()
    acts.near()
    acts.far(0)
    b_rows = rows_start(r.rows_b, r.cot, b_sems)
    mix.arrive()
    r.save("wide_m")
    got = dot(all_rows(r.first), columns(r.wide_m, pl.ds(0, HALF)))
    query = pl.ds(0, HALF)
    r.proj[:, :, :, query] = got.astype(BF).reshape(2, 4, 64, HALF)
    swap_q = push(
        r.proj.at[1 - c, :, :, query],
        r.qkv.at[c, :, :, query],
        r.swap_s.at[2],
        r.swap_r.at[2],
        partner,
    )
    r.qkv[c, :, :, query] = r.proj[c, :, :, query]
    scan.middle()
    down.far(0)
    got = dot(all_rows(r.first), columns(r.wide_m, pl.ds(HALF, HALF)))
    r.gate_lin[...] = got.reshape(2, 4, 64, HALF)
    swap_q.wait()
    r.save("qkv")

    @pl.loop(0, 4)
    def _(n):
        r.near[n] = chunk_near(
            features(r.qkv, n, 0), features(r.qkv, n, 1), r.cum[n], gate_of(r, n, 1), gate_of(r, n, 3)
        )

    scan.fold(r.states)
    acts.far(1, 2, 3)
    down.far(1, 2, 3)
    swap2 = Pieces(
        lambda n: r.normed.at[1 - c, n],
        lambda n: r.headnorm.at[c, n],
        r.norm_s,
        r.norm_r,
        partner,
    )

    @pl.loop(0, 4)
    def _(n):
        far, probs, mixing, mixed = chunk_out(
            features(r.qkv, n, 0),
            features(r.qkv, n, 2),
            r.cum[n],
            gate_of(r, n, 1),
            gate_of(r, n, 3),
            r.near[n],
            r.states[n],
        )
        r.far[n], r.probs[n], r.mixing[n], r.mixed[n] = far, probs, mixing, mixed
        normed = rms(mixed, r.head_gain[...])
        for s in range(2):
            r.normed[s, n] = normed[:, s * HALF : (s + 1) * HALF]
        swap2.start(n)

    r.headnorm[c] = r.normed[c]
    r.save("cum", "decays", "states", "near", "far", "probs", "mixing", "mixed", "gate_lin")
    rows_finish(b_rows, r.cot, b_sems)
    r.save("cot")
    acts.relay(0)
    down.relay(0)
    swap2.wait_recv(4)
    sums = RowSum(r, "mix", r.parts, lambda k: r.parts[c, k])
    for core in (1 - c, c):
        lin = r.gate_lin[core].reshape(256, HALF)
        branch = (r.headnorm[core].reshape(256, HALF) * (lin * jax.nn.sigmoid(lin))).astype(BF)
        r.branch[core] = branch.reshape(4, 64, HALF)

        @pl.loop(0, 4)
        def _(n):
            got = nt(branch, r.wide_m[n, :, :, 2 * HALF : 3 * HALF].reshape(512, HALF))
            r.parts[core, :, :, tile(n, 512)] = got.astype(BF).reshape(4, 64, 512)

        if core is not c:
            sums.pairs()
    r.save("headnorm", "branch")
    sums.hops()
    resid1 = r.inputs[...].astype(F32) + sums.result()
    r.resid1[...] = resid1
    r.second_own[...] = rms(resid1, r.norm2_gain[...]).astype(BF)
    s_rows = rows_start(r.second_own, r.second, s_sems)
    down.relay(1, 2, 3)
    acts.relay(1, 2, 3)
    down.arrive()

    @pl.loop(0, 3)
    def _(n):
        r.grad_hidden[:, tile(n)] = dot(
            all_rows(r.cot), columns(r.wide_f, tile(n, start=2 * UNITS_PAD))
        )

    rows_finish(s_rows, r.second, s_sems)
    r.save("second")
    acts.arrive()

    @pl.loop(0, 3)
    def _(n):
        second = all_rows(r.second)
        gate = dot(second, columns(r.wide_f, tile(n)))
        up = dot(second, columns(r.wide_f, tile(n, start=UNITS_PAD)))
        grad = r.grad_hidden[:, tile(n)]
        sig = jax.nn.sigmoid(gate)
        silu = gate * sig
        parts = (grad * up * sig * (1 + gate * (1 - sig)), grad * silu, silu * up)
        for m, part in enumerate(parts):
            r.acts[m, :, :, :, tile(n)] = part.astype(BF).reshape(2, 4, 64, HALF)

    r.save("acts")

    @pl.loop(0, 4)
    def _(n):
        got = nt(all_rows(r.acts, 0), r.wide_f[n, :, :, 0:UNITS_PAD].reshape(512, UNITS_PAD))
        got = got + nt(
            all_rows(r.acts, 1), r.wide_f[n, :, :, UNITS_PAD : 2 * UNITS_PAD].reshape(512, UNITS_PAD)
        )
        r.second_part[:, :, :, tile(n, 512)] = got.astype(BF).reshape(2, 4, 64, 512)

    r.save("second_part")

    @pl.loop(0, 4)
    def _(n):
        got = nt(all_rows(r.acts, 2), r.wide_f[n, :, :, 2 * UNITS_PAD :].reshape(512, UNITS_PAD))
        r.ffn_part[:, :, :, tile(n, 512)] = got.astype(BF).reshape(2, 4, 64, 512)

    r.save("ffn_part")
    swap.wait_send(2)
    swap2.wait_send(4)
    for sent in (k_deal, m_deal):
        deal_done(sent)
    for sent in (gates, f_deal):
        shuffle_done(sent)
    for part in (kv, mix, down, acts, scan, sums):
        part.done()
    r.finish()


def forward(operands):
    square = ((4, 64, 64), F32)
    rows = (2, 4, 64, 2048)
    scratch = dict(
        proj=pltpu.VMEM((2, 4, 64, 3 * HALF), BF),
        normed=pltpu.VMEM((2, 4, 64, HALF), F32),
        parts=pltpu.VMEM(rows, BF),
        second_own=pltpu.VMEM((64, 2048), BF),
        grad_hidden=pltpu.VMEM((512, UNITS_PAD), F32),
        wide_f=pltpu.VMEM((4, 4, 128, FFN), BF),
        wk=pltpu.VMEM((2, 2, 32, 2 * HALF), BF),
        wm=pltpu.VMEM((2, 2, 32, 3 * HALF), BF),
        wf=pltpu.VMEM((4, 32, FFN), BF),
        packed=pltpu.VMEM((4, 2, 64, 2 * SLOTS), F32),
        gates=pltpu.VMEM((4, 2, 64, 2 * SLOTS), F32),
        k_send=DMA((2, 2)),
        k_recv=DMA((4,)),
        m_send=DMA((2, 2)),
        m_recv=DMA((4,)),
        swap_s=DMA((3,)),
        swap_r=DMA((3,)),
        norm_s=DMA((4,)),
        norm_r=DMA((4,)),
    )
    for name in ("rows_a_", "rows_b_", "rows_s_"):
        scratch.update(rows_sems(name))
    for name in ("kv_spread", "m_spread", "d_spread", "f_spread"):
        scratch.update(spread_sems(name))
    for name in ("gate", "deal"):
        scratch.update(shuffle_sems(name))
    scratch.update(scan_scratch())
    scratch.update(sum_scratch("mix"))
    return remote_call(
        forward_kernel,
        1,
        {name: (value, ANY if name == "rows_b" else VMEM) for name, value in operands.items()},
        dict(
            first_own=((64, 2048), BF, VMEM),
            lowrank=((64, 16), F32, VMEM),
            resid1=((64, 2048), F32, VMEM),
        ),
        scratch,
        saved=dict(
            wide_k=((4, 4, 128, 2 * HALF), BF),
            wide_m=((4, 4, 128, 3 * HALF), BF),
            first=(rows, BF),
            cot=(rows, BF),
            second=(rows, BF),
            gate=((4, 4, 64, SLOTS), F32),
            qkv=((2, 4, 64, 3 * HALF), BF),
            cum=square,
            near=square,
            far=square,
            probs=square,
            mixing=square,
            decays=((4, SLOTS, 128), F32),
            states=((4, SLOTS, 1024), F32),
            mixed=((4, 64, DK), F32),
            gate_lin=((2, 4, 64, HALF), F32),
            headnorm=((2, 4, 64, HALF), F32),
            branch=((2, 4, 64, HALF), BF),
            acts=((3, 2, 4, 64, UNITS_PAD), BF),
            second_part=(rows, BF),
            ffn_part=(rows, BF),
        ),
    )


class WeightSum:
    def __init__(self, r, name, grads, cols, loaded):
        self.grads, self.cols, self.half, self.loaded = grads, cols, cols // 2, loaded
        self.far, self.landed, self.ready, self.past = sems_of(r, name + "b", 4)
        self.sems = sems_of(r, name + "s", 6)
        if loaded:
            self.own, self.own_sem = getattr(r, name + "own"), getattr(r, name + "own_s")
            self.held, self.held_sem = getattr(r, name + "held"), getattr(r, name + "held_s")
        self.fars, self.nears, self.owns, self.pasts = {}, {}, {}, {}

    def part(self, side):
        return pl.ds(side * self.half, self.half)

    def block(self, side, k, d, rows=slice(None)):
        x, y, z, c = here()
        if side == 0:
            return self.grads.at[wrap(x + d), wrap(y + k), rows, self.part(0)]
        return self.grads.at[wrap(x + k), wrap(y + d), rows, self.part(1)]

    def peer(self, side, d):
        x, y, z, c = here()
        return (wrap(x + d), y, z, c) if side == 0 else (x, wrap(y + d), z, c)

    def mine(self, side, k):
        return self.own.at[side, k] if self.loaded else self.block(side, k, 0)

    def load(self, side, k):
        if self.loaded:
            self.owns[side, k] = pltpu.make_async_copy(
                self.block(side, k, 0), self.own.at[side, k], self.own_sem.at[side, k]
            )
            self.owns[side, k].start()

    def push_far(self, src, side, k, d, n, rows):
        self.fars[side, k, n] = push(
            src,
            self.far.at[side, k, d // 2, rows],
            self.sems[0].at[side, k, n],
            self.sems[1].at[side, k, n],
            self.peer(side, d),
        )

    def push_one(self, side, k, d):
        if d == 2:
            for n, to in enumerate((1, 3)):
                self.pasts[side, k, n] = push(
                    self.block(side, k, 2, pl.ds(n * 64, 64)),
                    self.past.at[side, k, n],
                    self.sems[4].at[side, k, n],
                    self.sems[5].at[side, k, n],
                    self.peer(side, to),
                )
        else:
            rows = pl.ds(64 if d == 1 else 0, 64)
            self.push_far(self.block(side, k, d, rows), side, k, d, d // 2, rows)

    def send(self, e):
        for k in (1, 2, 3, 0):
            if e > 0:
                self.push_one(0, k, e)
            else:
                self.load(0, k)
            if k > 0:
                self.push_one(1, e, k)
        self.load(1, e)

    def relay(self, order):
        keys = [(side, k, n) for k in order for side in range(2) for n in range(2)]
        loads = {}

        def block(at):
            side, k, n = keys[at]
            return self.block(side, k, 2 * n + 1, pl.ds(n * 64, 64))

        def fetch(at):
            loads[at] = pltpu.make_async_copy(
                block(at), self.held.at[at % 4], self.held_sem.at[at % 4]
            )
            loads[at].start()

        if self.loaded:
            for at in range(4):
                fetch(at)
        for at, (side, k, n) in enumerate(keys):
            if self.loaded:
                loads[at].wait()
            self.pasts[side, k, n].wait_recv()
            mine = self.held.at[at % 4] if self.loaded else block(at)

            @pl.loop(0, 4)
            def _(t):
                rows = pl.ds(pl.multiple_of(t * 16, 16), 16)
                both = self.past[side, k, n, rows, :].astype(F32) + mine[rows, :].astype(F32)
                self.past[side, k, n, rows, :] = both.astype(BF)

            rows = pl.ds(n * 64, 64)
            self.push_far(self.past.at[side, k, n], side, k, 2 * n + 1, 2 + n, rows)
            if self.loaded and at + 4 < len(keys):
                fetch(at + 4)

    def arrive(self, side, k):
        if self.loaded:
            self.owns[side, k].wait()
        for n in range(4):
            self.fars[side, k, n].wait_recv()

    def total(self, side, k, rows):
        value = self.mine(side, k)[rows, :].astype(F32)
        for d in range(2):
            value = value + self.far[side, k, d, rows, :].astype(F32)
        return value

    def turn(self, k):
        for side in range(2):
            self.arrive(side, k)

            @pl.loop(0, 8)
            def _(t):
                rows = pl.ds(pl.multiple_of(t * 16, 16), 16)
                self.mine(side, k)[rows, :] = self.total(side, k, rows).astype(BF)

            self.nears[side, k] = push(
                self.mine(side, k),
                self.landed.at[side, k - 1],
                self.sems[2].at[side, k - 1],
                self.sems[3].at[side, k - 1],
                self.peer(1 - side, k),
            )

    def finish(self):
        for side in range(2):
            self.arrive(side, 0)
            for k in range(1, 4):
                self.nears[side, k].wait_recv()

            @pl.loop(0, 8)
            def _(t):
                rows = pl.ds(pl.multiple_of(t * 16, 16), 16)
                value = self.total(side, 0, rows)
                for k in range(3):
                    value = value + self.landed[side, k, rows, :].astype(F32)
                self.ready[rows, self.part(side)] = value.astype(BF)

    def done(self):
        for copies in (self.fars, self.nears, self.pasts):
            for copy in copies.values():
                copy.wait_send()


def weight_scratch(name, cols, loaded):
    half = cols // 2
    out = {
        f"{name}b0": pltpu.VMEM((2, 4, 2, 128, half), BF),
        f"{name}b1": pltpu.VMEM((2, 3, 128, half), BF),
        f"{name}b2": pltpu.VMEM((128, cols), BF),
        f"{name}b3": pltpu.VMEM((2, 4, 2, 64, half), BF),
    }
    kinds = ((2, 4, 4), (2, 4, 4), (2, 3), (2, 3), (2, 4, 2), (2, 4, 2))
    out.update({f"{name}s{n}": DMA(shape) for n, shape in enumerate(kinds)})
    if loaded:
        out[f"{name}own"] = pltpu.VMEM((2, 4, 128, half), BF)
        out[f"{name}own_s"] = DMA((2, 4))
        out[f"{name}held"] = pltpu.VMEM((4, 64, half), BF)
        out[f"{name}held_s"] = DMA((4,))
    return out


def return_start(ready, out, send, recv):
    x, y, z, c = here()
    dst, arrived = out.at[lax.rem(z, 2), c], recv.at[lax.rem(z, 2), c]
    sent = []
    for k in range(4):
        src = ready.at[pl.ds(k * 32, 32), :]
        same = jnp.logical_and(k == z, c == z // 2)
        copy = pltpu.make_async_remote_copy(
            src_ref=src,
            dst_ref=dst,
            send_sem=send.at[k],
            recv_sem=arrived,
            device_id=(x, y, k, z // 2),
            device_id_type=MESH,
        )

        @pl.when(same)
        def _():
            pltpu.make_async_copy(src, dst, arrived).start()

        @pl.when(jnp.logical_not(same))
        def _():
            copy.start()

        sent.append((same, copy))
    return sent


def return_wait(ready, out, recv):
    for j in range(2):
        for k in range(2):
            pltpu.make_async_copy(ready.at[pl.ds(0, 32), :], out.at[j, k], recv.at[j, k]).wait()


class SmallSum:
    def __init__(self, r, name, axes):
        self.now, self.held, self.send, self.recv = sems_of(r, name, 4)
        self.axes, self.sent = axes, []

    def start(self, n):
        place = dict(zip("xyzc", here()))
        axis, at = self.axes[n], place[self.axes[n]]
        size = 2 if axis == "c" else 4
        self.held[n, at] = self.now[...]
        self.sent = []
        for d in range(1, size):
            peer = dict(place)
            peer[axis] = wrap(at + d, size)
            self.sent.append(
                push(
                    self.held.at[n, at],
                    self.held.at[n, at],
                    self.send.at[n, d - 1],
                    self.recv.at[n, d - 1],
                    tuple(peer.values()),
                )
            )

    def collect(self, n):
        for copy in self.sent:
            copy.wait()
        value = self.held[n, 0]
        for k in range(1, 2 if self.axes[n] == "c" else 4):
            value = value + self.held[n, k]
        self.now[...] = value


def small_scratch(name, rows, count):
    return {
        f"{name}0": pltpu.VMEM((rows, HALF), F32),
        f"{name}1": pltpu.VMEM((count, 4, rows, HALF), F32),
        f"{name}2": DMA((count, 3)),
        f"{name}3": DMA((count, 3)),
    }


def backward_kernel(r):
    x, y, z, c = here()
    partner = (x, y, z, 1 - c)
    scan = Scan(r, True)
    greet(all_peers())
    mine = pltpu.make_async_copy(r.second_part.at[c], r.mine, r.mine_s.at[0])
    mine.start()
    r.start()
    greeted(all_peers())
    second = RowSum(r, "sec", r.second_part, lambda k: r.mine[k])
    ffn = RowSum(r, "ffn", r.ffn_part, lambda k: r.mine[k])
    units = WeightSum(r, "units", r.out_grads, FFN, True)
    tail = WeightSum(r, "tail", r.grads_tail, 2 * HALF, False)
    last = WeightSum(r, "last", r.grads_last, 3 * HALF, False)
    second.pairs()
    mine.wait()
    second.hops()

    r.need("acts", "second", "cot")
    for e in (1, 2, 3, 0):
        at = wrap(x + e)
        steps = [
            pltpu.make_async_copy(
                r.grads_last.at[n], r.out_grads.at[at, :, :, pl.ds(n * UNITS_PAD, UNITS_PAD)], r.stage_s.at[n]
            )
            for n in range(3)
        ]
        for n, left in enumerate((r.second, r.second, r.cot)):
            got = tn(left[:, :, :, tile(at, 512)].reshape(512, 512), all_rows(r.acts, n))
            r.grads_last[n] = got.astype(BF).reshape(4, 128, UNITS_PAD)
            steps[n].start()
        for copy in steps:
            copy.wait()
        units.send(e)
    r.need("resid1", "cot_own")
    e = second.result()
    second.done()
    mine = pltpu.make_async_copy(r.ffn_part.at[c], r.mine, r.mine_s.at[1])
    mine.start()
    grad, d_norm2 = rms_back(r.resid1[...], r.norm2_gain[...], e)
    group = SmallSum(r, "group", ("c", "z"))
    plane = SmallSum(r, "plane", ("y", "x"))
    tiny = SmallSum(r, "tiny", ("c", "z", "y", "x"))
    group.now[...] = jnp.zeros_like(group.now)

    def split_rows(dst, start, value):
        for n in range(value.shape[1] // HALF):
            dst[start + n : start + n + 1, :] = value[:, n * HALF : (n + 1) * HALF]

    split_rows(group.now, 16, d_norm2)
    grad_resid1 = r.cot_own[...].astype(F32) + grad
    r.attn_own[...] = grad_resid1.astype(BF)
    r.grad_resid1[...] = grad_resid1
    a_sems = sems_of(r, "rows_a_", 5)
    a_rows = rows_start(r.attn_own, r.attn, a_sems)
    rows_finish(a_rows, r.attn, a_sems)
    ffn.pairs()
    units.relay((1, 2, 3, 0))

    r.need("wide_m", "gate_lin", "headnorm")
    grad_branch = dot(all_rows(r.attn), columns(r.wide_m, pl.ds(2 * HALF, HALF)))
    lin, normed = all_rows(r.gate_lin), all_rows(r.headnorm)
    sig = jax.nn.sigmoid(lin)
    grad_lin = (grad_branch * normed * sig * (1 + lin * (1 - sig))).astype(BF)
    r.grad_lin[...] = grad_lin.reshape(2, 4, 64, HALF)
    r.grad_out[...] = (grad_branch * lin * sig).reshape(2, 4, 64, HALF)
    swap = push(r.grad_out.at[1 - c], r.grad_norm.at[c], r.swap_s.at[0], r.swap_r.at[0], partner)
    r.grad_norm[c] = r.grad_out[c]
    r.need("first", "branch")

    @pl.loop(0, 4)
    def _(n):
        got = tn(r.first[:, :, :, tile(n, 512)].reshape(512, 512), all_rows(r.grad_lin))
        r.grads_tail[n, :, :, 0:HALF] = got.astype(BF).reshape(4, 128, HALF)
        got = tn(r.attn[:, :, :, tile(n, 512)].reshape(512, 512), all_rows(r.branch))
        r.grads_tail[n, :, :, HALF : 2 * HALF] = got.astype(BF).reshape(4, 128, HALF)

    for e in (1, 2, 3, 0):
        tail.send(e)
    r.need("mixed", "qkv", "cum", "gate", "probs", "states", "decays")
    swap.wait()
    mine.wait()
    ffn.hops()

    r.d_head[...] = jnp.zeros_like(r.d_head)

    @pl.loop(0, 4)
    def _(n):
        e = jnp.concatenate([r.grad_norm[0, n], r.grad_norm[1, n]], axis=1)
        grad, d_head = rms_back(r.mixed[n], r.head_gain[...], e)
        r.d_head[0:1] += d_head
        g = grad.astype(BF)
        r.grad_mixed[n] = g
        dmix, dfar, dnear, dscore, ends_k, ends_v = chunk_back(
            features(r.qkv, n, 0),
            features(r.qkv, n, 2),
            g,
            r.cum[n],
            gate_of(r, n, 1),
            gate_of(r, n, 3),
            r.probs[n],
            r.states[n],
        )
        r.dmix[n], r.dfar[n], r.dnear[n], r.dscore[n] = dmix, dfar, dnear, dscore
        r.every[c, n] = jnp.concatenate([ends_k, ends_v, r.decays[n]], axis=1)
        scan.pair(n)

    split_rows(group.now, 24, r.d_head[0:1])
    scan.send()

    def pairs_of(n):
        r.daff[n], r.fresh[n] = chunk_pairs(
            features(r.qkv, n, 0),
            features(r.qkv, n, 1),
            r.cum[n],
            gate_of(r, n, 1),
            gate_of(r, n, 3),
            r.dmix[n],
            r.dscore[n],
            r.probs[n],
        )

    pl.loop(0, 2)(pairs_of)
    scan.middle()
    tail.relay((1, 2, 3, 0))
    pl.loop(2, 4)(pairs_of)
    for k in range(1, 4):
        units.turn(k)
    r.need("near", "far", "mixing")
    scan.fold(r.nexts)
    r.output[...] = (r.resid1[...] + ffn.result()).astype(BF)
    ffn.done()
    swap2 = Pieces(
        lambda n: r.dproj.at[1 - c, n], lambda n: r.dqkv.at[c, n], r.dqkv_s, r.dqkv_r, partner
    )

    @pl.loop(0, 4)
    def _(n):
        dq, dk, dv, dlogit = chunk_last(
            features(r.qkv, n, 0),
            features(r.qkv, n, 1),
            features(r.qkv, n, 2),
            r.grad_mixed[n],
            gate_of(r, n, 0),
            gate_of(r, n, 1),
            gate_of(r, n, 2),
            gate_of(r, n, 3),
            r.cum[n],
            r.near[n],
            r.far[n],
            r.probs[n],
            r.mixing[n],
            r.states[n],
            r.dfar[n],
            r.dnear[n],
            r.dscore[n],
            r.daff[n],
            r.fresh[n],
            r.nexts[n],
        )
        for m, part in enumerate((dq, dk, dv)):
            for s in range(2):
                r.dproj[s, n, :, pl.ds(m * HALF, HALF)] = part[
                    :, s * HALF : (s + 1) * HALF
                ].astype(BF)
        swap2.start(n)
        r.dlogit[n] = dlogit

    r.dqkv[c] = r.dproj[c]
    logits = shuffle_start(lambda k: r.dlogit.at[k], r.dl.at[z], *sems_of(r, "gate", 3))
    swap2.wait_recv(4)

    for e in (1, 2, 3, 0):
        at = wrap(x + e)
        got = tn(r.first[:, :, :, tile(at, 512)].reshape(512, 512), all_rows(r.dqkv))
        r.grads_last[at] = got.astype(BF).reshape(4, 128, 3 * HALF)
        last.send(e)

    shuffle_wait(logits)
    r.need("lowrank", "up", "down", "inputs", "wide_k")
    low = jnp.zeros((64, 16), F32)
    bias = []
    for h in range(4):
        dl = r.dl[h]
        low = low + nt(dl, r.up[:, h * SLOTS : (h + 1) * SLOTS].astype(F32), HIGH)
        group.now[0:16, h * SLOTS : (h + 1) * SLOTS] = tn(r.lowrank[...], dl, HIGH)
        bias.append(jnp.sum(dl, axis=0, keepdims=True))
    split_rows(group.now, 26, jnp.concatenate(bias, axis=1))
    r.low_own[...] = low
    l_sems, d_sems = sems_of(r, "rows_l_", 5), sems_of(r, "rows_d_", 5)
    l_rows = rows_start(r.low_own, r.lows, l_sems)
    group.start(0)
    first_part = r.attn
    first = RowSum(r, "fst", first_part, lambda k: first_part[c, k])
    for core in (1 - c, c):

        @pl.loop(0, 4)
        def _(n):
            dqkv = r.dqkv[core].reshape(256, 3 * HALF)
            got = nt(dqkv[:, HALF:], r.wide_k[n].reshape(512, 2 * HALF))
            left = jnp.concatenate([dqkv[:, 0:HALF], r.grad_lin[core].reshape(256, HALF)], axis=1)
            got = got + nt(left, r.wide_m[n, :, :, 0 : 2 * HALF].reshape(512, 2 * HALF))
            first_part[core, :, :, tile(n, 512)] = got.astype(BF).reshape(4, 64, 512)

        if core is not c:
            first.pairs()
            group.collect(0)
            group.start(1)

    first.hops()
    for k in range(1, 4):
        tail.turn(k)
    last.relay((1, 2, 3, 0))
    rows_finish(l_rows, r.lows, l_sems)
    group.collect(1)
    at = 2 * z + c
    plane.now[0:32] = group.now[...]
    plane.now[32:48] = tn(
        r.lows[...].reshape(512, 16), all_rows(r.first, slice(None), slice(None), slice(None), tile(at)).astype(F32), HIGH
    )
    plane.start(0)
    units.finish()
    units_back = shuffle_start(
        lambda k: units.ready.at[pl.ds(pl.multiple_of(k * 32, 32), 32), :],
        r.units_out.at[z],
        *sems_of(r, "back", 3),
    )
    tail.finish()
    tail_back = return_start(tail.ready, r.tail_out, r.tail_send, r.tail_recv)
    grad_first = first.result() + dot(low, r.down[...].astype(F32), precision=HIGH)
    grad, d_norm1 = rms_back(r.inputs[...].astype(F32), r.norm1_gain[...], grad_first)
    split_rows(tiny.now, 0, d_norm1)
    tiny.start(0)
    r.d_inputs[...] = r.grad_resid1[...] + grad
    tiny.collect(0)
    tiny.start(1)
    last.turn(1)
    last.turn(2)
    last.turn(3)
    plane.collect(0)
    plane.start(1)
    tiny.collect(1)
    tiny.start(2)
    last.finish()
    last_back = return_start(last.ready, r.last_out, r.last_send, r.last_recv)
    plane.collect(1)
    r.down_own[...] = plane.now[32:48]
    d_rows = rows_start(r.down_own, r.down_out, d_sems)
    tiny.collect(2)
    tiny.start(3)
    rows_finish(d_rows, r.down_out, d_sems)
    tiny.collect(3)
    r.small_out[0:32] = plane.now[0:32]
    r.small_out[32:40] = tiny.now[...]
    swap2.wait_send(4)
    shuffle_wait(units_back)
    shuffle_done(units_back)
    shuffle_done(logits)
    return_wait(tail.ready, r.tail_out, r.tail_recv)
    return_wait(last.ready, r.last_out, r.last_recv)
    deal_done(tail_back)
    deal_done(last_back)
    for part in (first, units, tail, last, scan):
        part.done()


def backward(operands):
    rows = (2, 4, 64, 2048)
    small = pltpu.VMEM((4, 64, 64), F32)
    scratch = dict(
        low_own=pltpu.VMEM((64, 16), F32),
        lows=pltpu.VMEM((2, 4, 64, 16), F32),
        down_own=pltpu.VMEM((16, HALF), F32),
        attn_own=pltpu.VMEM((64, 2048), BF),
        grad_resid1=pltpu.VMEM((64, 2048), F32),
        attn=pltpu.VMEM(rows, BF),
        grad_lin=pltpu.VMEM((2, 4, 64, HALF), BF),
        grad_out=pltpu.VMEM((2, 4, 64, HALF), F32),
        grad_norm=pltpu.VMEM((2, 4, 64, HALF), F32),
        grad_mixed=pltpu.VMEM((4, 64, DK), BF),
        d_head=pltpu.VMEM((8, DK), F32),
        dmix=small,
        dfar=small,
        dnear=small,
        dscore=small,
        daff=small,
        fresh=small,
        dlogit=small,
        dl=small,
        nexts=pltpu.VMEM((4, SLOTS, 1024), F32),
        dproj=pltpu.VMEM((2, 4, 64, 3 * HALF), BF),
        dqkv=pltpu.VMEM((2, 4, 64, 3 * HALF), BF),
        mine=pltpu.VMEM((4, 64, 2048), BF),
        mine_s=DMA((2,)),
        stage_s=DMA((3,)),
        grads_tail=pltpu.VMEM((4, 4, 128, 2 * HALF), BF),
        grads_last=pltpu.VMEM((4, 4, 128, 3 * HALF), BF),
        swap_s=DMA((1,)),
        swap_r=DMA((1,)),
        dqkv_s=DMA((4,)),
        dqkv_r=DMA((4,)),
        tail_send=DMA((4,)),
        tail_recv=DMA((2, 2)),
        last_send=DMA((4,)),
        last_recv=DMA((2, 2)),
    )
    for name, cols, loaded in (
        ("units", FFN, True),
        ("tail", 2 * HALF, False),
        ("last", 3 * HALF, False),
    ):
        scratch.update(weight_scratch(name, cols, loaded))
    scratch.update(sum_scratch("sec", "ffn", "fst"))
    for name in ("gate", "back"):
        scratch.update(shuffle_sems(name))
    scratch.update(rows_sems("rows_a_"))
    scratch.update(scan_scratch())
    for name in ("rows_l_", "rows_d_"):
        scratch.update(rows_sems(name))
    for name, height, count in (("group", 32, 2), ("plane", 48, 2), ("tiny", 8, 4)):
        scratch.update(small_scratch(name, height, count))
    in_hbm = ("second_part", "ffn_part")
    in_vmem = ("norm1_gain", "norm2_gain", "head_gain")
    order = ("acts", "second", "cot", "resid1", "cot_own", "wide_m", "gate_lin", "headnorm")
    order += tuple(name for name in operands if name not in order + in_hbm + in_vmem)
    direct = {name: (operands[name], ANY) for name in in_hbm}
    direct.update({name: (operands[name], VMEM) for name in in_vmem})
    return remote_call(
        backward_kernel,
        2,
        direct,
        dict(
            output=((64, 2048), BF, VMEM),
            d_inputs=((64, 2048), F32, VMEM),
            last_out=((2, 2, 32, 3 * HALF), BF, VMEM),
            tail_out=((2, 2, 32, 2 * HALF), BF, VMEM),
            units_out=((4, 32, FFN), BF, VMEM),
            small_out=((40, HALF), F32, VMEM),
            down_out=((2, 4, 16, HALF), F32, VMEM),
            out_grads=((4, 4, 128, FFN), BF, ANY),
        ),
        scratch,
        loaded={name: operands[name] for name in order},
    )


def results_kernel(*refs):
    sources, outs, held, sems = refs[:7], refs[7:23], refs[23:30], refs[30]
    copies = [
        pltpu.make_async_copy(src, dst, sems.at[n]) for n, (src, dst) in enumerate(zip(sources, held))
    ]
    for copy in copies:
        copy.start()
    for copy in copies:
        copy.wait()
    out, d_in, last, tail, units, small, factor = held
    output, d_inputs, norm1, q, k, v, g, o, down, up, bias, head, norm2, fg, fu, fd = outs
    output[...] = out[...]
    d_inputs[...] = d_in[...]
    for j in range(2):
        for n in range(2):
            at = slice((2 * j + n) * HALF, (2 * j + n + 1) * HALF)
            for m, ref in enumerate((q, k, v)):
                ref[:, at] = last[j, n, :, m * HALF : (m + 1) * HALF].astype(F32)
            g[:, at] = tail[j, n, :, 0:HALF].astype(F32)
            o[:, at] = tail[j, n, :, HALF : 2 * HALF].astype(F32)
    for n in range(4):
        at = slice(n * UNITS, (n + 1) * UNITS)
        for m, ref in enumerate((fg, fu, fd)):
            ref[:, at] = units[n, :, m * UNITS_PAD : m * UNITS_PAD + UNITS].astype(F32)
    up[...] = small[0:16]
    for n in range(8):
        cols = slice(n * HALF, (n + 1) * HALF)
        norm2[:, cols] = small[16 + n : 17 + n]
        norm1[:, cols] = small[32 + n : 33 + n]
        down[:, cols] = factor[n % 2, n // 2]
    for n in range(2):
        head[:, n * HALF : (n + 1) * HALF] = small[24 + n : 25 + n]
    bias[...] = small[26:27]


def results(b):
    shapes = [((64, 2048), BF), ((64, 2048), F32), ((1, 2048), F32)]
    shapes += [((32, 1024), F32)] * 5 + [((16, 2048), F32), ((16, 256), F32)]
    shapes += [((1, 256), F32), ((1, 512), F32), ((1, 2048), F32)] + [((32, 4 * UNITS), F32)] * 3
    names = ("output", "d_inputs", "last_out", "tail_out", "units_out", "small_out", "down_out")
    sources = [b[name] for name in names]
    call = pl.pallas_call(
        results_kernel,
        out_shape=[jax.ShapeDtypeStruct(shape, dtype) for shape, dtype in shapes],
        in_specs=[ANY] * 7,
        scratch_shapes=[pltpu.VMEM(v.shape, v.dtype) for v in sources] + [DMA((7,))],
        compiler_params=pltpu.CompilerParams(vmem_limit_bytes=63 * 2**20),
    )
    out = list(call(*sources))
    out[7], out[8] = out[7].T, out[8].T
    for n in (2, 10, 11, 12):
        out[n] = out[n][0]
    return tuple(out)


def rms(v, gain):
    return v * lax.rsqrt(jnp.mean(v * v, axis=-1, keepdims=True) + EPS) * gain


def rms_back(v, gain, e):
    r = lax.rsqrt(jnp.mean(v * v, axis=-1, keepdims=True) + EPS)
    grad = r * gain * e - v * (r * r * r) * jnp.mean(v * gain * e, axis=-1, keepdims=True)
    return grad, jnp.sum(e * v * r, axis=0, keepdims=True)


def body(
    inputs,
    offsets,
    norm1_gain,
    query_weight,
    key_weight,
    value_weight,
    gate_weight,
    out_weight,
    low_down,
    low_up,
    forget_bias,
    head_gain,
    norm2_gain,
    ffn_gate,
    ffn_up,
    ffn_down,
    cotangent,
):
    gain1, gain2, gain_head = norm1_gain[None], norm2_gain[None], head_gain[None]
    f = forward(
        dict(
            query_weight=query_weight,
            key_weight=key_weight,
            value_weight=value_weight,
            gate_weight=gate_weight,
            out_weight=out_weight.T,
            ffn_gate=ffn_gate,
            ffn_up=ffn_up,
            ffn_down=ffn_down,
            inputs=inputs,
            rows_b=cotangent,
            offsets=offsets[None],
            low_down=low_down.T,
            low_up=low_up,
            forget_bias=forget_bias[None],
            norm1_gain=gain1,
            norm2_gain=gain2,
            head_gain=gain_head,
        )
    )

    operands = dict(
        {name: value for name, value in f.items() if name != "first_own"},
        cot_own=cotangent,
        inputs=inputs,
        up=low_up,
        down=low_down.T,
        norm1_gain=gain1,
        norm2_gain=gain2,
        head_gain=gain_head,
    )
    b = backward(operands)
    return results(b)


def solution(mesh):
    fine = Mesh(mesh.devices.reshape(4, 4, 4, 2), ("x", "y", "z", "c"))
    seq = ("x", "y", "z")
    rows = P(("x", "y", "z", "c"), None)
    wide = P(seq, "c")
    placed = (
        (rows, P(seq), P())
        + (wide,) * 4
        + (P("c", seq), P(), P(), P(), P(), P(), wide, wide, wide, rows)
    )
    return jax.shard_map(
        body,
        mesh=fine,
        in_specs=placed,
        out_specs=(rows, rows, P())
        + (wide,) * 4
        + (P("c", seq), P(), P(), P(), P(), P(), wide, wide, wide),
        check_vma=False,
    )
```

```python
import functools

import jax
import jax.numpy as jnp
from jax import lax
from jax.experimental import pallas as pl
from jax.experimental.pallas import tpu as pltpu
from jax.sharding import Mesh
from jax.sharding import PartitionSpec as P

DK = 512
SLOTS = 64
CHUNK = 64
HALF = 256
UNITS = 704
UNITS_PAD = 768
EPS = 1e-06
SCALE = 0.125
BF = jnp.bfloat16
F32 = jnp.float32
HIGH = lax.Precision.HIGHEST
MESH = pl.DeviceIdType.MESH
ANY = pl.BlockSpec(memory_space=pl.ANY)
VMEM = pl.BlockSpec(memory_space=pltpu.VMEM)
DMA = pltpu.SemaphoreType.DMA
FFN = 3 * UNITS_PAD


def dot(left, right, dims=((1,), (0,)), precision=None):
    return lax.dot_general(
        left, right, (dims, ((), ())), precision=precision, preferred_element_type=F32
    )


def nt(left, right, precision=None):
    return dot(left, right, ((1,), (1,)), precision)


def tn(left, right, precision=None):
    return dot(left, right, ((0,), (0,)), precision)


def here():
    return tuple(lax.axis_index(a) for a in ("x", "y", "z", "c"))


def wrap(v, n=4):
    return lax.rem(v + n, n)


def greet(peers):
    barrier = pltpu.get_barrier_semaphore()
    for peer in peers:
        pl.semaphore_signal(barrier, inc=1, device_id=peer, device_id_type=MESH)


def greeted(peers):
    pl.semaphore_wait(pltpu.get_barrier_semaphore(), len(peers))


def push(src, dst, send, recv, peer):
    copy = pltpu.make_async_remote_copy(
        src_ref=src, dst_ref=dst, send_sem=send, recv_sem=recv, device_id=peer, device_id_type=MESH
    )
    copy.start()
    return copy


class Pieces:
    def __init__(self, src, dst, send, recv, peer):
        self.args = (src, dst, send, recv, peer)

    def copy(self, n):
        src, dst, send, recv, peer = self.args
        return pltpu.make_async_remote_copy(
            src_ref=src(n),
            dst_ref=dst(n),
            send_sem=send.at[n],
            recv_sem=recv.at[n],
            device_id=peer,
            device_id_type=MESH,
        )

    def start(self, n):
        self.copy(n).start()

    def wait_recv(self, count):
        for n in range(count):
            self.copy(n).wait_recv()

    def wait_send(self, count):
        for n in range(count):
            self.copy(n).wait_send()


class Refs:
    def start(self):
        self.loads = {}
        for n, name in enumerate(self.loaded):
            copy = pltpu.make_async_copy(
                getattr(self, "in_" + name), getattr(self, name), self.load_sem.at[n]
            )
            copy.start()
            self.loads[name] = copy
        self.saves = []

    def need(self, *names):
        for name in names:
            copy = self.loads.pop(name, None)
            if copy is not None:
                copy.wait()

    def save(self, *names):
        for name in names:
            copy = pltpu.make_async_copy(
                getattr(self, name),
                getattr(self, "out_" + name),
                self.save_sem.at[len(self.saves)],
            )
            copy.start()
            self.saves.append(copy)

    def finish(self):
        for copy in self.saves:
            copy.wait()


def remote_call(kernel, collective_id, operands, outs, scratch, loaded=(), saved=()):
    loaded, saved = dict(loaded), dict(saved)
    operands = dict(operands)
    operands.update({"in_" + name: (value, ANY) for name, value in loaded.items()})
    outs = dict(outs)
    outs.update({"out_" + name: (shape, dtype, ANY) for name, (shape, dtype) in saved.items()})
    scratch = dict(scratch)
    scratch.update({name: pltpu.VMEM(v.shape, v.dtype) for name, v in loaded.items()})
    scratch.update({name: pltpu.VMEM(shape, dtype) for name, (shape, dtype) in saved.items()})
    scratch["load_sem"] = DMA((max(len(loaded), 1),))
    scratch["save_sem"] = DMA((max(len(saved), 1),))
    names = list(operands) + list(outs) + list(scratch)

    def run(*refs):
        r = Refs()
        for name, ref in zip(names, refs):
            setattr(r, name, ref)
        r.loaded = list(loaded)
        kernel(r)

    results = pl.pallas_call(
        run,
        out_shape=[jax.ShapeDtypeStruct(shape, dtype) for shape, dtype, _ in outs.values()],
        in_specs=[spec for _, spec in operands.values()],
        out_specs=[spec for _, _, spec in outs.values()],
        scratch_shapes=list(scratch.values()),
        compiler_params=pltpu.CompilerParams(
            collective_id=collective_id, has_side_effects=True, vmem_limit_bytes=63 * 2**20
        ),
    )(*[array for array, _ in operands.values()])
    return {name.removeprefix("out_"): value for name, value in zip(outs, results)}


class Spread:
    def __init__(self, r, name, ref, start, width, ring=True):
        self.ref, self.start, self.half, self.ring = ref, start, width // 2, ring
        self.sems = sems_of(r, name, 4)
        self.nears, self.fars, self.arrived = {}, {}, set()

    def block(self, side, k, d=0, rows=slice(None)):
        x, y, z, c = here()
        part = pl.ds(self.start + side * self.half, self.half)
        if side == 0:
            return self.ref.at[wrap(x + d), wrap(y - k), rows, part]
        return self.ref.at[wrap(x - k), wrap(y + d), rows, part]

    def peer(self, side, d):
        x, y, z, c = here()
        return (wrap(x + d), y, z, c) if side == 0 else (x, wrap(y + d), z, c)

    def near(self):
        for d in range(1, 4):
            for side in range(2):
                block = self.block(side, 0)
                self.nears[side, d] = push(
                    block,
                    block,
                    self.sems[0].at[side, d - 1],
                    self.sems[1].at[side, d - 1],
                    self.peer(1 - side, d),
                )

    def pass_on(self, key, block, d):
        side, k, n = key
        self.fars[key] = push(
            block, block, self.sems[2].at[side, k, n], self.sems[3].at[side, k, n], self.peer(side, d)
        )

    def far(self, *steps):
        for k in steps:
            for side in range(2):
                if k > 0:
                    self.nears[side, k].wait_recv()
                for d in (1, 3) if self.ring else (1, 3, 2):
                    self.pass_on((side, k, d - 1), self.block(side, k), d)

    def wait(self, key):
        if key not in self.arrived:
            self.arrived.add(key)
            self.fars[key].wait_recv()

    def relay(self, *steps):
        for k in steps:
            for side in range(2):
                self.wait((side, k, 0))
                self.pass_on((side, k, 1), self.block(side, k, -1, pl.ds(0, 64)), 1)
                self.wait((side, k, 2))
                self.pass_on((side, k, 3), self.block(side, k, 1, pl.ds(64, 64)), 3)

    def arrive(self):
        for key in self.fars:
            self.wait(key)

    def done(self):
        for copy in list(self.nears.values()) + list(self.fars.values()):
            copy.wait_send()


def spread_sems(name):
    kinds = ((2, 3), (2, 3), (2, 4, 4), (2, 4, 4))
    return {f"{name}{n}": DMA(shape) for n, shape in enumerate(kinds)}


def rows_start(src, out, sems):
    x, y, z, c = here()
    hop_s, hop_r, pair_s, pair_r, own = sems
    half = src.shape[0] // 2
    mine = pltpu.make_async_copy(src, out.at[c, z], own)
    mine.start()
    hops = {}
    for h in range(2):
        rows = pl.ds(h * half, half)
        for d in (2, 1, 3):
            hops[h, d] = push(
                src.at[rows],
                out.at[c, z, rows],
                hop_s.at[h, d - 1],
                hop_r.at[h, d - 1],
                (x, y, wrap(z + d), c),
            )
    pairs = [push(src, out.at[c, z], pair_s.at[0, 3], pair_r.at[0, 3], (x, y, z, 1 - c))]
    return mine, hops, pairs


def rows_finish(started, out, sems):
    x, y, z, c = here()
    hop_s, hop_r, pair_s, pair_r, own = sems
    mine, hops, pairs = started
    half = out.shape[2] // 2
    for h, d in [(h, d) for h in range(2) for d in (1, 3, 2)]:
        hops[h, d].wait_recv()
        block = out.at[c, wrap(z - d), pl.ds(h * half, half)]
        pairs.append(
            push(block, block, pair_s.at[h, d - 1], pair_r.at[h, d - 1], (x, y, z, 1 - c))
        )
    mine.wait()
    for copy in hops.values():
        copy.wait_send()
    for copy in pairs:
        copy.wait()


def rows_sems(name):
    kinds = ((2, 3), (2, 3), (2, 4), (2, 4), ())
    return {f"{name}{n}": DMA(shape) for n, shape in enumerate(kinds)}


def group_peers():
    x, y, z, c = here()
    return [(x, y, wrap(z + d), k) for d in range(1, 4) for k in range(2)] + [(x, y, z, 1 - c)]


def row_peers():
    x, y, z, c = here()
    return [(x, y, wrap(z + d), c) for d in range(1, 4)] + [(x, y, z, 1 - c)]


def plane_peers():
    x, y, z, c = here()
    return [(wrap(x + d), y, z, c) for d in range(1, 4)] + [
        (x, wrap(y + d), z, c) for d in range(1, 4)
    ]


def all_peers():
    return group_peers() + plane_peers()


def sems_of(r, name, count):
    return [getattr(r, f"{name}{n}") for n in range(count)]


def deal_start(src, wide, send, recv):
    x, y, z, c = here()
    dst = wide.at[x, y, pl.ds(pl.multiple_of(z * 32, 32), 32), :]
    sent = []
    for j in range(2):
        for k in range(2):
            same = jnp.logical_and(2 * c + j == z, c == k)
            copy = pltpu.make_async_remote_copy(
                src_ref=src.at[j, k],
                dst_ref=dst,
                send_sem=send.at[j, k],
                recv_sem=recv.at[z],
                device_id=(x, y, 2 * c + j, k),
                device_id_type=MESH,
            )

            @pl.when(same)
            def _():
                pltpu.make_async_copy(src.at[j, k], dst, recv.at[z]).start()

            @pl.when(jnp.logical_not(same))
            def _():
                copy.start()

            sent.append((same, copy))
    return sent


def deal_wait(src, wide, recv):
    x, y, z, c = here()
    for s in range(4):
        dst = wide.at[x, y, pl.ds(s * 32, 32), :]
        pltpu.make_async_copy(src.at[0, 0], dst, recv.at[s]).wait()


def deal_done(sent):
    for same, copy in sent:

        @pl.when(jnp.logical_not(same))
        def _():
            copy.wait_send()


def shuffle_start(block, dst, send, recv, own):
    x, y, z, c = here()
    mine = pltpu.make_async_copy(block(z), dst, own)
    mine.start()
    sent = [
        push(block(wrap(z + d)), dst, send.at[d - 1], recv.at[d - 1], (x, y, wrap(z + d), c))
        for d in range(1, 4)
    ]
    return mine, sent


def shuffle_wait(started):
    started[0].wait()
    for copy in started[1]:
        copy.wait_recv()


def shuffle_done(started):
    for copy in started[1]:
        copy.wait_send()


def shuffle_sems(name):
    return {f"{name}0": DMA((3,)), f"{name}1": DMA((3,)), f"{name}2": DMA(())}


class RowSum:
    def __init__(self, r, name, parts, own):
        self.parts, self.own = parts, own
        self.theirs, self.landed = r.theirs, r.landed
        self.sems = sems_of(r, name + "s", 4)

    def pairs(self):
        x, y, z, c = here()
        self.pair = {
            k: push(
                self.parts.at[1 - c, wrap(z + 1 + k)],
                self.theirs.at[k],
                self.sems[0].at[k],
                self.sems[1].at[k],
                (x, y, z, 1 - c),
            )
            for k in (1, 0, 2, 3)
        }

    def hops(self):
        x, y, z, c = here()
        self.hop = {}
        for k in (1, 0, 2):
            to = wrap(z + 1 + k)
            self.pair[k].wait_recv()
            both = self.own(to).astype(F32) + self.theirs[k].astype(F32)
            self.theirs[k] = both.astype(BF)
            self.hop[k] = push(
                self.theirs.at[k],
                self.landed.at[k],
                self.sems[2].at[k],
                self.sems[3].at[k],
                (x, y, to, c),
            )

    def result(self):
        x, y, z, c = here()
        self.pair[3].wait_recv()
        value = self.own(z).astype(F32) + self.theirs[3].astype(F32)
        for k in range(3):
            self.hop[k].wait_recv()
            value = value + self.landed[k].astype(F32)
        return value

    def done(self):
        for copy in list(self.pair.values()) + list(self.hop.values()):
            copy.wait_send()


def sum_scratch(*names):
    out = dict(theirs=pltpu.VMEM((4, 64, 2048), BF), landed=pltpu.VMEM((3, 64, 2048), BF))
    for name in names:
        out.update({f"{name}s{n}": DMA((k,)) for n, k in enumerate((4, 4, 3, 3))})
    return out


class Scan:
    def __init__(self, r, back):
        self.back, self.every = back, r.every
        self.total, self.rows, self.cols, self.entry = r.total, r.scan_y, r.scan_x, r.entry
        self.lead_b, self.lead_a = r.lead_b, r.lead_a
        x, y, z, c = here()
        self.sems = sems_of(r, "scan", 8)
        self.swap = Pieces(
            lambda n: self.every.at[c, n],
            lambda n: self.every.at[c, n],
            self.sems[0],
            self.sems[1],
            (x, y, z, 1 - c),
        )
        self.order = [(n, k) for n in range(4) for k in range(2)]
        self.line = list(range(4))
        if back:
            self.order, self.line = self.order[::-1], self.line[::-1]

    def before(self, other, mine):
        return (other > mine) if self.back else (other < mine)

    def pack(self, block, state, decay):
        block[:, 0:512] = state.astype(BF)
        high = decay[:, 0:64].astype(BF).astype(F32)
        both = jnp.concatenate([high, decay[:, 0:64] - high], axis=1)
        block[:, 512:640] = both.astype(BF)

    def unpack(self, block):
        both = block[:, 512:640].astype(F32)
        keep = both[:, 0:64] + both[:, 64:128]
        return block[:, 0:512].astype(F32), jnp.concatenate([keep, keep], axis=1)

    def factor(self, k, n, width):
        return jnp.concatenate([self.every[k, n, :, 1024:1152]] * (width // 128), axis=1)

    def pair(self, n):
        self.swap.start(n)

    def send(self):
        x, y, z, c = here()
        self.swap.wait_recv(4)
        half = pl.ds(pl.multiple_of(c * DK, DK), DK)
        n, k = self.order[0]
        state = self.every[k, n, :, half]
        decay = self.every[k, n, :, 1024:1152]
        for n, k in self.order[1:]:
            state = self.factor(k, n, DK) * state + self.every[k, n, :, half]
            decay = self.every[k, n, :, 1024:1152] * decay
        self.pack(self.rows.at[y], state, decay)
        self.far = [
            push(
                self.rows.at[y],
                self.rows.at[y],
                self.sems[2].at[d - 1],
                self.sems[3].at[d - 1],
                (x, wrap(y + d), z, c),
            )
            for d in range(1, 4)
        ]

    def middle(self):
        x, y, z, c = here()
        for copy in self.far:
            copy.wait_recv()
        state, decay = jnp.zeros((SLOTS, DK), F32), jnp.ones((SLOTS, 128), F32)
        lead_b, lead_a = state, decay
        for k in self.line:
            term, keep = self.unpack(self.rows.at[k])
            wide = jnp.concatenate([keep] * 4, axis=1)
            valid = self.before(k, y)
            lead_b = jnp.where(valid, wide * lead_b + term, lead_b)
            lead_a = jnp.where(valid, keep * lead_a, lead_a)
            state, decay = wide * state + term, keep * decay
        self.lead_b[...], self.lead_a[...] = lead_b, lead_a
        self.pack(self.cols.at[x], state, decay)
        self.far += [
            push(
                self.cols.at[x],
                self.cols.at[x],
                self.sems[6].at[d - 1],
                self.sems[7].at[d - 1],
                (wrap(x + d), y, z, c),
            )
            for d in range(1, 4)
        ]

    def fold(self, out):
        x, y, z, c = here()
        for copy in self.far[3:]:
            copy.wait_recv()
        state = jnp.zeros((SLOTS, DK), F32)
        for k in self.line:
            term, keep = self.unpack(self.cols.at[k])
            fresh = jnp.concatenate([keep] * 4, axis=1) * state + term
            state = jnp.where(self.before(k, x), fresh, state)
        state = jnp.concatenate([self.lead_a[...]] * 4, axis=1) * state + self.lead_b[...]
        self.total[...] = state
        self.entry[c] = state
        self.last = push(
            self.total, self.entry.at[c], self.sems[4], self.sems[5], (x, y, z, 1 - c)
        )
        self.last.wait_recv()
        for s in range(2):
            state = self.entry[s]
            cols = pl.ds(s * DK, DK)
            for n, k in self.order:

                @pl.when(c == k)
                def _():
                    out[n, :, cols] = state

                state = self.factor(k, n, DK) * state + self.every[k, n, :, cols]

    def done(self):
        self.swap.wait_send(4)
        for copy in self.far + [self.last]:
            copy.wait_send()


def scan_scratch():
    out = dict(
        every=pltpu.VMEM((2, 4, SLOTS, 1152), F32),
        total=pltpu.VMEM((SLOTS, DK), F32),
        scan_y=pltpu.VMEM((4, SLOTS, 640), BF),
        scan_x=pltpu.VMEM((4, SLOTS, 640), BF),
        lead_b=pltpu.VMEM((SLOTS, DK), F32),
        lead_a=pltpu.VMEM((SLOTS, 128), F32),
        entry=pltpu.VMEM((2, SLOTS, DK), F32),
    )
    kinds = ((4,), (4,), (3,), (3,), (), (), (3,), (3,))
    out.update({f"scan{n}": DMA(shape) for n, shape in enumerate(kinds)})
    return out


def places():
    row = lax.broadcasted_iota(jnp.int32, (CHUNK, CHUNK), 0)
    col = lax.broadcasted_iota(jnp.int32, (CHUNK, CHUNK), 1)
    return row, col


def tri(lower):
    row, col = places()
    return ((row >= col) if lower else (row <= col)).astype(F32)


def seen_mask(offs):
    row, col = places()
    return jnp.logical_and(row >= col, offs >= (row - col).astype(F32))


def carried(cum, offs):
    return jnp.exp(cum) * (offs > places()[0].astype(F32)).astype(F32)


def reaching(cum, offs):
    final = offs[CHUNK - 1 : CHUNK]
    tail = (places()[0].astype(F32) >= CHUNK - 1 - final).astype(F32)
    return jnp.exp(cum[CHUNK - 1 : CHUNK] - cum) * tail


def features(ref, n, which):
    cols = pl.ds(which * HALF, HALF)
    return jnp.concatenate([ref[0, n, :, cols], ref[1, n, :, cols]], axis=1)


def tiles(value):
    return [value[8 * b : 8 * b + 8] for b in range(CHUNK // 8)]


def one_row(blocks, i):
    return blocks[i // 8][i % 8 : i % 8 + 1]


def spans(cum, i):
    last = one_row(cum, i)
    return [(b, jnp.exp(jnp.minimum(cum[b] - last, 0.0))) for b in range(i // 8, CHUNK // 8)]


def weigh(cum, write, columns):
    cum, write, cols = tiles(cum), tiles(write), tiles(columns)
    total = [jnp.zeros((8, SLOTS), F32) for _ in range(CHUNK // 8)]
    for i in range(CHUNK):
        scale = one_row(write, i)
        for b, span in spans(cum, i):
            total[b] = total[b] + cols[b][:, i : i + 1] * (span * scale)
    return jnp.concatenate(total, axis=0)


def weigh_slots(cum, write, values):
    cum, write, vals = tiles(cum), tiles(write), tiles(values)
    lane = lax.broadcasted_iota(jnp.int32, (8, CHUNK), 1)
    total = [jnp.zeros((8, CHUNK), F32) for _ in range(CHUNK // 8)]
    for i in range(CHUNK):
        scale = one_row(write, i)
        for b, span in spans(cum, i):
            got = jnp.sum(vals[b] * (span * scale), axis=1, keepdims=True)
            total[b] = jnp.where(lane == i, got, total[b])
    return jnp.concatenate(total, axis=0)


def chunk_ends(key, value, lam, write, offs):
    cum = dot(tri(True), lam, precision=HIGH)
    ending = (reaching(cum, offs) * write).astype(BF)
    keep = (offs[CHUNK - 1 : CHUNK, 0:1] > CHUNK - 1).astype(F32)
    keep = keep * jnp.exp(tn(lam, jnp.ones((CHUNK, 128), F32), HIGH))
    return cum, jnp.concatenate([tn(ending, key), tn(ending, value), keep], axis=1)


def chunk_near(query, key, cum, write, offs):
    return weigh(cum, write, jnp.where(seen_mask(offs), nt(query, key) * SCALE, 0.0))


def chunk_out(query, value, cum, write, offs, near, state):
    carry = carried(cum, offs)
    far = nt(query, state[:, 0:512].astype(BF)) * SCALE
    scores = near + carry * far
    scores = jnp.exp(scores - jnp.max(scores, axis=1, keepdims=True))
    probs = scores / jnp.sum(scores, axis=1, keepdims=True)
    mixing = jnp.where(seen_mask(offs), weigh_slots(cum, write, probs), 0.0)
    mixed = dot(mixing.astype(BF), value) + dot(
        (probs * carry).astype(BF), state[:, 512:1024].astype(BF)
    )
    return far, probs, mixing, mixed


def chunk_back(query, value, g, cum, write, offs, probs, state):
    carry = carried(cum, offs)
    dmix = jnp.where(seen_mask(offs), nt(g, value), 0.0)
    dfar = nt(g, state[:, 512:1024].astype(BF))
    dnear = weigh(cum, write, dmix)
    dprobs = dnear + carry * dfar
    dscore = probs * (dprobs - jnp.sum(probs * dprobs, axis=1, keepdims=True))
    ends_k = tn((SCALE * dscore * carry).astype(BF), query)
    ends_v = tn((probs * carry).astype(BF), g)
    return dmix, dfar, dnear, dscore, ends_k, ends_v


def chunk_pairs(query, key, cum, write, offs, dmix, dscore, probs):
    affinity = jnp.where(seen_mask(offs), nt(query, key) * SCALE, 0.0)
    cums, writes = tiles(cum), tiles(write)
    aff, dmx, dsc, prb = tiles(affinity), tiles(dmix), tiles(dscore), tiles(probs)
    lane = lax.broadcasted_iota(jnp.int32, (8, CHUNK), 1)
    daff = [jnp.zeros((8, CHUNK), F32) for _ in range(CHUNK // 8)]
    fresh = []
    for i in range(CHUNK):
        scale = one_row(writes, i)
        both = jnp.zeros((8, SLOTS), F32)
        for b, span in spans(cums, i):
            got = jnp.sum(dsc[b] * (span * scale), axis=1, keepdims=True)
            daff[b] = jnp.where(lane == i, got, daff[b])
            both = both + (dsc[b] * aff[b][:, i : i + 1] + prb[b] * dmx[b][:, i : i + 1]) * span
        fresh.append(jnp.sum(both, axis=0, keepdims=True))
    return jnp.concatenate(daff, axis=0), jnp.concatenate(fresh, axis=0)


def chunk_last(
    query, key, value, g, lam, write, slope, offs, cum, near, far, probs, mixing, state, dfar, dnear, dscore, daff, fresh, after
):
    carry, seen, reach = carried(cum, offs), seen_mask(offs), reaching(cum, offs)
    daff = jnp.where(seen, daff * SCALE, 0.0).astype(BF)
    ending = (reach * write).astype(BF)
    nk, nv = after[:, 0:512].astype(BF), after[:, 512:1024].astype(BF)
    dq = dot(daff, key) + dot((SCALE * dscore * carry).astype(BF), state[:, 0:512].astype(BF))
    dk = tn(daff, query) + dot(ending, nk)
    dv = tn(mixing.astype(BF), g) + dot(ending, nv)
    dend = (nt(key, nk) + nt(value, nv)) * reach
    dkeep = nt(jnp.ones((8, 1024), F32), after * state, HIGH)[0:1]
    keep = (offs[CHUNK - 1 : CHUNK] > CHUNK - 1).astype(F32) * jnp.exp(cum[CHUNK - 1 : CHUNK])
    scaled = write * dend
    dcum = dscore * near + probs * dnear + carry * (dscore * far + probs * dfar)
    dcum = dcum - write * fresh - scaled
    at_end = jnp.sum(scaled, axis=0, keepdims=True) + dkeep * keep
    dcum = dcum + jnp.where(places()[0] == CHUNK - 1, at_end, 0.0)
    dlam = dot(tri(False), dcum, precision=HIGH) - jnp.exp(lam) * (fresh + dend)
    return dq, dk, dv, dlam * slope


def log1p_small(u):
    series = u * (1 - u * (1 / 2 - u * (1 / 3 - u / 4)))
    return jnp.where(u < 0.01, series, jnp.log(1 + u))


def one_less_exp(v):
    series = -v * (1 + v * (1 / 2 + v * (1 / 6 + v / 24)))
    return jnp.where(v > -0.03, series, 1 - jnp.exp(v))


def forget_gate(logits):
    small = jnp.exp(-jnp.abs(logits))
    lam = (jnp.minimum(logits, 0.0) - log1p_small(small)) / 8
    slope = jnp.where(logits >= 0, small, 1.0) / (1 + small) / 8
    return lam, one_less_exp(lam), slope


def prepare(r):
    x, y, z, c = here()
    first = rms(r.inputs[...].astype(F32), r.norm1_gain[...]).astype(BF)
    r.first_own[...] = first
    for j in range(2):
        for k in range(2):
            cols = slice((2 * j + k) * HALF, (2 * j + k + 1) * HALF)
            for n, w in enumerate((r.key_weight, r.value_weight)):
                r.wk[j, k, :, n * HALF : (n + 1) * HALF] = w[:, cols]
            for n, w in enumerate((r.query_weight, r.gate_weight, r.out_weight)):
                r.wm[j, k, :, n * HALF : (n + 1) * HALF] = w[:, cols]
    lowrank = nt(first, r.low_down[...])
    r.lowrank[...] = lowrank
    logits = dot(lowrank, r.low_up[...].astype(F32), precision=HIGH) + r.forget_bias[...]
    lam, write, slope = forget_gate(logits.astype(BF).astype(F32))
    row = lax.broadcasted_iota(jnp.int32, (64, 128), 0)
    col = lax.broadcasted_iota(jnp.int32, (64, 128), 1)
    offs = jnp.where(col == row + 64 * c, r.offsets[...].astype(F32), 0.0)
    offs = jnp.broadcast_to(jnp.sum(offs, axis=1, keepdims=True), (64, SLOTS))
    for h in range(4):
        cols = slice(h * SLOTS, (h + 1) * SLOTS)
        r.packed[h, 0] = jnp.concatenate([lam[:, cols], write[:, cols]], axis=1)
        r.packed[h, 1] = jnp.concatenate([slope[:, cols], offs], axis=1)
    for k in range(4):
        for n, w in enumerate((r.ffn_gate, r.ffn_up, r.ffn_down)):
            piece = w[:, k * UNITS : (k + 1) * UNITS]
            pad = jnp.zeros((32, UNITS_PAD - UNITS), BF)
            r.wf[k, :, n * UNITS_PAD : (n + 1) * UNITS_PAD] = jnp.concatenate([piece, pad], axis=1)


def gate_of(r, n, kind):
    return r.gate[n, kind]


def tile(n, width=HALF, start=0):
    return pl.ds(pl.multiple_of(start + n * width, width), width)


def all_rows(ref, *at):
    value = ref[at] if at else ref[...]
    return value.reshape(512, value.shape[-1])


def columns(ref, cols):
    return ref[:, :, :, cols].reshape(2048, -1)


def forward_kernel(r):
    x, y, z, c = here()
    partner = (x, y, z, 1 - c)
    scan = Scan(r, False)
    r.start()
    greet(all_peers())
    prepare(r)
    greeted(all_peers())
    kv = Spread(r, "kv_spread", r.wide_k, 0, 2 * HALF, ring=False)
    mix = Spread(r, "m_spread", r.wide_m, 0, 3 * HALF)
    down = Spread(r, "d_spread", r.wide_f, 2 * UNITS_PAD, UNITS_PAD)
    acts = Spread(r, "f_spread", r.wide_f, 0, 2 * UNITS_PAD)
    a_sems, b_sems, s_sems = (sems_of(r, n, 5) for n in ("rows_a_", "rows_b_", "rows_s_"))
    k_deal = deal_start(r.wk, r.wide_k, r.k_send, r.k_recv)
    deal_wait(r.wk, r.wide_k, r.k_recv)
    kv.near()
    kv.far(0)
    a_rows = rows_start(r.first_own, r.first, a_sems)
    gates = shuffle_start(lambda k: r.packed.at[k], r.gates.at[z], *sems_of(r, "gate", 3))
    m_deal = deal_start(r.wm, r.wide_m, r.m_send, r.m_recv)
    kv.far(1, 2, 3)
    deal_wait(r.wm, r.wide_m, r.m_recv)
    mix.near()
    rows_finish(a_rows, r.first, a_sems)
    f_deal = shuffle_start(
        lambda k: r.wf.at[k],
        r.wide_f.at[x, y, pl.ds(pl.multiple_of(z * 32, 32), 32), :],
        *sems_of(r, "deal", 3),
    )
    shuffle_wait(gates)
    for n in range(4):
        for kind in range(4):
            r.gate[n, kind] = r.gates[n, kind // 2, :, (kind % 2) * SLOTS : (kind % 2 + 1) * SLOTS]
    kv.arrive()
    mix.far(0, 1, 2, 3)
    r.save("wide_k", "first", "gate")

    swap = Pieces(
        lambda n: r.proj.at[1 - c, :, :, tile(n, start=HALF)],
        lambda n: r.qkv.at[c, :, :, tile(n, start=HALF)],
        r.swap_s,
        r.swap_r,
        partner,
    )

    @pl.loop(0, 2)
    def _(n):
        got = dot(all_rows(r.first), columns(r.wide_k, tile(n)))
        r.proj[:, :, :, tile(n, start=HALF)] = got.astype(BF).reshape(2, 4, 64, HALF)
        swap.start(n)
        r.qkv[c, :, :, tile(n, start=HALF)] = r.proj[c, :, :, tile(n, start=HALF)]

    shuffle_wait(f_deal)
    down.near()
    swap.wait_recv(2)

    @pl.loop(0, 4)
    def _(n):
        cum, ends = chunk_ends(
            features(r.qkv, n, 1), features(r.qkv, n, 2), gate_of(r, n, 0), gate_of(r, n, 1), gate_of(r, n, 3)
        )
        r.cum[n] = cum
        r.every[c, n] = ends
        r.decays[n] = ends[:, 1024:1152]
        scan.pair(n)

    mix.relay(0, 1, 2, 3)
    scan.send()
    acts.near()
    acts.far(0)
    b_rows = rows_start(r.rows_b, r.cot, b_sems)
    mix.arrive()
    r.save("wide_m")
    got = dot(all_rows(r.first), columns(r.wide_m, pl.ds(0, HALF)))
    query = pl.ds(0, HALF)
    r.proj[:, :, :, query] = got.astype(BF).reshape(2, 4, 64, HALF)
    swap_q = push(
        r.proj.at[1 - c, :, :, query],
        r.qkv.at[c, :, :, query],
        r.swap_s.at[2],
        r.swap_r.at[2],
        partner,
    )
    r.qkv[c, :, :, query] = r.proj[c, :, :, query]
    scan.middle()
    down.far(0)
    got = dot(all_rows(r.first), columns(r.wide_m, pl.ds(HALF, HALF)))
    r.gate_lin[...] = got.reshape(2, 4, 64, HALF)
    swap_q.wait()
    r.save("qkv")

    @pl.loop(0, 4)
    def _(n):
        r.near[n] = chunk_near(
            features(r.qkv, n, 0), features(r.qkv, n, 1), r.cum[n], gate_of(r, n, 1), gate_of(r, n, 3)
        )

    scan.fold(r.states)
    acts.far(1, 2, 3)
    down.far(1, 2, 3)
    swap2 = Pieces(
        lambda n: r.normed.at[1 - c, n],
        lambda n: r.headnorm.at[c, n],
        r.norm_s,
        r.norm_r,
        partner,
    )

    @pl.loop(0, 4)
    def _(n):
        far, probs, mixing, mixed = chunk_out(
            features(r.qkv, n, 0),
            features(r.qkv, n, 2),
            r.cum[n],
            gate_of(r, n, 1),
            gate_of(r, n, 3),
            r.near[n],
            r.states[n],
        )
        r.far[n], r.probs[n], r.mixing[n], r.mixed[n] = far, probs, mixing, mixed
        normed = rms(mixed, r.head_gain[...])
        for s in range(2):
            r.normed[s, n] = normed[:, s * HALF : (s + 1) * HALF]
        swap2.start(n)

    r.headnorm[c] = r.normed[c]
    r.save("cum", "decays", "states", "near", "far", "probs", "mixing", "mixed", "gate_lin")
    rows_finish(b_rows, r.cot, b_sems)
    r.save("cot")
    acts.relay(0)
    down.relay(0)
    swap2.wait_recv(4)
    sums = RowSum(r, "mix", r.parts, lambda k: r.parts[c, k])
    for core in (1 - c, c):
        lin = r.gate_lin[core].reshape(256, HALF)
        branch = (r.headnorm[core].reshape(256, HALF) * (lin * jax.nn.sigmoid(lin))).astype(BF)
        r.branch[core] = branch.reshape(4, 64, HALF)

        @pl.loop(0, 4)
        def _(n):
            got = nt(branch, r.wide_m[n, :, :, 2 * HALF : 3 * HALF].reshape(512, HALF))
            r.parts[core, :, :, tile(n, 512)] = got.astype(BF).reshape(4, 64, 512)

        if core is not c:
            sums.pairs()
    r.save("headnorm", "branch")
    sums.hops()
    resid1 = r.inputs[...].astype(F32) + sums.result()
    r.resid1[...] = resid1
    r.second_own[...] = rms(resid1, r.norm2_gain[...]).astype(BF)
    s_rows = rows_start(r.second_own, r.second, s_sems)
    down.relay(1, 2, 3)
    acts.relay(1, 2, 3)
    down.arrive()

    @pl.loop(0, 3)
    def _(n):
        r.grad_hidden[:, tile(n)] = dot(
            all_rows(r.cot), columns(r.wide_f, tile(n, start=2 * UNITS_PAD))
        )

    rows_finish(s_rows, r.second, s_sems)
    r.save("second")
    acts.arrive()

    @pl.loop(0, 3)
    def _(n):
        second = all_rows(r.second)
        gate = dot(second, columns(r.wide_f, tile(n)))
        up = dot(second, columns(r.wide_f, tile(n, start=UNITS_PAD)))
        grad = r.grad_hidden[:, tile(n)]
        sig = jax.nn.sigmoid(gate)
        silu = gate * sig
        parts = (grad * up * sig * (1 + gate * (1 - sig)), grad * silu, silu * up)
        for m, part in enumerate(parts):
            r.acts[m, :, :, :, tile(n)] = part.astype(BF).reshape(2, 4, 64, HALF)

    r.save("acts")

    @pl.loop(0, 4)
    def _(n):
        got = nt(all_rows(r.acts, 0), r.wide_f[n, :, :, 0:UNITS_PAD].reshape(512, UNITS_PAD))
        got = got + nt(
            all_rows(r.acts, 1), r.wide_f[n, :, :, UNITS_PAD : 2 * UNITS_PAD].reshape(512, UNITS_PAD)
        )
        r.second_part[:, :, :, tile(n, 512)] = got.astype(BF).reshape(2, 4, 64, 512)

    r.save("second_part")

    @pl.loop(0, 4)
    def _(n):
        got = nt(all_rows(r.acts, 2), r.wide_f[n, :, :, 2 * UNITS_PAD :].reshape(512, UNITS_PAD))
        r.ffn_part[:, :, :, tile(n, 512)] = got.astype(BF).reshape(2, 4, 64, 512)

    r.save("ffn_part")
    swap.wait_send(2)
    swap2.wait_send(4)
    for sent in (k_deal, m_deal):
        deal_done(sent)
    for sent in (gates, f_deal):
        shuffle_done(sent)
    for part in (kv, mix, down, acts, scan, sums):
        part.done()
    r.finish()


def forward(operands):
    square = ((4, 64, 64), F32)
    rows = (2, 4, 64, 2048)
    scratch = dict(
        proj=pltpu.VMEM((2, 4, 64, 3 * HALF), BF),
        normed=pltpu.VMEM((2, 4, 64, HALF), F32),
        parts=pltpu.VMEM(rows, BF),
        second_own=pltpu.VMEM((64, 2048), BF),
        grad_hidden=pltpu.VMEM((512, UNITS_PAD), F32),
        wide_f=pltpu.VMEM((4, 4, 128, FFN), BF),
        wk=pltpu.VMEM((2, 2, 32, 2 * HALF), BF),
        wm=pltpu.VMEM((2, 2, 32, 3 * HALF), BF),
        wf=pltpu.VMEM((4, 32, FFN), BF),
        packed=pltpu.VMEM((4, 2, 64, 2 * SLOTS), F32),
        gates=pltpu.VMEM((4, 2, 64, 2 * SLOTS), F32),
        k_send=DMA((2, 2)),
        k_recv=DMA((4,)),
        m_send=DMA((2, 2)),
        m_recv=DMA((4,)),
        swap_s=DMA((3,)),
        swap_r=DMA((3,)),
        norm_s=DMA((4,)),
        norm_r=DMA((4,)),
    )
    for name in ("rows_a_", "rows_b_", "rows_s_"):
        scratch.update(rows_sems(name))
    for name in ("kv_spread", "m_spread", "d_spread", "f_spread"):
        scratch.update(spread_sems(name))
    for name in ("gate", "deal"):
        scratch.update(shuffle_sems(name))
    scratch.update(scan_scratch())
    scratch.update(sum_scratch("mix"))
    return remote_call(
        forward_kernel,
        1,
        {name: (value, ANY if name == "rows_b" else VMEM) for name, value in operands.items()},
        dict(
            first_own=((64, 2048), BF, VMEM),
            lowrank=((64, 16), F32, VMEM),
            resid1=((64, 2048), F32, VMEM),
        ),
        scratch,
        saved=dict(
            wide_k=((4, 4, 128, 2 * HALF), BF),
            wide_m=((4, 4, 128, 3 * HALF), BF),
            first=(rows, BF),
            cot=(rows, BF),
            second=(rows, BF),
            gate=((4, 4, 64, SLOTS), F32),
            qkv=((2, 4, 64, 3 * HALF), BF),
            cum=square,
            near=square,
            far=square,
            probs=square,
            mixing=square,
            decays=((4, SLOTS, 128), F32),
            states=((4, SLOTS, 1024), F32),
            mixed=((4, 64, DK), F32),
            gate_lin=((2, 4, 64, HALF), F32),
            headnorm=((2, 4, 64, HALF), F32),
            branch=((2, 4, 64, HALF), BF),
            acts=((3, 2, 4, 64, UNITS_PAD), BF),
            second_part=(rows, BF),
            ffn_part=(rows, BF),
        ),
    )


class WeightSum:
    def __init__(self, r, name, grads, cols, loaded):
        self.grads, self.cols, self.half, self.loaded = grads, cols, cols // 2, loaded
        self.far, self.landed, self.ready, self.past = sems_of(r, name + "b", 4)
        self.sems = sems_of(r, name + "s", 6)
        if loaded:
            self.own, self.own_sem = getattr(r, name + "own"), getattr(r, name + "own_s")
            self.held, self.held_sem = getattr(r, name + "held"), getattr(r, name + "held_s")
        self.fars, self.nears, self.owns, self.pasts = {}, {}, {}, {}

    def part(self, side):
        return pl.ds(side * self.half, self.half)

    def block(self, side, k, d, rows=slice(None)):
        x, y, z, c = here()
        if side == 0:
            return self.grads.at[wrap(x + d), wrap(y + k), rows, self.part(0)]
        return self.grads.at[wrap(x + k), wrap(y + d), rows, self.part(1)]

    def peer(self, side, d):
        x, y, z, c = here()
        return (wrap(x + d), y, z, c) if side == 0 else (x, wrap(y + d), z, c)

    def mine(self, side, k):
        return self.own.at[side, k] if self.loaded else self.block(side, k, 0)

    def load(self, side, k):
        if self.loaded:
            self.owns[side, k] = pltpu.make_async_copy(
                self.block(side, k, 0), self.own.at[side, k], self.own_sem.at[side, k]
            )
            self.owns[side, k].start()

    def push_far(self, src, side, k, d, n, rows):
        self.fars[side, k, n] = push(
            src,
            self.far.at[side, k, d // 2, rows],
            self.sems[0].at[side, k, n],
            self.sems[1].at[side, k, n],
            self.peer(side, d),
        )

    def push_one(self, side, k, d):
        if d == 2:
            for n, to in enumerate((1, 3)):
                self.pasts[side, k, n] = push(
                    self.block(side, k, 2, pl.ds(n * 64, 64)),
                    self.past.at[side, k, n],
                    self.sems[4].at[side, k, n],
                    self.sems[5].at[side, k, n],
                    self.peer(side, to),
                )
        else:
            rows = pl.ds(64 if d == 1 else 0, 64)
            self.push_far(self.block(side, k, d, rows), side, k, d, d // 2, rows)

    def send(self, e):
        for k in (1, 2, 3, 0):
            if e > 0:
                self.push_one(0, k, e)
            else:
                self.load(0, k)
            if k > 0:
                self.push_one(1, e, k)
        self.load(1, e)

    def relay(self, order):
        keys = [(side, k, n) for k in order for side in range(2) for n in range(2)]
        loads = {}

        def block(at):
            side, k, n = keys[at]
            return self.block(side, k, 2 * n + 1, pl.ds(n * 64, 64))

        def fetch(at):
            loads[at] = pltpu.make_async_copy(
                block(at), self.held.at[at % 4], self.held_sem.at[at % 4]
            )
            loads[at].start()

        if self.loaded:
            for at in range(4):
                fetch(at)
        for at, (side, k, n) in enumerate(keys):
            if self.loaded:
                loads[at].wait()
            self.pasts[side, k, n].wait_recv()
            mine = self.held.at[at % 4] if self.loaded else block(at)

            @pl.loop(0, 4)
            def _(t):
                rows = pl.ds(pl.multiple_of(t * 16, 16), 16)
                both = self.past[side, k, n, rows, :].astype(F32) + mine[rows, :].astype(F32)
                self.past[side, k, n, rows, :] = both.astype(BF)

            rows = pl.ds(n * 64, 64)
            self.push_far(self.past.at[side, k, n], side, k, 2 * n + 1, 2 + n, rows)
            if self.loaded and at + 4 < len(keys):
                fetch(at + 4)

    def arrive(self, side, k):
        if self.loaded:
            self.owns[side, k].wait()
        for n in range(4):
            self.fars[side, k, n].wait_recv()

    def total(self, side, k, rows):
        value = self.mine(side, k)[rows, :].astype(F32)
        for d in range(2):
            value = value + self.far[side, k, d, rows, :].astype(F32)
        return value

    def turn(self, k):
        for side in range(2):
            self.arrive(side, k)

            @pl.loop(0, 8)
            def _(t):
                rows = pl.ds(pl.multiple_of(t * 16, 16), 16)
                self.mine(side, k)[rows, :] = self.total(side, k, rows).astype(BF)

            self.nears[side, k] = push(
                self.mine(side, k),
                self.landed.at[side, k - 1],
                self.sems[2].at[side, k - 1],
                self.sems[3].at[side, k - 1],
                self.peer(1 - side, k),
            )

    def finish(self):
        for side in range(2):
            self.arrive(side, 0)
            for k in range(1, 4):
                self.nears[side, k].wait_recv()

            @pl.loop(0, 8)
            def _(t):
                rows = pl.ds(pl.multiple_of(t * 16, 16), 16)
                value = self.total(side, 0, rows)
                for k in range(3):
                    value = value + self.landed[side, k, rows, :].astype(F32)
                self.ready[rows, self.part(side)] = value.astype(BF)

    def done(self):
        for copies in (self.fars, self.nears, self.pasts):
            for copy in copies.values():
                copy.wait_send()


def weight_scratch(name, cols, loaded):
    half = cols // 2
    out = {
        f"{name}b0": pltpu.VMEM((2, 4, 2, 128, half), BF),
        f"{name}b1": pltpu.VMEM((2, 3, 128, half), BF),
        f"{name}b2": pltpu.VMEM((128, cols), BF),
        f"{name}b3": pltpu.VMEM((2, 4, 2, 64, half), BF),
    }
    kinds = ((2, 4, 4), (2, 4, 4), (2, 3), (2, 3), (2, 4, 2), (2, 4, 2))
    out.update({f"{name}s{n}": DMA(shape) for n, shape in enumerate(kinds)})
    if loaded:
        out[f"{name}own"] = pltpu.VMEM((2, 4, 128, half), BF)
        out[f"{name}own_s"] = DMA((2, 4))
        out[f"{name}held"] = pltpu.VMEM((4, 64, half), BF)
        out[f"{name}held_s"] = DMA((4,))
    return out


def return_start(ready, out, send, recv):
    x, y, z, c = here()
    dst, arrived = out.at[lax.rem(z, 2), c], recv.at[lax.rem(z, 2), c]
    sent = []
    for k in range(4):
        src = ready.at[pl.ds(k * 32, 32), :]
        same = jnp.logical_and(k == z, c == z // 2)
        copy = pltpu.make_async_remote_copy(
            src_ref=src,
            dst_ref=dst,
            send_sem=send.at[k],
            recv_sem=arrived,
            device_id=(x, y, k, z // 2),
            device_id_type=MESH,
        )

        @pl.when(same)
        def _():
            pltpu.make_async_copy(src, dst, arrived).start()

        @pl.when(jnp.logical_not(same))
        def _():
            copy.start()

        sent.append((same, copy))
    return sent


def return_wait(ready, out, recv):
    for j in range(2):
        for k in range(2):
            pltpu.make_async_copy(ready.at[pl.ds(0, 32), :], out.at[j, k], recv.at[j, k]).wait()


class SmallSum:
    def __init__(self, r, name, axes):
        self.now, self.held, self.send, self.recv = sems_of(r, name, 4)
        self.axes, self.sent = axes, []

    def start(self, n):
        place = dict(zip("xyzc", here()))
        axis, at = self.axes[n], place[self.axes[n]]
        size = 2 if axis == "c" else 4
        self.held[n, at] = self.now[...]
        self.sent = []
        for d in range(1, size):
            peer = dict(place)
            peer[axis] = wrap(at + d, size)
            self.sent.append(
                push(
                    self.held.at[n, at],
                    self.held.at[n, at],
                    self.send.at[n, d - 1],
                    self.recv.at[n, d - 1],
                    tuple(peer.values()),
                )
            )

    def collect(self, n):
        for copy in self.sent:
            copy.wait()
        value = self.held[n, 0]
        for k in range(1, 2 if self.axes[n] == "c" else 4):
            value = value + self.held[n, k]
        self.now[...] = value


def small_scratch(name, rows, count):
    return {
        f"{name}0": pltpu.VMEM((rows, HALF), F32),
        f"{name}1": pltpu.VMEM((count, 4, rows, HALF), F32),
        f"{name}2": DMA((count, 3)),
        f"{name}3": DMA((count, 3)),
    }


def backward_kernel(r):
    x, y, z, c = here()
    partner = (x, y, z, 1 - c)
    scan = Scan(r, True)
    greet(all_peers())
    mine = pltpu.make_async_copy(r.second_part.at[c], r.mine, r.mine_s.at[0])
    mine.start()
    r.start()
    greeted(all_peers())
    second = RowSum(r, "sec", r.second_part, lambda k: r.mine[k])
    ffn = RowSum(r, "ffn", r.ffn_part, lambda k: r.mine[k])
    units = WeightSum(r, "units", r.out_grads, FFN, True)
    tail = WeightSum(r, "tail", r.grads_tail, 2 * HALF, False)
    last = WeightSum(r, "last", r.grads_last, 3 * HALF, False)
    second.pairs()
    mine.wait()
    second.hops()

    r.need("acts", "second", "cot")
    for e in (1, 2, 3, 0):
        at = wrap(x + e)
        steps = [
            pltpu.make_async_copy(
                r.grads_last.at[n], r.out_grads.at[at, :, :, pl.ds(n * UNITS_PAD, UNITS_PAD)], r.stage_s.at[n]
            )
            for n in range(3)
        ]
        for n, left in enumerate((r.second, r.second, r.cot)):
            got = tn(left[:, :, :, tile(at, 512)].reshape(512, 512), all_rows(r.acts, n))
            r.grads_last[n] = got.astype(BF).reshape(4, 128, UNITS_PAD)
            steps[n].start()
        for copy in steps:
            copy.wait()
        units.send(e)
    r.need("resid1", "cot_own")
    e = second.result()
    second.done()
    mine = pltpu.make_async_copy(r.ffn_part.at[c], r.mine, r.mine_s.at[1])
    mine.start()
    grad, d_norm2 = rms_back(r.resid1[...], r.norm2_gain[...], e)
    group = SmallSum(r, "group", ("c", "z"))
    plane = SmallSum(r, "plane", ("y", "x"))
    tiny = SmallSum(r, "tiny", ("c", "z", "y", "x"))
    group.now[...] = jnp.zeros_like(group.now)

    def split_rows(dst, start, value):
        for n in range(value.shape[1] // HALF):
            dst[start + n : start + n + 1, :] = value[:, n * HALF : (n + 1) * HALF]

    split_rows(group.now, 16, d_norm2)
    grad_resid1 = r.cot_own[...].astype(F32) + grad
    r.attn_own[...] = grad_resid1.astype(BF)
    r.grad_resid1[...] = grad_resid1
    a_sems = sems_of(r, "rows_a_", 5)
    a_rows = rows_start(r.attn_own, r.attn, a_sems)
    rows_finish(a_rows, r.attn, a_sems)
    ffn.pairs()
    units.relay((1, 2, 3, 0))

    r.need("wide_m", "gate_lin", "headnorm")
    grad_branch = dot(all_rows(r.attn), columns(r.wide_m, pl.ds(2 * HALF, HALF)))
    lin, normed = all_rows(r.gate_lin), all_rows(r.headnorm)
    sig = jax.nn.sigmoid(lin)
    grad_lin = (grad_branch * normed * sig * (1 + lin * (1 - sig))).astype(BF)
    r.grad_lin[...] = grad_lin.reshape(2, 4, 64, HALF)
    r.grad_out[...] = (grad_branch * lin * sig).reshape(2, 4, 64, HALF)
    swap = push(r.grad_out.at[1 - c], r.grad_norm.at[c], r.swap_s.at[0], r.swap_r.at[0], partner)
    r.grad_norm[c] = r.grad_out[c]
    r.need("first", "branch")

    @pl.loop(0, 4)
    def _(n):
        got = tn(r.first[:, :, :, tile(n, 512)].reshape(512, 512), all_rows(r.grad_lin))
        r.grads_tail[n, :, :, 0:HALF] = got.astype(BF).reshape(4, 128, HALF)
        got = tn(r.attn[:, :, :, tile(n, 512)].reshape(512, 512), all_rows(r.branch))
        r.grads_tail[n, :, :, HALF : 2 * HALF] = got.astype(BF).reshape(4, 128, HALF)

    for e in (1, 2, 3, 0):
        tail.send(e)
    r.need("mixed", "qkv", "cum", "gate", "probs", "states", "decays")
    swap.wait()
    mine.wait()
    ffn.hops()

    r.d_head[...] = jnp.zeros_like(r.d_head)

    @pl.loop(0, 4)
    def _(n):
        e = jnp.concatenate([r.grad_norm[0, n], r.grad_norm[1, n]], axis=1)
        grad, d_head = rms_back(r.mixed[n], r.head_gain[...], e)
        r.d_head[0:1] += d_head
        g = grad.astype(BF)
        r.grad_mixed[n] = g
        dmix, dfar, dnear, dscore, ends_k, ends_v = chunk_back(
            features(r.qkv, n, 0),
            features(r.qkv, n, 2),
            g,
            r.cum[n],
            gate_of(r, n, 1),
            gate_of(r, n, 3),
            r.probs[n],
            r.states[n],
        )
        r.dmix[n], r.dfar[n], r.dnear[n], r.dscore[n] = dmix, dfar, dnear, dscore
        r.every[c, n] = jnp.concatenate([ends_k, ends_v, r.decays[n]], axis=1)
        scan.pair(n)

    split_rows(group.now, 24, r.d_head[0:1])
    scan.send()

    def pairs_of(n):
        r.daff[n], r.fresh[n] = chunk_pairs(
            features(r.qkv, n, 0),
            features(r.qkv, n, 1),
            r.cum[n],
            gate_of(r, n, 1),
            gate_of(r, n, 3),
            r.dmix[n],
            r.dscore[n],
            r.probs[n],
        )

    pl.loop(0, 2)(pairs_of)
    scan.middle()
    tail.relay((1, 2, 3, 0))
    pl.loop(2, 4)(pairs_of)
    for k in range(1, 4):
        units.turn(k)
    r.need("near", "far", "mixing")
    scan.fold(r.nexts)
    r.output[...] = (r.resid1[...] + ffn.result()).astype(BF)
    ffn.done()
    swap2 = Pieces(
        lambda n: r.dproj.at[1 - c, n], lambda n: r.dqkv.at[c, n], r.dqkv_s, r.dqkv_r, partner
    )

    @pl.loop(0, 4)
    def _(n):
        dq, dk, dv, dlogit = chunk_last(
            features(r.qkv, n, 0),
            features(r.qkv, n, 1),
            features(r.qkv, n, 2),
            r.grad_mixed[n],
            gate_of(r, n, 0),
            gate_of(r, n, 1),
            gate_of(r, n, 2),
            gate_of(r, n, 3),
            r.cum[n],
            r.near[n],
            r.far[n],
            r.probs[n],
            r.mixing[n],
            r.states[n],
            r.dfar[n],
            r.dnear[n],
            r.dscore[n],
            r.daff[n],
            r.fresh[n],
            r.nexts[n],
        )
        for m, part in enumerate((dq, dk, dv)):
            for s in range(2):
                r.dproj[s, n, :, pl.ds(m * HALF, HALF)] = part[
                    :, s * HALF : (s + 1) * HALF
                ].astype(BF)
        swap2.start(n)
        r.dlogit[n] = dlogit

    r.dqkv[c] = r.dproj[c]
    logits = shuffle_start(lambda k: r.dlogit.at[k], r.dl.at[z], *sems_of(r, "gate", 3))
    swap2.wait_recv(4)

    for e in (1, 2, 3, 0):
        at = wrap(x + e)
        got = tn(r.first[:, :, :, tile(at, 512)].reshape(512, 512), all_rows(r.dqkv))
        r.grads_last[at] = got.astype(BF).reshape(4, 128, 3 * HALF)
        last.send(e)

    shuffle_wait(logits)
    r.need("lowrank", "up", "down", "inputs", "wide_k")
    low = jnp.zeros((64, 16), F32)
    bias = []
    for h in range(4):
        dl = r.dl[h]
        low = low + nt(dl, r.up[:, h * SLOTS : (h + 1) * SLOTS].astype(F32), HIGH)
        group.now[0:16, h * SLOTS : (h + 1) * SLOTS] = tn(r.lowrank[...], dl, HIGH)
        bias.append(jnp.sum(dl, axis=0, keepdims=True))
    split_rows(group.now, 26, jnp.concatenate(bias, axis=1))
    r.low_own[...] = low
    l_sems, d_sems = sems_of(r, "rows_l_", 5), sems_of(r, "rows_d_", 5)
    l_rows = rows_start(r.low_own, r.lows, l_sems)
    group.start(0)
    first_part = r.attn
    first = RowSum(r, "fst", first_part, lambda k: first_part[c, k])
    for core in (1 - c, c):

        @pl.loop(0, 4)
        def _(n):
            dqkv = r.dqkv[core].reshape(256, 3 * HALF)
            got = nt(dqkv[:, HALF:], r.wide_k[n].reshape(512, 2 * HALF))
            left = jnp.concatenate([dqkv[:, 0:HALF], r.grad_lin[core].reshape(256, HALF)], axis=1)
            got = got + nt(left, r.wide_m[n, :, :, 0 : 2 * HALF].reshape(512, 2 * HALF))
            first_part[core, :, :, tile(n, 512)] = got.astype(BF).reshape(4, 64, 512)

        if core is not c:
            first.pairs()
            group.collect(0)
            group.start(1)

    first.hops()
    for k in range(1, 4):
        tail.turn(k)
    last.relay((1, 2, 3, 0))
    rows_finish(l_rows, r.lows, l_sems)
    group.collect(1)
    at = 2 * z + c
    plane.now[0:32] = group.now[...]
    plane.now[32:48] = tn(
        r.lows[...].reshape(512, 16), all_rows(r.first, slice(None), slice(None), slice(None), tile(at)).astype(F32), HIGH
    )
    plane.start(0)
    units.finish()
    units_back = shuffle_start(
        lambda k: units.ready.at[pl.ds(pl.multiple_of(k * 32, 32), 32), :],
        r.units_out.at[z],
        *sems_of(r, "back", 3),
    )
    tail.finish()
    tail_back = return_start(tail.ready, r.tail_out, r.tail_send, r.tail_recv)
    grad_first = first.result() + dot(low, r.down[...].astype(F32), precision=HIGH)
    grad, d_norm1 = rms_back(r.inputs[...].astype(F32), r.norm1_gain[...], grad_first)
    split_rows(tiny.now, 0, d_norm1)
    tiny.start(0)
    r.d_inputs[...] = r.grad_resid1[...] + grad
    tiny.collect(0)
    tiny.start(1)
    last.turn(1)
    last.turn(2)
    last.turn(3)
    plane.collect(0)
    plane.start(1)
    tiny.collect(1)
    tiny.start(2)
    last.finish()
    last_back = return_start(last.ready, r.last_out, r.last_send, r.last_recv)
    plane.collect(1)
    r.down_own[...] = plane.now[32:48]
    d_rows = rows_start(r.down_own, r.down_out, d_sems)
    tiny.collect(2)
    tiny.start(3)
    rows_finish(d_rows, r.down_out, d_sems)
    tiny.collect(3)
    r.small_out[0:32] = plane.now[0:32]
    r.small_out[32:40] = tiny.now[...]
    swap2.wait_send(4)
    shuffle_wait(units_back)
    shuffle_done(units_back)
    shuffle_done(logits)
    return_wait(tail.ready, r.tail_out, r.tail_recv)
    return_wait(last.ready, r.last_out, r.last_recv)
    deal_done(tail_back)
    deal_done(last_back)
    for part in (first, units, tail, last, scan):
        part.done()


def backward(operands):
    rows = (2, 4, 64, 2048)
    small = pltpu.VMEM((4, 64, 64), F32)
    scratch = dict(
        low_own=pltpu.VMEM((64, 16), F32),
        lows=pltpu.VMEM((2, 4, 64, 16), F32),
        down_own=pltpu.VMEM((16, HALF), F32),
        attn_own=pltpu.VMEM((64, 2048), BF),
        grad_resid1=pltpu.VMEM((64, 2048), F32),
        attn=pltpu.VMEM(rows, BF),
        grad_lin=pltpu.VMEM((2, 4, 64, HALF), BF),
        grad_out=pltpu.VMEM((2, 4, 64, HALF), F32),
        grad_norm=pltpu.VMEM((2, 4, 64, HALF), F32),
        grad_mixed=pltpu.VMEM((4, 64, DK), BF),
        d_head=pltpu.VMEM((8, DK), F32),
        dmix=small,
        dfar=small,
        dnear=small,
        dscore=small,
        daff=small,
        fresh=small,
        dlogit=small,
        dl=small,
        nexts=pltpu.VMEM((4, SLOTS, 1024), F32),
        dproj=pltpu.VMEM((2, 4, 64, 3 * HALF), BF),
        dqkv=pltpu.VMEM((2, 4, 64, 3 * HALF), BF),
        mine=pltpu.VMEM((4, 64, 2048), BF),
        mine_s=DMA((2,)),
        stage_s=DMA((3,)),
        grads_tail=pltpu.VMEM((4, 4, 128, 2 * HALF), BF),
        grads_last=pltpu.VMEM((4, 4, 128, 3 * HALF), BF),
        swap_s=DMA((1,)),
        swap_r=DMA((1,)),
        dqkv_s=DMA((4,)),
        dqkv_r=DMA((4,)),
        tail_send=DMA((4,)),
        tail_recv=DMA((2, 2)),
        last_send=DMA((4,)),
        last_recv=DMA((2, 2)),
    )
    for name, cols, loaded in (
        ("units", FFN, True),
        ("tail", 2 * HALF, False),
        ("last", 3 * HALF, False),
    ):
        scratch.update(weight_scratch(name, cols, loaded))
    scratch.update(sum_scratch("sec", "ffn", "fst"))
    for name in ("gate", "back"):
        scratch.update(shuffle_sems(name))
    scratch.update(rows_sems("rows_a_"))
    scratch.update(scan_scratch())
    for name in ("rows_l_", "rows_d_"):
        scratch.update(rows_sems(name))
    for name, height, count in (("group", 32, 2), ("plane", 48, 2), ("tiny", 8, 4)):
        scratch.update(small_scratch(name, height, count))
    in_hbm = ("second_part", "ffn_part")
    in_vmem = ("norm1_gain", "norm2_gain", "head_gain")
    order = ("acts", "second", "cot", "resid1", "cot_own", "wide_m", "gate_lin", "headnorm")
    order += tuple(name for name in operands if name not in order + in_hbm + in_vmem)
    direct = {name: (operands[name], ANY) for name in in_hbm}
    direct.update({name: (operands[name], VMEM) for name in in_vmem})
    return remote_call(
        backward_kernel,
        2,
        direct,
        dict(
            output=((64, 2048), BF, VMEM),
            d_inputs=((64, 2048), F32, VMEM),
            last_out=((2, 2, 32, 3 * HALF), BF, VMEM),
            tail_out=((2, 2, 32, 2 * HALF), BF, VMEM),
            units_out=((4, 32, FFN), BF, VMEM),
            small_out=((40, HALF), F32, VMEM),
            down_out=((2, 4, 16, HALF), F32, VMEM),
            out_grads=((4, 4, 128, FFN), BF, ANY),
        ),
        scratch,
        loaded={name: operands[name] for name in order},
    )


def results_kernel(*refs):
    sources, outs, held, sems = refs[:7], refs[7:23], refs[23:30], refs[30]
    copies = [
        pltpu.make_async_copy(src, dst, sems.at[n]) for n, (src, dst) in enumerate(zip(sources, held))
    ]
    for copy in copies:
        copy.start()
    for copy in copies:
        copy.wait()
    out, d_in, last, tail, units, small, factor = held
    output, d_inputs, norm1, q, k, v, g, o, down, up, bias, head, norm2, fg, fu, fd = outs
    output[...] = out[...]
    d_inputs[...] = d_in[...]
    for j in range(2):
        for n in range(2):
            at = slice((2 * j + n) * HALF, (2 * j + n + 1) * HALF)
            for m, ref in enumerate((q, k, v)):
                ref[:, at] = last[j, n, :, m * HALF : (m + 1) * HALF].astype(F32)
            g[:, at] = tail[j, n, :, 0:HALF].astype(F32)
            o[:, at] = tail[j, n, :, HALF : 2 * HALF].astype(F32)
    for n in range(4):
        at = slice(n * UNITS, (n + 1) * UNITS)
        for m, ref in enumerate((fg, fu, fd)):
            ref[:, at] = units[n, :, m * UNITS_PAD : m * UNITS_PAD + UNITS].astype(F32)
    up[...] = small[0:16]
    for n in range(8):
        cols = slice(n * HALF, (n + 1) * HALF)
        norm2[:, cols] = small[16 + n : 17 + n]
        norm1[:, cols] = small[32 + n : 33 + n]
        down[:, cols] = factor[n % 2, n // 2]
    for n in range(2):
        head[:, n * HALF : (n + 1) * HALF] = small[24 + n : 25 + n]
    bias[...] = small[26:27]


def results(b):
    shapes = [((64, 2048), BF), ((64, 2048), F32), ((1, 2048), F32)]
    shapes += [((32, 1024), F32)] * 5 + [((16, 2048), F32), ((16, 256), F32)]
    shapes += [((1, 256), F32), ((1, 512), F32), ((1, 2048), F32)] + [((32, 4 * UNITS), F32)] * 3
    names = ("output", "d_inputs", "last_out", "tail_out", "units_out", "small_out", "down_out")
    sources = [b[name] for name in names]
    call = pl.pallas_call(
        results_kernel,
        out_shape=[jax.ShapeDtypeStruct(shape, dtype) for shape, dtype in shapes],
        in_specs=[ANY] * 7,
        scratch_shapes=[pltpu.VMEM(v.shape, v.dtype) for v in sources] + [DMA((7,))],
        compiler_params=pltpu.CompilerParams(vmem_limit_bytes=63 * 2**20),
    )
    out = list(call(*sources))
    out[7], out[8] = out[7].T, out[8].T
    for n in (2, 10, 11, 12):
        out[n] = out[n][0]
    return tuple(out)


def rms(v, gain):
    return v * lax.rsqrt(jnp.mean(v * v, axis=-1, keepdims=True) + EPS) * gain


def rms_back(v, gain, e):
    r = lax.rsqrt(jnp.mean(v * v, axis=-1, keepdims=True) + EPS)
    grad = r * gain * e - v * (r * r * r) * jnp.mean(v * gain * e, axis=-1, keepdims=True)
    return grad, jnp.sum(e * v * r, axis=0, keepdims=True)


def body(
    inputs,
    offsets,
    norm1_gain,
    query_weight,
    key_weight,
    value_weight,
    gate_weight,
    out_weight,
    low_down,
    low_up,
    forget_bias,
    head_gain,
    norm2_gain,
    ffn_gate,
    ffn_up,
    ffn_down,
    cotangent,
):
    gain1, gain2, gain_head = norm1_gain[None], norm2_gain[None], head_gain[None]
    f = forward(
        dict(
            query_weight=query_weight,
            key_weight=key_weight,
            value_weight=value_weight,
            gate_weight=gate_weight,
            out_weight=out_weight.T,
            ffn_gate=ffn_gate,
            ffn_up=ffn_up,
            ffn_down=ffn_down,
            inputs=inputs,
            rows_b=cotangent,
            offsets=offsets[None],
            low_down=low_down.T,
            low_up=low_up,
            forget_bias=forget_bias[None],
            norm1_gain=gain1,
            norm2_gain=gain2,
            head_gain=gain_head,
        )
    )

    operands = dict(
        {name: value for name, value in f.items() if name != "first_own"},
        cot_own=cotangent,
        inputs=inputs,
        up=low_up,
        down=low_down.T,
        norm1_gain=gain1,
        norm2_gain=gain2,
        head_gain=gain_head,
    )
    b = backward(operands)
    return results(b)


def solution(mesh):
    fine = Mesh(mesh.devices.reshape(4, 4, 4, 2), ("x", "y", "z", "c"))
    seq = ("x", "y", "z")
    rows = P(("x", "y", "z", "c"), None)
    wide = P(seq, "c")
    placed = (
        (rows, P(seq), P())
        + (wide,) * 4
        + (P("c", seq), P(), P(), P(), P(), P(), wide, wide, wide, rows)
    )
    return jax.shard_map(
        body,
        mesh=fine,
        in_specs=placed,
        out_specs=(rows, rows, P())
        + (wide,) * 4
        + (P("c", seq), P(), P(), P(), P(), P(), wide, wide, wide),
        check_vma=False,
    )
```
